32 devices in a mesh: seq: 16 (over z, y, x), head: 2 (over core).
Axes of the slice: x: 2, y: 2, z: 4, core: 2. Of those that a mesh axis runs over, the one named last changes fastest.
Arguments:
- queries: bfloat16 [2048, 1024], P('seq', 'head'), may hold values from -6 to 6
- key_rows: bfloat16 [2048, 1024], P('seq', 'head'), may hold values from -6 to 6
- values: bfloat16 [2048, 2048], P('seq', 'head'), may hold values from -6 to 6
- out_gate: bfloat16 [2048, 2048], P('seq', 'head'), may hold values from -6 to 6
- write_rate: float32 [16, 2048], P('head', 'seq'), may hold values from 0 to 1
- log_decay: float32 [16, 2048], P('head', 'seq'), may hold values from -1 to 0, as said below
- norm_gain: float32 [128], replicated, may hold values from 0.1 to 1.9
- out_weight: bfloat16 [2048, 2048], P('head'), may hold values from -0.125 to 0.125
Outputs:
- layer_out: bfloat16 [2048, 2048], P('seq', 'head')
The draws below stay inside these ranges and needn't reach their ends.
Inputs may be any that keep to these rules, and one draw needn't show every extreme that they name: `log_decay`: log decay of each value head and token, negative.
All inputs are finite; a program needn't handle non-finite values.
Results may differ from the reference program's by a relative error of at most 0.009.
Values may be sent and summed in bfloat16 or wider, within the bound.
No kernel may reach another device: no remote copies, remote signals or barrier semaphores. Data moves between devices by JAX's collectives and lax.ppermute only.
A program may use at most 320 MiB of HBM per device.

```python
import math
import jax
import jax.numpy as jnp
from jax import lax

D = 2048
VALUE_HEAD_COUNT = 16
HK = 8
DK = 128
DV = 128
SPAN = 64
TOK_DEV = 128
PROMPT_TOKENS = 2048


def slow_heads(key):
    share = 0.5
    return jax.random.uniform(jax.random.fold_in(key, 11), (VALUE_HEAD_COUNT,)) < share


def draw_write_rate(key, part):
    sluggish_mask = slow_heads(key)
    fast_vals = jax.random.uniform(jax.random.fold_in(key, 23), (VALUE_HEAD_COUNT, PROMPT_TOKENS), jnp.float32, 0.3, 0.9)
    slow_log = jax.random.uniform(jax.random.fold_in(key, 29), (VALUE_HEAD_COUNT, PROMPT_TOKENS), jnp.float32, math.log(0.25), math.log(0.6))
    slow_vals = jnp.exp(slow_log) * (DK / PROMPT_TOKENS)
    return jnp.where(sluggish_mask[:, None], slow_vals, fast_vals).astype(jnp.float32)


def draw_log_decay(key, part):
    sluggish_mask = slow_heads(key)
    horizon = jax.random.uniform(jax.random.fold_in(key, 31), (VALUE_HEAD_COUNT,), jnp.float32, 30.0, 50.0)
    slow_total = jax.random.uniform(jax.random.fold_in(key, 33), (VALUE_HEAD_COUNT,), jnp.float32, 0.25, 0.5)
    baseline_rate = jnp.where(sluggish_mask, slow_total / PROMPT_TOKENS, math.log(10.0) / horizon)
    segment_log = jax.random.uniform(jax.random.fold_in(key, 37), (VALUE_HEAD_COUNT, PROMPT_TOKENS // TOK_DEV), jnp.float32, math.log(0.7), math.log(1.4))
    section_factor = jnp.repeat(jnp.exp(segment_log), TOK_DEV, axis=1)
    token_noise = jax.random.uniform(jax.random.fold_in(key, 39), (VALUE_HEAD_COUNT, PROMPT_TOKENS), jnp.float32, 0.5, 1.5)
    spike_positions = jax.random.randint(jax.random.fold_in(key, 41), (VALUE_HEAD_COUNT, 2), 0, PROMPT_TOKENS)
    spike_depth = jax.random.uniform(jax.random.fold_in(key, 43), (VALUE_HEAD_COUNT, 2), jnp.float32, 0.223, 0.4)
    token_positions = jnp.arange(PROMPT_TOKENS, dtype=jnp.int32)
    spike_loss = jnp.where(token_positions[None, :] == spike_positions[:, 0:1], spike_depth[:, 0:1], 0.0)
    spike_loss = spike_loss + jnp.where(token_positions[None, :] == spike_positions[:, 1:2], spike_depth[:, 1:2], 0.0)
    spike_loss = jnp.where(sluggish_mask[:, None], spike_loss, 0.0)
    return (-(baseline_rate[:, None] * section_factor * token_noise) - spike_loss).astype(jnp.float32)


def block_scale(own_key, dims, cuts, smallest, top_value):
    loudness, own = 1.0, jax.random.fold_in(own_key, 6)
    for dim, blocks in cuts:
        draws = jnp.exp(jax.random.uniform(jax.random.fold_in(own, dim), (blocks,), jnp.float32, smallest / len(cuts), top_value / len(cuts)))
        loudness = loudness * jnp.repeat(draws, dims[dim] // blocks).reshape([-1 if axis == dim else 1 for axis in range(len(dims))])
    return loudness


def bell_draw(stream_key, dims, scale, bound, cuts=(), kind=jnp.bfloat16):
    array = scale * jax.random.normal(stream_key, dims, jnp.float32)
    if cuts:
        array = array * block_scale(stream_key, dims, cuts, -0.22, 0.18)
    return jnp.clip(array, -bound, bound).astype(kind)


def setup_inputs(seed: int = 0) -> dict:
    arg_keys = jax.random.split(jax.random.key(seed), 9)
    queries = bell_draw(arg_keys[0], (PROMPT_TOKENS, HK * DK), 1.0, 6.0, ((0, 16), (1, 2)))
    key_rows = bell_draw(arg_keys[1], (PROMPT_TOKENS, HK * DK), 1.0, 6.0, ((0, 16), (1, 2)))
    values = bell_draw(arg_keys[2], (PROMPT_TOKENS, VALUE_HEAD_COUNT * DV), 1.0, 6.0, ((0, 16), (1, 2)))
    out_gate = bell_draw(arg_keys[3], (PROMPT_TOKENS, VALUE_HEAD_COUNT * DV), 1.0, 6.0, ((0, 16), (1, 2)))
    write_rate = draw_write_rate(jax.random.fold_in(arg_keys[8], 71), 0)
    log_decay = draw_log_decay(jax.random.fold_in(arg_keys[8], 71), 0)
    norm_gain = jnp.clip(1.0 + 0.18 * jax.random.normal(arg_keys[6], (DV,), jnp.float32), 0.1, 1.9)
    out_weight = bell_draw(arg_keys[7], (VALUE_HEAD_COUNT * DV, D), (VALUE_HEAD_COUNT * DV) ** -0.5, 0.125, ((0, 2),))
    return {"queries": queries, "key_rows": key_rows, "values": values, "out_gate": out_gate, "write_rate": write_rate, "log_decay": log_decay, "norm_gain": norm_gain, "out_weight": out_weight}


epsilon = 1e-06
highest = lax.Precision.HIGHEST

def unit_rows(vectors):
    return vectors / jnp.sqrt(lax.optimization_barrier(jnp.sum(vectors * vectors, axis=-1, keepdims=True)) + epsilon)

def head_blocks(row_data, head_count, head_width, repeat, normalize):
    row_count = row_data.shape[0]
    vectors = row_data.astype(jnp.float32).reshape(row_count, head_count, head_width)
    if normalize:
        vectors = unit_rows(vectors)
    vectors = jnp.repeat(vectors, repeat, axis=1)
    return vectors.reshape(row_count // SPAN, SPAN, head_count * repeat, head_width).transpose(0, 2, 1, 3)

def block_terms(query_blk, key_blk, value_blk, rate_blk, decay_blk):
    length = query_blk.shape[-2]
    log_sums = jnp.cumsum(decay_blk, axis=-1)
    row_ids = lax.broadcasted_iota(jnp.int32, (length, length), 0)
    col_ids = lax.broadcasted_iota(jnp.int32, (length, length), 1)
    lower_mask = row_ids >= col_ids
    strict_mask = row_ids > col_ids
    log_gap = log_sums[..., :, None] - log_sums[..., None, :]
    decay_mat = jnp.where(lower_mask, jnp.exp(jnp.where(lower_mask, log_gap, 0.0)), 0.0)
    key_dots = jnp.einsum('...id,...jd->...ij', key_blk, key_blk, precision=highest)
    coupling = jnp.where(strict_mask, rate_blk[..., :, None] * key_dots * decay_mat, 0.0)
    scores = jnp.einsum('...id,...jd->...ij', query_blk, key_blk, precision=highest) * decay_mat
    growth = jnp.exp(log_sums)
    right_sides = jnp.concatenate([rate_blk[..., None] * value_blk, (rate_blk * growth)[..., None] * key_blk], axis=-1)
    powered = coupling
    solved = right_sides - jnp.einsum('...ij,...jd->...id', powered, right_sides, precision=highest)
    for doubling in range(length.bit_length() - 2):
        powered = jnp.einsum('...ij,...jk->...ik', powered, powered, precision=highest)
        solved = solved + jnp.einsum('...ij,...jd->...id', powered, solved, precision=highest)
    value_width = value_blk.shape[-1]
    updates = solved[..., :value_width]
    weights = solved[..., value_width:]
    log_total = log_sums[..., -1:]
    key_decay = key_blk * jnp.exp(log_total - log_sums)[..., None]
    query_decay = query_blk * growth[..., None]
    keep_rate = jnp.exp(log_total)[..., None]
    return (updates, weights, scores, query_decay, key_decay, keep_rate)

def block_advance(memory, pieces):
    updates, weights, scores, query_decay, key_decay, keep_rate = pieces
    residue = updates - jnp.einsum('...cd,...de->...ce', weights, memory, precision=highest)
    output = jnp.einsum('...cd,...de->...ce', query_decay, memory, precision=highest) + jnp.einsum('...ij,...je->...ie', scores, residue, precision=highest)
    memory = keep_rate * memory + jnp.einsum('...cd,...ce->...de', key_decay, residue, precision=highest)
    return (memory, output)

def gated_norm(output, gate_vals, gain_row):
    inverse = lax.rsqrt(lax.optimization_barrier(jnp.mean(output * output, axis=-1, keepdims=True)) + epsilon)
    return (output * inverse * gain_row * jax.nn.silu(gate_vals)).astype(jnp.bfloat16)

def reference(queries, key_rows, values, out_gate, write_rate, log_decay, norm_gain, out_weight):
    total_rows = queries.shape[0]
    blocks = total_rows // SPAN
    repeat = VALUE_HEAD_COUNT // HK
    sliced = (queries.reshape(blocks, SPAN, HK * DK), key_rows.reshape(blocks, SPAN, HK * DK), values.reshape(blocks, SPAN, VALUE_HEAD_COUNT * DV), out_gate.reshape(blocks, SPAN, VALUE_HEAD_COUNT * DV), write_rate.reshape(VALUE_HEAD_COUNT, blocks, SPAN).transpose(1, 0, 2), log_decay.reshape(VALUE_HEAD_COUNT, blocks, SPAN).transpose(1, 0, 2))

    def advance(memory, inputs):
        query_in, key_in, value_in, gate_in, rate_in, decay_in = inputs
        query_blk = head_blocks(query_in, HK, DK, repeat, True)[0] * DK ** (-0.5)
        key_blk = head_blocks(key_in, HK, DK, repeat, True)[0]
        value_blk = head_blocks(value_in, VALUE_HEAD_COUNT, DV, 1, False)[0]
        pieces = block_terms(query_blk, key_blk, value_blk, rate_in, decay_in)
        memory, output = block_advance(memory, pieces)
        gate_vals = gate_in.astype(jnp.float32).reshape(SPAN, VALUE_HEAD_COUNT, DV)
        normed = gated_norm(output.transpose(1, 0, 2), gate_vals, norm_gain)
        return (memory, normed.reshape(SPAN, VALUE_HEAD_COUNT * DV))
    zero_memory = jnp.zeros((VALUE_HEAD_COUNT, DK, DV), jnp.float32)
    _, normed = lax.scan(advance, zero_memory, sliced)
    normed = normed.reshape(total_rows, VALUE_HEAD_COUNT * DV)
    return jnp.dot(normed, out_weight, preferred_element_type=jnp.float32).astype(jnp.bfloat16)
```

```python
import functools

import jax
import jax.numpy as jnp
from jax import lax
from jax.experimental import pallas as pl
from jax.experimental.pallas import tpu as pltpu
from jax.sharding import PartitionSpec as P

F32 = jnp.float32
BF16 = jnp.bfloat16
EPS = 1e-06
LEAF = 16
PAD = 16
SMALL = pltpu.CompilerParams(vmem_limit_bytes=24 * 1024 * 1024)


def dot(a, b):
    return jnp.dot(a.astype(BF16), b.astype(BF16), preferred_element_type=F32)


def dot_nt(a, b):
    return lax.dot_general(
        a.astype(BF16), b.astype(BF16), (((1,), (1,)), ((), ())), preferred_element_type=F32
    )


def dot_tn(a, b):
    return lax.dot_general(
        a.astype(BF16), b.astype(BF16), (((0,), (0,)), ((), ())), preferred_element_type=F32
    )


def exact_dot(a, b, dims):
    return lax.dot_general(
        a, b, (dims, ((), ())), precision=lax.Precision.HIGHEST, preferred_element_type=F32
    )


def parts(x):
    first = x.astype(BF16)
    rest = x - first.astype(F32)
    second = rest.astype(BF16)
    third = (rest - second.astype(F32)).astype(BF16)
    return [first, second, third]


def iota2(shape, dim):
    return lax.broadcasted_iota(jnp.int32, shape, dim)


def call(body, outs, count, scratch=(), flops=0):
    return pl.pallas_call(
        body,
        out_shape=outs,
        in_specs=[pl.BlockSpec(memory_space=pltpu.SMEM)]
        + [pl.BlockSpec(memory_space=pltpu.VMEM)] * count,
        out_specs=jax.tree.map(lambda _: pl.BlockSpec(memory_space=pltpu.VMEM), outs),
        scratch_shapes=list(scratch),
        compiler_params=SMALL,
        cost_estimate=pl.CostEstimate(flops=flops, bytes_accessed=1 << 20, transcendentals=0),
    )


def pack_body(dk, dv, rep, where, q_ref, k_ref, v_ref, rate_ref, decay_ref, *outs):
    tokens = q_ref.shape[0]
    rank = where[0]
    for shift, out in enumerate(outs):
        other = rank ^ shift
        col = pl.multiple_of(other * dk, dk)
        out[0:tokens, 0:dk] = k_ref[:, pl.ds(col, dk)]
        out[0:tokens, dk : 2 * dk] = q_ref[:, pl.ds(col, dk)]
        wide = pl.multiple_of(other * (rep * dv), rep * dv)
        out[0:tokens, 2 * dk :] = v_ref[:, pl.ds(wide, rep * dv)]
        rows = jnp.concatenate(
            [rate_ref[pl.ds(other * rep, rep), :], decay_ref[pl.ds(other * rep, rep), :]], axis=0
        )
        terms = parts(rows)
        fill = jnp.zeros((PAD - 6 * rep, tokens), F32)
        tail = jnp.concatenate([t.astype(F32) for t in terms] + [fill], axis=0)
        out[tokens:, 0:tokens] = tail.astype(BF16)
        out[tokens:, tokens:] = jnp.zeros((PAD, out.shape[1] - tokens), BF16)


def unit_rows(x):
    return x * lax.rsqrt(jnp.sum(x * x, axis=-1, keepdims=True) + EPS)


def rate_rows(packs, tokens, rep):
    rows = []
    for pack in packs:
        tail = pack[tokens:, 0:tokens].astype(F32)
        n = 2 * rep
        rows.append(tail[0:n] + tail[n : 2 * n] + tail[2 * n : 3 * n])
    return jnp.concatenate(rows, axis=0)


def decay_terms(packs, tokens, rep):
    rows = rate_rows(packs, tokens, rep)
    i = iota2((tokens, tokens), 0)
    j = iota2((tokens, tokens), 1)
    lower = (i >= j).astype(F32)
    unit = (i == j).astype(F32)
    cum_rows = exact_dot(rows, lower, ((1,), (1,)))
    cum_cols = exact_dot(lower, rows, ((1,), (1,)))
    cols = exact_dot(unit, rows, ((1,), (1,)))
    return i, j, cum_rows, cum_cols, cols


def map_body(dk, dv, rep, where, *refs):
    packs, (mf_ref, wu_ref, ab_ref) = refs[:-4], refs[-4:-1]
    scr = refs[-1]
    blocks = len(packs)
    tokens = packs[0].shape[0] - PAD
    rank = where[0]
    for shift, pack in enumerate(packs):
        scr[rank ^ shift] = pack[...]
    ordered = [scr[c] for c in range(blocks)]
    i, j, cum_rows, cum_cols, cols = decay_terms(ordered, tokens, rep)
    unit = (i == j).astype(F32)
    jobs = [(c, h) for c in range(blocks) for h in range(rep)]
    keys, dots = [], []
    for c in range(blocks):
        kn = unit_rows(ordered[c][0:tokens, 0:dk].astype(F32))
        keys.append(kn)
        dots.append(dot_nt(kn, kn))
    lows, rhs, tails, keeps = [], [], [], []
    for c, h in jobs:
        at = c * 2 * rep + h
        rate = cols[:, at : at + 1]
        cum_col = cum_cols[:, at + rep : at + rep + 1]
        cum_row = cum_rows[at + rep : at + rep + 1, :]
        gap = jnp.where(i > j, cum_col - cum_row, 0.0)
        lows.append(jnp.where(i > j, rate * dots[c] * jnp.exp(gap), 0.0))
        value = ordered[c][0:tokens, 2 * dk + h * dv : 2 * dk + (h + 1) * dv].astype(F32)
        rhs.append(
            jnp.concatenate([(rate * jnp.exp(cum_col)) * keys[c], rate * value], axis=1)
        )
        last = cum_row[:, tokens - 1 : tokens]
        tails.append(keys[c] * jnp.exp(last - cum_col))
        keeps.append(jnp.exp(last))
    leaf = (i // LEAF) == (j // LEAF)
    power = [jnp.where(leaf, low, 0.0) for low in lows]
    inverse = [unit - p for p in power]
    power = [dot(p, p) for p in power]
    size = 4
    while size < LEAF:
        both = [dot(p, jnp.concatenate([p, t], axis=1)) for p, t in zip(power, inverse)]
        power = [b[:, 0:tokens] for b in both]
        inverse = [t + b[:, tokens:] for t, b in zip(inverse, both)]
        size *= 2
    inverse = [t + dot(p, t) for p, t in zip(power, inverse)]
    size = LEAF
    while size < tokens:
        off = ((i // size) != (j // size)) & ((i // (2 * size)) == (j // (2 * size)))
        mid = [dot(jnp.where(off, low, 0.0), t) for low, t in zip(lows, inverse)]
        inverse = [t - dot(t, m) for m, t in zip(mid, inverse)]
        size *= 2
    solved = [r + dot(t - unit, r) for t, r in zip(inverse, rhs)]
    for n in range(len(jobs)):
        wu_ref[n] = solved[n].astype(BF16)
    moved = [dot_tn(t, s) for t, s in zip(tails, solved)]
    unit_k = unit if dk == tokens else (iota2((dk, dk), 0) == iota2((dk, dk), 1)).astype(F32)
    state = [jnp.concatenate([unit_k, jnp.zeros((dk, dv), F32)], axis=1) for _ in range(rep)]
    total = [jnp.ones((1, 1), F32) for _ in range(rep)]
    for c in range(blocks):
        for h in range(rep):
            n = c * rep + h
            ab_ref[n] = state[h].astype(BF16)
            feed = jnp.concatenate([jnp.zeros((dk, dk), F32), moved[n][:, dk:]], axis=1)
            state[h] = keeps[n] * state[h] - dot(moved[n][:, 0:dk], state[h]) + feed
            total[h] = total[h] * keeps[n]
    for h in range(rep):
        delta = total[h] * unit_k - state[h][:, 0:dk]
        mf_ref[h * dk : (h + 1) * dk, 0:dk] = delta.astype(BF16)
        mf_ref[h * dk : (h + 1) * dk, dk:] = state[h][:, dk:].astype(BF16)
    store_keeps(mf_ref, rep * dk, total)


def store_keeps(ref, row, totals):
    width = ref.shape[1]
    rows = [jnp.broadcast_to(t, (1, width)) for total in totals for t in parts(total)]
    rows = [t.astype(F32) for t in rows]
    rows.append(jnp.zeros((PAD - len(rows), width), F32))
    ref[row:, :] = jnp.concatenate(rows, axis=0).astype(BF16)


def load_map(ref, h, dk, rep):
    tail = ref[rep * dk :, 0:dk].astype(F32)
    keep = tail[3 * h : 3 * h + 1] + tail[3 * h + 1 : 3 * h + 2] + tail[3 * h + 2 : 3 * h + 3]
    rows = slice(h * dk, (h + 1) * dk)
    return keep, ref[rows, 0:dk], ref[rows, dk:].astype(F32)


def advance(keep, delta, feed, state):
    return keep * state - dot(delta, state) + feed


def join_body(dk, dv, rep, whole, where, late_ref, early_ref, out_ref):
    totals = []
    for h in range(rep):
        keep, delta, feed = load_map(late_ref, h, dk, rep)
        keep_e, delta_e, feed_e = load_map(early_ref, h, dk, rep)
        rows = slice(h * dk, (h + 1) * dk)
        feed_new = advance(keep, delta, feed, feed_e)
        if not whole:
            out_ref[rows, :] = feed_new.astype(BF16)
            continue
        delta_new = keep * delta_e.astype(F32) + keep_e * delta.astype(F32) - dot(delta, delta_e)
        out_ref[rows, 0:dk] = delta_new.astype(BF16)
        out_ref[rows, dk:] = feed_new.astype(BF16)
        totals.append((keep * keep_e)[:, 0:1])
    if whole:
        store_keeps(out_ref, rep * dk, totals)


def terms_body(dk, dv, rep, where, *refs):
    wu_ref, ab_ref = refs[-5:-3]
    packs, x_ref, y_ref, scr = refs[:-5], refs[-3], refs[-2], refs[-1]
    blocks = len(packs)
    tokens = packs[0].shape[0] - PAD
    rank = where[0]
    for shift, pack in enumerate(packs):
        scr[rank ^ shift] = pack[...]
    ordered = [scr[c] for c in range(blocks)]
    i, j, cum_rows, cum_cols, cols = decay_terms(ordered, tokens, rep)
    scores, grown = [], []
    for c in range(blocks):
        kn = unit_rows(ordered[c][0:tokens, 0:dk].astype(F32))
        qn = unit_rows(ordered[c][0:tokens, dk : 2 * dk].astype(F32)) * dk**-0.5
        both = dot_nt(qn, kn)
        for h in range(rep):
            at = c * 2 * rep + h + rep
            cum_col, cum_row = cum_cols[:, at : at + 1], cum_rows[at : at + 1, :]
            gap = jnp.where(i >= j, cum_col - cum_row, 0.0)
            scores.append(jnp.where(i >= j, both * jnp.exp(gap), 0.0))
            grown.append(qn * jnp.exp(cum_col))
    inner = [dot(s, wu_ref[n]) for n, s in enumerate(scores)]
    first = [(grown[n] - inner[n][:, 0:dk]).astype(BF16) for n in range(len(inner))]
    outer = [dot(f, ab_ref[n]) for n, f in enumerate(first)]
    for n in range(len(inner)):
        c, h = n // rep, n % rep
        rows = slice(c * tokens, (c + 1) * tokens)
        x_ref[h, rows, :] = outer[n][:, 0:dk].astype(BF16)
        y_ref[h, rows, :] = inner[n][:, dk:] + outer[n][:, dk:]


def output_body(dk, dv, rep, where, x_ref, y_ref, late_ref, early_ref, *outs):
    *outs, scr = outs
    blocks = len(outs)
    tokens = outs[0].shape[0]
    rank = where[0]
    for h in range(rep):
        keep, delta, feed = load_map(late_ref, h, dk, rep)
        state = advance(keep, delta, feed, early_ref[h * dk : (h + 1) * dk, :].astype(F32))
        out = (dot(x_ref[h], state) + y_ref[h]).astype(BF16)
        for c in range(blocks):
            scr[c, :, h * dv : (h + 1) * dv] = out[c * tokens : (c + 1) * tokens]
    for shift, out_ref in enumerate(outs):
        out_ref[...] = scr[rank ^ shift]


def project_body(dv, rep, where, gate_ref, gain_ref, w_ref, *refs):
    *pieces, send_ref, normed_ref = refs
    rank, half = where[0], where[1]
    width = rep * dv
    for shift, piece in enumerate(pieces):
        col = pl.multiple_of((rank ^ shift) * width, width)
        gate = gate_ref[:, pl.ds(col, width)].astype(F32)
        gate = gate / (1.0 + jnp.exp(-gate))
        for h in range(rep):
            o = piece[:, h * dv : (h + 1) * dv].astype(F32)
            inverse = lax.rsqrt(jnp.mean(o * o, axis=-1, keepdims=True) + EPS)
            done = o * inverse * gain_ref[...] * gate[:, h * dv : (h + 1) * dv]
            at = pl.multiple_of(col + h * dv, dv)
            normed_ref[:, pl.ds(at, dv)] = done.astype(BF16)
    columns = send_ref.shape[1]
    start = (1 - half) * columns
    normed = normed_ref[...]
    step = 256
    for n in range(columns // step):
        at = pl.multiple_of(start + n * step, step)
        send_ref[:, n * step : (n + 1) * step] = dot(normed, w_ref[:, pl.ds(at, step)]).astype(BF16)


def own_body(where, w_ref, normed_ref, out_ref):
    columns = out_ref.shape[1]
    start = where[1] * columns
    normed = normed_ref[...]
    step = 256
    for n in range(columns // step):
        at = pl.multiple_of(start + n * step, step)
        out_ref[:, n * step : (n + 1) * step] = dot(normed, w_ref[:, pl.ds(at, step)])


def per_device(queries, key_rows, values, out_gate, write_rate, log_decay, norm_gain, out_weight):
    tokens = queries.shape[0]
    value_heads = write_rate.shape[0]
    dv = norm_gain.shape[0]
    dk = dv
    group = queries.shape[1] // dk
    rep = value_heads // group
    ranks = lax.axis_size("seq")
    halves = lax.axis_size("head")
    groups = ranks // group
    assert ranks % group == 0 and group & (group - 1) == 0 and halves == 2
    columns = out_weight.shape[1] // halves
    index = lax.axis_index("seq")
    where = jnp.stack([index % group, lax.axis_index("head")]).astype(jnp.int32)
    shape = jax.ShapeDtypeStruct
    sizes = (dk, dv, rep)

    def swap(x, shift):
        pairs = [(i, (i // group) * group + ((i % group) ^ shift)) for i in range(ranks)]
        return lax.ppermute(x, "seq", pairs)

    def later(x, shift):
        pairs = [(i, i + shift * group) for i in range(ranks - shift * group)]
        return lax.ppermute(x, "seq", pairs)

    packed = shape((tokens + PAD, 2 * dk + rep * dv), BF16)
    packs = call(functools.partial(pack_body, *sizes), [packed] * group, 5)(
        where, queries, key_rows, values, write_rate, log_decay
    )
    packs = [packs[0]] + [swap(packs[s], s) for s in range(1, group)]

    jobs = group * rep
    buffer = pltpu.VMEM((group,) + packed.shape, BF16)
    cube = 2 * tokens * tokens * (dk + dv)
    map_shape = shape((rep * dk + PAD, dk + dv), BF16)
    own_map, wu, ab = call(
        functools.partial(map_body, *sizes),
        [map_shape, shape((jobs, tokens, dk + dv), BF16), shape((jobs, dk, dk + dv), BF16)],
        group,
        [buffer],
        jobs * 16 * cube,
    )(where, *packs)

    feed_shape = shape((rep * dk, dv), BF16)
    entry = jnp.zeros(map_shape.shape, BF16)
    feed = jnp.zeros(feed_shape.shape, BF16)
    window, send = 0, own_map
    while window < groups - 1:
        came = later(send, window + 1)
        last = 2 * window + 1 >= groups - 1
        if window == 0:
            entry = came
        elif last:
            feed = came
        else:
            entry = call(functools.partial(join_body, *sizes, True), map_shape, 2)(
                where, entry, came
            )
        window = 2 * window + 1
        if window < groups - 1:
            final = 2 * window + 1 >= groups - 1
            send = call(
                functools.partial(join_body, *sizes, not final),
                feed_shape if final else map_shape,
                2,
            )(where, own_map, entry)
    x, y = call(
        functools.partial(terms_body, *sizes),
        [shape((rep, group * tokens, dk), BF16), shape((rep, group * tokens, dv), F32)],
        group + 2,
        [buffer],
        jobs * 4 * cube,
    )(where, *packs, wu, ab)
    piece = shape((tokens, rep * dv), BF16)
    pieces = call(
        functools.partial(output_body, *sizes),
        [piece] * group,
        4,
        [pltpu.VMEM((group,) + piece.shape, BF16)],
        cube * jobs,
    )(where, x, y, entry, feed)
    pieces = [pieces[0]] + [swap(pieces[s], s) for s in range(1, group)]

    work = 2 * tokens * columns * value_heads * dv
    away, normed = call(
        functools.partial(project_body, dv, rep),
        [shape((tokens, columns), BF16), shape((tokens, value_heads * dv), BF16)],
        3 + group,
        (),
        work,
    )(where, out_gate, norm_gain.reshape(1, dv), out_weight, *pieces)
    came = lax.ppermute(away, "head", [(0, 1), (1, 0)])
    own = call(own_body, shape((tokens, columns), F32), 2, (), work)(where, out_weight, normed)
    return (own + came.astype(F32)).astype(BF16)


def solution(mesh):
    return jax.shard_map(
        per_device,
        mesh=mesh,
        in_specs=(
            P("seq", "head"),
            P("seq", "head"),
            P("seq", "head"),
            P("seq", "head"),
            P("head", "seq"),
            P("head", "seq"),
            P(),
            P("head", None),
        ),
        out_specs=P("seq", "head"),
        check_vma=False,
    )
```

```python
import functools

import jax
import jax.numpy as jnp
from jax import lax
from jax.experimental import pallas as pl
from jax.experimental.pallas import tpu as pltpu
from jax.sharding import PartitionSpec as P

F32 = jnp.float32
BF16 = jnp.bfloat16
EPS = 1e-06
LEAF = 16
PAD = 16
SMALL = pltpu.CompilerParams(vmem_limit_bytes=24 * 1024 * 1024)


def dot(a, b):
    return jnp.dot(a.astype(BF16), b.astype(BF16), preferred_element_type=F32)


def dot_nt(a, b):
    return lax.dot_general(
        a.astype(BF16), b.astype(BF16), (((1,), (1,)), ((), ())), preferred_element_type=F32
    )


def dot_tn(a, b):
    return lax.dot_general(
        a.astype(BF16), b.astype(BF16), (((0,), (0,)), ((), ())), preferred_element_type=F32
    )


def exact_dot(a, b, dims):
    return lax.dot_general(
        a, b, (dims, ((), ())), precision=lax.Precision.HIGHEST, preferred_element_type=F32
    )


def parts(x):
    first = x.astype(BF16)
    rest = x - first.astype(F32)
    second = rest.astype(BF16)
    third = (rest - second.astype(F32)).astype(BF16)
    return [first, second, third]


def iota2(shape, dim):
    return lax.broadcasted_iota(jnp.int32, shape, dim)


def call(body, outs, specs, scratch=(), flops=0):
    return pl.pallas_call(
        body,
        out_shape=outs,
        in_specs=[pl.BlockSpec(memory_space=space) for space in specs],
        out_specs=jax.tree.map(lambda _: pl.BlockSpec(memory_space=pltpu.VMEM), outs),
        scratch_shapes=list(scratch),
        compiler_params=SMALL,
        cost_estimate=pl.CostEstimate(flops=flops, bytes_accessed=1 << 20, transcendentals=0),
    )


def pack_body(dk, dv, rep, q_ref, k_ref, v_ref, rate_ref, decay_ref, out, rate, decay, sems):
    tokens = q_ref.shape[0]
    count = out.shape[0]
    copies = [(rate_ref, rate), (decay_ref, decay)]
    for p in range(count):
        key = slice((p // rep) * dk, (p // rep + 1) * dk)
        rows = slice(0, tokens)
        copies.append((k_ref.at[:, key], out.at[p, rows, 0:dk]))
        copies.append((q_ref.at[:, key], out.at[p, rows, dk : 2 * dk]))
        copies.append((v_ref.at[:, p * dv : (p + 1) * dv], out.at[p, rows, 2 * dk :]))
    copies = [
        pltpu.make_async_copy(src, dst, sems.at[n]) for n, (src, dst) in enumerate(copies)
    ]
    for copy in copies:
        copy.start()
    for copy in copies[:2]:
        copy.wait()
    fill = jnp.zeros((PAD - 6, tokens), F32)
    for p in range(count):
        terms = parts(jnp.concatenate([rate[p : p + 1, :], decay[p : p + 1, :]], axis=0))
        tail = jnp.concatenate([t.astype(F32) for t in terms] + [fill], axis=0)
        out[p, tokens:, 0:tokens] = tail.astype(BF16)
        out[p, tokens:, tokens:] = jnp.zeros((PAD, out.shape[2] - tokens), BF16)
    for copy in copies[2:]:
        copy.wait()


def unit_rows(x):
    return x * lax.rsqrt(jnp.sum(x * x, axis=-1, keepdims=True) + EPS)


def decay_terms(pack_ref, tokens):
    rows = []
    for c in range(pack_ref.shape[0]):
        tail = pack_ref[c, tokens:, 0:tokens].astype(F32)
        rows.append(tail[0:2] + tail[2:4] + tail[4:6])
    rows = jnp.concatenate(rows, axis=0)
    i = iota2((tokens, tokens), 0)
    j = iota2((tokens, tokens), 1)
    lower = (i >= j).astype(F32)
    unit = (i == j).astype(F32)
    cum_rows = exact_dot(rows, lower, ((1,), (1,)))
    cum_cols = exact_dot(lower, rows, ((1,), (1,)))
    cols = exact_dot(unit, rows, ((1,), (1,)))
    return i, j, cum_rows, cum_cols, cols


def advance(keep, delta, feed, state):
    return keep * state - dot(delta, state) + feed


def join(late, early, whole=True):
    keep, delta, feed = late
    keep_e, delta_e, feed_e = early
    if not whole:
        return None, None, advance(keep, delta, feed, feed_e)
    dk = delta.shape[1]
    both = dot(delta, jnp.concatenate([delta_e, feed_e], axis=1))
    delta_new = keep * delta_e + keep_e * delta - both[:, 0:dk]
    return keep * keep_e, delta_new, keep * feed_e + feed - both[:, dk:]


def map_body(dk, dv, need_map, pack_ref, map_ref, wu_ref, delta_ref, feed_ref, keep_ref):
    blocks = pack_ref.shape[0]
    tokens = pack_ref.shape[1] - PAD
    i, j, cum_rows, cum_cols, cols = decay_terms(pack_ref, tokens)
    unit = (i == j).astype(F32)
    lows, rhs, tails, keeps = [], [], [], []
    for c in range(blocks):
        key = unit_rows(pack_ref[c, 0:tokens, 0:dk].astype(F32))
        value = pack_ref[c, 0:tokens, 2 * dk :].astype(F32)
        rate = cols[:, 2 * c : 2 * c + 1]
        cum_col = cum_cols[:, 2 * c + 1 : 2 * c + 2]
        cum_row = cum_rows[2 * c + 1 : 2 * c + 2, :]
        gap = jnp.where(i > j, cum_col - cum_row, 0.0)
        lows.append(jnp.where(i > j, rate * dot_nt(key, key) * jnp.exp(gap), 0.0))
        rhs.append(jnp.concatenate([(rate * jnp.exp(cum_col)) * key, rate * value], axis=1))
        last = cum_row[:, tokens - 1 : tokens]
        tails.append(key * jnp.exp(last - cum_col))
        keeps.append(jnp.exp(last))
    leaf = (i // LEAF) == (j // LEAF)
    power = [jnp.where(leaf, low, 0.0) for low in lows]
    inverse = [unit - p for p in power]
    power = [dot(p, p) for p in power]
    size = 4
    while size < LEAF:
        both = [dot(p, jnp.concatenate([p, t], axis=1)) for p, t in zip(power, inverse)]
        power = [b[:, 0:tokens] for b in both]
        inverse = [t + b[:, tokens:] for t, b in zip(inverse, both)]
        size *= 2
    inverse = [t + dot(p, t) for p, t in zip(power, inverse)]
    size = LEAF
    while size < tokens:
        off = ((i // size) != (j // size)) & ((i // (2 * size)) == (j // (2 * size)))
        mid = [dot(jnp.where(off, low, 0.0), t) for low, t in zip(lows, inverse)]
        inverse = [t - dot(t, m) for m, t in zip(mid, inverse)]
        size *= 2
    solved = [r + dot(t - unit, r) for t, r in zip(inverse, rhs)]
    for c in range(blocks):
        wu_ref[c] = solved[c].astype(BF16)
    moved = [dot_tn(t, s) for t, s in zip(tails, solved)]
    maps = [(keeps[c], moved[c][:, 0:dk], moved[c][:, dk:]) for c in range(blocks)]
    for c in range(blocks):
        delta_ref[c] = maps[c][1].astype(BF16)
        feed_ref[c] = maps[c][2]
        keep_ref[c : c + 1, :] = jnp.broadcast_to(keeps[c], (1, keep_ref.shape[1]))
    while len(maps) > 1:
        maps = [
            join(maps[n + 1], maps[n], need_map or n > 0) for n in range(0, len(maps), 2)
        ]
    if need_map:
        store_map(map_ref, dk, maps[0])
    else:
        map_ref[...] = maps[0][2].astype(BF16)


def store_map(ref, dk, entry):
    keep, delta, feed = entry
    ref[0:dk, 0:dk] = delta.astype(BF16)
    ref[0:dk, dk:] = feed.astype(BF16)
    width = ref.shape[1]
    rows = [jnp.broadcast_to(t.astype(F32), (1, width)) for t in parts(keep)]
    rows.append(jnp.zeros((PAD - 3, width), F32))
    ref[dk:, :] = jnp.concatenate(rows, axis=0).astype(BF16)


def load_map(ref, dk):
    tail = ref[dk:, 0:1].astype(F32)
    return tail[0:1] + tail[1:2] + tail[2:3], ref[0:dk, 0:dk].astype(F32), ref[0:dk, dk:].astype(F32)


def join_body(dk, whole, late_ref, early_ref, out_ref):
    entry = join(load_map(late_ref, dk), load_map(early_ref, dk), whole)
    if whole:
        store_map(out_ref, dk, entry)
    else:
        out_ref[...] = entry[2].astype(BF16)


def terms_body(dk, dv, pack_ref, wu_ref, delta_ref, feed_ref, keep_ref, x_ref, y_ref):
    blocks = pack_ref.shape[0]
    tokens = pack_ref.shape[1] - PAD
    i, j, cum_rows, cum_cols, _ = decay_terms(pack_ref, tokens)
    inner, first = [], []
    for c in range(blocks):
        key = unit_rows(pack_ref[c, 0:tokens, 0:dk].astype(F32))
        query = unit_rows(pack_ref[c, 0:tokens, dk : 2 * dk].astype(F32)) * dk**-0.5
        cum_col = cum_cols[:, 2 * c + 1 : 2 * c + 2]
        cum_row = cum_rows[2 * c + 1 : 2 * c + 2, :]
        gap = jnp.where(i >= j, cum_col - cum_row, 0.0)
        scores = jnp.where(i >= j, dot_nt(query, key) * jnp.exp(gap), 0.0)
        inner.append(dot(scores, wu_ref[c]))
        first.append((query * jnp.exp(cum_col) - inner[c][:, 0:dk]).astype(BF16))
    unit = (iota2((dk, dk), 0) == iota2((dk, dk), 1)).astype(F32)
    keep = keep_ref[0:1, 0:1]
    state = jnp.concatenate([keep * unit - delta_ref[0].astype(F32), feed_ref[0]], axis=1)
    x_ref[0] = first[0]
    y_ref[0] = inner[0][:, dk:]
    for c in range(1, blocks):
        outer = dot(first[c], state)
        x_ref[c] = outer[:, 0:dk].astype(BF16)
        y_ref[c] = inner[c][:, dk:] + outer[:, dk:]
        if c + 1 < blocks:
            feed = jnp.concatenate([jnp.zeros((dk, dk), F32), feed_ref[c]], axis=1)
            state = advance(keep_ref[c : c + 1, 0:1], delta_ref[c], feed, state)


def output_body(dk, x_ref, y_ref, feed_ref, late_ref, out_ref):
    state = feed_ref[...].astype(F32)
    if late_ref is not None:
        state = advance(*load_map(late_ref, dk), state)
    state = state.astype(BF16)
    for c in range(out_ref.shape[0]):
        out_ref[c] = (dot(x_ref[c], state) + y_ref[c]).astype(BF16)


def project_body(dv, where, gate_ref, gain_ref, w_ref, pieces, send_ref, normed_ref):
    half = where[0]
    for p in range(pieces.shape[0]):
        cols = slice(p * dv, (p + 1) * dv)
        gate = gate_ref[:, cols].astype(F32)
        o = pieces[p].astype(F32)
        inverse = lax.rsqrt(jnp.mean(o * o, axis=-1, keepdims=True) + EPS)
        done = o * inverse * gain_ref[...] * (gate / (1.0 + jnp.exp(-gate)))
        normed_ref[:, cols] = done.astype(BF16)
    columns = send_ref.shape[1]
    start = (1 - half) * columns
    normed = normed_ref[...]
    step = 256
    for n in range(columns // step):
        at = pl.multiple_of(start + n * step, step)
        send_ref[:, n * step : (n + 1) * step] = dot(normed, w_ref[:, pl.ds(at, step)]).astype(BF16)


def own_body(where, w_ref, normed_ref, out_ref):
    columns = out_ref.shape[1]
    start = where[0] * columns
    normed = normed_ref[...]
    step = 256
    for n in range(columns // step):
        at = pl.multiple_of(start + n * step, step)
        out_ref[:, n * step : (n + 1) * step] = dot(normed, w_ref[:, pl.ds(at, step)])


def per_device(queries, key_rows, values, out_gate, write_rate, log_decay, norm_gain, out_weight):
    tokens = queries.shape[0]
    group = write_rate.shape[0]
    dv = norm_gain.shape[0]
    dk = dv
    rep = group // (queries.shape[1] // dk)
    ranks = lax.axis_size("seq")
    halves = lax.axis_size("head")
    groups = ranks // group
    assert ranks % group == 0 and group & (group - 1) == 0 and halves == 2
    columns = out_weight.shape[1] // halves
    where = lax.axis_index("head").astype(jnp.int32).reshape(1)
    shape = jax.ShapeDtypeStruct
    vmem, hbm, smem = pltpu.VMEM, pltpu.HBM, pltpu.SMEM
    members = [[g * group + n for n in range(group)] for g in range(groups)]

    def regroup(x):
        return lax.all_to_all(x, "seq", 0, 0, axis_index_groups=members)

    def later(x, shift):
        pairs = [(i, i + shift * group) for i in range(ranks - shift * group)]
        return lax.ppermute(x, "seq", pairs)

    pack = call(
        functools.partial(pack_body, dk, dv, rep),
        shape((group, tokens + PAD, 2 * dk + dv), BF16),
        [hbm] * 5,
        [
            pltpu.VMEM(write_rate.shape, F32),
            pltpu.VMEM(log_decay.shape, F32),
            pltpu.SemaphoreType.DMA((2 + 3 * group,)),
        ],
    )(queries, key_rows, values, write_rate, log_decay)
    pack = regroup(pack)

    need_map = groups > 2
    cube = 2 * tokens * tokens * (dk + dv)
    map_shape = shape((dk + PAD, dk + dv), BF16)
    feed_shape = shape((dk, dv), BF16)
    own, wu, delta, feeds, keep = call(
        functools.partial(map_body, dk, dv, need_map),
        [
            map_shape if need_map else feed_shape,
            shape((group, tokens, dk + dv), BF16),
            shape((group, dk, dk), BF16),
            shape((group, dk, dv), F32),
            shape((group, dk), F32),
        ],
        [vmem],
        (),
        group * 16 * cube,
    )(pack)

    entry, feed = None, jnp.zeros(feed_shape.shape, BF16)
    window, send = 0, own
    while window < groups - 1:
        came = later(send, window + 1)
        last = 2 * window + 1 >= groups - 1
        if last:
            feed = came
        elif window == 0:
            entry = came
        else:
            entry = call(functools.partial(join_body, dk, True), map_shape, [vmem] * 2)(entry, came)
        window = 2 * window + 1
        if window < groups - 1:
            whole = 2 * window + 1 < groups - 1
            send = call(
                functools.partial(join_body, dk, whole),
                map_shape if whole else feed_shape,
                [vmem] * 2,
            )(own, entry)
    x, y = call(
        functools.partial(terms_body, dk, dv),
        [shape((group, tokens, dk), BF16), shape((group, tokens, dv), F32)],
        [vmem] * 5,
        (),
        group * 4 * cube,
    )(pack, wu, delta, feeds, keep)
    late = [] if entry is None else [entry]
    body = functools.partial(output_body, dk)
    if entry is None:
        body = lambda x, y, feed, out: output_body(dk, x, y, feed, None, out)
    pieces = call(
        body, shape((group, tokens, dv), BF16), [vmem] * (3 + len(late)), (), cube * group
    )(x, y, feed, *late)
    pieces = regroup(pieces)

    work = 2 * tokens * columns * group * dv
    away, normed = call(
        functools.partial(project_body, dv),
        [shape((tokens, columns), BF16), shape((tokens, group * dv), BF16)],
        [smem] + [vmem] * 4,
        (),
        work,
    )(where, out_gate, norm_gain.reshape(1, dv), out_weight, pieces)
    came = lax.ppermute(away, "head", [(0, 1), (1, 0)])
    own = call(own_body, shape((tokens, columns), F32), [smem, vmem, vmem], (), work)(
        where, out_weight, normed
    )
    return (own + came.astype(F32)).astype(BF16)


def solution(mesh):
    return jax.shard_map(
        per_device,
        mesh=mesh,
        in_specs=(
            P("seq", "head"),
            P("seq", "head"),
            P("seq", "head"),
            P("seq", "head"),
            P("head", "seq"),
            P("head", "seq"),
            P(),
            P("head", None),
        ),
        out_specs=P("seq", "head"),
        check_vma=False,
    )
```

```python
import functools

import jax
import jax.numpy as jnp
from jax import lax
from jax.experimental import pallas as pl
from jax.experimental.pallas import tpu as pltpu
from jax.sharding import PartitionSpec as P

F32 = jnp.float32
BF16 = jnp.bfloat16
EPS = 1e-06
LEAF = 16
PAD = 16
SMALL = pltpu.CompilerParams(vmem_limit_bytes=24 * 1024 * 1024)


def dot(a, b):
    return jnp.dot(a.astype(BF16), b.astype(BF16), preferred_element_type=F32)


def dot_nt(a, b):
    return lax.dot_general(
        a.astype(BF16), b.astype(BF16), (((1,), (1,)), ((), ())), preferred_element_type=F32
    )


def dot_tn(a, b):
    return lax.dot_general(
        a.astype(BF16), b.astype(BF16), (((0,), (0,)), ((), ())), preferred_element_type=F32
    )


def exact_dot(a, b, dims):
    return lax.dot_general(
        a, b, (dims, ((), ())), precision=lax.Precision.HIGHEST, preferred_element_type=F32
    )


def parts(x):
    first = x.astype(BF16)
    rest = x - first.astype(F32)
    second = rest.astype(BF16)
    third = (rest - second.astype(F32)).astype(BF16)
    return [first, second, third]


def iota2(shape, dim):
    return lax.broadcasted_iota(jnp.int32, shape, dim)


def call(body, outs, specs, scratch=(), flops=0):
    return pl.pallas_call(
        body,
        out_shape=outs,
        in_specs=[pl.BlockSpec(memory_space=space) for space in specs],
        out_specs=jax.tree.map(lambda _: pl.BlockSpec(memory_space=pltpu.VMEM), outs),
        scratch_shapes=list(scratch),
        compiler_params=SMALL,
        cost_estimate=pl.CostEstimate(flops=flops, bytes_accessed=1 << 20, transcendentals=0),
    )


def unit_rows(x):
    return x * lax.rsqrt(jnp.sum(x * x, axis=-1, keepdims=True) + EPS)


def advance(keep, delta, feed, state):
    return keep * state - dot(delta, state) + feed


def join(late, early, whole=True):
    keep, delta, feed = late
    keep_e, delta_e, feed_e = early
    if not whole:
        return None, None, advance(keep, delta, feed, feed_e)
    dk = delta.shape[1]
    both = dot(delta, jnp.concatenate([delta_e, feed_e], axis=1))
    delta_new = keep * delta_e + keep_e * delta - both[:, 0:dk]
    return keep * keep_e, delta_new, keep * feed_e + feed - both[:, dk:]


def slot_rows(ref, rank, slots):
    return [ref[pl.ds(rank ^ s, 1), :] for s in range(slots)]


def key_block(ref, rank, rep, m, dk):
    at = pl.multiple_of(((rank // rep) ^ m) * dk, dk)
    return unit_rows(ref[:, pl.ds(at, dk)].astype(F32))


def map_body(dk, dv, rep, where, k_in, v_in, rate_in, decay_in, *refs):
    *maps, wu_ref, sums_ref, cols_ref, k_ref, v_ref, rate_ref, decay_ref, sems = refs
    slots = len(maps)
    tokens = k_in.shape[0]
    rank = where[0]
    pairs = [(rate_in, rate_ref), (decay_in, decay_ref), (k_in, k_ref), (v_in, v_ref)]
    copies = [pltpu.make_async_copy(*p, sems.at[n]) for n, p in enumerate(pairs)]
    for copy in copies:
        copy.start()
    i = iota2((tokens, tokens), 0)
    j = iota2((tokens, tokens), 1)
    lower = (i >= j).astype(F32)
    unit = (i == j).astype(F32)
    copies[0].wait()
    copies[1].wait()
    decays = jnp.concatenate(slot_rows(decay_ref, rank, slots), axis=0)
    rates = jnp.concatenate(slot_rows(rate_ref, rank, slots), axis=0)
    cum_rows = exact_dot(decays, lower, ((1,), (1,)))
    cum_cols = exact_dot(lower, decays, ((1,), (1,)))
    rate_cols = exact_dot(unit, rates, ((1,), (1,)))
    sums_ref[...] = cum_rows
    cols_ref[...] = cum_cols
    copies[2].wait()
    keys = [key_block(k_ref, rank, rep, m, dk) for m in range(slots // rep)]
    dots = [dot_nt(key, key) for key in keys]
    copies[3].wait()
    lows, rhs, tails, keeps = [], [], [], []
    for s in range(slots):
        key = keys[s // rep]
        at = pl.multiple_of((rank ^ s) * dv, dv)
        value = v_ref[:, pl.ds(at, dv)].astype(F32)
        rate = rate_cols[:, s : s + 1]
        cum_col = cum_cols[:, s : s + 1]
        cum_row = cum_rows[s : s + 1, :]
        gap = jnp.where(i > j, cum_col - cum_row, 0.0)
        lows.append(jnp.where(i > j, rate * dots[s // rep] * jnp.exp(gap), 0.0))
        rhs.append(jnp.concatenate([(rate * jnp.exp(cum_col)) * key, rate * value], axis=1))
        last = cum_row[:, tokens - 1 : tokens]
        tails.append(key * jnp.exp(last - cum_col))
        keeps.append(jnp.exp(last))
    leaf = (i // LEAF) == (j // LEAF)
    power = [jnp.where(leaf, low, 0.0) for low in lows]
    inverse = [unit - p for p in power]
    power = [dot(p, p) for p in power]
    size = 4
    while size < LEAF:
        both = [dot(p, jnp.concatenate([p, t], axis=1)) for p, t in zip(power, inverse)]
        power = [b[:, 0:tokens] for b in both]
        inverse = [t + b[:, tokens:] for t, b in zip(inverse, both)]
        size *= 2
    inverse = [t + dot(p, t) for p, t in zip(power, inverse)]
    size = LEAF
    while size < tokens:
        off = ((i // size) != (j // size)) & ((i // (2 * size)) == (j // (2 * size)))
        mid = [dot(jnp.where(off, low, 0.0), t) for low, t in zip(lows, inverse)]
        inverse = [t - dot(t, m) for m, t in zip(mid, inverse)]
        size *= 2
    solved = [r + dot(t - unit, r) for t, r in zip(inverse, rhs)]
    for s in range(slots):
        wu_ref[s] = solved[s].astype(BF16)
    moved = [dot_tn(t, r) for t, r in zip(tails, solved)]
    for s in range(slots):
        store_map(maps[s], dk, (keeps[s], moved[s][:, 0:dk], moved[s][:, dk:]))


def terms_body(dk, rep, where, q_ref, k_ref, wu_ref, sums_ref, cols_ref, x_ref, y_ref):
    slots = wu_ref.shape[0]
    tokens = q_ref.shape[0]
    rank = where[0]
    i = iota2((tokens, tokens), 0)
    j = iota2((tokens, tokens), 1)
    queries, dots = [], []
    for m in range(slots // rep):
        query = key_block(q_ref, rank, rep, m, dk) * dk**-0.5
        queries.append(query)
        dots.append(dot_nt(query, key_block(k_ref, rank, rep, m, dk)))
    for s in range(slots):
        cum_col = cols_ref[:, s : s + 1]
        gap = jnp.where(i >= j, cum_col - sums_ref[s : s + 1, :], 0.0)
        scores = jnp.where(i >= j, dots[s // rep] * jnp.exp(gap), 0.0)
        inner = dot(scores, wu_ref[s])
        x_ref[s] = (queries[s // rep] * jnp.exp(cum_col) - inner[:, 0:dk]).astype(BF16)
        y_ref[s] = inner[:, dk:]


def store_map(ref, dk, entry):
    keep, delta, feed = entry
    ref[0:dk, 0:dk] = delta.astype(BF16)
    ref[0:dk, dk:] = feed.astype(BF16)
    width = ref.shape[1]
    rows = [jnp.broadcast_to(t.astype(F32), (1, width)) for t in parts(keep)]
    rows.append(jnp.zeros((PAD - 3, width), F32))
    ref[dk:, :] = jnp.concatenate(rows, axis=0).astype(BF16)


def load_map(ref, dk):
    tail = ref[dk:, 0:1].astype(F32)
    return tail[0:1] + tail[1:2] + tail[2:3], ref[0:dk, 0:dk].astype(F32), ref[0:dk, dk:].astype(F32)


def join_body(dk, whole, late_ref, early_ref, out_ref):
    entry = join(load_map(late_ref, dk), load_map(early_ref, dk), whole)
    if whole:
        store_map(out_ref, dk, entry)
    else:
        out_ref[...] = entry[2].astype(BF16)


def in_order(rank, refs, scr):
    for s, ref in enumerate(refs):
        scr[rank ^ s] = ref[...]
    return [load_map(scr.at[c], scr.shape[1] - PAD) for c in range(len(refs))]


def total_body(dk, need_map, where, *refs):
    *maps, out_ref, scr = refs
    maps = in_order(where[0], maps, scr)
    while len(maps) > 1:
        maps = [
            join(maps[n + 1], maps[n], need_map or n > 0) for n in range(0, len(maps), 2)
        ]
    if need_map:
        store_map(out_ref, dk, maps[0])
    else:
        out_ref[...] = maps[0][2].astype(BF16)


def prefix_body(dk, where, *refs):
    *maps, a_ref, b_ref, scr = refs
    maps = in_order(where[0], maps, scr)
    a_ref[0] = (iota2((dk, dk), 0) == iota2((dk, dk), 1)).astype(BF16)
    b_ref[0] = jnp.zeros(b_ref.shape[1:], F32)
    unit = (iota2((dk, dk), 0) == iota2((dk, dk), 1)).astype(F32)
    keep, delta, feed = maps[0]
    state = jnp.concatenate([keep * unit - delta, feed], axis=1)
    for c in range(1, len(maps)):
        a_ref[c] = state[:, 0:dk].astype(BF16)
        b_ref[c] = state[:, dk:]
        if c + 1 < len(maps):
            keep, delta, feed = maps[c]
            feed = jnp.concatenate([jnp.zeros((dk, dk), F32), feed], axis=1)
            state = advance(keep, delta, feed, state)


def enter_body(dk, where, a_ref, b_ref, feed_ref, *refs):
    *late, scr = refs
    late, outs = late[: len(late) - a_ref.shape[0]], late[len(late) - a_ref.shape[0] :]
    state = feed_ref[...].astype(F32)
    if late:
        state = advance(*load_map(late[0], dk), state)
    for c in range(len(outs)):
        scr[c] = (dot(a_ref[c], state) + b_ref[c]).astype(BF16)
    for s, out in enumerate(outs):
        out[...] = scr[where[0] ^ s]


def project_body(dv, where, x_ref, y_ref, gate_ref, gain_ref, w_ref, *refs):
    *states, send_ref, normed_ref = refs
    rank, half = where[0], where[1]
    outs = [dot(x_ref[s], state[...]) + y_ref[s] for s, state in enumerate(states)]
    for s, o in enumerate(outs):
        at = pl.multiple_of((rank ^ s) * dv, dv)
        gate = gate_ref[:, pl.ds(at, dv)].astype(F32)
        inverse = lax.rsqrt(jnp.mean(o * o, axis=-1, keepdims=True) + EPS)
        done = o * inverse * gain_ref[...] * (gate / (1.0 + jnp.exp(-gate)))
        normed_ref[:, pl.ds(at, dv)] = done.astype(BF16)
    columns = send_ref.shape[1]
    start = (1 - half) * columns
    normed = normed_ref[...]
    step = 256
    for n in range(columns // step):
        at = pl.multiple_of(start + n * step, step)
        send_ref[:, n * step : (n + 1) * step] = dot(normed, w_ref[:, pl.ds(at, step)]).astype(BF16)


def own_body(where, w_ref, normed_ref, out_ref):
    columns = out_ref.shape[1]
    start = where[1] * columns
    normed = normed_ref[...]
    step = 256
    for n in range(columns // step):
        at = pl.multiple_of(start + n * step, step)
        out_ref[:, n * step : (n + 1) * step] = dot(normed, w_ref[:, pl.ds(at, step)])


def per_device(queries, key_rows, values, out_gate, write_rate, log_decay, norm_gain, out_weight):
    tokens = queries.shape[0]
    group = write_rate.shape[0]
    dv = norm_gain.shape[0]
    dk = dv
    rep = group // (queries.shape[1] // dk)
    ranks = lax.axis_size("seq")
    halves = lax.axis_size("head")
    groups = ranks // group
    assert ranks % group == 0 and group & (group - 1) == 0 and halves == 2
    columns = out_weight.shape[1] // halves
    index = lax.axis_index("seq")
    where = jnp.stack([index % group, lax.axis_index("head")]).astype(jnp.int32)
    shape = jax.ShapeDtypeStruct
    vmem, hbm, smem = pltpu.VMEM, pltpu.HBM, pltpu.SMEM
    cube = 2 * tokens * tokens * (dk + dv)
    need_map = groups > 2
    map_shape = shape((dk + PAD, dk + dv), BF16)
    feed_shape = shape((dk, dv), BF16)
    ordered = pltpu.VMEM((group,) + map_shape.shape, BF16)

    def swap(slots):
        came = [slots[0]]
        for s in range(1, group):
            pairs = [(i, (i // group) * group + ((i % group) ^ s)) for i in range(ranks)]
            came.append(lax.ppermute(slots[s], "seq", pairs))
        return came

    def later(x, shift):
        pairs = [(i, i + shift * group) for i in range(ranks - shift * group)]
        return lax.ppermute(x, "seq", pairs)

    pinned = [
        pltpu.with_memory_space_constraint(x, hbm)
        for x in (key_rows, values, write_rate, log_decay)
    ]
    *maps, wu, sums, cols = call(
        functools.partial(map_body, dk, dv, rep),
        [map_shape] * group
        + [
            shape((group, tokens, dk + dv), BF16),
            shape((group, tokens), F32),
            shape((tokens, group), F32),
        ],
        [smem] + [hbm] * 4,
        [
            pltpu.VMEM(key_rows.shape, BF16),
            pltpu.VMEM(values.shape, BF16),
            pltpu.VMEM(write_rate.shape, F32),
            pltpu.VMEM(log_decay.shape, F32),
            pltpu.SemaphoreType.DMA((4,)),
        ],
        group * 16 * cube,
    )(where, *pinned)
    maps = swap(maps)
    x, y = call(
        functools.partial(terms_body, dk, rep),
        [shape((group, tokens, dk), BF16), shape((group, tokens, dv), F32)],
        [smem] + [vmem] * 5,
        (),
        group * 4 * cube,
    )(where, queries, key_rows, wu, sums, cols)
    own = call(
        functools.partial(total_body, dk, need_map),
        map_shape if need_map else feed_shape,
        [smem] + [vmem] * group,
        [ordered],
        group * cube,
    )(where, *maps)

    entry, feed = None, jnp.zeros(feed_shape.shape, BF16)
    window, send = 0, own
    while window < groups - 1:
        came = later(send, window + 1)
        last = 2 * window + 1 >= groups - 1
        if last:
            feed = came
        elif window == 0:
            entry = came
        else:
            entry = call(functools.partial(join_body, dk, True), map_shape, [vmem] * 2)(entry, came)
        window = 2 * window + 1
        if window < groups - 1:
            whole = 2 * window + 1 < groups - 1
            send = call(
                functools.partial(join_body, dk, whole),
                map_shape if whole else feed_shape,
                [vmem] * 2,
            )(own, entry)
    a, b = call(
        functools.partial(prefix_body, dk),
        [shape((group, dk, dk), BF16), shape((group, dk, dv), F32)],
        [smem] + [vmem] * group,
        [ordered],
        group * 4 * cube,
    )(where, *maps)
    late = [] if entry is None else [entry]
    states = call(
        functools.partial(enter_body, dk),
        [feed_shape] * group,
        [smem] + [vmem] * (3 + len(late)),
        [pltpu.VMEM((group, dk, dv), BF16)],
        cube * group,
    )(where, a, b, feed, *late)
    states = swap(states)

    work = 2 * tokens * columns * group * dv
    away, normed = call(
        functools.partial(project_body, dv),
        [shape((tokens, columns), BF16), shape((tokens, group * dv), BF16)],
        [smem] + [vmem] * (5 + group),
        (),
        work,
    )(where, x, y, out_gate, norm_gain.reshape(1, dv), out_weight, *states)
    came = lax.ppermute(away, "head", [(0, 1), (1, 0)])
    own = call(own_body, shape((tokens, columns), F32), [smem, vmem, vmem], (), work)(
        where, out_weight, normed
    )
    return (own + came.astype(F32)).astype(BF16)


def solution(mesh):
    return jax.shard_map(
        per_device,
        mesh=mesh,
        in_specs=(
            P("seq", "head"),
            P("seq", "head"),
            P("seq", "head"),
            P("seq", "head"),
            P("head", "seq"),
            P("head", "seq"),
            P(),
            P("head", None),
        ),
        out_specs=P("seq", "head"),
        check_vma=False,
    )
```

```python
import functools

import jax
import jax.numpy as jnp
from jax import lax
from jax.experimental import pallas as pl
from jax.experimental.pallas import tpu as pltpu
from jax.sharding import PartitionSpec as P

F32 = jnp.float32
BF16 = jnp.bfloat16
EPS = 1e-06
LEAF = 16
PAD = 16
SMALL = pltpu.CompilerParams(vmem_limit_bytes=24 * 1024 * 1024)


def dot(a, b):
    return jnp.dot(a.astype(BF16), b.astype(BF16), preferred_element_type=F32)


def dot_nt(a, b):
    return lax.dot_general(
        a.astype(BF16), b.astype(BF16), (((1,), (1,)), ((), ())), preferred_element_type=F32
    )


def dot_tn(a, b):
    return lax.dot_general(
        a.astype(BF16), b.astype(BF16), (((0,), (0,)), ((), ())), preferred_element_type=F32
    )


def exact_dot(a, b, dims):
    return lax.dot_general(
        a, b, (dims, ((), ())), precision=lax.Precision.HIGHEST, preferred_element_type=F32
    )


def parts(x):
    first = x.astype(BF16)
    rest = x - first.astype(F32)
    second = rest.astype(BF16)
    third = (rest - second.astype(F32)).astype(BF16)
    return [first, second, third]


def iota2(shape, dim):
    return lax.broadcasted_iota(jnp.int32, shape, dim)


def call(body, outs, specs, scratch=(), flops=0):
    return pl.pallas_call(
        body,
        out_shape=outs,
        in_specs=[pl.BlockSpec(memory_space=space) for space in specs],
        out_specs=jax.tree.map(lambda _: pl.BlockSpec(memory_space=pltpu.VMEM), outs),
        scratch_shapes=list(scratch),
        compiler_params=SMALL,
        cost_estimate=pl.CostEstimate(flops=flops, bytes_accessed=1 << 20, transcendentals=0),
    )


def unit_rows(x):
    return x * lax.rsqrt(jnp.sum(x * x, axis=-1, keepdims=True) + EPS)


def advance(keep, delta, feed, state):
    return keep * state - dot(delta, state) + feed


def join(late, early, whole=True):
    keep, delta, feed = late
    keep_e, delta_e, feed_e = early
    if not whole:
        return None, None, advance(keep, delta, feed, feed_e)
    dk = delta.shape[1]
    both = dot(delta, jnp.concatenate([delta_e, feed_e], axis=1))
    delta_new = keep * delta_e + keep_e * delta - both[:, 0:dk]
    return keep * keep_e, delta_new, keep * feed_e + feed - both[:, dk:]


def key_block(ref, col, dk):
    return unit_rows(ref[:, pl.ds(pl.multiple_of(col * dk, dk), dk)].astype(F32))


def slot_rows(ref, rank, slots, rep):
    return jnp.concatenate(
        [ref[pl.ds((rank ^ s) * rep + h, 1), :] for s in slots for h in range(rep)], axis=0
    )


def inverse_of(lows, i, j):
    tokens = i.shape[0]
    unit = (i == j).astype(F32)
    leaf = (i // LEAF) == (j // LEAF)
    power = [jnp.where(leaf, low, 0.0) for low in lows]
    inverse = [unit - p for p in power]
    power = [dot(p, p) for p in power]
    size = 4
    while size < LEAF:
        both = [dot(p, jnp.concatenate([p, t], axis=1)) for p, t in zip(power, inverse)]
        power = [b[:, 0:tokens] for b in both]
        inverse = [t + b[:, tokens:] for t, b in zip(inverse, both)]
        size *= 2
    inverse = [t + dot(p, t) for p, t in zip(power, inverse)]
    size = LEAF
    while size < tokens:
        off = ((i // size) != (j // size)) & ((i // (2 * size)) == (j // (2 * size)))
        mid = [dot(jnp.where(off, low, 0.0), t) for low, t in zip(lows, inverse)]
        inverse = [t - dot(t, m) for m, t in zip(mid, inverse)]
        size *= 2
    return inverse, unit


def map_body(dk, dv, rep, slots, where, k_in, v_in, rate_in, decay_in, *refs):
    count = len(slots)
    maps, refs = refs[:count], refs[count:]
    wu_ref, sums_ref, cols_ref, k_ref, v_ref, rate_ref, decay_ref, sems = refs
    tokens = k_in.shape[0]
    rank = where[0]
    pairs = [(rate_in, rate_ref), (decay_in, decay_ref), (k_in, k_ref), (v_in, v_ref)]
    copies = [pltpu.make_async_copy(*p, sems.at[n]) for n, p in enumerate(pairs)]
    for copy in copies:
        copy.start()
    i = iota2((tokens, tokens), 0)
    j = iota2((tokens, tokens), 1)
    lower = (i >= j).astype(F32)
    unit = (i == j).astype(F32)
    copies[0].wait()
    copies[1].wait()
    decays = slot_rows(decay_ref, rank, slots, rep)
    rates = slot_rows(rate_ref, rank, slots, rep)
    cum_rows = exact_dot(decays, lower, ((1,), (1,)))
    cum_cols = exact_dot(lower, decays, ((1,), (1,)))
    rate_cols = exact_dot(unit, rates, ((1,), (1,)))
    sums_ref[...] = cum_rows
    cols_ref[...] = cum_cols
    copies[2].wait()
    keys = [key_block(k_ref, rank ^ s, dk) for s in slots]
    dots = [dot_nt(key, key) for key in keys]
    copies[3].wait()
    lows, rhs, tails, keeps = [], [], [], []
    for n in range(count * rep):
        key = keys[n // rep]
        at = pl.multiple_of(((rank ^ slots[n // rep]) * rep + n % rep) * dv, dv)
        value = v_ref[:, pl.ds(at, dv)].astype(F32)
        rate = rate_cols[:, n : n + 1]
        cum_col = cum_cols[:, n : n + 1]
        cum_row = cum_rows[n : n + 1, :]
        gap = jnp.where(i > j, cum_col - cum_row, 0.0)
        lows.append(jnp.where(i > j, rate * dots[n // rep] * jnp.exp(gap), 0.0))
        rhs.append(jnp.concatenate([(rate * jnp.exp(cum_col)) * key, rate * value], axis=1))
        last = cum_row[:, tokens - 1 : tokens]
        tails.append(key * jnp.exp(last - cum_col))
        keeps.append(jnp.exp(last))
    inverse, unit = inverse_of(lows, i, j)
    solved = [r + dot(t - unit, r) for t, r in zip(inverse, rhs)]
    for n in range(count * rep):
        wu_ref[n] = solved[n].astype(BF16)
    moved = [dot_tn(t, r) for t, r in zip(tails, solved)]
    entries = [(e, m[:, 0:dk], m[:, dk:]) for e, m in zip(keeps, moved)]
    for n, ref in enumerate(maps):
        store_maps(ref, entries[n * rep : (n + 1) * rep])


def terms_body(dk, rep, slots, where, q_ref, k_ref, wu_ref, sums_ref, cols_ref, x_ref, y_ref):
    tokens = q_ref.shape[0]
    rank = where[0]
    i = iota2((tokens, tokens), 0)
    j = iota2((tokens, tokens), 1)
    queries, dots = [], []
    for s in slots:
        query = key_block(q_ref, rank ^ s, dk) * dk**-0.5
        queries.append(query)
        dots.append(dot_nt(query, key_block(k_ref, rank ^ s, dk)))
    for n in range(len(slots) * rep):
        cum_col = cols_ref[:, n : n + 1]
        gap = jnp.where(i >= j, cum_col - sums_ref[n : n + 1, :], 0.0)
        scores = jnp.where(i >= j, dots[n // rep] * jnp.exp(gap), 0.0)
        inner = dot(scores, wu_ref[n])
        x_ref[n] = (queries[n // rep] * jnp.exp(cum_col) - inner[:, 0:dk]).astype(BF16)
        y_ref[n] = inner[:, dk:]


def store_maps(ref, entries):
    dk = entries[0][1].shape[0]
    for h, (_, delta, feed) in enumerate(entries):
        rows = slice(h * dk, (h + 1) * dk)
        ref[rows, 0:dk] = delta.astype(BF16)
        ref[rows, dk:] = feed.astype(BF16)
    width = ref.shape[1]
    rows = [jnp.broadcast_to(t.astype(F32), (1, width)) for e in entries for t in parts(e[0])]
    rows.append(jnp.zeros((PAD - len(rows), width), F32))
    ref[len(entries) * dk :, :] = jnp.concatenate(rows, axis=0).astype(BF16)


def load_maps(ref, dk, rep):
    tail = ref[rep * dk :, 0:dk].astype(F32)
    out = []
    for h in range(rep):
        keep = (tail[3 * h : 3 * h + 1] + tail[3 * h + 1 : 3 * h + 2]) + tail[3 * h + 2 : 3 * h + 3]
        rows = slice(h * dk, (h + 1) * dk)
        out.append((keep[:, 0:1], ref[rows, 0:dk].astype(F32), ref[rows, dk:].astype(F32)))
    return out


def pick(flag, yes, no):
    return [tuple(jnp.where(flag == 1, a, b) for a, b in zip(y, n)) for y, n in zip(yes, no)]


def in_order(rank, refs, scr, dk, rep):
    for s, ref in enumerate(refs):
        scr[rank ^ s] = ref[...]
    return [load_maps(scr.at[c], dk, rep) for c in range(len(refs))]


def total_body(dk, rep, whole, where, *refs):
    *maps, out_ref, scr = refs
    maps = in_order(where[0], maps, scr, dk, rep)
    while len(maps) > 1:
        maps = [
            [join(l, e, whole or n > 0) for l, e in zip(maps[n + 1], maps[n])]
            for n in range(0, len(maps), 2)
        ]
    store_send(out_ref, maps[0], whole)


def store_send(ref, entries, whole):
    if whole:
        store_maps(ref, entries)
        return
    for h, (_, _, feed) in enumerate(entries):
        ref[h * feed.shape[0] : (h + 1) * feed.shape[0], :] = feed.astype(BF16)


def block_body(dk, rep, step, whole, where, own_ref, came_ref, out_ref):
    own, came = load_maps(own_ref, dk, rep), load_maps(came_ref, dk, rep)
    flag = (where[2] >> step) & 1
    late, early = pick(flag, own, came), pick(flag, came, own)
    store_send(out_ref, [join(l, e, whole) for l, e in zip(late, early)], whole)


def entry_body(dk, rep, step, where, entry_ref, came_ref, out_ref):
    entry, came = load_maps(entry_ref, dk, rep), load_maps(came_ref, dk, rep)
    flag = (where[2] >> step) & 1
    store_maps(out_ref, pick(flag, [join(l, e) for l, e in zip(entry, came)], entry))


def first_entry_body(dk, rep, where, came_ref, out_ref):
    came = load_maps(came_ref, dk, rep)
    none = [(jnp.ones_like(k), jnp.zeros_like(d), jnp.zeros_like(f)) for k, d, f in came]
    store_maps(out_ref, pick(where[2] & 1, came, none))


def prefix_body(dk, rep, where, *refs):
    *maps, a_ref, b_ref, scr = refs
    maps = in_order(where[0], maps, scr, dk, rep)
    unit = (iota2((dk, dk), 0) == iota2((dk, dk), 1)).astype(F32)
    none = jnp.zeros((dk, dk), F32)
    states = [jnp.concatenate([unit, none], axis=1) for _ in range(rep)]
    for c in range(len(maps)):
        for h in range(rep):
            a_ref[c, h] = states[h][:, 0:dk].astype(BF16)
            b_ref[c, h] = states[h][:, dk:]
            keep, delta, feed = maps[c][h]
            if c == 0:
                states[h] = jnp.concatenate([keep * unit - delta, feed], axis=1)
            elif c + 1 < len(maps):
                feed = jnp.concatenate([none, feed], axis=1)
                states[h] = advance(keep, delta, feed, states[h])


def enter_body(dk, rep, step, where, a_ref, b_ref, feed_ref, *refs):
    *refs, scr = refs
    blocks = a_ref.shape[0]
    late, outs = refs[: len(refs) - blocks], refs[len(refs) - blocks :]
    flag = (where[2] >> step) & 1
    entry = load_maps(late[0], dk, rep) if late else None
    for h in range(rep):
        rows = slice(h * dk, (h + 1) * dk)
        state = jnp.where(flag == 1, feed_ref[rows, :].astype(F32), 0.0)
        if late:
            state = advance(*entry[h], state)
        for c in range(blocks):
            scr[c, rows, :] = (dot(a_ref[c, h], state) + b_ref[c, h]).astype(BF16)
    for s, out in enumerate(outs):
        out[...] = scr[where[0] ^ s]


def split_slots(group):
    first = list(range(1, group // 2 + 1))
    return first, [s for s in range(group) if s not in first]


def project_body(dk, dv, rep, slots, cut, where, *refs):
    x0, y0, x1, y1, gate_ref, gain_ref, w_ref, *states, send_ref, normed_ref = refs
    rank, half = where[0], where[1]
    outs = []
    for n, s in enumerate(slots):
        x_ref, y_ref, at = (x0, y0, n) if n < cut else (x1, y1, n - cut)
        for h in range(rep):
            state = states[s][h * dk : (h + 1) * dk, :]
            outs.append((s, h, dot(x_ref[at * rep + h], state) + y_ref[at * rep + h]))
    for s, h, o in outs:
        at = pl.multiple_of(((rank ^ s) * rep + h) * dv, dv)
        gate = gate_ref[:, pl.ds(at, dv)].astype(F32)
        inverse = lax.rsqrt(jnp.mean(o * o, axis=-1, keepdims=True) + EPS)
        done = o * inverse * gain_ref[...] * (gate / (1.0 + jnp.exp(-gate)))
        normed_ref[:, pl.ds(at, dv)] = done.astype(BF16)
    columns = send_ref.shape[1]
    start = (1 - half) * columns
    normed = normed_ref[...]
    step = 256
    for n in range(columns // step):
        at = pl.multiple_of(start + n * step, step)
        send_ref[:, n * step : (n + 1) * step] = dot(normed, w_ref[:, pl.ds(at, step)]).astype(BF16)


def own_body(where, w_ref, normed_ref, out_ref):
    columns = out_ref.shape[1]
    start = where[1] * columns
    normed = normed_ref[...]
    step = 256
    for n in range(columns // step):
        at = pl.multiple_of(start + n * step, step)
        out_ref[:, n * step : (n + 1) * step] = dot(normed, w_ref[:, pl.ds(at, step)])


def per_device(queries, key_rows, values, out_gate, write_rate, log_decay, norm_gain, out_weight):
    tokens = queries.shape[0]
    heads = write_rate.shape[0]
    dv = norm_gain.shape[0]
    dk = dv
    group = queries.shape[1] // dk
    rep = heads // group
    ranks = lax.axis_size("seq")
    halves = lax.axis_size("head")
    groups = ranks // group
    assert ranks % group == 0 and halves == 2
    assert group & (group - 1) == 0 and groups & (groups - 1) == 0
    steps = groups.bit_length() - 1
    columns = out_weight.shape[1] // halves
    index = lax.axis_index("seq")
    where = jnp.stack([index % group, lax.axis_index("head"), index // group]).astype(jnp.int32)
    shape = jax.ShapeDtypeStruct
    vmem, hbm, smem = pltpu.VMEM, pltpu.HBM, pltpu.SMEM
    cube = 2 * tokens * tokens * (dk + dv)
    map_shape = shape((rep * dk + PAD, dk + dv), BF16)
    feed_shape = shape((rep * dk, dv), BF16)
    ordered = pltpu.VMEM((group,) + map_shape.shape, BF16)
    first, last = split_slots(group)

    def swap(x, flip):
        return lax.ppermute(x, "seq", [(i, i ^ flip) for i in range(ranks)])

    pinned = [
        pltpu.with_memory_space_constraint(x, hbm)
        for x in (key_rows, values, write_rate, log_decay)
    ]
    maps, terms = [None] * group, []
    for slots in (first, last):
        jobs = len(slots) * rep
        *made, wu, sums, cols = call(
            functools.partial(map_body, dk, dv, rep, slots),
            [map_shape] * len(slots)
            + [
                shape((jobs, tokens, dk + dv), BF16),
                shape((jobs, tokens), F32),
                shape((tokens, jobs), F32),
            ],
            [smem] + [hbm] * 4,
            [
                pltpu.VMEM(key_rows.shape, BF16),
                pltpu.VMEM(values.shape, BF16),
                pltpu.VMEM(write_rate.shape, F32),
                pltpu.VMEM(log_decay.shape, F32),
                pltpu.SemaphoreType.DMA((4,)),
            ],
            jobs * 16 * cube,
        )(where, *pinned)
        for s, x in zip(slots, made):
            maps[s] = swap(x, s) if s else x
        terms.append((wu, sums, cols))
    xy = []
    for slots, (wu, sums, cols) in zip((first, last), terms):
        jobs = len(slots) * rep
        xy += call(
            functools.partial(terms_body, dk, rep, slots),
            [shape((jobs, tokens, dk), BF16), shape((jobs, tokens, dv), F32)],
            [smem] + [vmem] * 5,
            (),
            jobs * 4 * cube,
        )(where, queries, key_rows, wu, sums, cols)
    send = call(
        functools.partial(total_body, dk, rep, steps > 1),
        map_shape if steps > 1 else feed_shape,
        [smem] + [vmem] * group,
        [ordered],
        heads * cube,
    )(where, *maps)

    entry, feed = None, jnp.zeros(feed_shape.shape, BF16)
    for step in range(steps):
        came = swap(send, group << step)
        if step == steps - 1:
            feed = came
            continue
        whole = step + 2 < steps
        send = call(
            functools.partial(block_body, dk, rep, step, whole),
            map_shape if whole else feed_shape,
            [smem] + [vmem] * 2,
        )(where, send, came)
        if entry is None:
            entry = call(
                functools.partial(first_entry_body, dk, rep), map_shape, [smem, vmem]
            )(where, came)
        else:
            entry = call(
                functools.partial(entry_body, dk, rep, step), map_shape, [smem] + [vmem] * 2
            )(where, entry, came)
    a, b = call(
        functools.partial(prefix_body, dk, rep),
        [shape((group, rep, dk, dk), BF16), shape((group, rep, dk, dv), F32)],
        [smem] + [vmem] * group,
        [ordered],
        heads * 4 * cube,
    )(where, *maps)
    late = [] if entry is None else [entry]
    states = call(
        functools.partial(enter_body, dk, rep, max(steps - 1, 0)),
        [feed_shape] * group,
        [smem] + [vmem] * (3 + len(late)),
        [pltpu.VMEM((group,) + feed_shape.shape, BF16)],
        cube * heads,
    )(where, a, b, feed, *late)
    states = [states[0]] + [swap(states[s], s) for s in range(1, group)]

    work = 2 * tokens * columns * heads * dv
    away, normed = call(
        functools.partial(project_body, dk, dv, rep, first + last, len(first)),
        [shape((tokens, columns), BF16), shape((tokens, heads * dv), BF16)],
        [smem] + [vmem] * (7 + group),
        (),
        work,
    )(where, *xy, out_gate, norm_gain.reshape(1, dv), out_weight, *states)
    came = lax.ppermute(away, "head", [(0, 1), (1, 0)])
    own = call(own_body, shape((tokens, columns), F32), [smem, vmem, vmem], (), work)(
        where, out_weight, normed
    )
    return (own + came.astype(F32)).astype(BF16)


def solution(mesh):
    return jax.shard_map(
        per_device,
        mesh=mesh,
        in_specs=(
            P("seq", "head"),
            P("seq", "head"),
            P("seq", "head"),
            P("seq", "head"),
            P("head", "seq"),
            P("head", "seq"),
            P(),
            P("head", None),
        ),
        out_specs=P("seq", "head"),
        check_vma=False,
    )
```

```python
import functools

import jax
import jax.numpy as jnp
from jax import lax
from jax.experimental import pallas as pl
from jax.experimental.pallas import tpu as pltpu
from jax.sharding import PartitionSpec as P

F32 = jnp.float32
BF16 = jnp.bfloat16
EPS = 1e-06
LEAF = 16
PAD = 16
SMALL = pltpu.CompilerParams(vmem_limit_bytes=24 * 1024 * 1024)


def dot(a, b):
    return jnp.dot(a.astype(BF16), b.astype(BF16), preferred_element_type=F32)


def dot_nt(a, b):
    return lax.dot_general(
        a.astype(BF16), b.astype(BF16), (((1,), (1,)), ((), ())), preferred_element_type=F32
    )


def dot_tn(a, b):
    return lax.dot_general(
        a.astype(BF16), b.astype(BF16), (((0,), (0,)), ((), ())), preferred_element_type=F32
    )


def exact_dot(a, b, dims):
    return lax.dot_general(
        a, b, (dims, ((), ())), precision=lax.Precision.HIGHEST, preferred_element_type=F32
    )


def parts(x):
    first = x.astype(BF16)
    rest = x - first.astype(F32)
    second = rest.astype(BF16)
    third = (rest - second.astype(F32)).astype(BF16)
    return [first, second, third]


def iota2(shape, dim):
    return lax.broadcasted_iota(jnp.int32, shape, dim)


def call(body, outs, specs, scratch=(), flops=0):
    return pl.pallas_call(
        body,
        out_shape=outs,
        in_specs=[pl.BlockSpec(memory_space=space) for space in specs],
        out_specs=jax.tree.map(lambda _: pl.BlockSpec(memory_space=pltpu.VMEM), outs),
        scratch_shapes=list(scratch),
        compiler_params=SMALL,
        cost_estimate=pl.CostEstimate(flops=flops, bytes_accessed=1 << 20, transcendentals=0),
    )


def unit_rows(x):
    return x * lax.rsqrt(jnp.sum(x * x, axis=-1, keepdims=True) + EPS)


def advance(keep, delta, feed, state):
    return keep * state - dot(delta, state) + feed


def join(late, early, whole=True):
    keep, delta, feed = late
    keep_e, delta_e, feed_e = early
    if not whole:
        return None, None, advance(keep, delta, feed, feed_e)
    dk = delta.shape[1]
    both = dot(delta, jnp.concatenate([delta_e, feed_e], axis=1))
    delta_new = keep * delta_e + keep_e * delta - both[:, 0:dk]
    return keep * keep_e, delta_new, keep * feed_e + feed - both[:, dk:]


def key_block(ref, col, dk):
    return unit_rows(ref[:, pl.ds(pl.multiple_of(col * dk, dk), dk)].astype(F32))


def slot_rows(ref, rank, slots, rep):
    return jnp.concatenate(
        [ref[pl.ds((rank ^ s) * rep + h, 1), :] for s in slots for h in range(rep)], axis=0
    )


def solve(lows, sides, i, j):
    tokens = i.shape[0]
    leaf = (i // LEAF) == (j // LEAF)
    power = [jnp.where(leaf, low, 0.0).astype(BF16) for low in lows]
    full = [
        jnp.concatenate([jnp.where(leaf, 0.0, low), side], axis=1) for low, side in zip(lows, sides)
    ]
    full = neumann(power, full, LEAF)
    power = [f[:, 0:tokens].astype(BF16) for f in full]
    return neumann(power, [f[:, tokens:] for f in full], tokens // LEAF)


def neumann(power, sides, order):
    width = power[0].shape[1]
    sign, reach = -1.0, 1
    while 2 * reach < order:
        both = [
            dot(p, jnp.concatenate([p, s.astype(BF16)], axis=1)) for p, s in zip(power, sides)
        ]
        power = [b[:, 0:width].astype(BF16) for b in both]
        sides = [s + sign * b[:, width:] for s, b in zip(sides, both)]
        sign, reach = 1.0, 2 * reach
    return [s + sign * dot(p, s) for p, s in zip(power, sides)]


def map_body(dk, dv, rep, slots, where, k_in, v_in, rate_in, decay_in, *refs):
    count = len(slots)
    maps, refs = refs[:count], refs[count:]
    wu_ref, sums_ref, cols_ref, k_ref, v_ref, rate_ref, decay_ref, sems = refs
    tokens = k_in.shape[0]
    rank = where[0]
    pairs = [(rate_in, rate_ref), (decay_in, decay_ref), (k_in, k_ref), (v_in, v_ref)]
    copies = [pltpu.make_async_copy(*p, sems.at[n]) for n, p in enumerate(pairs)]
    for copy in copies:
        copy.start()
    i = iota2((tokens, tokens), 0)
    j = iota2((tokens, tokens), 1)
    lower = (i >= j).astype(F32)
    unit = (i == j).astype(F32)
    copies[0].wait()
    copies[1].wait()
    decays = slot_rows(decay_ref, rank, slots, rep)
    rates = slot_rows(rate_ref, rank, slots, rep)
    cum_rows = exact_dot(decays, lower, ((1,), (1,)))
    cum_cols = exact_dot(lower, decays, ((1,), (1,)))
    rate_cols = exact_dot(unit, rates, ((1,), (1,)))
    sums_ref[...] = cum_rows
    cols_ref[...] = cum_cols
    copies[2].wait()
    keys = [key_block(k_ref, rank ^ s, dk) for s in slots]
    dots = [dot_nt(key, key) for key in keys]
    copies[3].wait()
    lows, rhs, tails, keeps = [], [], [], []
    for n in range(count * rep):
        key = keys[n // rep]
        at = pl.multiple_of(((rank ^ slots[n // rep]) * rep + n % rep) * dv, dv)
        value = v_ref[:, pl.ds(at, dv)].astype(F32)
        rate = rate_cols[:, n : n + 1]
        cum_col = cum_cols[:, n : n + 1]
        cum_row = cum_rows[n : n + 1, :]
        gap = jnp.where(i > j, cum_col - cum_row, 0.0)
        lows.append(jnp.where(i > j, rate * dots[n // rep] * jnp.exp(gap), 0.0))
        rhs.append(jnp.concatenate([(rate * jnp.exp(cum_col)) * key, rate * value], axis=1))
        last = cum_row[:, tokens - 1 : tokens]
        tails.append(key * jnp.exp(last - cum_col))
        keeps.append(jnp.exp(last))
    solved = solve(lows, rhs, i, j)
    for n in range(count * rep):
        wu_ref[n] = solved[n].astype(BF16)
    moved = [dot_tn(t, r) for t, r in zip(tails, solved)]
    entries = [(e, m[:, 0:dk], m[:, dk:]) for e, m in zip(keeps, moved)]
    for n, ref in enumerate(maps):
        store_maps(ref, entries[n * rep : (n + 1) * rep])


def terms_body(dk, rep, slots, where, q_ref, k_ref, wu_ref, sums_ref, cols_ref, x_ref, y_ref):
    tokens = q_ref.shape[0]
    rank = where[0]
    i = iota2((tokens, tokens), 0)
    j = iota2((tokens, tokens), 1)
    queries, dots = [], []
    for s in slots:
        query = key_block(q_ref, rank ^ s, dk) * dk**-0.5
        queries.append(query)
        dots.append(dot_nt(query, key_block(k_ref, rank ^ s, dk)))
    for n in range(len(slots) * rep):
        cum_col = cols_ref[:, n : n + 1]
        gap = jnp.where(i >= j, cum_col - sums_ref[n : n + 1, :], 0.0)
        scores = jnp.where(i >= j, dots[n // rep] * jnp.exp(gap), 0.0)
        inner = dot(scores, wu_ref[n])
        x_ref[n] = (queries[n // rep] * jnp.exp(cum_col) - inner[:, 0:dk]).astype(BF16)
        y_ref[n] = inner[:, dk:]


def store_maps(ref, entries):
    dk = entries[0][1].shape[0]
    for h, (_, delta, feed) in enumerate(entries):
        rows = slice(h * dk, (h + 1) * dk)
        ref[rows, 0:dk] = delta.astype(BF16)
        ref[rows, dk:] = feed.astype(BF16)
    width = ref.shape[1]
    rows = [jnp.broadcast_to(t.astype(F32), (1, width)) for e in entries for t in parts(e[0])]
    rows.append(jnp.zeros((PAD - len(rows), width), F32))
    ref[len(entries) * dk :, :] = jnp.concatenate(rows, axis=0).astype(BF16)


def load_maps(ref, dk, rep):
    tail = ref[rep * dk :, 0:dk].astype(F32)
    out = []
    for h in range(rep):
        keep = (tail[3 * h : 3 * h + 1] + tail[3 * h + 1 : 3 * h + 2]) + tail[3 * h + 2 : 3 * h + 3]
        rows = slice(h * dk, (h + 1) * dk)
        out.append((keep[:, 0:1], ref[rows, 0:dk].astype(F32), ref[rows, dk:].astype(F32)))
    return out


def pick(flag, yes, no):
    return [tuple(jnp.where(flag == 1, a, b) for a, b in zip(y, n)) for y, n in zip(yes, no)]


def in_order(rank, refs, scr, dk, rep):
    for s, ref in enumerate(refs):
        scr[rank ^ s] = ref[...]
    return [load_maps(scr.at[c], dk, rep) for c in range(len(refs))]


def total_body(dk, rep, whole, where, *refs):
    *maps, _, out_ref, scr = refs
    maps = in_order(where[0], maps, scr, dk, rep)
    while len(maps) > 1:
        maps = [
            [join(l, e, whole or n > 0) for l, e in zip(maps[n + 1], maps[n])]
            for n in range(0, len(maps), 2)
        ]
    store_send(out_ref, maps[0], whole)


def store_send(ref, entries, whole):
    if whole:
        store_maps(ref, entries)
        return
    for h, (_, _, feed) in enumerate(entries):
        ref[h * feed.shape[0] : (h + 1) * feed.shape[0], :] = feed.astype(BF16)


def block_body(dk, rep, step, whole, where, own_ref, came_ref, out_ref):
    own, came = load_maps(own_ref, dk, rep), load_maps(came_ref, dk, rep)
    flag = (where[2] >> step) & 1
    late, early = pick(flag, own, came), pick(flag, came, own)
    store_send(out_ref, [join(l, e, whole) for l, e in zip(late, early)], whole)


def prefix_body(dk, rep, count, where, *refs):
    came, maps, (a_ref, b_ref, scr) = refs[:count], refs[count:-3], refs[-3:]
    maps = in_order(where[0], maps, scr, dk, rep)
    unit = (iota2((dk, dk), 0) == iota2((dk, dk), 1)).astype(F32)
    none = jnp.zeros((dk, dk), F32)
    entry = [(jnp.ones((1, 1), F32), none, none) for _ in range(rep)]
    for step, ref in enumerate(came):
        block = load_maps(ref, dk, rep)
        if step > 0:
            block = [join(l, e) for l, e in zip(entry, block)]
        entry = pick((where[2] >> step) & 1, block, entry)
    states = [jnp.concatenate([k * unit - d, f], axis=1) for k, d, f in entry]
    for c in range(len(maps)):
        for h in range(rep):
            a_ref[c, h] = states[h][:, 0:dk].astype(BF16)
            b_ref[c, h] = states[h][:, dk:]
            keep, delta, feed = maps[c][h]
            if c + 1 < len(maps):
                feed = jnp.concatenate([none, feed], axis=1)
                states[h] = advance(keep, delta, feed, states[h])


def enter_body(dk, rep, step, where, a_ref, b_ref, feed_ref, *outs):
    flag = (where[2] >> step) & 1
    feed = jnp.where(flag == 1, feed_ref[...].astype(F32), 0.0).astype(BF16)
    for s, out in enumerate(outs):
        for h in range(rep):
            rows = slice(h * dk, (h + 1) * dk)
            at = where[0] ^ s
            out[rows, :] = (dot(a_ref[at, h], feed[rows]) + b_ref[at, h]).astype(BF16)


def project_body(dk, dv, rep, where, x_ref, y_ref, gate_ref, gain_ref, w_ref, *refs):
    *states, send_ref, normed_ref = refs
    rank, half = where[0], where[1]
    outs = []
    for n in range(len(states) * rep):
        state = states[n // rep][n % rep * dk : (n % rep + 1) * dk, :]
        outs.append(dot(x_ref[n], state) + y_ref[n])
    for n, o in enumerate(outs):
        at = pl.multiple_of(((rank ^ (n // rep)) * rep + n % rep) * dv, dv)
        gate = gate_ref[:, pl.ds(at, dv)].astype(F32)
        inverse = lax.rsqrt(jnp.mean(o * o, axis=-1, keepdims=True) + EPS)
        done = o * inverse * gain_ref[...] * (gate / (1.0 + jnp.exp(-gate)))
        normed_ref[:, pl.ds(at, dv)] = done.astype(BF16)
    columns = send_ref.shape[1]
    start = (1 - half) * columns
    normed = normed_ref[...]
    step = 256
    for n in range(columns // step):
        at = pl.multiple_of(start + n * step, step)
        send_ref[:, n * step : (n + 1) * step] = dot(normed, w_ref[:, pl.ds(at, step)]).astype(BF16)


def own_body(where, w_ref, normed_ref, out_ref):
    columns = out_ref.shape[1]
    start = where[1] * columns
    normed = normed_ref[...]
    step = 256
    for n in range(columns // step):
        at = pl.multiple_of(start + n * step, step)
        out_ref[:, n * step : (n + 1) * step] = dot(normed, w_ref[:, pl.ds(at, step)])


def per_device(queries, key_rows, values, out_gate, write_rate, log_decay, norm_gain, out_weight):
    tokens = queries.shape[0]
    heads = write_rate.shape[0]
    dv = norm_gain.shape[0]
    dk = dv
    group = queries.shape[1] // dk
    rep = heads // group
    ranks = lax.axis_size("seq")
    halves = lax.axis_size("head")
    groups = ranks // group
    assert ranks % group == 0 and halves == 2
    assert group & (group - 1) == 0 and groups & (groups - 1) == 0
    steps = groups.bit_length() - 1
    columns = out_weight.shape[1] // halves
    index = lax.axis_index("seq")
    where = jnp.stack([index % group, lax.axis_index("head"), index // group]).astype(jnp.int32)
    shape = jax.ShapeDtypeStruct
    vmem, hbm, smem = pltpu.VMEM, pltpu.HBM, pltpu.SMEM
    cube = 2 * tokens * tokens * (dk + dv)
    map_shape = shape((rep * dk + PAD, dk + dv), BF16)
    feed_shape = shape((rep * dk, dv), BF16)
    ordered = pltpu.VMEM((group,) + map_shape.shape, BF16)
    slots = list(range(group))

    def swap(x, flip):
        return lax.ppermute(x, "seq", [(i, i ^ flip) for i in range(ranks)])

    def swap_slots(made):
        came = {s: swap(made[s], s) for s in sorted(slots[1:], key=lambda s: -s.bit_count())}
        return [made[0]] + [came[s] for s in slots[1:]]

    pinned = [
        pltpu.with_memory_space_constraint(x, hbm)
        for x in (key_rows, values, write_rate, log_decay)
    ]
    *maps, wu, sums, cols = call(
        functools.partial(map_body, dk, dv, rep, slots),
        [map_shape] * group
        + [
            shape((heads, tokens, dk + dv), BF16),
            shape((heads, tokens), F32),
            shape((tokens, heads), F32),
        ],
        [smem] + [hbm] * 4,
        [
            pltpu.VMEM(key_rows.shape, BF16),
            pltpu.VMEM(values.shape, BF16),
            pltpu.VMEM(write_rate.shape, F32),
            pltpu.VMEM(log_decay.shape, F32),
            pltpu.SemaphoreType.DMA((4,)),
        ],
        heads * 16 * cube,
    )(where, *pinned)
    maps = swap_slots(maps)
    x, y = call(
        functools.partial(terms_body, dk, rep, slots),
        [shape((heads, tokens, dk), BF16), shape((heads, tokens, dv), F32)],
        [smem] + [vmem] * 5,
        (),
        heads * 4 * cube,
    )(where, queries, key_rows, wu, sums, cols)
    send = call(
        functools.partial(total_body, dk, rep, steps > 1),
        map_shape if steps > 1 else feed_shape,
        [smem] + [vmem] * group + [pl.ANY],
        [ordered],
        heads * cube,
    )(where, *maps, y)

    blocks, feed = [], jnp.zeros(feed_shape.shape, BF16)
    for step in range(steps):
        came = swap(send, group << step)
        if step == steps - 1:
            feed = came
            continue
        whole = step + 2 < steps
        send = call(
            functools.partial(block_body, dk, rep, step, whole),
            map_shape if whole else feed_shape,
            [smem] + [vmem] * 2,
        )(where, send, came)
        blocks.append(came)
    a, b = call(
        functools.partial(prefix_body, dk, rep, len(blocks)),
        [shape((group, rep, dk, dk), BF16), shape((group, rep, dk, dv), F32)],
        [smem] + [vmem] * (len(blocks) + group),
        [ordered],
        heads * 4 * cube,
    )(where, *blocks, *maps)
    states = call(
        functools.partial(enter_body, dk, rep, max(steps - 1, 0)),
        [feed_shape] * group,
        [smem] + [vmem] * 3,
        (),
        cube * heads,
    )(where, a, b, feed)
    states = swap_slots(states)

    work = 2 * tokens * columns * heads * dv
    away, normed = call(
        functools.partial(project_body, dk, dv, rep),
        [shape((tokens, columns), BF16), shape((tokens, heads * dv), BF16)],
        [smem] + [vmem] * (5 + group),
        (),
        work,
    )(where, x, y, out_gate, norm_gain.reshape(1, dv), out_weight, *states)
    came = lax.ppermute(away, "head", [(0, 1), (1, 0)])
    own = call(own_body, shape((tokens, columns), F32), [smem, vmem, vmem], (), work)(
        where, out_weight, normed
    )
    return (own + came.astype(F32)).astype(BF16)


def solution(mesh):
    return jax.shard_map(
        per_device,
        mesh=mesh,
        in_specs=(
            P("seq", "head"),
            P("seq", "head"),
            P("seq", "head"),
            P("seq", "head"),
            P("head", "seq"),
            P("head", "seq"),
            P(),
            P("head", None),
        ),
        out_specs=P("seq", "head"),
        check_vma=False,
    )
```

```python
import functools

import jax
import jax.numpy as jnp
from jax import lax
from jax.experimental import pallas as pl
from jax.experimental.pallas import tpu as pltpu
from jax.sharding import PartitionSpec as P

F32 = jnp.float32
BF16 = jnp.bfloat16
EPS = 1e-06
LEAF = 16
PAD = 16
SMALL = pltpu.CompilerParams(vmem_limit_bytes=24 * 1024 * 1024)


def dot(a, b):
    return jnp.dot(a.astype(BF16), b.astype(BF16), preferred_element_type=F32)


def dot_nt(a, b):
    return lax.dot_general(
        a.astype(BF16), b.astype(BF16), (((1,), (1,)), ((), ())), preferred_element_type=F32
    )


def dot_tn(a, b):
    return lax.dot_general(
        a.astype(BF16), b.astype(BF16), (((0,), (0,)), ((), ())), preferred_element_type=F32
    )


def exact_dot(a, b, dims):
    return lax.dot_general(
        a, b, (dims, ((), ())), precision=lax.Precision.HIGHEST, preferred_element_type=F32
    )


def parts(x):
    first = x.astype(BF16)
    rest = x - first.astype(F32)
    second = rest.astype(BF16)
    third = (rest - second.astype(F32)).astype(BF16)
    return [first, second, third]


def iota2(shape, dim):
    return lax.broadcasted_iota(jnp.int32, shape, dim)


def call(body, outs, specs, scratch=(), flops=0):
    return pl.pallas_call(
        body,
        out_shape=outs,
        in_specs=[pl.BlockSpec(memory_space=space) for space in specs],
        out_specs=jax.tree.map(lambda _: pl.BlockSpec(memory_space=pltpu.VMEM), outs),
        scratch_shapes=list(scratch),
        compiler_params=SMALL,
        cost_estimate=pl.CostEstimate(flops=flops, bytes_accessed=1 << 20, transcendentals=0),
    )


def unit_rows(x):
    return x * lax.rsqrt(jnp.sum(x * x, axis=-1, keepdims=True) + EPS)


def advance(keep, delta, feed, state):
    return keep * state - dot(delta, state) + feed


def join(late, early, whole=True):
    keep, delta, feed = late
    keep_e, delta_e, feed_e = early
    if not whole:
        return None, None, advance(keep, delta, feed, feed_e)
    dk = delta.shape[1]
    both = dot(delta, jnp.concatenate([delta_e, feed_e], axis=1))
    delta_new = keep * delta_e + keep_e * delta - both[:, 0:dk]
    return keep * keep_e, delta_new, keep * feed_e + feed - both[:, dk:]


def key_block(ref, col, dk):
    return unit_rows(ref[:, pl.ds(pl.multiple_of(col * dk, dk), dk)].astype(F32))


def slot_rows(ref, rank, slots, rep):
    return jnp.concatenate(
        [ref[pl.ds((rank ^ s) * rep + h, 1), :] for s in slots for h in range(rep)], axis=0
    )


def solve(lows, sides, i, j):
    tokens = i.shape[0]
    leaf = (i // LEAF) == (j // LEAF)
    power = [jnp.where(leaf, low, 0.0).astype(BF16) for low in lows]
    full = [
        jnp.concatenate([jnp.where(leaf, 0.0, low), side], axis=1) for low, side in zip(lows, sides)
    ]
    full = neumann(power, full, LEAF)
    power = [f[:, 0:tokens].astype(BF16) for f in full]
    return neumann(power, [f[:, tokens:] for f in full], tokens // LEAF)


def neumann(power, sides, order):
    width = power[0].shape[1]
    sign, reach = -1.0, 1
    while 2 * reach < order:
        both = [
            dot(p, jnp.concatenate([p, s.astype(BF16)], axis=1)) for p, s in zip(power, sides)
        ]
        power = [b[:, 0:width].astype(BF16) for b in both]
        sides = [s + sign * b[:, width:] for s, b in zip(sides, both)]
        sign, reach = 1.0, 2 * reach
    return [s + sign * dot(p, s) for p, s in zip(power, sides)]


def pack_body(dk, dv, rep, where, k_in, v_in, rate_in, decay_in, *refs):
    *outs, rate_ref, decay_ref, sems = refs
    tokens = k_in.shape[0]
    rank = where[0]
    pairs = [(rate_in, rate_ref), (decay_in, decay_ref)]
    for s, out in enumerate(outs):
        at = pl.multiple_of((rank ^ s) * dk, dk)
        pairs.append((k_in.at[:, pl.ds(at, dk)], out.at[0:tokens, 0:dk]))
        at = pl.multiple_of((rank ^ s) * rep * dv, rep * dv)
        pairs.append((v_in.at[:, pl.ds(at, rep * dv)], out.at[0:tokens, dk:]))
    copies = [pltpu.make_async_copy(*p, sems.at[n]) for n, p in enumerate(pairs)]
    for copy in copies:
        copy.start()
    copies[0].wait()
    copies[1].wait()
    for s, out in enumerate(outs):
        rows = [slot_rows(ref, rank, [s], rep) for ref in (rate_ref, decay_ref)]
        terms = [t.astype(F32) for t in parts(jnp.concatenate(rows, axis=0))]
        terms.append(jnp.zeros((PAD - 6 * rep, tokens), F32))
        out[tokens:, 0:tokens] = jnp.concatenate(terms, axis=0).astype(BF16)
        out[tokens:, tokens:] = jnp.zeros((PAD, out.shape[1] - tokens), BF16)
    for copy in copies[2:]:
        copy.wait()


def block_sides(decays, rates, tokens):
    i = iota2((tokens, tokens), 0)
    j = iota2((tokens, tokens), 1)
    lower = (i >= j).astype(F32)
    unit = (i == j).astype(F32)
    cum_rows = exact_dot(decays, lower, ((1,), (1,)))
    cum_cols = exact_dot(lower, decays, ((1,), (1,)))
    rate_cols = exact_dot(unit, rates, ((1,), (1,)))
    return i, j, cum_rows, cum_cols, rate_cols


def solve_blocks(keys, values, sides, rep):
    i, j, cum_rows, cum_cols, rate_cols = sides
    dots = [dot_nt(key, key) for key in keys]
    lows, rhs = [], []
    for n, value in enumerate(values):
        rate = rate_cols[:, n : n + 1]
        cum_col = cum_cols[:, n : n + 1]
        gap = jnp.where(i > j, cum_col - cum_rows[n : n + 1, :], 0.0)
        lows.append(jnp.where(i > j, rate * dots[n // rep] * jnp.exp(gap), 0.0))
        rhs.append(
            jnp.concatenate([(rate * jnp.exp(cum_col)) * keys[n // rep], rate * value], axis=1)
        )
    return solve(lows, rhs, i, j)


def owner_body(dk, dv, rep, where, *refs):
    *packs, _, send_ref, delta_ref, feed_ref, keep_ref, scr = refs
    blocks = len(packs)
    tokens = packs[0].shape[0] - PAD
    for s, pack in enumerate(packs):
        scr[where[0] ^ s] = pack[...]
    tails = [scr[c, tokens:, 0:tokens].astype(F32) for c in range(blocks)]
    size = 2 * rep
    tails = [t[0:size] + t[size : 2 * size] + t[2 * size : 3 * size] for t in tails]
    rates = jnp.concatenate([t[0:rep] for t in tails], axis=0)
    decays = jnp.concatenate([t[rep:] for t in tails], axis=0)
    sides = block_sides(decays, rates, tokens)
    cum_rows, cum_cols = sides[2], sides[3]
    keys = [unit_rows(scr[c, 0:tokens, 0:dk].astype(F32)) for c in range(blocks)]
    jobs = [(c, h) for c in range(blocks) for h in range(rep)]
    values = [scr[c, 0:tokens, dk + h * dv : dk + (h + 1) * dv].astype(F32) for c, h in jobs]
    solved = solve_blocks(keys, values, sides, rep)
    entries = []
    for n, (c, h) in enumerate(jobs):
        last = cum_rows[n : n + 1, tokens - 1 : tokens]
        moved = dot_tn(keys[c] * jnp.exp(last - cum_cols[:, n : n + 1]), solved[n])
        entries.append((jnp.exp(last), moved[:, 0:dk], moved[:, dk:]))
        delta_ref[n] = moved[:, 0:dk].astype(BF16)
        feed_ref[n] = moved[:, dk:]
        keep_ref[n : n + 1, :] = jnp.broadcast_to(jnp.exp(last), (1, keep_ref.shape[1]))
    for h in range(rep):
        send_ref[h * dk : (h + 1) * dk, :] = fold(entries[h::rep], False)[2].astype(BF16)


def fold(maps, whole):
    while len(maps) > 1:
        maps = [join(maps[n + 1], maps[n], whole or n > 0) for n in range(0, len(maps), 2)]
    return maps[0]


def block_maps(delta_ref, feed_ref, keep_ref, rep):
    maps = [
        (keep_ref[n : n + 1, 0:1], delta_ref[n].astype(F32), feed_ref[n])
        for n in range(delta_ref.shape[0])
    ]
    return [maps[h::rep] for h in range(rep)]


def total_body(rep, delta_ref, feed_ref, keep_ref, out_ref):
    store_maps(out_ref, [fold(m, True) for m in block_maps(delta_ref, feed_ref, keep_ref, rep)])


def terms_body(dk, dv, rep, slots, where, q_in, k_in, v_in, rate_in, decay_in, *refs):
    x_ref, y_ref, q_ref, k_ref, v_ref, rate_ref, decay_ref, sems = refs
    tokens = k_in.shape[0]
    rank = where[0]
    pairs = [(rate_in, rate_ref), (decay_in, decay_ref), (k_in, k_ref), (v_in, v_ref), (q_in, q_ref)]
    copies = [pltpu.make_async_copy(*p, sems.at[n]) for n, p in enumerate(pairs)]
    for copy in copies:
        copy.start()
    copies[0].wait()
    copies[1].wait()
    sides = block_sides(
        slot_rows(decay_ref, rank, slots, rep), slot_rows(rate_ref, rank, slots, rep), tokens
    )
    i, j, cum_rows, cum_cols, _ = sides
    copies[2].wait()
    keys = [key_block(k_ref, rank ^ s, dk) for s in slots]
    copies[3].wait()
    values = []
    for n in range(len(slots) * rep):
        at = pl.multiple_of(((rank ^ slots[n // rep]) * rep + n % rep) * dv, dv)
        values.append(v_ref[:, pl.ds(at, dv)].astype(F32))
    solved = solve_blocks(keys, values, sides, rep)
    copies[4].wait()
    queries = [key_block(q_ref, rank ^ s, dk) * dk**-0.5 for s in slots]
    dots = [dot_nt(query, key) for query, key in zip(queries, keys)]
    for n in range(len(slots) * rep):
        cum_col = cum_cols[:, n : n + 1]
        gap = jnp.where(i >= j, cum_col - cum_rows[n : n + 1, :], 0.0)
        scores = jnp.where(i >= j, dots[n // rep] * jnp.exp(gap), 0.0)
        inner = dot(scores, solved[n])
        x_ref[n] = (queries[n // rep] * jnp.exp(cum_col) - inner[:, 0:dk]).astype(BF16)
        y_ref[n] = inner[:, dk:]


def store_maps(ref, entries):
    dk = entries[0][1].shape[0]
    for h, (_, delta, feed) in enumerate(entries):
        rows = slice(h * dk, (h + 1) * dk)
        ref[rows, 0:dk] = delta.astype(BF16)
        ref[rows, dk:] = feed.astype(BF16)
    width = ref.shape[1]
    rows = [jnp.broadcast_to(t.astype(F32), (1, width)) for e in entries for t in parts(e[0])]
    rows.append(jnp.zeros((PAD - len(rows), width), F32))
    ref[len(entries) * dk :, :] = jnp.concatenate(rows, axis=0).astype(BF16)


def load_maps(ref, dk, rep):
    tail = ref[rep * dk :, 0:dk].astype(F32)
    out = []
    for h in range(rep):
        keep = (tail[3 * h : 3 * h + 1] + tail[3 * h + 1 : 3 * h + 2]) + tail[3 * h + 2 : 3 * h + 3]
        rows = slice(h * dk, (h + 1) * dk)
        out.append((keep[:, 0:1], ref[rows, 0:dk].astype(F32), ref[rows, dk:].astype(F32)))
    return out


def pick(flag, yes, no):
    return [tuple(jnp.where(flag == 1, a, b) for a, b in zip(y, n)) for y, n in zip(yes, no)]


def store_send(ref, entries, whole):
    if whole:
        store_maps(ref, entries)
        return
    for h, (_, _, feed) in enumerate(entries):
        ref[h * feed.shape[0] : (h + 1) * feed.shape[0], :] = feed.astype(BF16)


def block_body(dk, rep, step, whole, where, own_ref, came_ref, out_ref):
    own, came = load_maps(own_ref, dk, rep), load_maps(came_ref, dk, rep)
    flag = (where[2] >> step) & 1
    late, early = pick(flag, own, came), pick(flag, came, own)
    store_send(out_ref, [join(l, e, whole) for l, e in zip(late, early)], whole)


def four_join_body(dk, rep, own_ref, came_ref, out_ref):
    own = load_maps(own_ref, dk, rep)
    for h, entry in enumerate(own):
        rows = slice(h * dk, (h + 1) * dk)
        out_ref[rows, :] = advance(*entry, came_ref[rows, :].astype(F32)).astype(BF16)


def four_entry(dk, rep, group, feed_ref, map_ref):
    entry = []
    for h, (keep, delta, feed) in enumerate(load_maps(map_ref, dk, rep)):
        before = feed_ref[h * dk : (h + 1) * dk, :].astype(F32)
        entry.append(
            (
                jnp.where(group == 3, keep, 1.0),
                jnp.where(group == 3, delta, 0.0),
                jnp.where(group == 3, feed, jnp.where(group == 1, before, 0.0)),
            )
        )
    return entry


def block_entry(dk, rep, group, *came):
    none = jnp.zeros((dk, dk), F32)
    entry = [(jnp.ones((1, 1), F32), none, none) for _ in range(rep)]
    for step, ref in enumerate(came):
        block = load_maps(ref, dk, rep)
        if step > 0:
            block = [join(l, e) for l, e in zip(entry, block)]
        entry = pick((group >> step) & 1, block, entry)
    return entry


def prefix_body(dk, rep, entry_of, where, delta_ref, feed_ref, keep_ref, *refs):
    *came, a_ref, b_ref = refs
    maps = block_maps(delta_ref, feed_ref, keep_ref, rep)
    unit = (iota2((dk, dk), 0) == iota2((dk, dk), 1)).astype(F32)
    none = jnp.zeros((dk, dk), F32)
    entry = entry_of(dk, rep, where[2], *came)
    states = [jnp.concatenate([k * unit - d, f], axis=1) for k, d, f in entry]
    for c in range(a_ref.shape[0]):
        for h in range(rep):
            a_ref[c, h] = states[h][:, 0:dk].astype(BF16)
            b_ref[c, h] = states[h][:, dk:]
            keep, delta, feed = maps[h][c]
            if c + 1 < a_ref.shape[0]:
                feed = jnp.concatenate([none, feed], axis=1)
                states[h] = advance(keep, delta, feed, states[h])


def enter_body(dk, rep, feed_of, where, a_ref, b_ref, *refs):
    feeds, outs = refs[: len(refs) - a_ref.shape[0]], refs[len(refs) - a_ref.shape[0] :]
    feed = feed_of(where[2], *feeds).astype(BF16)
    for s, out in enumerate(outs):
        for h in range(rep):
            rows = slice(h * dk, (h + 1) * dk)
            at = where[0] ^ s
            out[rows, :] = (dot(a_ref[at, h], feed[rows]) + b_ref[at, h]).astype(BF16)


def four_feed(group, to_third, to_second):
    late = jnp.where(group == 3, to_third[...].astype(F32), 0.0)
    return jnp.where(group == 2, to_second[...].astype(F32), late)


def block_feed(step, group, feed_ref):
    return jnp.where((group >> step) & 1 == 1, feed_ref[...].astype(F32), 0.0)


def project_body(dk, dv, rep, slot, where, x_ref, y_ref, gate_ref, gain_ref, w_ref, state, *refs):
    *before, out_ref, normed_ref = refs
    own = (where[0] ^ slot) * rep
    outs = []
    for h in range(rep):
        n = slot * rep + h
        outs.append(dot(x_ref[n], state[h * dk : (h + 1) * dk, :]) + y_ref[n])
    for h, o in enumerate(outs):
        gate = gate_ref[:, pl.ds(pl.multiple_of((own + h) * dv, dv), dv)].astype(F32)
        inverse = lax.rsqrt(jnp.mean(o * o, axis=-1, keepdims=True) + EPS)
        done = o * inverse * gain_ref[...] * (gate / (1.0 + jnp.exp(-gate)))
        normed_ref[:, h * dv : (h + 1) * dv] = done.astype(BF16)
    columns = out_ref.shape[1]
    start = (1 - where[1]) * columns
    normed = normed_ref[...]
    rows = pl.ds(pl.multiple_of(own * dv, rep * dv), rep * dv)
    step = 256
    for n in range(columns // step):
        at = pl.multiple_of(start + n * step, step)
        cut = slice(n * step, (n + 1) * step)
        total = dot(normed, w_ref[rows, pl.ds(at, step)])
        if before:
            total = total + before[0][:, cut]
        out_ref[:, cut] = total.astype(out_ref.dtype)


def own_body(where, w_ref, *refs):
    *pieces, out_ref = refs
    columns = out_ref.shape[1]
    start = where[1] * columns
    width = pieces[0].shape[1]
    step = 256
    for n in range(columns // step):
        at = pl.multiple_of(start + n * step, step)
        total = 0.0
        for s, piece in enumerate(pieces):
            rows = pl.ds(pl.multiple_of((where[0] ^ s) * width, width), width)
            total = total + dot(piece[...], w_ref[rows, pl.ds(at, step)])
        out_ref[:, n * step : (n + 1) * step] = total


def per_device(queries, key_rows, values, out_gate, write_rate, log_decay, norm_gain, out_weight):
    tokens = queries.shape[0]
    heads = write_rate.shape[0]
    dv = norm_gain.shape[0]
    dk = dv
    group = queries.shape[1] // dk
    rep = heads // group
    ranks = lax.axis_size("seq")
    halves = lax.axis_size("head")
    groups = ranks // group
    assert ranks % group == 0 and halves == 2
    assert group & (group - 1) == 0 and groups & (groups - 1) == 0
    steps = groups.bit_length() - 1
    columns = out_weight.shape[1] // halves
    index = lax.axis_index("seq")
    where = jnp.stack([index % group, lax.axis_index("head"), index // group]).astype(jnp.int32)
    shape = jax.ShapeDtypeStruct
    vmem, hbm, smem = pltpu.VMEM, pltpu.HBM, pltpu.SMEM
    cube = 2 * tokens * tokens * (dk + dv)
    map_shape = shape((rep * dk + PAD, dk + dv), BF16)
    feed_shape = shape((rep * dk, dv), BF16)
    slots = list(range(group))

    def swap(x, flip, ends=None):
        pairs = [(i, i ^ flip) for i in range(ranks) if ends is None or i // group in ends]
        return lax.ppermute(x, "seq", pairs)

    def swap_slots(made):
        return [made[0]] + [swap(made[s], s) for s in slots[1:]]

    q_in, k_in, v_in, rate_in, decay_in = [
        pltpu.with_memory_space_constraint(x, hbm)
        for x in (queries, key_rows, values, write_rate, log_decay)
    ]
    small = [pltpu.VMEM(write_rate.shape, F32), pltpu.VMEM(log_decay.shape, F32)]
    pack_shape = shape((tokens + PAD, dk + rep * dv), BF16)
    packs = call(
        functools.partial(pack_body, dk, dv, rep),
        [pack_shape] * group,
        [smem] + [hbm] * 4,
        small + [pltpu.SemaphoreType.DMA((2 + 2 * group,))],
    )(where, k_in, v_in, rate_in, decay_in)
    packs = swap_slots(packs)
    x, y = call(
        functools.partial(terms_body, dk, dv, rep, slots),
        [shape((heads, tokens, dk), BF16), shape((heads, tokens, dv), F32)],
        [smem] + [hbm] * 5,
        [pltpu.VMEM(z.shape, BF16) for z in (queries, key_rows, values)]
        + small
        + [pltpu.SemaphoreType.DMA((5,))],
        heads * 16 * cube,
    )(where, q_in, k_in, v_in, rate_in, decay_in)
    jobs = group * rep
    feed, *blocks = call(
        functools.partial(owner_body, dk, dv, rep),
        [
            feed_shape,
            shape((jobs, dk, dk), BF16),
            shape((jobs, dk, dv), F32),
            shape((jobs, dk), F32),
        ],
        [smem] + [vmem] * group + [pl.ANY],
        [pltpu.VMEM((group,) + pack_shape.shape, BF16)],
        jobs * 16 * cube,
    )(where, *packs, y)

    came, feeds = [], [feed]
    entry_of, feed_of = block_entry, lambda group, feed: jnp.zeros(feed_shape.shape, F32)
    if steps == 1:
        feeds = [swap(feed, group)]
        feed_of = functools.partial(block_feed, 0)
    if steps > 1:
        if steps == 2:
            before = swap(feed, group)
        own = call(
            functools.partial(total_body, rep), map_shape, [vmem] * 3, (), jobs * 2 * cube
        )(*blocks)
    if steps == 2:
        came = [before, swap(own, group, (2, 3))]
        joined = call(
            functools.partial(four_join_body, dk, rep), feed_shape, [vmem] * 2, (), jobs * 64 * cube
        )(own, before)
        feeds = [swap(joined, 2 * group, (1, 3)), swap(joined, 3 * group, (1, 2))]
        entry_of, feed_of = four_entry, four_feed
    if steps > 2:
        send = own
        for step in range(steps):
            got = swap(send, group << step)
            if step == steps - 1:
                feeds = [got]
                continue
            whole = step + 2 < steps
            send = call(
                functools.partial(block_body, dk, rep, step, whole),
                map_shape if whole else feed_shape,
                [smem] + [vmem] * 2,
            )(where, send, got)
            came.append(got)
        feed_of = functools.partial(block_feed, steps - 1)
    a, b = call(
        functools.partial(prefix_body, dk, rep, entry_of),
        [shape((group, rep, dk, dk), BF16), shape((group, rep, dk, dv), F32)],
        [smem] + [vmem] * (3 + len(came)),
        (),
        jobs * 4 * cube,
    )(where, *blocks, *came)
    states = call(
        functools.partial(enter_body, dk, rep, feed_of),
        [feed_shape] * group,
        [smem] + [vmem] * (2 + len(feeds)),
        (),
        cube * jobs,
    )(where, a, b, *feeds)
    states = swap_slots(states)

    work = 2 * tokens * columns * heads * dv
    away, normed = [], []
    for s, state in enumerate(states):
        kind = F32 if s < group - 1 else BF16
        total, piece = call(
            functools.partial(project_body, dk, dv, rep, s),
            [shape((tokens, columns), kind), shape((tokens, rep * dv), BF16)],
            [smem] + [vmem] * (6 + len(away)),
            (),
            work // group,
        )(where, x, y, out_gate, norm_gain.reshape(1, dv), out_weight, state, *away)
        away = [total]
        normed.append(piece)
    came = lax.ppermute(away[0], "head", [(0, 1), (1, 0)])
    own = call(own_body, shape((tokens, columns), F32), [smem] + [vmem] * (1 + group), (), work)(
        where, out_weight, *normed
    )
    return (own + came.astype(F32)).astype(BF16)


def solution(mesh):
    return jax.shard_map(
        per_device,
        mesh=mesh,
        in_specs=(
            P("seq", "head"),
            P("seq", "head"),
            P("seq", "head"),
            P("seq", "head"),
            P("head", "seq"),
            P("head", "seq"),
            P(),
            P("head", None),
        ),
        out_specs=P("seq", "head"),
        check_vma=False,
    )
```

```python
import functools

import jax
import jax.numpy as jnp
from jax import lax
from jax.experimental import pallas as pl
from jax.experimental.pallas import tpu as pltpu
from jax.sharding import PartitionSpec as P

F32 = jnp.float32
BF16 = jnp.bfloat16
EPS = 1e-06
LEAF = 16
PAD = 16
SMALL = pltpu.CompilerParams(vmem_limit_bytes=24 * 1024 * 1024)


def dot(a, b):
    return jnp.dot(a.astype(BF16), b.astype(BF16), preferred_element_type=F32)


def dot_nt(a, b):
    return lax.dot_general(
        a.astype(BF16), b.astype(BF16), (((1,), (1,)), ((), ())), preferred_element_type=F32
    )


def dot_tn(a, b):
    return lax.dot_general(
        a.astype(BF16), b.astype(BF16), (((0,), (0,)), ((), ())), preferred_element_type=F32
    )


def exact_dot(a, b, dims):
    return lax.dot_general(
        a, b, (dims, ((), ())), precision=lax.Precision.HIGHEST, preferred_element_type=F32
    )


def parts(x):
    first = x.astype(BF16)
    rest = x - first.astype(F32)
    second = rest.astype(BF16)
    third = (rest - second.astype(F32)).astype(BF16)
    return [first, second, third]


def iota2(shape, dim):
    return lax.broadcasted_iota(jnp.int32, shape, dim)


def call(body, outs, specs, scratch=(), flops=0):
    return pl.pallas_call(
        body,
        out_shape=outs,
        in_specs=[pl.BlockSpec(memory_space=space) for space in specs],
        out_specs=jax.tree.map(lambda _: pl.BlockSpec(memory_space=pltpu.VMEM), outs),
        scratch_shapes=list(scratch),
        compiler_params=SMALL,
        cost_estimate=pl.CostEstimate(flops=flops, bytes_accessed=1 << 20, transcendentals=0),
    )


def unit_rows(x):
    return x * lax.rsqrt(jnp.sum(x * x, axis=-1, keepdims=True) + EPS)


def advance(keep, delta, feed, state):
    return keep * state - dot(delta, state) + feed


def join(late, early, whole=True):
    keep, delta, feed = late
    keep_e, delta_e, feed_e = early
    if not whole:
        return None, None, advance(keep, delta, feed, feed_e)
    dk = delta.shape[1]
    both = dot(delta, jnp.concatenate([delta_e, feed_e], axis=1))
    delta_new = keep * delta_e + keep_e * delta - both[:, 0:dk]
    return keep * keep_e, delta_new, keep * feed_e + feed - both[:, dk:]


def key_block(ref, col, dk):
    return unit_rows(ref[:, pl.ds(pl.multiple_of(col * dk, dk), dk)].astype(F32))


def slot_rows(ref, rank, slots, rep):
    return jnp.concatenate(
        [ref[pl.ds((rank ^ s) * rep + h, 1), :] for s in slots for h in range(rep)], axis=0
    )


def solve(lows, sides, i, j):
    tokens = i.shape[0]
    leaf = (i // LEAF) == (j // LEAF)
    unit = (i == j).astype(F32)
    power = [jnp.where(leaf, low, 0.0) for low in lows]
    inverse = [unit - p for p in power]
    power = [p.astype(BF16) for p in power]
    power = [dot(p, p).astype(BF16) for p in power]
    inverse = neumann(power, inverse, LEAF // 2, 1.0)
    full = [
        jnp.concatenate([jnp.where(leaf, 0.0, low), side], axis=1) for low, side in zip(lows, sides)
    ]
    full = [f + dot(t - unit, f) for t, f in zip(inverse, full)]
    power = [f[:, 0:tokens].astype(BF16) for f in full]
    return neumann(power, [f[:, tokens:] for f in full], tokens // LEAF, -1.0)


def neumann(power, sides, order, sign):
    width = power[0].shape[1]
    reach = 1
    while 2 * reach < order:
        both = [
            dot(p, jnp.concatenate([p, s.astype(BF16)], axis=1)) for p, s in zip(power, sides)
        ]
        power = [b[:, 0:width].astype(BF16) for b in both]
        sides = [s + sign * b[:, width:] for s, b in zip(sides, both)]
        sign, reach = 1.0, 2 * reach
    return [s + sign * dot(p, s) for p, s in zip(power, sides)]


def pack_body(dk, dv, rep, where, k_in, v_in, rate_in, decay_in, *refs):
    *outs, rate_ref, decay_ref, sems = refs
    tokens = k_in.shape[0]
    rank = where[0]
    pairs = [(rate_in, rate_ref), (decay_in, decay_ref)]
    for s, out in enumerate(outs):
        at = pl.multiple_of((rank ^ s) * dk, dk)
        pairs.append((k_in.at[:, pl.ds(at, dk)], out.at[0:tokens, 0:dk]))
        at = pl.multiple_of((rank ^ s) * rep * dv, rep * dv)
        pairs.append((v_in.at[:, pl.ds(at, rep * dv)], out.at[0:tokens, dk:]))
    copies = [pltpu.make_async_copy(*p, sems.at[n]) for n, p in enumerate(pairs)]
    for copy in copies:
        copy.start()
    copies[0].wait()
    copies[1].wait()
    for s, out in enumerate(outs):
        rows = [slot_rows(ref, rank, [s], rep) for ref in (rate_ref, decay_ref)]
        terms = [t.astype(F32) for t in parts(jnp.concatenate(rows, axis=0))]
        terms.append(jnp.zeros((PAD - 6 * rep, tokens), F32))
        out[tokens:, 0:tokens] = jnp.concatenate(terms, axis=0).astype(BF16)
        out[tokens:, tokens:] = jnp.zeros((PAD, out.shape[1] - tokens), BF16)
    for copy in copies[2:]:
        copy.wait()


def block_sides(decays, rates, tokens):
    i = iota2((tokens, tokens), 0)
    j = iota2((tokens, tokens), 1)
    lower = (i >= j).astype(F32)
    unit = (i == j).astype(F32)
    cum_rows = exact_dot(decays, lower, ((1,), (1,)))
    cum_cols = exact_dot(lower, decays, ((1,), (1,)))
    rate_cols = exact_dot(unit, rates, ((1,), (1,)))
    return i, j, cum_rows, cum_cols, rate_cols


def solve_blocks(keys, values, sides, rep):
    i, j, cum_rows, cum_cols, rate_cols = sides
    dots = [dot_nt(key, key) for key in keys]
    lows, rhs = [], []
    for n, value in enumerate(values):
        rate = rate_cols[:, n : n + 1]
        cum_col = cum_cols[:, n : n + 1]
        gap = jnp.where(i > j, cum_col - cum_rows[n : n + 1, :], 0.0)
        lows.append(jnp.where(i > j, rate * dots[n // rep] * jnp.exp(gap), 0.0))
        rhs.append(
            jnp.concatenate([(rate * jnp.exp(cum_col)) * keys[n // rep], rate * value], axis=1)
        )
    return solve(lows, rhs, i, j)


def owner_body(dk, dv, rep, where, *refs):
    *packs, _, send_ref, delta_ref, feed_ref, keep_ref, scr = refs
    blocks = len(packs)
    tokens = packs[0].shape[0] - PAD
    for s, pack in enumerate(packs):
        scr[where[0] ^ s] = pack[...]
    tails = [scr[c, tokens:, 0:tokens].astype(F32) for c in range(blocks)]
    size = 2 * rep
    tails = [t[0:size] + t[size : 2 * size] + t[2 * size : 3 * size] for t in tails]
    rates = jnp.concatenate([t[0:rep] for t in tails], axis=0)
    decays = jnp.concatenate([t[rep:] for t in tails], axis=0)
    sides = block_sides(decays, rates, tokens)
    cum_rows, cum_cols = sides[2], sides[3]
    keys = [unit_rows(scr[c, 0:tokens, 0:dk].astype(F32)) for c in range(blocks)]
    jobs = [(c, h) for c in range(blocks) for h in range(rep)]
    values = [scr[c, 0:tokens, dk + h * dv : dk + (h + 1) * dv].astype(F32) for c, h in jobs]
    solved = solve_blocks(keys, values, sides, rep)
    entries = []
    for n, (c, h) in enumerate(jobs):
        last = cum_rows[n : n + 1, tokens - 1 : tokens]
        moved = dot_tn(keys[c] * jnp.exp(last - cum_cols[:, n : n + 1]), solved[n])
        entries.append((jnp.exp(last), moved[:, 0:dk], moved[:, dk:]))
        delta_ref[n] = moved[:, 0:dk].astype(BF16)
        feed_ref[n] = moved[:, dk:]
        keep_ref[n : n + 1, :] = jnp.broadcast_to(jnp.exp(last), (1, keep_ref.shape[1]))
    for h in range(rep):
        send_ref[h * dk : (h + 1) * dk, :] = fold(entries[h::rep], False)[2].astype(BF16)


def fold(maps, whole):
    while len(maps) > 1:
        maps = [join(maps[n + 1], maps[n], whole or n > 0) for n in range(0, len(maps), 2)]
    return maps[0]


def block_maps(delta_ref, feed_ref, keep_ref, rep):
    maps = [
        (keep_ref[n : n + 1, 0:1], delta_ref[n].astype(F32), feed_ref[n])
        for n in range(delta_ref.shape[0])
    ]
    return [maps[h::rep] for h in range(rep)]


def total_body(rep, delta_ref, feed_ref, keep_ref, out_ref):
    store_maps(out_ref, [fold(m, True) for m in block_maps(delta_ref, feed_ref, keep_ref, rep)])


def terms_body(dk, dv, rep, slots, where, q_in, k_in, v_in, rate_in, decay_in, *refs):
    x_ref, y_ref, q_ref, k_ref, v_ref, rate_ref, decay_ref, sems = refs
    tokens = k_in.shape[0]
    rank = where[0]
    pairs = [(rate_in, rate_ref), (decay_in, decay_ref), (k_in, k_ref), (v_in, v_ref), (q_in, q_ref)]
    copies = [pltpu.make_async_copy(*p, sems.at[n]) for n, p in enumerate(pairs)]
    for copy in copies:
        copy.start()
    copies[0].wait()
    copies[1].wait()
    sides = block_sides(
        slot_rows(decay_ref, rank, slots, rep), slot_rows(rate_ref, rank, slots, rep), tokens
    )
    i, j, cum_rows, cum_cols, _ = sides
    copies[2].wait()
    keys = [key_block(k_ref, rank ^ s, dk) for s in slots]
    copies[3].wait()
    values = []
    for n in range(len(slots) * rep):
        at = pl.multiple_of(((rank ^ slots[n // rep]) * rep + n % rep) * dv, dv)
        values.append(v_ref[:, pl.ds(at, dv)].astype(F32))
    solved = solve_blocks(keys, values, sides, rep)
    copies[4].wait()
    queries = [key_block(q_ref, rank ^ s, dk) * dk**-0.5 for s in slots]
    dots = [dot_nt(query, key) for query, key in zip(queries, keys)]
    for n in range(len(slots) * rep):
        cum_col = cum_cols[:, n : n + 1]
        gap = jnp.where(i >= j, cum_col - cum_rows[n : n + 1, :], 0.0)
        scores = jnp.where(i >= j, dots[n // rep] * jnp.exp(gap), 0.0)
        inner = dot(scores, solved[n])
        x_ref[n] = (queries[n // rep] * jnp.exp(cum_col) - inner[:, 0:dk]).astype(BF16)
        y_ref[n] = inner[:, dk:]


def store_maps(ref, entries):
    dk = entries[0][1].shape[0]
    for h, (_, delta, feed) in enumerate(entries):
        rows = slice(h * dk, (h + 1) * dk)
        ref[rows, 0:dk] = delta.astype(BF16)
        ref[rows, dk:] = feed.astype(BF16)
    width = ref.shape[1]
    rows = [jnp.broadcast_to(t.astype(F32), (1, width)) for e in entries for t in parts(e[0])]
    rows.append(jnp.zeros((PAD - len(rows), width), F32))
    ref[len(entries) * dk :, :] = jnp.concatenate(rows, axis=0).astype(BF16)


def load_maps(ref, dk, rep):
    tail = ref[rep * dk :, 0:dk].astype(F32)
    out = []
    for h in range(rep):
        keep = (tail[3 * h : 3 * h + 1] + tail[3 * h + 1 : 3 * h + 2]) + tail[3 * h + 2 : 3 * h + 3]
        rows = slice(h * dk, (h + 1) * dk)
        out.append((keep[:, 0:1], ref[rows, 0:dk].astype(F32), ref[rows, dk:].astype(F32)))
    return out


def pick(flag, yes, no):
    return [tuple(jnp.where(flag == 1, a, b) for a, b in zip(y, n)) for y, n in zip(yes, no)]


def store_send(ref, entries, whole):
    if whole:
        store_maps(ref, entries)
        return
    for h, (_, _, feed) in enumerate(entries):
        ref[h * feed.shape[0] : (h + 1) * feed.shape[0], :] = feed.astype(BF16)


def block_body(dk, rep, step, whole, where, own_ref, came_ref, out_ref):
    own, came = load_maps(own_ref, dk, rep), load_maps(came_ref, dk, rep)
    flag = (where[2] >> step) & 1
    late, early = pick(flag, own, came), pick(flag, came, own)
    store_send(out_ref, [join(l, e, whole) for l, e in zip(late, early)], whole)


def four_join_body(dk, rep, where, own_ref, came_ref, out_ref):
    odd = where[2] & 1
    for h, (keep, delta, feed) in enumerate(load_maps(own_ref, dk, rep)):
        rows = slice(h * dk, (h + 1) * dk)
        before = came_ref[rows, :].astype(F32)
        out_ref[rows, :] = jnp.where(
            odd == 1, advance(keep, delta, feed, before), feed
        ).astype(BF16)


def four_entry(dk, rep, group, map_ref):
    entry = []
    for keep, delta, feed in load_maps(map_ref, dk, rep):
        entry.append(
            (
                jnp.where(group > 0, keep, 1.0),
                jnp.where(group > 0, delta, 0.0),
                jnp.where(group > 0, feed, 0.0),
            )
        )
    return entry


def block_entry(dk, rep, group, *came):
    none = jnp.zeros((dk, dk), F32)
    entry = [(jnp.ones((1, 1), F32), none, none) for _ in range(rep)]
    for step, ref in enumerate(came):
        block = load_maps(ref, dk, rep)
        if step > 0:
            block = [join(l, e) for l, e in zip(entry, block)]
        entry = pick((group >> step) & 1, block, entry)
    return entry


def prefix_body(dk, rep, entry_of, where, delta_ref, feed_ref, keep_ref, *refs):
    *came, a_ref, b_ref = refs
    maps = block_maps(delta_ref, feed_ref, keep_ref, rep)
    unit = (iota2((dk, dk), 0) == iota2((dk, dk), 1)).astype(F32)
    none = jnp.zeros((dk, dk), F32)
    entry = entry_of(dk, rep, where[2], *came)
    states = [jnp.concatenate([k * unit - d, f], axis=1) for k, d, f in entry]
    for c in range(a_ref.shape[0]):
        for h in range(rep):
            a_ref[c, h] = states[h][:, 0:dk].astype(BF16)
            b_ref[c, h] = states[h][:, dk:]
            keep, delta, feed = maps[h][c]
            if c + 1 < a_ref.shape[0]:
                feed = jnp.concatenate([none, feed], axis=1)
                states[h] = advance(keep, delta, feed, states[h])


def enter_body(dk, rep, feed_of, where, a_ref, b_ref, *refs):
    feeds, outs = refs[: len(refs) - a_ref.shape[0]], refs[len(refs) - a_ref.shape[0] :]
    feed = feed_of(where[2], *feeds).astype(BF16)
    for s, out in enumerate(outs):
        for h in range(rep):
            rows = slice(h * dk, (h + 1) * dk)
            at = where[0] ^ s
            out[rows, :] = (dot(a_ref[at, h], feed[rows]) + b_ref[at, h]).astype(BF16)


def block_feed(step, group, feed_ref):
    return jnp.where((group >> step) & 1 == 1, feed_ref[...].astype(F32), 0.0)


def project_body(dk, dv, rep, slot, where, x_ref, y_ref, gate_ref, gain_ref, w_ref, state, *refs):
    *before, out_ref, normed_ref = refs
    own = (where[0] ^ slot) * rep
    outs = []
    for h in range(rep):
        n = slot * rep + h
        outs.append(dot(x_ref[n], state[h * dk : (h + 1) * dk, :]) + y_ref[n])
    for h, o in enumerate(outs):
        gate = gate_ref[:, pl.ds(pl.multiple_of((own + h) * dv, dv), dv)].astype(F32)
        inverse = lax.rsqrt(jnp.mean(o * o, axis=-1, keepdims=True) + EPS)
        done = o * inverse * gain_ref[...] * (gate / (1.0 + jnp.exp(-gate)))
        normed_ref[:, h * dv : (h + 1) * dv] = done.astype(BF16)
    columns = out_ref.shape[1]
    start = (1 - where[1]) * columns
    normed = normed_ref[...]
    rows = pl.ds(pl.multiple_of(own * dv, rep * dv), rep * dv)
    step = 256
    for n in range(columns // step):
        at = pl.multiple_of(start + n * step, step)
        cut = slice(n * step, (n + 1) * step)
        total = dot(normed, w_ref[rows, pl.ds(at, step)])
        if before:
            total = total + before[0][:, cut]
        out_ref[:, cut] = total.astype(out_ref.dtype)


def own_body(where, w_ref, *refs):
    *pieces, out_ref = refs
    columns = out_ref.shape[1]
    start = where[1] * columns
    width = pieces[0].shape[1]
    step = 256
    for n in range(columns // step):
        at = pl.multiple_of(start + n * step, step)
        total = 0.0
        for s, piece in enumerate(pieces):
            rows = pl.ds(pl.multiple_of((where[0] ^ s) * width, width), width)
            total = total + dot(piece[...], w_ref[rows, pl.ds(at, step)])
        out_ref[:, n * step : (n + 1) * step] = total


def per_device(queries, key_rows, values, out_gate, write_rate, log_decay, norm_gain, out_weight):
    tokens = queries.shape[0]
    heads = write_rate.shape[0]
    dv = norm_gain.shape[0]
    dk = dv
    group = queries.shape[1] // dk
    rep = heads // group
    ranks = lax.axis_size("seq")
    halves = lax.axis_size("head")
    groups = ranks // group
    assert ranks % group == 0 and halves == 2
    assert group & (group - 1) == 0 and groups & (groups - 1) == 0
    steps = groups.bit_length() - 1
    columns = out_weight.shape[1] // halves
    index = lax.axis_index("seq")
    where = jnp.stack([index % group, lax.axis_index("head"), index // group]).astype(jnp.int32)
    shape = jax.ShapeDtypeStruct
    vmem, hbm, smem = pltpu.VMEM, pltpu.HBM, pltpu.SMEM
    cube = 2 * tokens * tokens * (dk + dv)
    map_shape = shape((rep * dk + PAD, dk + dv), BF16)
    feed_shape = shape((rep * dk, dv), BF16)
    slots = list(range(group))

    def swap(x, flip):
        return lax.ppermute(x, "seq", [(i, i ^ flip) for i in range(ranks)])

    def swap_slots(made):
        return [made[0]] + [swap(made[s], s) for s in slots[1:]]

    q_in, k_in, v_in, rate_in, decay_in = [
        pltpu.with_memory_space_constraint(x, hbm)
        for x in (queries, key_rows, values, write_rate, log_decay)
    ]
    small = [pltpu.VMEM(write_rate.shape, F32), pltpu.VMEM(log_decay.shape, F32)]
    pack_shape = shape((tokens + PAD, dk + rep * dv), BF16)
    packs = call(
        functools.partial(pack_body, dk, dv, rep),
        [pack_shape] * group,
        [smem] + [hbm] * 4,
        small + [pltpu.SemaphoreType.DMA((2 + 2 * group,))],
    )(where, k_in, v_in, rate_in, decay_in)
    packs = swap_slots(packs)
    x, y = call(
        functools.partial(terms_body, dk, dv, rep, slots),
        [shape((heads, tokens, dk), BF16), shape((heads, tokens, dv), F32)],
        [smem] + [hbm] * 5,
        [pltpu.VMEM(z.shape, BF16) for z in (queries, key_rows, values)]
        + small
        + [pltpu.SemaphoreType.DMA((5,))],
        heads * 16 * cube,
    )(where, q_in, k_in, v_in, rate_in, decay_in)
    jobs = group * rep
    feed, *blocks = call(
        functools.partial(owner_body, dk, dv, rep),
        [
            feed_shape,
            shape((jobs, dk, dk), BF16),
            shape((jobs, dk, dv), F32),
            shape((jobs, dk), F32),
        ],
        [smem] + [vmem] * group + [pl.ANY],
        [pltpu.VMEM((group,) + pack_shape.shape, BF16)],
        jobs * 16 * cube,
    )(where, *packs, y)

    came, feeds = [], [feed]
    entry_of, feed_of = block_entry, lambda group, feed: jnp.zeros(feed_shape.shape, F32)
    if steps == 1:
        feeds = [swap(feed, group)]
        feed_of = functools.partial(block_feed, 0)
    if steps > 1:
        if steps == 2:
            before = swap(feed, group)
        own = call(
            functools.partial(total_body, rep), map_shape, [vmem] * 3, (), jobs * 2 * cube
        )(*blocks)
    if steps == 2:
        ring = [(i, (i + group) % ranks) for i in range(ranks)]
        came = [lax.ppermute(own, "seq", ring)]
        joined = call(
            functools.partial(four_join_body, dk, rep),
            feed_shape,
            [smem] + [vmem] * 2,
            (),
            jobs * 64 * cube,
        )(where, own, before)
        feeds = [swap(joined, 2 * group)]
        entry_of, feed_of = four_entry, functools.partial(block_feed, 1)
    if steps > 2:
        send = own
        for step in range(steps):
            got = swap(send, group << step)
            if step == steps - 1:
                feeds = [got]
                continue
            whole = step + 2 < steps
            send = call(
                functools.partial(block_body, dk, rep, step, whole),
                map_shape if whole else feed_shape,
                [smem] + [vmem] * 2,
            )(where, send, got)
            came.append(got)
        feed_of = functools.partial(block_feed, steps - 1)
    a, b = call(
        functools.partial(prefix_body, dk, rep, entry_of),
        [shape((group, rep, dk, dk), BF16), shape((group, rep, dk, dv), F32)],
        [smem] + [vmem] * (3 + len(came)),
        (),
        jobs * 4 * cube,
    )(where, *blocks, *came)
    states = call(
        functools.partial(enter_body, dk, rep, feed_of),
        [feed_shape] * group,
        [smem] + [vmem] * (2 + len(feeds)),
        (),
        cube * jobs,
    )(where, a, b, *feeds)
    states = swap_slots(states)

    work = 2 * tokens * columns * heads * dv
    away, normed = [], []
    for s, state in enumerate(states):
        kind = F32 if s < group - 1 else BF16
        total, piece = call(
            functools.partial(project_body, dk, dv, rep, s),
            [shape((tokens, columns), kind), shape((tokens, rep * dv), BF16)],
            [smem] + [vmem] * (6 + len(away)),
            (),
            work // group,
        )(where, x, y, out_gate, norm_gain.reshape(1, dv), out_weight, state, *away)
        away = [total]
        normed.append(piece)
    came = lax.ppermute(away[0], "head", [(0, 1), (1, 0)])
    own = call(own_body, shape((tokens, columns), F32), [smem] + [vmem] * (1 + group), (), work)(
        where, out_weight, *normed
    )
    return (own + came.astype(F32)).astype(BF16)


def solution(mesh):
    return jax.shard_map(
        per_device,
        mesh=mesh,
        in_specs=(
            P("seq", "head"),
            P("seq", "head"),
            P("seq", "head"),
            P("seq", "head"),
            P("head", "seq"),
            P("head", "seq"),
            P(),
            P("head", None),
        ),
        out_specs=P("seq", "head"),
        check_vma=False,
    )
```

```python
import functools

import jax
import jax.numpy as jnp
from jax import lax
from jax.experimental import pallas as pl
from jax.experimental.pallas import tpu as pltpu
from jax.sharding import PartitionSpec as P

F32 = jnp.float32
BF16 = jnp.bfloat16
EPS = 1e-06
LEAF = 16
PAD = 16
SMALL = pltpu.CompilerParams(vmem_limit_bytes=24 * 1024 * 1024)


def dot(a, b):
    return jnp.dot(a.astype(BF16), b.astype(BF16), preferred_element_type=F32)


def dot_nt(a, b):
    return lax.dot_general(
        a.astype(BF16), b.astype(BF16), (((1,), (1,)), ((), ())), preferred_element_type=F32
    )


def dot_tn(a, b):
    return lax.dot_general(
        a.astype(BF16), b.astype(BF16), (((0,), (0,)), ((), ())), preferred_element_type=F32
    )


def exact_dot(a, b, dims):
    return lax.dot_general(
        a, b, (dims, ((), ())), precision=lax.Precision.HIGHEST, preferred_element_type=F32
    )


def parts(x):
    first = x.astype(BF16)
    rest = x - first.astype(F32)
    second = rest.astype(BF16)
    third = (rest - second.astype(F32)).astype(BF16)
    return [first, second, third]


def iota2(shape, dim):
    return lax.broadcasted_iota(jnp.int32, shape, dim)


def call(body, outs, specs, scratch=(), flops=0):
    return pl.pallas_call(
        body,
        out_shape=outs,
        in_specs=[pl.BlockSpec(memory_space=space) for space in specs],
        out_specs=jax.tree.map(lambda _: pl.BlockSpec(memory_space=pltpu.VMEM), outs),
        scratch_shapes=list(scratch),
        compiler_params=SMALL,
        cost_estimate=pl.CostEstimate(flops=flops, bytes_accessed=1 << 20, transcendentals=0),
    )


def unit_rows(x):
    return x * lax.rsqrt(jnp.sum(x * x, axis=-1, keepdims=True) + EPS)


def advance(keep, delta, feed, state):
    return keep * state - dot(delta, state) + feed


def join(late, early, whole=True):
    keep, delta, feed = late
    keep_e, delta_e, feed_e = early
    if not whole:
        return None, None, advance(keep, delta, feed, feed_e)
    dk = delta.shape[1]
    both = dot(delta, jnp.concatenate([delta_e, feed_e], axis=1))
    delta_new = keep * delta_e + keep_e * delta - both[:, 0:dk]
    return keep * keep_e, delta_new, keep * feed_e + feed - both[:, dk:]


def key_block(ref, col, dk):
    return unit_rows(ref[:, pl.ds(pl.multiple_of(col * dk, dk), dk)].astype(F32))


def slot_rows(ref, rank, slots, rep):
    return jnp.concatenate(
        [ref[pl.ds((rank ^ s) * rep + h, 1), :] for s in slots for h in range(rep)], axis=0
    )


def solve(lows, sides, i, j):
    tokens = i.shape[0]
    leaf = (i // LEAF) == (j // LEAF)
    unit = (i == j).astype(F32)
    power = [jnp.where(leaf, low, 0.0) for low in lows]
    inverse = [unit - p for p in power]
    power = [p.astype(BF16) for p in power]
    power = [dot(p, p).astype(BF16) for p in power]
    inverse = neumann(power, inverse, LEAF // 2, 1.0)
    full = [
        jnp.concatenate([jnp.where(leaf, 0.0, low), side], axis=1) for low, side in zip(lows, sides)
    ]
    full = [f + dot(t - unit, f) for t, f in zip(inverse, full)]
    power = [f[:, 0:tokens].astype(BF16) for f in full]
    return neumann(power, [f[:, tokens:] for f in full], tokens // LEAF, -1.0)


def neumann(power, sides, order, sign):
    width = power[0].shape[1]
    reach = 1
    while 2 * reach < order:
        both = [
            dot(p, jnp.concatenate([p, s.astype(BF16)], axis=1)) for p, s in zip(power, sides)
        ]
        power = [b[:, 0:width].astype(BF16) for b in both]
        sides = [s + sign * b[:, width:] for s, b in zip(sides, both)]
        sign, reach = 1.0, 2 * reach
    return [s + sign * dot(p, s) for p, s in zip(power, sides)]


def placed(body, group):
    def run(*refs):
        index = lax.axis_index("seq")
        spot = (index & (group - 1), lax.axis_index("head"), index >> (group.bit_length() - 1))
        body(spot, *refs)

    return run


def pack_body(dk, dv, rep, where, k_in, v_in, rate_in, decay_in, *refs):
    *outs, rate_ref, decay_ref, sems = refs
    tokens = k_in.shape[0]
    rank = where[0]
    pairs = [(rate_in, rate_ref), (decay_in, decay_ref)]
    for s, out in enumerate(outs):
        at = pl.multiple_of((rank ^ s) * dk, dk)
        pairs.append((k_in.at[:, pl.ds(at, dk)], out.at[0:tokens, 0:dk]))
        at = pl.multiple_of((rank ^ s) * rep * dv, rep * dv)
        pairs.append((v_in.at[:, pl.ds(at, rep * dv)], out.at[0:tokens, dk:]))
    copies = [pltpu.make_async_copy(*p, sems.at[n]) for n, p in enumerate(pairs)]
    for copy in copies:
        copy.start()
    copies[0].wait()
    copies[1].wait()
    for s, out in enumerate(outs):
        rows = [slot_rows(ref, rank, [s], rep) for ref in (rate_ref, decay_ref)]
        terms = [t.astype(F32) for t in parts(jnp.concatenate(rows, axis=0))]
        terms.append(jnp.zeros((PAD - 6 * rep, tokens), F32))
        out[tokens:, 0:tokens] = jnp.concatenate(terms, axis=0).astype(BF16)
        out[tokens:, tokens:] = jnp.zeros((PAD, out.shape[1] - tokens), BF16)
    for copy in copies[2:]:
        copy.wait()


def block_sides(decays, rates, tokens):
    i = iota2((tokens, tokens), 0)
    j = iota2((tokens, tokens), 1)
    lower = (i >= j).astype(F32)
    unit = (i == j).astype(F32)
    cum_rows = exact_dot(decays, lower, ((1,), (1,)))
    cum_cols = exact_dot(lower, decays, ((1,), (1,)))
    rate_cols = exact_dot(unit, rates, ((1,), (1,)))
    return i, j, cum_rows, cum_cols, rate_cols


def solve_blocks(keys, values, sides, rep):
    i, j, cum_rows, cum_cols, rate_cols = sides
    dots = [dot_nt(key, key) for key in keys]
    lows, rhs = [], []
    for n, value in enumerate(values):
        rate = rate_cols[:, n : n + 1]
        cum_col = cum_cols[:, n : n + 1]
        gap = jnp.where(i > j, cum_col - cum_rows[n : n + 1, :], 0.0)
        lows.append(jnp.where(i > j, rate * dots[n // rep] * jnp.exp(gap), 0.0))
        rhs.append(
            jnp.concatenate([(rate * jnp.exp(cum_col)) * keys[n // rep], rate * value], axis=1)
        )
    return solve(lows, rhs, i, j)


def owner_body(dk, dv, rep, where, *refs):
    *packs, _, send_ref, delta_ref, feed_ref, keep_ref, scr = refs
    blocks = len(packs)
    tokens = packs[0].shape[0] - PAD
    for s, pack in enumerate(packs):
        scr[where[0] ^ s] = pack[...]
    tails = [scr[c, tokens:, 0:tokens].astype(F32) for c in range(blocks)]
    size = 2 * rep
    tails = [t[0:size] + t[size : 2 * size] + t[2 * size : 3 * size] for t in tails]
    rates = jnp.concatenate([t[0:rep] for t in tails], axis=0)
    decays = jnp.concatenate([t[rep:] for t in tails], axis=0)
    sides = block_sides(decays, rates, tokens)
    cum_rows, cum_cols = sides[2], sides[3]
    keys = [unit_rows(scr[c, 0:tokens, 0:dk].astype(F32)) for c in range(blocks)]
    jobs = [(c, h) for c in range(blocks) for h in range(rep)]
    values = [scr[c, 0:tokens, dk + h * dv : dk + (h + 1) * dv].astype(F32) for c, h in jobs]
    solved = solve_blocks(keys, values, sides, rep)
    entries = []
    for n, (c, h) in enumerate(jobs):
        last = cum_rows[n : n + 1, tokens - 1 : tokens]
        moved = dot_tn(keys[c] * jnp.exp(last - cum_cols[:, n : n + 1]), solved[n])
        entries.append((jnp.exp(last), moved[:, 0:dk], moved[:, dk:]))
        delta_ref[n] = moved[:, 0:dk].astype(BF16)
        feed_ref[n] = moved[:, dk:]
        keep_ref[n : n + 1, :] = jnp.broadcast_to(jnp.exp(last), (1, keep_ref.shape[1]))
    for h in range(rep):
        send_ref[h * dk : (h + 1) * dk, :] = fold(entries[h::rep], False)[2].astype(BF16)


def fold(maps, whole):
    while len(maps) > 1:
        maps = [join(maps[n + 1], maps[n], whole or n > 0) for n in range(0, len(maps), 2)]
    return maps[0]


def block_maps(delta_ref, feed_ref, keep_ref, rep):
    maps = [
        (keep_ref[n : n + 1, 0:1], delta_ref[n].astype(F32), feed_ref[n])
        for n in range(delta_ref.shape[0])
    ]
    return [maps[h::rep] for h in range(rep)]


def total_body(rep, delta_ref, feed_ref, keep_ref, out_ref):
    store_maps(out_ref, [fold(m, True) for m in block_maps(delta_ref, feed_ref, keep_ref, rep)])


def terms_body(dk, dv, rep, slots, where, q_in, k_in, v_in, rate_in, decay_in, *refs):
    x_ref, y_ref, q_ref, k_ref, v_ref, rate_ref, decay_ref, sems = refs
    tokens = k_in.shape[0]
    rank = where[0]
    pairs = [(rate_in, rate_ref), (decay_in, decay_ref), (k_in, k_ref), (v_in, v_ref), (q_in, q_ref)]
    copies = [pltpu.make_async_copy(*p, sems.at[n]) for n, p in enumerate(pairs)]
    for copy in copies:
        copy.start()
    copies[0].wait()
    copies[1].wait()
    sides = block_sides(
        slot_rows(decay_ref, rank, slots, rep), slot_rows(rate_ref, rank, slots, rep), tokens
    )
    i, j, cum_rows, cum_cols, _ = sides
    copies[2].wait()
    keys = [key_block(k_ref, rank ^ s, dk) for s in slots]
    copies[3].wait()
    values = []
    for n in range(len(slots) * rep):
        at = pl.multiple_of(((rank ^ slots[n // rep]) * rep + n % rep) * dv, dv)
        values.append(v_ref[:, pl.ds(at, dv)].astype(F32))
    solved = solve_blocks(keys, values, sides, rep)
    copies[4].wait()
    queries = [key_block(q_ref, rank ^ s, dk) * dk**-0.5 for s in slots]
    dots = [dot_nt(query, key) for query, key in zip(queries, keys)]
    for n in range(len(slots) * rep):
        cum_col = cum_cols[:, n : n + 1]
        gap = jnp.where(i >= j, cum_col - cum_rows[n : n + 1, :], 0.0)
        scores = jnp.where(i >= j, dots[n // rep] * jnp.exp(gap), 0.0)
        inner = dot(scores, solved[n])
        x_ref[n] = (queries[n // rep] * jnp.exp(cum_col) - inner[:, 0:dk]).astype(BF16)
        y_ref[n] = inner[:, dk:]


def store_maps(ref, entries):
    dk = entries[0][1].shape[0]
    for h, (_, delta, feed) in enumerate(entries):
        rows = slice(h * dk, (h + 1) * dk)
        ref[rows, 0:dk] = delta.astype(BF16)
        ref[rows, dk:] = feed.astype(BF16)
    width = ref.shape[1]
    rows = [jnp.broadcast_to(t.astype(F32), (1, width)) for e in entries for t in parts(e[0])]
    rows.append(jnp.zeros((PAD - len(rows), width), F32))
    ref[len(entries) * dk :, :] = jnp.concatenate(rows, axis=0).astype(BF16)


def load_maps(ref, dk, rep):
    tail = ref[rep * dk :, 0:dk].astype(F32)
    out = []
    for h in range(rep):
        keep = (tail[3 * h : 3 * h + 1] + tail[3 * h + 1 : 3 * h + 2]) + tail[3 * h + 2 : 3 * h + 3]
        rows = slice(h * dk, (h + 1) * dk)
        out.append((keep[:, 0:1], ref[rows, 0:dk].astype(F32), ref[rows, dk:].astype(F32)))
    return out


def pick(flag, yes, no):
    return [tuple(jnp.where(flag == 1, a, b) for a, b in zip(y, n)) for y, n in zip(yes, no)]


def store_send(ref, entries, whole):
    if whole:
        store_maps(ref, entries)
        return
    for h, (_, _, feed) in enumerate(entries):
        ref[h * feed.shape[0] : (h + 1) * feed.shape[0], :] = feed.astype(BF16)


def block_body(dk, rep, step, whole, where, own_ref, came_ref, out_ref):
    own, came = load_maps(own_ref, dk, rep), load_maps(came_ref, dk, rep)
    flag = (where[2] >> step) & 1
    late, early = pick(flag, own, came), pick(flag, came, own)
    store_send(out_ref, [join(l, e, whole) for l, e in zip(late, early)], whole)


def four_join_body(dk, rep, where, own_ref, came_ref, out_ref):
    odd = where[2] & 1
    for h, (keep, delta, feed) in enumerate(load_maps(own_ref, dk, rep)):
        rows = slice(h * dk, (h + 1) * dk)
        before = came_ref[rows, :].astype(F32)
        out_ref[rows, :] = jnp.where(
            odd == 1, advance(keep, delta, feed, before), feed
        ).astype(BF16)


def four_entry(dk, rep, group, map_ref):
    entry = []
    for keep, delta, feed in load_maps(map_ref, dk, rep):
        entry.append(
            (
                jnp.where(group > 0, keep, 1.0),
                jnp.where(group > 0, delta, 0.0),
                jnp.where(group > 0, feed, 0.0),
            )
        )
    return entry


def block_entry(dk, rep, group, *came):
    none = jnp.zeros((dk, dk), F32)
    entry = [(jnp.ones((1, 1), F32), none, none) for _ in range(rep)]
    for step, ref in enumerate(came):
        block = load_maps(ref, dk, rep)
        if step > 0:
            block = [join(l, e) for l, e in zip(entry, block)]
        entry = pick((group >> step) & 1, block, entry)
    return entry


def prefix_body(dk, rep, entry_of, where, delta_ref, feed_ref, keep_ref, *refs):
    *came, a_ref, b_ref = refs
    maps = block_maps(delta_ref, feed_ref, keep_ref, rep)
    unit = (iota2((dk, dk), 0) == iota2((dk, dk), 1)).astype(F32)
    none = jnp.zeros((dk, dk), F32)
    entry = entry_of(dk, rep, where[2], *came)
    states = [jnp.concatenate([k * unit - d, f], axis=1) for k, d, f in entry]
    for c in range(a_ref.shape[0]):
        for h in range(rep):
            a_ref[c, h] = states[h][:, 0:dk].astype(BF16)
            b_ref[c, h] = states[h][:, dk:]
            keep, delta, feed = maps[h][c]
            if c + 1 < a_ref.shape[0]:
                feed = jnp.concatenate([none, feed], axis=1)
                states[h] = advance(keep, delta, feed, states[h])


def enter_body(dk, rep, feed_of, where, a_ref, b_ref, *refs):
    feeds, outs = refs[: len(refs) - a_ref.shape[0]], refs[len(refs) - a_ref.shape[0] :]
    feed = feed_of(where[2], *feeds).astype(BF16)
    for s, out in enumerate(outs):
        for h in range(rep):
            rows = slice(h * dk, (h + 1) * dk)
            at = where[0] ^ s
            out[rows, :] = (dot(a_ref[at, h], feed[rows]) + b_ref[at, h]).astype(BF16)


def block_feed(step, group, feed_ref):
    return jnp.where((group >> step) & 1 == 1, feed_ref[...].astype(F32), 0.0)


def project_body(dk, dv, rep, slot, where, x_ref, y_ref, gate_ref, gain_ref, w_ref, state, *refs):
    *before, out_ref, normed_ref = refs
    own = (where[0] ^ slot) * rep
    outs = []
    for h in range(rep):
        n = slot * rep + h
        outs.append(dot(x_ref[n], state[h * dk : (h + 1) * dk, :]) + y_ref[n])
    for h, o in enumerate(outs):
        gate = gate_ref[:, pl.ds(pl.multiple_of((own + h) * dv, dv), dv)].astype(F32)
        inverse = lax.rsqrt(jnp.mean(o * o, axis=-1, keepdims=True) + EPS)
        done = o * inverse * gain_ref[...] * (gate / (1.0 + jnp.exp(-gate)))
        normed_ref[:, h * dv : (h + 1) * dv] = done.astype(BF16)
    columns = out_ref.shape[1]
    start = (1 - where[1]) * columns
    normed = normed_ref[...]
    rows = pl.ds(pl.multiple_of(own * dv, rep * dv), rep * dv)
    step = 256
    for n in range(columns // step):
        at = pl.multiple_of(start + n * step, step)
        cut = slice(n * step, (n + 1) * step)
        total = dot(normed, w_ref[rows, pl.ds(at, step)])
        if before:
            total = total + before[0][:, cut]
        out_ref[:, cut] = total.astype(out_ref.dtype)


def own_body(where, w_ref, *refs):
    *pieces, out_ref = refs
    columns = out_ref.shape[1]
    start = where[1] * columns
    width = pieces[0].shape[1]
    step = 256
    for n in range(columns // step):
        at = pl.multiple_of(start + n * step, step)
        total = 0.0
        for s, piece in enumerate(pieces):
            rows = pl.ds(pl.multiple_of((where[0] ^ s) * width, width), width)
            total = total + dot(piece[...], w_ref[rows, pl.ds(at, step)])
        out_ref[:, n * step : (n + 1) * step] = total


def per_device(queries, key_rows, values, out_gate, write_rate, log_decay, norm_gain, out_weight):
    tokens = queries.shape[0]
    heads = write_rate.shape[0]
    dv = norm_gain.shape[0]
    dk = dv
    group = queries.shape[1] // dk
    rep = heads // group
    ranks = lax.axis_size("seq")
    halves = lax.axis_size("head")
    groups = ranks // group
    assert ranks % group == 0 and halves == 2
    assert group & (group - 1) == 0 and groups & (groups - 1) == 0
    steps = groups.bit_length() - 1
    columns = out_weight.shape[1] // halves
    shape = jax.ShapeDtypeStruct
    vmem, hbm = pltpu.VMEM, pltpu.HBM
    cube = 2 * tokens * tokens * (dk + dv)
    map_shape = shape((rep * dk + PAD, dk + dv), BF16)
    feed_shape = shape((rep * dk, dv), BF16)
    slots = list(range(group))

    def swap(x, flip):
        return lax.ppermute(x, "seq", [(i, i ^ flip) for i in range(ranks)])

    def swap_slots(made):
        return [made[0]] + [swap(made[s], s) for s in slots[1:]]

    q_in, k_in, v_in, rate_in, decay_in = [
        pltpu.with_memory_space_constraint(x, hbm)
        for x in (queries, key_rows, values, write_rate, log_decay)
    ]
    small = [pltpu.VMEM(write_rate.shape, F32), pltpu.VMEM(log_decay.shape, F32)]
    pack_shape = shape((tokens + PAD, dk + rep * dv), BF16)
    packs = call(
        placed(functools.partial(pack_body, dk, dv, rep), group),
        [pack_shape] * group,
        [hbm] * 4,
        small + [pltpu.SemaphoreType.DMA((2 + 2 * group,))],
    )(k_in, v_in, rate_in, decay_in)
    packs = swap_slots(packs)
    x, y = call(
        placed(functools.partial(terms_body, dk, dv, rep, slots), group),
        [shape((heads, tokens, dk), BF16), shape((heads, tokens, dv), F32)],
        [hbm] * 5,
        [pltpu.VMEM(z.shape, BF16) for z in (queries, key_rows, values)]
        + small
        + [pltpu.SemaphoreType.DMA((5,))],
        heads * 16 * cube,
    )(q_in, k_in, v_in, rate_in, decay_in)
    jobs = group * rep
    feed, *blocks = call(
        placed(functools.partial(owner_body, dk, dv, rep), group),
        [
            feed_shape,
            shape((jobs, dk, dk), BF16),
            shape((jobs, dk, dv), F32),
            shape((jobs, dk), F32),
        ],
        [vmem] * group + [pl.ANY],
        [pltpu.VMEM((group,) + pack_shape.shape, BF16)],
        jobs * 16 * cube,
    )(*packs, y)

    came, feeds = [], [feed]
    entry_of, feed_of = block_entry, lambda group, feed: jnp.zeros(feed_shape.shape, F32)
    if steps == 1:
        feeds = [swap(feed, group)]
        feed_of = functools.partial(block_feed, 0)
    if steps > 1:
        if steps == 2:
            before = swap(feed, group)
        own = call(
            functools.partial(total_body, rep), map_shape, [vmem] * 3, (), jobs * 2 * cube
        )(*blocks)
    if steps == 2:
        ring = [(i, (i + group) % ranks) for i in range(ranks)]
        came = [lax.ppermute(own, "seq", ring)]
        joined = call(
            placed(functools.partial(four_join_body, dk, rep), group),
            feed_shape,
            [vmem] * 2,
            (),
            jobs * 64 * cube,
        )(own, before)
        feeds = [swap(joined, 2 * group)]
        entry_of, feed_of = four_entry, functools.partial(block_feed, 1)
    if steps > 2:
        send = own
        for step in range(steps):
            got = swap(send, group << step)
            if step == steps - 1:
                feeds = [got]
                continue
            whole = step + 2 < steps
            send = call(
                placed(functools.partial(block_body, dk, rep, step, whole), group),
                map_shape if whole else feed_shape,
                [vmem] * 2,
            )(send, got)
            came.append(got)
        feed_of = functools.partial(block_feed, steps - 1)
    a, b = call(
        placed(functools.partial(prefix_body, dk, rep, entry_of), group),
        [shape((group, rep, dk, dk), BF16), shape((group, rep, dk, dv), F32)],
        [vmem] * (3 + len(came)),
        (),
        jobs * 4 * cube,
    )(*blocks, *came)
    states = call(
        placed(functools.partial(enter_body, dk, rep, feed_of), group),
        [feed_shape] * group,
        [vmem] * (2 + len(feeds)),
        (),
        cube * jobs,
    )(a, b, *feeds)
    states = swap_slots(states)

    work = 2 * tokens * columns * heads * dv
    away, normed = [], []
    for s, state in enumerate(states):
        kind = F32 if s < group - 1 else BF16
        total, piece = call(
            placed(functools.partial(project_body, dk, dv, rep, s), group),
            [shape((tokens, columns), kind), shape((tokens, rep * dv), BF16)],
            [vmem] * (6 + len(away)),
            (),
            work // group,
        )(x, y, out_gate, norm_gain.reshape(1, dv), out_weight, state, *away)
        away = [total]
        normed.append(piece)
    came = lax.ppermute(away[0], "head", [(0, 1), (1, 0)])
    own = call(placed(own_body, group), shape((tokens, columns), F32), [vmem] * (1 + group), (), work)(
        out_weight, *normed
    )
    return (own + came.astype(F32)).astype(BF16)


def solution(mesh):
    return jax.shard_map(
        per_device,
        mesh=mesh,
        in_specs=(
            P("seq", "head"),
            P("seq", "head"),
            P("seq", "head"),
            P("seq", "head"),
            P("head", "seq"),
            P("head", "seq"),
            P(),
            P("head", None),
        ),
        out_specs=P("seq", "head"),
        check_vma=False,
    )
```

```python
import functools

import jax
import jax.numpy as jnp
from jax import lax
from jax.experimental import pallas as pl
from jax.experimental.pallas import tpu as pltpu
from jax.sharding import PartitionSpec as P

F32 = jnp.float32
BF16 = jnp.bfloat16
EPS = 1e-06
LEAF = 16
PAD = 16
SMALL = pltpu.CompilerParams(vmem_limit_bytes=24 * 1024 * 1024)


def dot(a, b):
    return jnp.dot(a.astype(BF16), b.astype(BF16), preferred_element_type=F32)


def dot_nt(a, b):
    return lax.dot_general(
        a.astype(BF16), b.astype(BF16), (((1,), (1,)), ((), ())), preferred_element_type=F32
    )


def dot_tn(a, b):
    return lax.dot_general(
        a.astype(BF16), b.astype(BF16), (((0,), (0,)), ((), ())), preferred_element_type=F32
    )


def exact_dot(a, b, dims):
    return lax.dot_general(
        a, b, (dims, ((), ())), precision=lax.Precision.HIGHEST, preferred_element_type=F32
    )


def parts(x):
    first = x.astype(BF16)
    rest = x - first.astype(F32)
    second = rest.astype(BF16)
    third = (rest - second.astype(F32)).astype(BF16)
    return [first, second, third]


def iota2(shape, dim):
    return lax.broadcasted_iota(jnp.int32, shape, dim)


def call(body, outs, specs, scratch=(), flops=0):
    return pl.pallas_call(
        body,
        out_shape=outs,
        in_specs=[pl.BlockSpec(memory_space=space) for space in specs],
        out_specs=jax.tree.map(lambda _: pl.BlockSpec(memory_space=pltpu.VMEM), outs),
        scratch_shapes=list(scratch),
        compiler_params=SMALL,
        cost_estimate=pl.CostEstimate(flops=flops, bytes_accessed=1 << 20, transcendentals=0),
    )


def unit_rows(x):
    return x * lax.rsqrt(jnp.sum(x * x, axis=-1, keepdims=True) + EPS)


def advance(keep, delta, feed, state):
    return keep * state - dot(delta, state) + feed


def join(late, early, whole=True):
    keep, delta, feed = late
    keep_e, delta_e, feed_e = early
    if not whole:
        return None, None, advance(keep, delta, feed, feed_e)
    dk = delta.shape[1]
    both = dot(delta, jnp.concatenate([delta_e, feed_e], axis=1))
    delta_new = keep * delta_e + keep_e * delta - both[:, 0:dk]
    return keep * keep_e, delta_new, keep * feed_e + feed - both[:, dk:]


def key_block(ref, col, dk):
    return unit_rows(ref[:, pl.ds(pl.multiple_of(col * dk, dk), dk)].astype(F32))


def slot_rows(ref, rank, slots, rep):
    return jnp.concatenate(
        [ref[pl.ds((rank ^ s) * rep + h, 1), :] for s in slots for h in range(rep)], axis=0
    )


def solve(lows, sides, i, j):
    tokens = i.shape[0]
    leaf = (i // LEAF) == (j // LEAF)
    unit = (i == j).astype(F32)
    power = [jnp.where(leaf, low, 0.0) for low in lows]
    inverse = [unit - p for p in power]
    power = [p.astype(BF16) for p in power]
    power = [dot(p, p).astype(BF16) for p in power]
    inverse = neumann(power, inverse, LEAF // 2, 1.0)
    full = [
        jnp.concatenate([jnp.where(leaf, 0.0, low), side], axis=1) for low, side in zip(lows, sides)
    ]
    full = [f + dot(t - unit, f) for t, f in zip(inverse, full)]
    power = [f[:, 0:tokens].astype(BF16) for f in full]
    return neumann(power, [f[:, tokens:] for f in full], tokens // LEAF, -1.0)


def neumann(power, sides, order, sign):
    width = power[0].shape[1]
    reach = 1
    while 2 * reach < order:
        both = [
            dot(p, jnp.concatenate([p, s.astype(BF16)], axis=1)) for p, s in zip(power, sides)
        ]
        power = [b[:, 0:width].astype(BF16) for b in both]
        sides = [s + sign * b[:, width:] for s, b in zip(sides, both)]
        sign, reach = 1.0, 2 * reach
    return [s + sign * dot(p, s) for p, s in zip(power, sides)]


def placed(body, group):
    def run(*refs):
        index = lax.axis_index("seq")
        spot = (index & (group - 1), lax.axis_index("head"), index >> (group.bit_length() - 1))
        body(spot, *refs)

    return run


def pack_body(dk, dv, rep, where, k_in, v_in, rate_in, decay_in, *refs):
    *outs, rate_ref, decay_ref, sems = refs
    tokens = k_in.shape[0]
    rank = where[0]
    pairs = [(rate_in, rate_ref), (decay_in, decay_ref)]
    for s, out in enumerate(outs):
        at = pl.multiple_of((rank ^ s) * dk, dk)
        pairs.append((k_in.at[:, pl.ds(at, dk)], out.at[0:tokens, :]))
        for h in range(rep):
            at = pl.multiple_of(((rank ^ s) * rep + h) * dv, dv)
            rows = out.at[(h + 1) * tokens : (h + 2) * tokens, :]
            pairs.append((v_in.at[:, pl.ds(at, dv)], rows))
    copies = [pltpu.make_async_copy(*p, sems.at[n]) for n, p in enumerate(pairs)]
    for copy in copies:
        copy.start()
    copies[0].wait()
    copies[1].wait()
    for s, out in enumerate(outs):
        rows = [slot_rows(ref, rank, [s], rep) for ref in (rate_ref, decay_ref)]
        terms = [t.astype(F32) for t in parts(jnp.concatenate(rows, axis=0))]
        terms.append(jnp.zeros((PAD - 6 * rep, tokens), F32))
        out[(rep + 1) * tokens :, :] = jnp.concatenate(terms, axis=0).astype(BF16)
    for copy in copies[2:]:
        copy.wait()


def block_sides(decays, rates, tokens):
    i = iota2((tokens, tokens), 0)
    j = iota2((tokens, tokens), 1)
    lower = (i >= j).astype(F32)
    unit = (i == j).astype(F32)
    cum_rows = exact_dot(decays, lower, ((1,), (1,)))
    cum_cols = exact_dot(lower, decays, ((1,), (1,)))
    rate_cols = exact_dot(unit, rates, ((1,), (1,)))
    return i, j, cum_rows, cum_cols, rate_cols


def solve_blocks(keys, values, sides, rep):
    i, j, cum_rows, cum_cols, rate_cols = sides
    dots = [dot_nt(key, key) for key in keys]
    lows, rhs = [], []
    for n, value in enumerate(values):
        rate = rate_cols[:, n : n + 1]
        cum_col = cum_cols[:, n : n + 1]
        gap = jnp.where(i > j, cum_col - cum_rows[n : n + 1, :], 0.0)
        lows.append(jnp.where(i > j, rate * dots[n // rep] * jnp.exp(gap), 0.0))
        rhs.append(
            jnp.concatenate([(rate * jnp.exp(cum_col)) * keys[n // rep], rate * value], axis=1)
        )
    return solve(lows, rhs, i, j)


def owner_body(dk, dv, rep, where, *refs):
    *packs, _, send_ref, delta_ref, feed_ref, keep_ref, scr = refs
    blocks = len(packs)
    tokens = (packs[0].shape[0] - PAD) // (rep + 1)
    for s, pack in enumerate(packs):
        scr[where[0] ^ s] = pack[...]
    tails = [scr[c, (rep + 1) * tokens :, :].astype(F32) for c in range(blocks)]
    size = 2 * rep
    tails = [t[0:size] + t[size : 2 * size] + t[2 * size : 3 * size] for t in tails]
    rates = jnp.concatenate([t[0:rep] for t in tails], axis=0)
    decays = jnp.concatenate([t[rep:] for t in tails], axis=0)
    sides = block_sides(decays, rates, tokens)
    cum_rows, cum_cols = sides[2], sides[3]
    keys = [unit_rows(scr[c, 0:tokens, :].astype(F32)) for c in range(blocks)]
    jobs = [(c, h) for c in range(blocks) for h in range(rep)]
    values = [scr[c, (h + 1) * tokens : (h + 2) * tokens, :].astype(F32) for c, h in jobs]
    solved = solve_blocks(keys, values, sides, rep)
    entries = []
    for n, (c, h) in enumerate(jobs):
        last = cum_rows[n : n + 1, tokens - 1 : tokens]
        moved = dot_tn(keys[c] * jnp.exp(last - cum_cols[:, n : n + 1]), solved[n])
        entries.append((jnp.exp(last), moved[:, 0:dk], moved[:, dk:]))
        delta_ref[n] = moved[:, 0:dk].astype(BF16)
        feed_ref[n] = moved[:, dk:]
        keep_ref[n : n + 1, :] = jnp.broadcast_to(jnp.exp(last), (1, keep_ref.shape[1]))
    for h in range(rep):
        send_ref[h * dk : (h + 1) * dk, :] = fold(entries[h::rep], False)[2].astype(BF16)


def fold(maps, whole):
    while len(maps) > 1:
        maps = [join(maps[n + 1], maps[n], whole or n > 0) for n in range(0, len(maps), 2)]
    return maps[0]


def block_maps(delta_ref, feed_ref, keep_ref, rep):
    maps = [
        (keep_ref[n : n + 1, 0:1], delta_ref[n].astype(F32), feed_ref[n])
        for n in range(delta_ref.shape[0])
    ]
    return [maps[h::rep] for h in range(rep)]


def total_body(rep, delta_ref, feed_ref, keep_ref, out_ref):
    store_maps(out_ref, [fold(m, True) for m in block_maps(delta_ref, feed_ref, keep_ref, rep)])


def terms_body(dk, dv, rep, slots, where, q_in, k_in, v_in, rate_in, decay_in, *refs):
    x_ref, y_ref, q_ref, k_ref, v_ref, rate_ref, decay_ref, sems = refs
    tokens = k_in.shape[0]
    rank = where[0]
    pairs = [(rate_in, rate_ref), (decay_in, decay_ref), (k_in, k_ref), (v_in, v_ref), (q_in, q_ref)]
    copies = [pltpu.make_async_copy(*p, sems.at[n]) for n, p in enumerate(pairs)]
    for copy in copies:
        copy.start()
    copies[0].wait()
    copies[1].wait()
    sides = block_sides(
        slot_rows(decay_ref, rank, slots, rep), slot_rows(rate_ref, rank, slots, rep), tokens
    )
    i, j, cum_rows, cum_cols, _ = sides
    copies[2].wait()
    keys = [key_block(k_ref, rank ^ s, dk) for s in slots]
    copies[3].wait()
    values = []
    for n in range(len(slots) * rep):
        at = pl.multiple_of(((rank ^ slots[n // rep]) * rep + n % rep) * dv, dv)
        values.append(v_ref[:, pl.ds(at, dv)].astype(F32))
    solved = solve_blocks(keys, values, sides, rep)
    copies[4].wait()
    queries = [key_block(q_ref, rank ^ s, dk) * dk**-0.5 for s in slots]
    dots = [dot_nt(query, key) for query, key in zip(queries, keys)]
    for n in range(len(slots) * rep):
        cum_col = cum_cols[:, n : n + 1]
        gap = jnp.where(i >= j, cum_col - cum_rows[n : n + 1, :], 0.0)
        scores = jnp.where(i >= j, dots[n // rep] * jnp.exp(gap), 0.0)
        inner = dot(scores, solved[n])
        x_ref[n] = (queries[n // rep] * jnp.exp(cum_col) - inner[:, 0:dk]).astype(BF16)
        y_ref[n] = inner[:, dk:]


def store_maps(ref, entries):
    dk = entries[0][1].shape[0]
    for h, (_, delta, feed) in enumerate(entries):
        rows = slice(h * dk, (h + 1) * dk)
        ref[rows, 0:dk] = delta.astype(BF16)
        ref[rows, dk:] = feed.astype(BF16)
    width = ref.shape[1]
    rows = [jnp.broadcast_to(t.astype(F32), (1, width)) for e in entries for t in parts(e[0])]
    rows.append(jnp.zeros((PAD - len(rows), width), F32))
    ref[len(entries) * dk :, :] = jnp.concatenate(rows, axis=0).astype(BF16)


def load_maps(ref, dk, rep):
    tail = ref[rep * dk :, 0:dk].astype(F32)
    out = []
    for h in range(rep):
        keep = (tail[3 * h : 3 * h + 1] + tail[3 * h + 1 : 3 * h + 2]) + tail[3 * h + 2 : 3 * h + 3]
        rows = slice(h * dk, (h + 1) * dk)
        out.append((keep[:, 0:1], ref[rows, 0:dk].astype(F32), ref[rows, dk:].astype(F32)))
    return out


def pick(flag, yes, no):
    return [tuple(jnp.where(flag == 1, a, b) for a, b in zip(y, n)) for y, n in zip(yes, no)]


def store_send(ref, entries, whole):
    if whole:
        store_maps(ref, entries)
        return
    for h, (_, _, feed) in enumerate(entries):
        ref[h * feed.shape[0] : (h + 1) * feed.shape[0], :] = feed.astype(BF16)


def block_body(dk, rep, step, whole, where, own_ref, came_ref, out_ref):
    own, came = load_maps(own_ref, dk, rep), load_maps(came_ref, dk, rep)
    flag = (where[2] >> step) & 1
    late, early = pick(flag, own, came), pick(flag, came, own)
    store_send(out_ref, [join(l, e, whole) for l, e in zip(late, early)], whole)


def four_join_body(dk, rep, own_ref, came_ref, out_ref):
    for h, entry in enumerate(load_maps(own_ref, dk, rep)):
        rows = slice(h * dk, (h + 1) * dk)
        out_ref[rows, :] = advance(*entry, came_ref[rows, :].astype(F32)).astype(BF16)


def four_entry(dk, rep, group, feed_ref, map_ref):
    entry = []
    for h, (keep, delta, feed) in enumerate(load_maps(map_ref, dk, rep)):
        before = feed_ref[h * dk : (h + 1) * dk, :].astype(F32)
        entry.append(
            (
                jnp.where(group == 3, keep, 1.0),
                jnp.where(group == 3, delta, 0.0),
                jnp.where(group == 3, feed, jnp.where(group == 1, before, 0.0)),
            )
        )
    return entry


def four_feed(group, to_third, to_second):
    late = jnp.where(group == 3, to_third[...].astype(F32), 0.0)
    return jnp.where(group == 2, to_second[...].astype(F32), late)


def block_entry(dk, rep, group, *came):
    none = jnp.zeros((dk, dk), F32)
    entry = [(jnp.ones((1, 1), F32), none, none) for _ in range(rep)]
    for step, ref in enumerate(came):
        block = load_maps(ref, dk, rep)
        if step > 0:
            block = [join(l, e) for l, e in zip(entry, block)]
        entry = pick((group >> step) & 1, block, entry)
    return entry


def prefix_body(dk, rep, entry_of, where, delta_ref, feed_ref, keep_ref, *refs):
    *came, a_ref, b_ref = refs
    maps = block_maps(delta_ref, feed_ref, keep_ref, rep)
    unit = (iota2((dk, dk), 0) == iota2((dk, dk), 1)).astype(F32)
    none = jnp.zeros((dk, dk), F32)
    entry = entry_of(dk, rep, where[2], *came)
    states = [jnp.concatenate([k * unit - d, f], axis=1) for k, d, f in entry]
    for c in range(a_ref.shape[0]):
        for h in range(rep):
            a_ref[c, h] = states[h][:, 0:dk].astype(BF16)
            b_ref[c, h] = states[h][:, dk:]
            keep, delta, feed = maps[h][c]
            if c + 1 < a_ref.shape[0]:
                feed = jnp.concatenate([none, feed], axis=1)
                states[h] = advance(keep, delta, feed, states[h])


def enter_body(dk, rep, feed_of, where, a_ref, b_ref, *refs):
    feeds, outs = refs[: len(refs) - a_ref.shape[0]], refs[len(refs) - a_ref.shape[0] :]
    feed = feed_of(where[2], *feeds).astype(BF16)
    for s, out in enumerate(outs):
        for h in range(rep):
            rows = slice(h * dk, (h + 1) * dk)
            at = where[0] ^ s
            out[rows, :] = (dot(a_ref[at, h], feed[rows]) + b_ref[at, h]).astype(BF16)


def block_feed(step, group, feed_ref):
    return jnp.where((group >> step) & 1 == 1, feed_ref[...].astype(F32), 0.0)


def project_body(dk, dv, rep, slot, where, x_ref, y_ref, gate_ref, gain_ref, w_ref, state, *refs):
    *before, out_ref, normed_ref = refs
    own = (where[0] ^ slot) * rep
    outs = []
    for h in range(rep):
        n = slot * rep + h
        outs.append(dot(x_ref[n], state[h * dk : (h + 1) * dk, :]) + y_ref[n])
    for h, o in enumerate(outs):
        gate = gate_ref[:, pl.ds(pl.multiple_of((own + h) * dv, dv), dv)].astype(F32)
        inverse = lax.rsqrt(jnp.mean(o * o, axis=-1, keepdims=True) + EPS)
        done = o * inverse * gain_ref[...] * (gate / (1.0 + jnp.exp(-gate)))
        normed_ref[:, h * dv : (h + 1) * dv] = done.astype(BF16)
    columns = out_ref.shape[1]
    start = (1 - where[1]) * columns
    normed = normed_ref[...]
    rows = pl.ds(pl.multiple_of(own * dv, rep * dv), rep * dv)
    step = 256
    for n in range(columns // step):
        at = pl.multiple_of(start + n * step, step)
        cut = slice(n * step, (n + 1) * step)
        total = dot(normed, w_ref[rows, pl.ds(at, step)])
        if before:
            total = total + before[0][:, cut]
        out_ref[:, cut] = total.astype(out_ref.dtype)


def own_body(where, w_ref, *refs):
    *pieces, out_ref = refs
    columns = out_ref.shape[1]
    start = where[1] * columns
    width = pieces[0].shape[1]
    step = 256
    for n in range(columns // step):
        at = pl.multiple_of(start + n * step, step)
        total = 0.0
        for s, piece in enumerate(pieces):
            rows = pl.ds(pl.multiple_of((where[0] ^ s) * width, width), width)
            total = total + dot(piece[...], w_ref[rows, pl.ds(at, step)])
        out_ref[:, n * step : (n + 1) * step] = total


def per_device(queries, key_rows, values, out_gate, write_rate, log_decay, norm_gain, out_weight):
    tokens = queries.shape[0]
    heads = write_rate.shape[0]
    dv = norm_gain.shape[0]
    dk = dv
    group = queries.shape[1] // dk
    rep = heads // group
    ranks = lax.axis_size("seq")
    halves = lax.axis_size("head")
    groups = ranks // group
    assert ranks % group == 0 and halves == 2
    assert group & (group - 1) == 0 and groups & (groups - 1) == 0
    steps = groups.bit_length() - 1
    columns = out_weight.shape[1] // halves
    shape = jax.ShapeDtypeStruct
    vmem, hbm = pltpu.VMEM, pltpu.HBM
    cube = 2 * tokens * tokens * (dk + dv)
    map_shape = shape((rep * dk + PAD, dk + dv), BF16)
    feed_shape = shape((rep * dk, dv), BF16)
    slots = list(range(group))

    def swap(x, flip, ends=None):
        moves = [flip if ends is None or i // group in ends else 0 for i in range(ranks)]
        return lax.ppermute(x, "seq", [(i, i ^ move) for i, move in enumerate(moves)])

    def swap_slots(made):
        return [made[0]] + [swap(made[s], s) for s in slots[1:]]

    q_in, k_in, v_in, rate_in, decay_in = [
        pltpu.with_memory_space_constraint(x, hbm)
        for x in (queries, key_rows, values, write_rate, log_decay)
    ]
    small = [pltpu.VMEM(write_rate.shape, F32), pltpu.VMEM(log_decay.shape, F32)]
    pack_shape = shape(((rep + 1) * tokens + PAD, dk), BF16)
    packs = call(
        placed(functools.partial(pack_body, dk, dv, rep), group),
        [pack_shape] * group,
        [hbm] * 4,
        small + [pltpu.SemaphoreType.DMA((2 + (rep + 1) * group,))],
    )(k_in, v_in, rate_in, decay_in)
    packs = swap_slots(packs)
    x, y = call(
        placed(functools.partial(terms_body, dk, dv, rep, slots), group),
        [shape((heads, tokens, dk), BF16), shape((heads, tokens, dv), F32)],
        [hbm] * 5,
        [pltpu.VMEM(z.shape, BF16) for z in (queries, key_rows, values)]
        + small
        + [pltpu.SemaphoreType.DMA((5,))],
        heads * 16 * cube,
    )(q_in, k_in, v_in, rate_in, decay_in)
    jobs = group * rep
    feed, *blocks = call(
        placed(functools.partial(owner_body, dk, dv, rep), group),
        [
            feed_shape,
            shape((jobs, dk, dk), BF16),
            shape((jobs, dk, dv), F32),
            shape((jobs, dk), F32),
        ],
        [vmem] * group + [pl.ANY],
        [pltpu.VMEM((group,) + pack_shape.shape, BF16)],
        jobs * 16 * cube,
    )(*packs, y)

    came, feeds = [], [feed]
    entry_of, feed_of = block_entry, lambda group, feed: jnp.zeros(feed_shape.shape, F32)
    if steps == 1:
        feeds = [swap(feed, group)]
        feed_of = functools.partial(block_feed, 0)
    if steps > 1:
        if steps == 2:
            before = swap(feed, group, (0, 1))
        own = call(
            functools.partial(total_body, rep), map_shape, [vmem] * 3, (), jobs * 2 * cube
        )(*blocks)
    if steps == 2:
        came = [before, swap(own, group, (2, 3))]
        joined = call(
            functools.partial(four_join_body, dk, rep),
            feed_shape,
            [vmem] * 2,
            (),
            jobs * 64 * cube,
        )(own, before)
        feeds = [swap(joined, 2 * group, (1, 3)), swap(joined, 3 * group, (1, 2))]
        entry_of, feed_of = four_entry, four_feed
    if steps > 2:
        send = own
        for step in range(steps):
            got = swap(send, group << step)
            if step == steps - 1:
                feeds = [got]
                continue
            whole = step + 2 < steps
            send = call(
                placed(functools.partial(block_body, dk, rep, step, whole), group),
                map_shape if whole else feed_shape,
                [vmem] * 2,
            )(send, got)
            came.append(got)
        feed_of = functools.partial(block_feed, steps - 1)
    a, b = call(
        placed(functools.partial(prefix_body, dk, rep, entry_of), group),
        [shape((group, rep, dk, dk), BF16), shape((group, rep, dk, dv), F32)],
        [vmem] * (3 + len(came)),
        (),
        jobs * 4 * cube,
    )(*blocks, *came)
    states = call(
        placed(functools.partial(enter_body, dk, rep, feed_of), group),
        [feed_shape] * group,
        [vmem] * (2 + len(feeds)),
        (),
        cube * jobs,
    )(a, b, *feeds)
    states = swap_slots(states)

    work = 2 * tokens * columns * heads * dv
    away, normed = [], []
    for s, state in enumerate(states):
        kind = F32 if s < group - 1 else BF16
        total, piece = call(
            placed(functools.partial(project_body, dk, dv, rep, s), group),
            [shape((tokens, columns), kind), shape((tokens, rep * dv), BF16)],
            [vmem] * (6 + len(away)),
            (),
            work // group,
        )(x, y, out_gate, norm_gain.reshape(1, dv), out_weight, state, *away)
        away = [total]
        normed.append(piece)
    came = lax.ppermute(away[0], "head", [(0, 1), (1, 0)])
    own = call(placed(own_body, group), shape((tokens, columns), F32), [vmem] * (1 + group), (), work)(
        out_weight, *normed
    )
    return (own + came.astype(F32)).astype(BF16)


def solution(mesh):
    return jax.shard_map(
        per_device,
        mesh=mesh,
        in_specs=(
            P("seq", "head"),
            P("seq", "head"),
            P("seq", "head"),
            P("seq", "head"),
            P("head", "seq"),
            P("head", "seq"),
            P(),
            P("head", None),
        ),
        out_specs=P("seq", "head"),
        check_vma=False,
    )
```

```python
import functools

import jax
import jax.numpy as jnp
from jax import lax
from jax.experimental import pallas as pl
from jax.experimental.pallas import tpu as pltpu
from jax.sharding import PartitionSpec as P

F32 = jnp.float32
BF16 = jnp.bfloat16
EPS = 1e-06
LEAF = 16
PAD = 16
SMALL = pltpu.CompilerParams(vmem_limit_bytes=24 * 1024 * 1024)


def dot(a, b):
    return jnp.dot(a.astype(BF16), b.astype(BF16), preferred_element_type=F32)


def dot_nt(a, b):
    return lax.dot_general(
        a.astype(BF16), b.astype(BF16), (((1,), (1,)), ((), ())), preferred_element_type=F32
    )


def dot_tn(a, b):
    return lax.dot_general(
        a.astype(BF16), b.astype(BF16), (((0,), (0,)), ((), ())), preferred_element_type=F32
    )


def exact_dot(a, b, dims):
    return lax.dot_general(
        a, b, (dims, ((), ())), precision=lax.Precision.HIGHEST, preferred_element_type=F32
    )


def parts(x):
    first = x.astype(BF16)
    rest = x - first.astype(F32)
    second = rest.astype(BF16)
    third = (rest - second.astype(F32)).astype(BF16)
    return [first, second, third]


def iota2(shape, dim):
    return lax.broadcasted_iota(jnp.int32, shape, dim)


def call(body, outs, specs, scratch=(), flops=0):
    return pl.pallas_call(
        body,
        out_shape=outs,
        in_specs=[pl.BlockSpec(memory_space=space) for space in specs],
        out_specs=jax.tree.map(lambda _: pl.BlockSpec(memory_space=pltpu.VMEM), outs),
        scratch_shapes=list(scratch),
        compiler_params=SMALL,
        cost_estimate=pl.CostEstimate(flops=flops, bytes_accessed=1 << 20, transcendentals=0),
    )


def unit_rows(x):
    return x * lax.rsqrt(jnp.sum(x * x, axis=-1, keepdims=True) + EPS)


def advance(keep, delta, feed, state):
    return keep * state - dot(delta, state) + feed


def join(late, early, whole=True):
    keep, delta, feed = late
    keep_e, delta_e, feed_e = early
    if not whole:
        return None, None, advance(keep, delta, feed, feed_e)
    dk = delta.shape[1]
    both = dot(delta, jnp.concatenate([delta_e, feed_e], axis=1))
    delta_new = keep * delta_e + keep_e * delta - both[:, 0:dk]
    return keep * keep_e, delta_new, keep * feed_e + feed - both[:, dk:]


def key_block(ref, col, dk):
    return unit_rows(ref[:, pl.ds(pl.multiple_of(col * dk, dk), dk)].astype(F32))


def slot_rows(ref, rank, slots, rep):
    return jnp.concatenate(
        [ref[pl.ds((rank ^ s) * rep + h, 1), :] for s in slots for h in range(rep)], axis=0
    )


def solve(lows, sides, i, j):
    tokens = i.shape[0]
    leaf = (i // LEAF) == (j // LEAF)
    unit = (i == j).astype(F32)
    power = [jnp.where(leaf, low, 0.0) for low in lows]
    inverse = [unit - p for p in power]
    power = [p.astype(BF16) for p in power]
    power = [dot(p, p).astype(BF16) for p in power]
    inverse = neumann(power, inverse, LEAF // 2, 1.0)
    full = [
        jnp.concatenate([jnp.where(leaf, 0.0, low), side], axis=1) for low, side in zip(lows, sides)
    ]
    full = [f + dot(t - unit, f) for t, f in zip(inverse, full)]
    power = [f[:, 0:tokens].astype(BF16) for f in full]
    return neumann(power, [f[:, tokens:] for f in full], tokens // LEAF, -1.0)


def neumann(power, sides, order, sign):
    width = power[0].shape[1]
    reach = 1
    while 2 * reach < order:
        both = [
            dot(p, jnp.concatenate([p, s.astype(BF16)], axis=1)) for p, s in zip(power, sides)
        ]
        power = [b[:, 0:width].astype(BF16) for b in both]
        sides = [s + sign * b[:, width:] for s, b in zip(sides, both)]
        sign, reach = 1.0, 2 * reach
    return [s + sign * dot(p, s) for p, s in zip(power, sides)]


def placed(body, group):
    def run(*refs):
        index = lax.axis_index("seq")
        spot = (index & (group - 1), lax.axis_index("head"), index >> (group.bit_length() - 1))
        body(spot, *refs)

    return run


def pack_body(dk, dv, rep, slots, where, k_in, v_in, rate_in, decay_in, *refs):
    *outs, rate_ref, decay_ref, sems = refs
    tokens = k_in.shape[0]
    rank = where[0]
    pairs = [(rate_in, rate_ref), (decay_in, decay_ref)]
    for s, out in zip(slots, outs):
        at = pl.multiple_of((rank ^ s) * dk, dk)
        pairs.append((k_in.at[:, pl.ds(at, dk)], out.at[0:tokens, :]))
        for h in range(rep):
            at = pl.multiple_of(((rank ^ s) * rep + h) * dv, dv)
            rows = out.at[(h + 1) * tokens : (h + 2) * tokens, :]
            pairs.append((v_in.at[:, pl.ds(at, dv)], rows))
    copies = [pltpu.make_async_copy(*p, sems.at[n]) for n, p in enumerate(pairs)]
    for copy in copies:
        copy.start()
    copies[0].wait()
    copies[1].wait()
    for s, out in zip(slots, outs):
        rows = [slot_rows(ref, rank, [s], rep) for ref in (rate_ref, decay_ref)]
        terms = [t.astype(F32) for t in parts(jnp.concatenate(rows, axis=0))]
        terms.append(jnp.zeros((PAD - 6 * rep, tokens), F32))
        out[(rep + 1) * tokens :, :] = jnp.concatenate(terms, axis=0).astype(BF16)
    for copy in copies[2:]:
        copy.wait()


def block_sides(decays, rates, tokens):
    i = iota2((tokens, tokens), 0)
    j = iota2((tokens, tokens), 1)
    lower = (i >= j).astype(F32)
    unit = (i == j).astype(F32)
    cum_rows = exact_dot(decays, lower, ((1,), (1,)))
    cum_cols = exact_dot(lower, decays, ((1,), (1,)))
    rate_cols = exact_dot(unit, rates, ((1,), (1,)))
    return i, j, cum_rows, cum_cols, rate_cols


def solve_blocks(keys, values, sides, rep):
    i, j, cum_rows, cum_cols, rate_cols = sides
    dots = [dot_nt(key, key) for key in keys]
    lows, rhs = [], []
    for n, value in enumerate(values):
        rate = rate_cols[:, n : n + 1]
        cum_col = cum_cols[:, n : n + 1]
        gap = jnp.where(i > j, cum_col - cum_rows[n : n + 1, :], 0.0)
        lows.append(jnp.where(i > j, rate * dots[n // rep] * jnp.exp(gap), 0.0))
        rhs.append(
            jnp.concatenate([(rate * jnp.exp(cum_col)) * keys[n // rep], rate * value], axis=1)
        )
    return solve(lows, rhs, i, j)


def owner_body(dk, dv, rep, slots, where, *refs):
    *packs, _, send_ref, delta_ref, feed_ref, keep_ref, scr = refs
    blocks = len(packs)
    tokens = (packs[0].shape[0] - PAD) // (rep + 1)
    for s, pack in zip(slots, packs):
        scr[where[0] ^ s] = pack[...]
    tails = [scr[c, (rep + 1) * tokens :, :].astype(F32) for c in range(blocks)]
    size = 2 * rep
    tails = [t[0:size] + t[size : 2 * size] + t[2 * size : 3 * size] for t in tails]
    rates = jnp.concatenate([t[0:rep] for t in tails], axis=0)
    decays = jnp.concatenate([t[rep:] for t in tails], axis=0)
    sides = block_sides(decays, rates, tokens)
    cum_rows, cum_cols = sides[2], sides[3]
    keys = [unit_rows(scr[c, 0:tokens, :].astype(F32)) for c in range(blocks)]
    jobs = [(c, h) for c in range(blocks) for h in range(rep)]
    values = [scr[c, (h + 1) * tokens : (h + 2) * tokens, :].astype(F32) for c, h in jobs]
    solved = solve_blocks(keys, values, sides, rep)
    entries = []
    for n, (c, h) in enumerate(jobs):
        last = cum_rows[n : n + 1, tokens - 1 : tokens]
        moved = dot_tn(keys[c] * jnp.exp(last - cum_cols[:, n : n + 1]), solved[n])
        entries.append((jnp.exp(last), moved[:, 0:dk], moved[:, dk:]))
        delta_ref[n] = moved[:, 0:dk].astype(BF16)
        feed_ref[n] = moved[:, dk:]
        keep_ref[n : n + 1, :] = jnp.broadcast_to(jnp.exp(last), (1, keep_ref.shape[1]))
    for h in range(rep):
        send_ref[h * dk : (h + 1) * dk, :] = fold(entries[h::rep], False)[2].astype(BF16)


def fold(maps, whole):
    while len(maps) > 1:
        maps = [join(maps[n + 1], maps[n], whole or n > 0) for n in range(0, len(maps), 2)]
    return maps[0]


def block_maps(delta_ref, feed_ref, keep_ref, rep):
    maps = [
        (keep_ref[n : n + 1, 0:1], delta_ref[n].astype(F32), feed_ref[n])
        for n in range(delta_ref.shape[0])
    ]
    return [maps[h::rep] for h in range(rep)]


def total_body(rep, whole, delta_ref, feed_ref, keep_ref, out_ref):
    entries = [fold(m, True) for m in block_maps(delta_ref, feed_ref, keep_ref, rep)]
    store_maps(out_ref, entries, whole)


def terms_body(dk, dv, rep, slots, where, q_in, k_in, v_in, rate_in, decay_in, *refs):
    x_ref, y_ref, q_ref, k_ref, v_ref, rate_ref, decay_ref, sems = refs
    tokens = k_in.shape[0]
    rank = where[0]
    pairs = [(rate_in, rate_ref), (decay_in, decay_ref), (k_in, k_ref), (v_in, v_ref), (q_in, q_ref)]
    copies = [pltpu.make_async_copy(*p, sems.at[n]) for n, p in enumerate(pairs)]
    for copy in copies:
        copy.start()
    copies[0].wait()
    copies[1].wait()
    sides = block_sides(
        slot_rows(decay_ref, rank, slots, rep), slot_rows(rate_ref, rank, slots, rep), tokens
    )
    i, j, cum_rows, cum_cols, _ = sides
    copies[2].wait()
    keys = [key_block(k_ref, rank ^ s, dk) for s in slots]
    copies[3].wait()
    values = []
    for n in range(len(slots) * rep):
        at = pl.multiple_of(((rank ^ slots[n // rep]) * rep + n % rep) * dv, dv)
        values.append(v_ref[:, pl.ds(at, dv)].astype(F32))
    solved = solve_blocks(keys, values, sides, rep)
    copies[4].wait()
    queries = [key_block(q_ref, rank ^ s, dk) * dk**-0.5 for s in slots]
    dots = [dot_nt(query, key) for query, key in zip(queries, keys)]
    for n in range(len(slots) * rep):
        cum_col = cum_cols[:, n : n + 1]
        gap = jnp.where(i >= j, cum_col - cum_rows[n : n + 1, :], 0.0)
        scores = jnp.where(i >= j, dots[n // rep] * jnp.exp(gap), 0.0)
        inner = dot(scores, solved[n])
        x_ref[n] = (queries[n // rep] * jnp.exp(cum_col) - inner[:, 0:dk]).astype(BF16)
        y_ref[n] = inner[:, dk:]


def store_maps(ref, entries, whole=True):
    dk = entries[0][1].shape[0]
    for h, (_, delta, feed) in enumerate(entries):
        rows = slice(h * dk, (h + 1) * dk)
        ref[rows, 0:dk] = delta.astype(BF16)
        if whole:
            ref[rows, dk:] = feed.astype(BF16)
    width = ref.shape[1]
    rows = [jnp.broadcast_to(t.astype(F32), (1, width)) for e in entries for t in parts(e[0])]
    rows.append(jnp.zeros((PAD - len(rows), width), F32))
    ref[len(entries) * dk :, :] = jnp.concatenate(rows, axis=0).astype(BF16)


def load_maps(ref, dk, rep, feeds=None):
    tail = ref[rep * dk :, 0:dk].astype(F32)
    out = []
    for h in range(rep):
        keep = (tail[3 * h : 3 * h + 1] + tail[3 * h + 1 : 3 * h + 2]) + tail[3 * h + 2 : 3 * h + 3]
        rows = slice(h * dk, (h + 1) * dk)
        feed = ref[rows, dk:] if feeds is None else feeds[rows, :]
        out.append((keep[:, 0:1], ref[rows, 0:dk].astype(F32), feed.astype(F32)))
    return out


def pick(flag, yes, no):
    return [tuple(jnp.where(flag == 1, a, b) for a, b in zip(y, n)) for y, n in zip(yes, no)]


def store_send(ref, entries, whole):
    if whole:
        store_maps(ref, entries)
        return
    for h, (_, _, feed) in enumerate(entries):
        ref[h * feed.shape[0] : (h + 1) * feed.shape[0], :] = feed.astype(BF16)


def block_body(dk, rep, step, whole, where, own_ref, came_ref, out_ref):
    own, came = load_maps(own_ref, dk, rep), load_maps(came_ref, dk, rep)
    flag = (where[2] >> step) & 1
    late, early = pick(flag, own, came), pick(flag, came, own)
    store_send(out_ref, [join(l, e, whole) for l, e in zip(late, early)], whole)


def four_join_body(dk, rep, delta_ref, feed_ref, came_ref, out_ref):
    for h, entry in enumerate(load_maps(delta_ref, dk, rep, feed_ref)):
        rows = slice(h * dk, (h + 1) * dk)
        out_ref[rows, :] = advance(*entry, came_ref[rows, :].astype(F32)).astype(BF16)


def four_entry(dk, rep, group, feed_ref, delta_ref):
    entry = []
    for keep, delta, feed in load_maps(delta_ref, dk, rep, feed_ref):
        entry.append(
            (
                jnp.where(group == 3, keep, 1.0),
                jnp.where(group == 3, delta, 0.0),
                jnp.where(group & 1 == 1, feed, 0.0),
            )
        )
    return entry


def four_feed(group, to_third, to_second):
    late = jnp.where(group == 3, to_third[...].astype(F32), 0.0)
    return jnp.where(group == 2, to_second[...].astype(F32), late)


def block_entry(dk, rep, group, *came):
    none = jnp.zeros((dk, dk), F32)
    entry = [(jnp.ones((1, 1), F32), none, none) for _ in range(rep)]
    for step, ref in enumerate(came):
        block = load_maps(ref, dk, rep)
        if step > 0:
            block = [join(l, e) for l, e in zip(entry, block)]
        entry = pick((group >> step) & 1, block, entry)
    return entry


def prefix_body(dk, rep, entry_of, where, delta_ref, feed_ref, keep_ref, *refs):
    *came, a_ref, b_ref = refs
    maps = block_maps(delta_ref, feed_ref, keep_ref, rep)
    unit = (iota2((dk, dk), 0) == iota2((dk, dk), 1)).astype(F32)
    none = jnp.zeros((dk, dk), F32)
    entry = entry_of(dk, rep, where[2], *came)
    states = [jnp.concatenate([k * unit - d, f], axis=1) for k, d, f in entry]
    for c in range(a_ref.shape[0]):
        for h in range(rep):
            a_ref[c, h] = states[h][:, 0:dk].astype(BF16)
            b_ref[c, h] = states[h][:, dk:]
            keep, delta, feed = maps[h][c]
            if c + 1 < a_ref.shape[0]:
                feed = jnp.concatenate([none, feed], axis=1)
                states[h] = advance(keep, delta, feed, states[h])


def enter_body(dk, rep, slots, feed_of, where, a_ref, b_ref, *refs):
    feeds, outs = refs[: len(refs) - a_ref.shape[0]], refs[len(refs) - a_ref.shape[0] :]
    feed = feed_of(where[2], *feeds).astype(BF16)
    for s, out in zip(slots, outs):
        for h in range(rep):
            rows = slice(h * dk, (h + 1) * dk)
            at = where[0] ^ s
            out[rows, :] = (dot(a_ref[at, h], feed[rows]) + b_ref[at, h]).astype(BF16)


def block_feed(step, group, feed_ref):
    return jnp.where((group >> step) & 1 == 1, feed_ref[...].astype(F32), 0.0)


def project_body(dk, dv, rep, slots, at, where, x_ref, y_ref, gate_ref, gain_ref, w_ref, state, *refs):
    *before, out_ref, normed_ref = refs
    own = (where[0] ^ slots[at]) * rep
    outs = []
    for h in range(rep):
        n = at * rep + h
        outs.append(dot(x_ref[n], state[h * dk : (h + 1) * dk, :]) + y_ref[n])
    for h, o in enumerate(outs):
        gate = gate_ref[:, pl.ds(pl.multiple_of((own + h) * dv, dv), dv)].astype(F32)
        inverse = lax.rsqrt(jnp.mean(o * o, axis=-1, keepdims=True) + EPS)
        done = o * inverse * gain_ref[...] * (gate / (1.0 + jnp.exp(-gate)))
        normed_ref[:, h * dv : (h + 1) * dv] = done.astype(BF16)
    columns = out_ref.shape[1]
    start = (1 - where[1]) * columns
    normed = normed_ref[...]
    rows = pl.ds(pl.multiple_of(own * dv, rep * dv), rep * dv)
    step = 256
    for n in range(columns // step):
        at = pl.multiple_of(start + n * step, step)
        cut = slice(n * step, (n + 1) * step)
        total = dot(normed, w_ref[rows, pl.ds(at, step)])
        if before:
            total = total + before[0][:, cut]
        out_ref[:, cut] = total.astype(out_ref.dtype)


def own_body(slots, where, w_ref, *refs):
    *pieces, out_ref = refs
    columns = out_ref.shape[1]
    start = where[1] * columns
    width = pieces[0].shape[1]
    step = 256
    for n in range(columns // step):
        at = pl.multiple_of(start + n * step, step)
        total = 0.0
        for s, piece in zip(slots, pieces):
            rows = pl.ds(pl.multiple_of((where[0] ^ s) * width, width), width)
            total = total + dot(piece[...], w_ref[rows, pl.ds(at, step)])
        out_ref[:, n * step : (n + 1) * step] = total


def per_device(queries, key_rows, values, out_gate, write_rate, log_decay, norm_gain, out_weight):
    tokens = queries.shape[0]
    heads = write_rate.shape[0]
    dv = norm_gain.shape[0]
    dk = dv
    group = queries.shape[1] // dk
    rep = heads // group
    ranks = lax.axis_size("seq")
    halves = lax.axis_size("head")
    groups = ranks // group
    assert ranks % group == 0 and halves == 2
    assert group & (group - 1) == 0 and groups & (groups - 1) == 0
    steps = groups.bit_length() - 1
    columns = out_weight.shape[1] // halves
    shape = jax.ShapeDtypeStruct
    vmem, hbm = pltpu.VMEM, pltpu.HBM
    cube = 2 * tokens * tokens * (dk + dv)
    map_shape = shape((rep * dk + PAD, dk + dv), BF16)
    feed_shape = shape((rep * dk, dv), BF16)
    slots = sorted(range(group), key=lambda s: (s > 0, -s.bit_count(), s))

    def swap(x, flip):
        return lax.ppermute(x, "seq", [(i, i ^ flip) for i in range(ranks)])

    def cycle(x, tour):
        after = dict(zip(tour, tour[1:] + tour[:1]))
        pairs = [(i, after[i // group] * group + i % group) for i in range(ranks)]
        return lax.ppermute(x, "seq", pairs)

    def swap_slots(made):
        return [swap(x, s) if s else x for s, x in zip(slots, made)]

    q_in, k_in, v_in, rate_in, decay_in = [
        pltpu.with_memory_space_constraint(x, hbm)
        for x in (queries, key_rows, values, write_rate, log_decay)
    ]
    small = [pltpu.VMEM(write_rate.shape, F32), pltpu.VMEM(log_decay.shape, F32)]
    pack_shape = shape(((rep + 1) * tokens + PAD, dk), BF16)
    packs = call(
        placed(functools.partial(pack_body, dk, dv, rep, slots), group),
        [pack_shape] * group,
        [hbm] * 4,
        small + [pltpu.SemaphoreType.DMA((2 + (rep + 1) * group,))],
    )(k_in, v_in, rate_in, decay_in)
    packs = swap_slots(packs)
    x, y = call(
        placed(functools.partial(terms_body, dk, dv, rep, slots), group),
        [shape((heads, tokens, dk), BF16), shape((heads, tokens, dv), F32)],
        [hbm] * 5,
        [pltpu.VMEM(z.shape, BF16) for z in (queries, key_rows, values)]
        + small
        + [pltpu.SemaphoreType.DMA((5,))],
        heads * 16 * cube,
    )(q_in, k_in, v_in, rate_in, decay_in)
    jobs = group * rep
    feed, *blocks = call(
        placed(functools.partial(owner_body, dk, dv, rep, slots), group),
        [
            feed_shape,
            shape((jobs, dk, dk), BF16),
            shape((jobs, dk, dv), F32),
            shape((jobs, dk), F32),
        ],
        [vmem] * group + [pl.ANY],
        [pltpu.VMEM((group,) + pack_shape.shape, BF16)],
        jobs * 16 * cube,
    )(*packs, y)

    came, feeds = [], [feed]
    entry_of, feed_of = block_entry, lambda group, feed: jnp.zeros(feed_shape.shape, F32)
    if steps == 1:
        feeds = [swap(feed, group)]
        feed_of = functools.partial(block_feed, 0)
    if steps > 1:
        if steps == 2:
            before = swap(feed, group)
        wide = map_shape if steps > 2 else shape((map_shape.shape[0], dk), BF16)
        own = call(
            functools.partial(total_body, rep, steps > 2), wide, [vmem] * 3, (), jobs * 2 * cube
        )(*blocks)
    if steps == 2:
        came = [before, swap(own, group)]
        joined = call(
            functools.partial(four_join_body, dk, rep),
            feed_shape,
            [vmem] * 3,
            (),
            jobs * 64 * cube,
        )(own, feed, before)
        feeds = [cycle(joined, [0, 1, 3, 2]), cycle(joined, [0, 1, 2, 3])]
        entry_of, feed_of = four_entry, four_feed
    if steps > 2:
        send = own
        for step in range(steps):
            got = swap(send, group << step)
            if step == steps - 1:
                feeds = [got]
                continue
            whole = step + 2 < steps
            send = call(
                placed(functools.partial(block_body, dk, rep, step, whole), group),
                map_shape if whole else feed_shape,
                [vmem] * 2,
            )(send, got)
            came.append(got)
        feed_of = functools.partial(block_feed, steps - 1)
    a, b = call(
        placed(functools.partial(prefix_body, dk, rep, entry_of), group),
        [shape((group, rep, dk, dk), BF16), shape((group, rep, dk, dv), F32)],
        [vmem] * (3 + len(came)),
        (),
        jobs * 4 * cube,
    )(*blocks, *came)
    states = call(
        placed(functools.partial(enter_body, dk, rep, slots, feed_of), group),
        [feed_shape] * group,
        [vmem] * (2 + len(feeds)),
        (),
        cube * jobs,
    )(a, b, *feeds)
    states = swap_slots(states)

    work = 2 * tokens * columns * heads * dv
    away, normed = [], []
    for n, state in enumerate(states):
        kind = F32 if n < group - 1 else BF16
        total, piece = call(
            placed(functools.partial(project_body, dk, dv, rep, slots, n), group),
            [shape((tokens, columns), kind), shape((tokens, rep * dv), BF16)],
            [vmem] * (6 + len(away)),
            (),
            work // group,
        )(x, y, out_gate, norm_gain.reshape(1, dv), out_weight, state, *away)
        away = [total]
        normed.append(piece)
    came = lax.ppermute(away[0], "head", [(0, 1), (1, 0)])
    own = call(placed(functools.partial(own_body, slots), group), shape((tokens, columns), F32), [vmem] * (1 + group), (), work)(
        out_weight, *normed
    )
    return (own + came.astype(F32)).astype(BF16)


def solution(mesh):
    return jax.shard_map(
        per_device,
        mesh=mesh,
        in_specs=(
            P("seq", "head"),
            P("seq", "head"),
            P("seq", "head"),
            P("seq", "head"),
            P("head", "seq"),
            P("head", "seq"),
            P(),
            P("head", None),
        ),
        out_specs=P("seq", "head"),
        check_vma=False,
    )
```

```python
import functools

import jax
import jax.numpy as jnp
from jax import lax
from jax.experimental import pallas as pl
from jax.experimental.pallas import tpu as pltpu
from jax.sharding import PartitionSpec as P

F32 = jnp.float32
BF16 = jnp.bfloat16
EPS = 1e-06
LEAF = 16
PAD = 16
SMALL = pltpu.CompilerParams(vmem_limit_bytes=24 * 1024 * 1024)


def dot(a, b):
    return jnp.dot(a.astype(BF16), b.astype(BF16), preferred_element_type=F32)


def dot_nt(a, b):
    return lax.dot_general(
        a.astype(BF16), b.astype(BF16), (((1,), (1,)), ((), ())), preferred_element_type=F32
    )


def dot_tn(a, b):
    return lax.dot_general(
        a.astype(BF16), b.astype(BF16), (((0,), (0,)), ((), ())), preferred_element_type=F32
    )


def sums_along(rows, mask):
    first, second, third = parts(rows)
    mask = mask.astype(F32).astype(BF16)
    across = dot_nt(first, mask) + (dot_nt(second, mask) + dot_nt(third, mask))
    down = dot_nt(mask, first) + (dot_nt(mask, second) + dot_nt(mask, third))
    return across, down


def parts(x):
    first = x.astype(BF16)
    rest = x - first.astype(F32)
    second = rest.astype(BF16)
    third = (rest - second.astype(F32)).astype(BF16)
    return [first, second, third]


def iota2(shape, dim):
    return lax.broadcasted_iota(jnp.int32, shape, dim)


def call(body, outs, specs, scratch=(), flops=0):
    return pl.pallas_call(
        body,
        out_shape=outs,
        in_specs=[pl.BlockSpec(memory_space=space) for space in specs],
        out_specs=jax.tree.map(lambda _: pl.BlockSpec(memory_space=pltpu.VMEM), outs),
        scratch_shapes=list(scratch),
        compiler_params=SMALL,
        cost_estimate=pl.CostEstimate(flops=flops, bytes_accessed=1 << 20, transcendentals=0),
    )


def unit_rows(x):
    return x * lax.rsqrt(jnp.sum(x * x, axis=-1, keepdims=True) + EPS)


def advance(keep, delta, feed, state):
    return keep * state - dot(delta, state) + feed


def join(late, early, whole=True):
    keep, delta, feed = late
    keep_e, delta_e, feed_e = early
    if not whole:
        return None, None, advance(keep, delta, feed, feed_e)
    dk = delta.shape[1]
    both = dot(delta, jnp.concatenate([delta_e, feed_e], axis=1))
    delta_new = keep * delta_e + keep_e * delta - both[:, 0:dk]
    return keep * keep_e, delta_new, keep * feed_e + feed - both[:, dk:]


def key_block(ref, col, dk):
    return unit_rows(ref[:, pl.ds(pl.multiple_of(col * dk, dk), dk)].astype(F32))


def slot_rows(ref, rank, slots, rep):
    return jnp.concatenate(
        [ref[pl.ds((rank ^ s) * rep + h, 1), :] for s in slots for h in range(rep)], axis=0
    )


def solve(lows, sides, i, j):
    tokens = i.shape[0]
    leaf = (i // LEAF) == (j // LEAF)
    unit = (i == j).astype(F32)
    power = [jnp.where(leaf, low, 0.0) for low in lows]
    inverse = [unit - p for p in power]
    power = [p.astype(BF16) for p in power]
    power = [dot(p, p).astype(BF16) for p in power]
    inverse = neumann(power, inverse, LEAF // 2, 1.0)
    full = [
        jnp.concatenate([jnp.where(leaf, 0.0, low), side], axis=1) for low, side in zip(lows, sides)
    ]
    full = [f + dot(t - unit, f) for t, f in zip(inverse, full)]
    power = [f[:, 0:tokens].astype(BF16) for f in full]
    return neumann(power, [f[:, tokens:] for f in full], tokens // LEAF, -1.0)


def neumann(power, sides, order, sign):
    width = power[0].shape[1]
    reach = 1
    while 2 * reach < order:
        both = [
            dot(p, jnp.concatenate([p, s.astype(BF16)], axis=1)) for p, s in zip(power, sides)
        ]
        power = [b[:, 0:width].astype(BF16) for b in both]
        sides = [s + sign * b[:, width:] for s, b in zip(sides, both)]
        sign, reach = 1.0, 2 * reach
    return [s + sign * dot(p, s) for p, s in zip(power, sides)]


def placed(body, group):
    def run(*refs):
        index = lax.axis_index("seq")
        spot = (index & (group - 1), lax.axis_index("head"), index >> (group.bit_length() - 1))
        body(spot, *refs)

    return run


def pack_body(dk, dv, rep, slots, where, k_in, v_in, rate_in, decay_in, *refs):
    *outs, rate_ref, decay_ref, sems = refs
    tokens = k_in.shape[0]
    rank = where[0]
    pairs = [(rate_in, rate_ref), (decay_in, decay_ref)]
    for s, out in zip(slots, outs):
        at = pl.multiple_of((rank ^ s) * dk, dk)
        pairs.append((k_in.at[:, pl.ds(at, dk)], out.at[0:tokens, :]))
        for h in range(rep):
            at = pl.multiple_of(((rank ^ s) * rep + h) * dv, dv)
            rows = out.at[(h + 1) * tokens : (h + 2) * tokens, :]
            pairs.append((v_in.at[:, pl.ds(at, dv)], rows))
    copies = [pltpu.make_async_copy(*p, sems.at[n]) for n, p in enumerate(pairs)]
    for copy in copies:
        copy.start()
    copies[0].wait()
    copies[1].wait()
    for s, out in zip(slots, outs):
        rows = [slot_rows(ref, rank, [s], rep) for ref in (rate_ref, decay_ref)]
        terms = [t.astype(F32) for t in parts(jnp.concatenate(rows, axis=0))]
        terms.append(jnp.zeros((PAD - 6 * rep, tokens), F32))
        out[(rep + 1) * tokens :, :] = jnp.concatenate(terms, axis=0).astype(BF16)
    for copy in copies[2:]:
        copy.wait()


def block_sides(decays, rates, tokens):
    i = iota2((tokens, tokens), 0)
    j = iota2((tokens, tokens), 1)
    cum_rows, cum_cols = sums_along(decays, i >= j)
    _, rate_cols = sums_along(rates, i == j)
    return i, j, cum_rows, cum_cols, rate_cols


def solve_blocks(keys, values, sides, rep):
    i, j, cum_rows, cum_cols, rate_cols = sides
    dots = [dot_nt(key, key) for key in keys]
    lows, rhs = [], []
    for n, value in enumerate(values):
        rate = rate_cols[:, n : n + 1]
        cum_col = cum_cols[:, n : n + 1]
        gap = jnp.where(i > j, cum_col - cum_rows[n : n + 1, :], 0.0)
        lows.append(jnp.where(i > j, rate * dots[n // rep] * jnp.exp(gap), 0.0))
        rhs.append(
            jnp.concatenate([(rate * jnp.exp(cum_col)) * keys[n // rep], rate * value], axis=1)
        )
    return solve(lows, rhs, i, j)


def owner_body(dk, dv, rep, slots, where, *refs):
    *packs, _, send_ref, delta_ref, feed_ref, keep_ref, scr = refs
    blocks = len(packs)
    tokens = (packs[0].shape[0] - PAD) // (rep + 1)
    for s, pack in zip(slots, packs):
        scr[where[0] ^ s] = pack[...]
    tails = [scr[c, (rep + 1) * tokens :, :].astype(F32) for c in range(blocks)]
    size = 2 * rep
    tails = [t[0:size] + t[size : 2 * size] + t[2 * size : 3 * size] for t in tails]
    rates = jnp.concatenate([t[0:rep] for t in tails], axis=0)
    decays = jnp.concatenate([t[rep:] for t in tails], axis=0)
    sides = block_sides(decays, rates, tokens)
    cum_rows, cum_cols = sides[2], sides[3]
    keys = [unit_rows(scr[c, 0:tokens, :].astype(F32)) for c in range(blocks)]
    jobs = [(c, h) for c in range(blocks) for h in range(rep)]
    values = [scr[c, (h + 1) * tokens : (h + 2) * tokens, :].astype(F32) for c, h in jobs]
    solved = solve_blocks(keys, values, sides, rep)
    entries = []
    for n, (c, h) in enumerate(jobs):
        last = cum_rows[n : n + 1, tokens - 1 : tokens]
        moved = dot_tn(keys[c] * jnp.exp(last - cum_cols[:, n : n + 1]), solved[n])
        entries.append((jnp.exp(last), moved[:, 0:dk], moved[:, dk:]))
        delta_ref[n] = moved[:, 0:dk].astype(BF16)
        feed_ref[n] = moved[:, dk:]
        keep_ref[n : n + 1, :] = jnp.broadcast_to(jnp.exp(last), (1, keep_ref.shape[1]))
    for h in range(rep):
        send_ref[h * dk : (h + 1) * dk, :] = fold(entries[h::rep], False)[2].astype(BF16)


def fold(maps, whole):
    while len(maps) > 1:
        maps = [join(maps[n + 1], maps[n], whole or n > 0) for n in range(0, len(maps), 2)]
    return maps[0]


def block_maps(delta_ref, feed_ref, keep_ref, rep):
    maps = [
        (keep_ref[n : n + 1, 0:1], delta_ref[n].astype(F32), feed_ref[n])
        for n in range(delta_ref.shape[0])
    ]
    return [maps[h::rep] for h in range(rep)]


def total_body(rep, delta_ref, feed_ref, keep_ref, out_ref):
    store_maps(out_ref, [fold(m, True) for m in block_maps(delta_ref, feed_ref, keep_ref, rep)])


def terms_body(dk, dv, rep, slots, where, q_in, k_in, v_in, rate_in, decay_in, *refs):
    x_ref, y_ref, q_ref, k_ref, v_ref, rate_ref, decay_ref, sems = refs
    tokens = k_in.shape[0]
    rank = where[0]
    pairs = [(rate_in, rate_ref), (decay_in, decay_ref), (k_in, k_ref), (v_in, v_ref), (q_in, q_ref)]
    copies = [pltpu.make_async_copy(*p, sems.at[n]) for n, p in enumerate(pairs)]
    for copy in copies:
        copy.start()
    copies[0].wait()
    copies[1].wait()
    sides = block_sides(
        slot_rows(decay_ref, rank, slots, rep), slot_rows(rate_ref, rank, slots, rep), tokens
    )
    i, j, cum_rows, cum_cols, _ = sides
    copies[2].wait()
    keys = [key_block(k_ref, rank ^ s, dk) for s in slots]
    copies[3].wait()
    values = []
    for n in range(len(slots) * rep):
        at = pl.multiple_of(((rank ^ slots[n // rep]) * rep + n % rep) * dv, dv)
        values.append(v_ref[:, pl.ds(at, dv)].astype(F32))
    solved = solve_blocks(keys, values, sides, rep)
    copies[4].wait()
    queries = [key_block(q_ref, rank ^ s, dk) * dk**-0.5 for s in slots]
    dots = [dot_nt(query, key) for query, key in zip(queries, keys)]
    for n in range(len(slots) * rep):
        cum_col = cum_cols[:, n : n + 1]
        gap = jnp.where(i >= j, cum_col - cum_rows[n : n + 1, :], 0.0)
        scores = jnp.where(i >= j, dots[n // rep] * jnp.exp(gap), 0.0)
        inner = dot(scores, solved[n])
        x_ref[n] = (queries[n // rep] * jnp.exp(cum_col) - inner[:, 0:dk]).astype(BF16)
        y_ref[n] = inner[:, dk:]


def store_maps(ref, entries):
    dk = entries[0][1].shape[0]
    for h, (_, delta, feed) in enumerate(entries):
        rows = slice(h * dk, (h + 1) * dk)
        ref[rows, 0:dk] = delta.astype(BF16)
        ref[rows, dk:] = feed.astype(BF16)
    width = ref.shape[1]
    rows = [jnp.broadcast_to(t.astype(F32), (1, width)) for e in entries for t in parts(e[0])]
    rows.append(jnp.zeros((PAD - len(rows), width), F32))
    ref[len(entries) * dk :, :] = jnp.concatenate(rows, axis=0).astype(BF16)


def load_maps(ref, dk, rep):
    tail = ref[rep * dk :, 0:dk].astype(F32)
    out = []
    for h in range(rep):
        keep = (tail[3 * h : 3 * h + 1] + tail[3 * h + 1 : 3 * h + 2]) + tail[3 * h + 2 : 3 * h + 3]
        rows = slice(h * dk, (h + 1) * dk)
        out.append((keep[:, 0:1], ref[rows, 0:dk].astype(F32), ref[rows, dk:].astype(F32)))
    return out


def pick(flag, yes, no):
    return [tuple(jnp.where(flag == 1, a, b) for a, b in zip(y, n)) for y, n in zip(yes, no)]


def store_send(ref, entries, whole):
    if whole:
        store_maps(ref, entries)
        return
    for h, (_, _, feed) in enumerate(entries):
        ref[h * feed.shape[0] : (h + 1) * feed.shape[0], :] = feed.astype(BF16)


def block_body(dk, rep, step, whole, where, own_ref, came_ref, out_ref):
    own, came = load_maps(own_ref, dk, rep), load_maps(came_ref, dk, rep)
    flag = (where[2] >> step) & 1
    late, early = pick(flag, own, came), pick(flag, came, own)
    store_send(out_ref, [join(l, e, whole) for l, e in zip(late, early)], whole)


def four_join_body(dk, rep, where, own_ref, came_ref, out_ref):
    odd = where[2] & 1
    for h, (keep, delta, feed) in enumerate(load_maps(own_ref, dk, rep)):
        rows = slice(h * dk, (h + 1) * dk)
        before = came_ref[rows, :].astype(F32)
        out_ref[rows, :] = jnp.where(
            odd == 1, advance(keep, delta, feed, before), feed
        ).astype(BF16)


def four_entry(dk, rep, group, map_ref):
    entry = []
    for keep, delta, feed in load_maps(map_ref, dk, rep):
        entry.append(
            (
                jnp.where(group > 0, keep, 1.0),
                jnp.where(group > 0, delta, 0.0),
                jnp.where(group > 0, feed, 0.0),
            )
        )
    return entry


def block_entry(dk, rep, group, *came):
    none = jnp.zeros((dk, dk), F32)
    entry = [(jnp.ones((1, 1), F32), none, none) for _ in range(rep)]
    for step, ref in enumerate(came):
        block = load_maps(ref, dk, rep)
        if step > 0:
            block = [join(l, e) for l, e in zip(entry, block)]
        entry = pick((group >> step) & 1, block, entry)
    return entry


def prefix_body(dk, rep, entry_of, where, delta_ref, feed_ref, keep_ref, *refs):
    *came, a_ref, b_ref = refs
    maps = block_maps(delta_ref, feed_ref, keep_ref, rep)
    unit = (iota2((dk, dk), 0) == iota2((dk, dk), 1)).astype(F32)
    none = jnp.zeros((dk, dk), F32)
    entry = entry_of(dk, rep, where[2], *came)
    states = [jnp.concatenate([k * unit - d, f], axis=1) for k, d, f in entry]
    for c in range(a_ref.shape[0]):
        for h in range(rep):
            a_ref[c, h] = states[h][:, 0:dk].astype(BF16)
            b_ref[c, h] = states[h][:, dk:]
            keep, delta, feed = maps[h][c]
            if c + 1 < a_ref.shape[0]:
                feed = jnp.concatenate([none, feed], axis=1)
                states[h] = advance(keep, delta, feed, states[h])


def enter_body(dk, rep, slots, feed_of, where, a_ref, b_ref, *refs):
    feeds, outs = refs[: len(refs) - a_ref.shape[0]], refs[len(refs) - a_ref.shape[0] :]
    feed = feed_of(where[2], *feeds).astype(BF16)
    for s, out in zip(slots, outs):
        for h in range(rep):
            rows = slice(h * dk, (h + 1) * dk)
            at = where[0] ^ s
            out[rows, :] = (dot(a_ref[at, h], feed[rows]) + b_ref[at, h]).astype(BF16)


def block_feed(step, group, feed_ref):
    return jnp.where((group >> step) & 1 == 1, feed_ref[...].astype(F32), 0.0)


def project_body(dk, dv, rep, slots, at, where, x_ref, y_ref, gate_ref, gain_ref, w_ref, state, *refs):
    *before, out_ref, normed_ref = refs
    own = (where[0] ^ slots[at]) * rep
    outs = []
    for h in range(rep):
        n = at * rep + h
        outs.append(dot(x_ref[n], state[h * dk : (h + 1) * dk, :]) + y_ref[n])
    for h, o in enumerate(outs):
        gate = gate_ref[:, pl.ds(pl.multiple_of((own + h) * dv, dv), dv)].astype(F32)
        inverse = lax.rsqrt(jnp.mean(o * o, axis=-1, keepdims=True) + EPS)
        done = o * inverse * gain_ref[...] * (gate / (1.0 + jnp.exp(-gate)))
        normed_ref[:, h * dv : (h + 1) * dv] = done.astype(BF16)
    columns = out_ref.shape[1]
    start = (1 - where[1]) * columns
    normed = normed_ref[...]
    rows = pl.ds(pl.multiple_of(own * dv, rep * dv), rep * dv)
    step = 256
    for n in range(columns // step):
        at = pl.multiple_of(start + n * step, step)
        cut = slice(n * step, (n + 1) * step)
        total = dot(normed, w_ref[rows, pl.ds(at, step)])
        if before:
            total = total + before[0][:, cut]
        out_ref[:, cut] = total.astype(out_ref.dtype)


def own_body(slots, where, w_ref, *refs):
    *pieces, out_ref = refs
    columns = out_ref.shape[1]
    start = where[1] * columns
    width = pieces[0].shape[1]
    step = 256
    for n in range(columns // step):
        at = pl.multiple_of(start + n * step, step)
        total = 0.0
        for s, piece in zip(slots, pieces):
            rows = pl.ds(pl.multiple_of((where[0] ^ s) * width, width), width)
            total = total + dot(piece[...], w_ref[rows, pl.ds(at, step)])
        out_ref[:, n * step : (n + 1) * step] = total


def add_body(own_ref, came_ref, out_ref, rows_ref, sems):
    count, height = rows_ref.shape[0], rows_ref.shape[1]
    copies = []
    for n in range(count):
        rows = slice(n * height, (n + 1) * height)
        total = own_ref[rows, :] + came_ref[rows, :].astype(F32)
        rows_ref[n] = total.astype(BF16)
        copies.append(pltpu.make_async_copy(rows_ref.at[n], out_ref.at[rows, :], sems.at[n]))
        copies[-1].start()
    for copy in copies:
        copy.wait()


def per_device(queries, key_rows, values, out_gate, write_rate, log_decay, norm_gain, out_weight):
    tokens = queries.shape[0]
    heads = write_rate.shape[0]
    dv = norm_gain.shape[0]
    dk = dv
    group = queries.shape[1] // dk
    rep = heads // group
    ranks = lax.axis_size("seq")
    halves = lax.axis_size("head")
    groups = ranks // group
    assert ranks % group == 0 and halves == 2
    assert group & (group - 1) == 0 and groups & (groups - 1) == 0
    steps = groups.bit_length() - 1
    columns = out_weight.shape[1] // halves
    shape = jax.ShapeDtypeStruct
    vmem, hbm = pltpu.VMEM, pltpu.HBM
    cube = 2 * tokens * tokens * (dk + dv)
    map_shape = shape((rep * dk + PAD, dk + dv), BF16)
    feed_shape = shape((rep * dk, dv), BF16)
    slots = sorted(range(group), key=lambda s: (s > 0, -s.bit_count(), s))

    def swap(x, flip):
        return lax.ppermute(x, "seq", [(i, i ^ flip) for i in range(ranks)])

    def cycle(x, tour):
        after = dict(zip(tour, tour[1:] + tour[:1]))
        pairs = [(i, after[i // group] * group + i % group) for i in range(ranks)]
        return lax.ppermute(x, "seq", pairs)

    def swap_slots(made):
        return [swap(x, s) if s else x for s, x in zip(slots, made)]

    q_in, k_in, v_in, rate_in, decay_in = [
        pltpu.with_memory_space_constraint(x, hbm)
        for x in (queries, key_rows, values, write_rate, log_decay)
    ]
    small = [pltpu.VMEM(write_rate.shape, F32), pltpu.VMEM(log_decay.shape, F32)]
    pack_shape = shape(((rep + 1) * tokens + PAD, dk), BF16)
    packs = call(
        placed(functools.partial(pack_body, dk, dv, rep, slots), group),
        [pack_shape] * group,
        [hbm] * 4,
        small + [pltpu.SemaphoreType.DMA((2 + (rep + 1) * group,))],
    )(k_in, v_in, rate_in, decay_in)
    packs = swap_slots(packs)
    x, y = call(
        placed(functools.partial(terms_body, dk, dv, rep, slots), group),
        [shape((heads, tokens, dk), BF16), shape((heads, tokens, dv), F32)],
        [hbm] * 5,
        [pltpu.VMEM(z.shape, BF16) for z in (queries, key_rows, values)]
        + small
        + [pltpu.SemaphoreType.DMA((5,))],
        heads * 16 * cube,
    )(q_in, k_in, v_in, rate_in, decay_in)
    jobs = group * rep
    feed, *blocks = call(
        placed(functools.partial(owner_body, dk, dv, rep, slots), group),
        [
            feed_shape,
            shape((jobs, dk, dk), BF16),
            shape((jobs, dk, dv), F32),
            shape((jobs, dk), F32),
        ],
        [vmem] * group + [pl.ANY],
        [pltpu.VMEM((group,) + pack_shape.shape, BF16)],
        jobs * 16 * cube,
    )(*packs, y)

    came, feeds = [], [feed]
    entry_of, feed_of = block_entry, lambda group, feed: jnp.zeros(feed_shape.shape, F32)
    if steps == 1:
        feeds = [swap(feed, group)]
        feed_of = functools.partial(block_feed, 0)
    if steps > 1:
        if steps == 2:
            before = swap(feed, group)
        own = call(
            functools.partial(total_body, rep), map_shape, [vmem] * 3, (), jobs * 2 * cube
        )(*blocks)
    if steps == 2:
        came = [cycle(own, [0, 1, 2, 3])]
        joined = call(
            placed(functools.partial(four_join_body, dk, rep), group),
            feed_shape,
            [vmem] * 2,
            (),
            jobs * 64 * cube,
        )(own, before)
        feeds = [swap(joined, 2 * group)]
        entry_of, feed_of = four_entry, functools.partial(block_feed, 1)
    if steps > 2:
        send = own
        for step in range(steps):
            got = swap(send, group << step)
            if step == steps - 1:
                feeds = [got]
                continue
            whole = step + 2 < steps
            send = call(
                placed(functools.partial(block_body, dk, rep, step, whole), group),
                map_shape if whole else feed_shape,
                [vmem] * 2,
            )(send, got)
            came.append(got)
        feed_of = functools.partial(block_feed, steps - 1)
    a, b = call(
        placed(functools.partial(prefix_body, dk, rep, entry_of), group),
        [shape((group, rep, dk, dk), BF16), shape((group, rep, dk, dv), F32)],
        [vmem] * (3 + len(came)),
        (),
        jobs * 4 * cube,
    )(*blocks, *came)
    states = call(
        placed(functools.partial(enter_body, dk, rep, slots, feed_of), group),
        [feed_shape] * group,
        [vmem] * (2 + len(feeds)),
        (),
        cube * jobs,
    )(a, b, *feeds)
    states = swap_slots(states)

    work = 2 * tokens * columns * heads * dv
    away, normed = [], []
    for n, state in enumerate(states):
        kind = F32 if n < group - 1 else BF16
        total, piece = call(
            placed(functools.partial(project_body, dk, dv, rep, slots, n), group),
            [shape((tokens, columns), kind), shape((tokens, rep * dv), BF16)],
            [vmem] * (6 + len(away)),
            (),
            work // group,
        )(x, y, out_gate, norm_gain.reshape(1, dv), out_weight, state, *away)
        away = [total]
        normed.append(piece)
    came = lax.ppermute(away[0], "head", [(0, 1), (1, 0)])
    own = call(placed(functools.partial(own_body, slots), group), shape((tokens, columns), F32), [vmem] * (1 + group), (), work)(
        out_weight, *normed
    )
    cuts = 4
    return pl.pallas_call(
        add_body,
        out_shape=shape((tokens, columns), BF16),
        in_specs=[pl.BlockSpec(memory_space=vmem)] * 2,
        out_specs=pl.BlockSpec(memory_space=hbm),
        scratch_shapes=[
            pltpu.VMEM((cuts, tokens // cuts, columns), BF16),
            pltpu.SemaphoreType.DMA((cuts,)),
        ],
        compiler_params=SMALL,
    )(own, came)


def solution(mesh):
    return jax.shard_map(
        per_device,
        mesh=mesh,
        in_specs=(
            P("seq", "head"),
            P("seq", "head"),
            P("seq", "head"),
            P("seq", "head"),
            P("head", "seq"),
            P("head", "seq"),
            P(),
            P("head", None),
        ),
        out_specs=P("seq", "head"),
        check_vma=False,
    )
```

```python
import functools

import jax
import jax.numpy as jnp
from jax import lax
from jax.experimental import pallas as pl
from jax.experimental.pallas import tpu as pltpu
from jax.sharding import PartitionSpec as P

F32 = jnp.float32
BF16 = jnp.bfloat16
EPS = 1e-06
LEAF = 16
PAD = 16
SMALL = pltpu.CompilerParams(vmem_limit_bytes=24 * 1024 * 1024)


def dot(a, b):
    return jnp.dot(a.astype(BF16), b.astype(BF16), preferred_element_type=F32)


def dot_nt(a, b):
    return lax.dot_general(
        a.astype(BF16), b.astype(BF16), (((1,), (1,)), ((), ())), preferred_element_type=F32
    )


def dot_tn(a, b):
    return lax.dot_general(
        a.astype(BF16), b.astype(BF16), (((0,), (0,)), ((), ())), preferred_element_type=F32
    )


def exact_dot(a, b, dims):
    return lax.dot_general(
        a, b, (dims, ((), ())), precision=lax.Precision.HIGHEST, preferred_element_type=F32
    )


def parts(x):
    first = x.astype(BF16)
    rest = x - first.astype(F32)
    second = rest.astype(BF16)
    third = (rest - second.astype(F32)).astype(BF16)
    return [first, second, third]


def iota2(shape, dim):
    return lax.broadcasted_iota(jnp.int32, shape, dim)


def call(body, outs, specs, scratch=(), flops=0):
    return pl.pallas_call(
        body,
        out_shape=outs,
        in_specs=[pl.BlockSpec(memory_space=space) for space in specs],
        out_specs=jax.tree.map(lambda _: pl.BlockSpec(memory_space=pltpu.VMEM), outs),
        scratch_shapes=list(scratch),
        compiler_params=SMALL,
        cost_estimate=pl.CostEstimate(flops=flops, bytes_accessed=1 << 20, transcendentals=0),
    )


def unit_rows(x):
    return x * lax.rsqrt(jnp.sum(x * x, axis=-1, keepdims=True) + EPS)


def advance(keep, delta, feed, state):
    return keep * state - dot(delta, state) + feed


def join(late, early, whole=True):
    keep, delta, feed = late
    keep_e, delta_e, feed_e = early
    if not whole:
        return None, None, advance(keep, delta, feed, feed_e)
    dk = delta.shape[1]
    both = dot(delta, jnp.concatenate([delta_e, feed_e], axis=1))
    delta_new = keep * delta_e + keep_e * delta - both[:, 0:dk]
    return keep * keep_e, delta_new, keep * feed_e + feed - both[:, dk:]


def key_block(ref, col, dk):
    return unit_rows(ref[:, pl.ds(pl.multiple_of(col * dk, dk), dk)].astype(F32))


def slot_rows(ref, rank, slots, rep):
    return jnp.concatenate(
        [ref[pl.ds((rank ^ s) * rep + h, 1), :] for s in slots for h in range(rep)], axis=0
    )


def solve(lows, sides, i, j):
    tokens = i.shape[0]
    leaf = (i // LEAF) == (j // LEAF)
    unit = (i == j).astype(F32)
    power = [jnp.where(leaf, low, 0.0) for low in lows]
    inverse = [unit - p for p in power]
    power = [p.astype(BF16) for p in power]
    power = [dot(p, p).astype(BF16) for p in power]
    inverse = neumann(power, inverse, LEAF // 2, 1.0)
    full = [
        jnp.concatenate([jnp.where(leaf, 0.0, low), side], axis=1) for low, side in zip(lows, sides)
    ]
    full = [f + dot(t - unit, f) for t, f in zip(inverse, full)]
    power = [f[:, 0:tokens].astype(BF16) for f in full]
    return neumann(power, [f[:, tokens:] for f in full], tokens // LEAF, -1.0)


def neumann(power, sides, order, sign):
    width = power[0].shape[1]
    reach = 1
    while 2 * reach < order:
        both = [
            dot(p, jnp.concatenate([p, s.astype(BF16)], axis=1)) for p, s in zip(power, sides)
        ]
        power = [b[:, 0:width].astype(BF16) for b in both]
        sides = [s + sign * b[:, width:] for s, b in zip(sides, both)]
        sign, reach = 1.0, 2 * reach
    return [s + sign * dot(p, s) for p, s in zip(power, sides)]


def placed(body, group):
    def run(*refs):
        index = lax.axis_index("seq")
        spot = (index & (group - 1), lax.axis_index("head"), index >> (group.bit_length() - 1))
        body(spot, *refs)

    return run


def pack_body(dk, dv, rep, slots, where, k_in, v_in, rate_in, decay_in, *refs):
    *outs, rate_ref, decay_ref, sems = refs
    tokens = k_in.shape[0]
    rank = where[0]
    pairs = [(rate_in, rate_ref), (decay_in, decay_ref)]
    for s, out in zip(slots, outs):
        at = pl.multiple_of((rank ^ s) * dk, dk)
        pairs.append((k_in.at[:, pl.ds(at, dk)], out.at[0:tokens, :]))
        for h in range(rep):
            at = pl.multiple_of(((rank ^ s) * rep + h) * dv, dv)
            rows = out.at[(h + 1) * tokens : (h + 2) * tokens, :]
            pairs.append((v_in.at[:, pl.ds(at, dv)], rows))
    copies = [pltpu.make_async_copy(*p, sems.at[n]) for n, p in enumerate(pairs)]
    for copy in copies:
        copy.start()
    copies[0].wait()
    copies[1].wait()
    for s, out in zip(slots, outs):
        rows = [slot_rows(ref, rank, [s], rep) for ref in (rate_ref, decay_ref)]
        terms = [t.astype(F32) for t in parts(jnp.concatenate(rows, axis=0))]
        terms.append(jnp.zeros((PAD - 6 * rep, tokens), F32))
        out[(rep + 1) * tokens :, :] = jnp.concatenate(terms, axis=0).astype(BF16)
    for copy in copies[2:]:
        copy.wait()


def block_sides(decays, rates, tokens):
    i = iota2((tokens, tokens), 0)
    j = iota2((tokens, tokens), 1)
    lower = (i >= j).astype(F32)
    unit = (i == j).astype(F32)
    cum_rows = exact_dot(decays, lower, ((1,), (1,)))
    cum_cols = exact_dot(lower, decays, ((1,), (1,)))
    rate_cols = exact_dot(unit, rates, ((1,), (1,)))
    return i, j, cum_rows, cum_cols, rate_cols


def solve_blocks(keys, values, sides, rep):
    i, j, cum_rows, cum_cols, rate_cols = sides
    dots = [dot_nt(key, key) for key in keys]
    lows, rhs = [], []
    for n, value in enumerate(values):
        rate = rate_cols[:, n : n + 1]
        cum_col = cum_cols[:, n : n + 1]
        gap = jnp.where(i > j, cum_col - cum_rows[n : n + 1, :], 0.0)
        lows.append(jnp.where(i > j, rate * dots[n // rep] * jnp.exp(gap), 0.0))
        rhs.append(
            jnp.concatenate([(rate * jnp.exp(cum_col)) * keys[n // rep], rate * value], axis=1)
        )
    return solve(lows, rhs, i, j)


def owner_body(dk, dv, rep, slots, where, *refs):
    *packs, _, send_ref, delta_ref, feed_ref, keep_ref, scr = refs
    blocks = len(packs)
    tokens = (packs[0].shape[0] - PAD) // (rep + 1)
    for s, pack in zip(slots, packs):
        scr[where[0] ^ s] = pack[...]
    tails = [scr[c, (rep + 1) * tokens :, :].astype(F32) for c in range(blocks)]
    size = 2 * rep
    tails = [t[0:size] + t[size : 2 * size] + t[2 * size : 3 * size] for t in tails]
    rates = jnp.concatenate([t[0:rep] for t in tails], axis=0)
    decays = jnp.concatenate([t[rep:] for t in tails], axis=0)
    sides = block_sides(decays, rates, tokens)
    cum_rows, cum_cols = sides[2], sides[3]
    keys = [unit_rows(scr[c, 0:tokens, :].astype(F32)) for c in range(blocks)]
    jobs = [(c, h) for c in range(blocks) for h in range(rep)]
    values = [scr[c, (h + 1) * tokens : (h + 2) * tokens, :].astype(F32) for c, h in jobs]
    solved = solve_blocks(keys, values, sides, rep)
    entries = []
    for n, (c, h) in enumerate(jobs):
        last = cum_rows[n : n + 1, tokens - 1 : tokens]
        moved = dot_tn(keys[c] * jnp.exp(last - cum_cols[:, n : n + 1]), solved[n])
        entries.append((jnp.exp(last), moved[:, 0:dk], moved[:, dk:]))
        delta_ref[n] = moved[:, 0:dk].astype(BF16)
        feed_ref[n] = moved[:, dk:]
        keep_ref[n : n + 1, :] = jnp.broadcast_to(jnp.exp(last), (1, keep_ref.shape[1]))
    for h in range(rep):
        send_ref[h * dk : (h + 1) * dk, :] = fold(entries[h::rep], False)[2].astype(BF16)


def fold(maps, whole):
    while len(maps) > 1:
        maps = [join(maps[n + 1], maps[n], whole or n > 0) for n in range(0, len(maps), 2)]
    return maps[0]


def block_maps(delta_ref, feed_ref, keep_ref, rep):
    maps = [
        (keep_ref[n : n + 1, 0:1], delta_ref[n].astype(F32), feed_ref[n])
        for n in range(delta_ref.shape[0])
    ]
    return [maps[h::rep] for h in range(rep)]


def total_body(rep, whole, delta_ref, feed_ref, keep_ref, out_ref):
    entries = [fold(m, True) for m in block_maps(delta_ref, feed_ref, keep_ref, rep)]
    store_maps(out_ref, entries, whole)


def terms_body(dk, dv, rep, slots, where, q_in, k_in, v_in, rate_in, decay_in, *refs):
    x_ref, y_ref, q_ref, k_ref, v_ref, rate_ref, decay_ref, sems = refs
    tokens = k_in.shape[0]
    rank = where[0]
    pairs = [(rate_in, rate_ref), (decay_in, decay_ref), (k_in, k_ref), (v_in, v_ref), (q_in, q_ref)]
    copies = [pltpu.make_async_copy(*p, sems.at[n]) for n, p in enumerate(pairs)]
    for copy in copies:
        copy.start()
    copies[0].wait()
    copies[1].wait()
    sides = block_sides(
        slot_rows(decay_ref, rank, slots, rep), slot_rows(rate_ref, rank, slots, rep), tokens
    )
    i, j, cum_rows, cum_cols, _ = sides
    copies[2].wait()
    keys = [key_block(k_ref, rank ^ s, dk) for s in slots]
    copies[3].wait()
    values = []
    for n in range(len(slots) * rep):
        at = pl.multiple_of(((rank ^ slots[n // rep]) * rep + n % rep) * dv, dv)
        values.append(v_ref[:, pl.ds(at, dv)].astype(F32))
    solved = solve_blocks(keys, values, sides, rep)
    copies[4].wait()
    queries = [key_block(q_ref, rank ^ s, dk) * dk**-0.5 for s in slots]
    dots = [dot_nt(query, key) for query, key in zip(queries, keys)]
    for n in range(len(slots) * rep):
        cum_col = cum_cols[:, n : n + 1]
        gap = jnp.where(i >= j, cum_col - cum_rows[n : n + 1, :], 0.0)
        scores = jnp.where(i >= j, dots[n // rep] * jnp.exp(gap), 0.0)
        inner = dot(scores, solved[n])
        x_ref[n] = (queries[n // rep] * jnp.exp(cum_col) - inner[:, 0:dk]).astype(BF16)
        y_ref[n] = inner[:, dk:]


def store_maps(ref, entries, whole=True):
    dk = entries[0][1].shape[0]
    for h, (_, delta, feed) in enumerate(entries):
        rows = slice(h * dk, (h + 1) * dk)
        ref[rows, 0:dk] = delta.astype(BF16)
        if whole:
            ref[rows, dk:] = feed.astype(BF16)
    width = ref.shape[1]
    rows = [jnp.broadcast_to(t.astype(F32), (1, width)) for e in entries for t in parts(e[0])]
    rows.append(jnp.zeros((PAD - len(rows), width), F32))
    ref[len(entries) * dk :, :] = jnp.concatenate(rows, axis=0).astype(BF16)


def load_maps(ref, dk, rep, feeds=None):
    tail = ref[rep * dk :, 0:dk].astype(F32)
    out = []
    for h in range(rep):
        keep = (tail[3 * h : 3 * h + 1] + tail[3 * h + 1 : 3 * h + 2]) + tail[3 * h + 2 : 3 * h + 3]
        rows = slice(h * dk, (h + 1) * dk)
        feed = ref[rows, dk:] if feeds is None else feeds[rows, :]
        out.append((keep[:, 0:1], ref[rows, 0:dk].astype(F32), feed.astype(F32)))
    return out


def pick(flag, yes, no):
    return [tuple(jnp.where(flag == 1, a, b) for a, b in zip(y, n)) for y, n in zip(yes, no)]


def store_send(ref, entries, whole):
    if whole:
        store_maps(ref, entries)
        return
    for h, (_, _, feed) in enumerate(entries):
        ref[h * feed.shape[0] : (h + 1) * feed.shape[0], :] = feed.astype(BF16)


def block_body(dk, rep, step, whole, where, own_ref, came_ref, out_ref):
    own, came = load_maps(own_ref, dk, rep), load_maps(came_ref, dk, rep)
    flag = (where[2] >> step) & 1
    late, early = pick(flag, own, came), pick(flag, came, own)
    store_send(out_ref, [join(l, e, whole) for l, e in zip(late, early)], whole)


def four_join_body(dk, rep, delta_ref, feed_ref, came_ref, out_ref):
    for h, entry in enumerate(load_maps(delta_ref, dk, rep, feed_ref)):
        rows = slice(h * dk, (h + 1) * dk)
        out_ref[rows, :] = advance(*entry, came_ref[rows, :].astype(F32)).astype(BF16)


def four_entry(dk, rep, group, feed_ref, delta_ref):
    entry = []
    for keep, delta, feed in load_maps(delta_ref, dk, rep, feed_ref):
        entry.append(
            (
                jnp.where(group == 3, keep, 1.0),
                jnp.where(group == 3, delta, 0.0),
                jnp.where(group & 1 == 1, feed, 0.0),
            )
        )
    return entry


def four_feed(group, to_third, to_second):
    late = jnp.where(group == 3, to_third[...].astype(F32), 0.0)
    return jnp.where(group == 2, to_second[...].astype(F32), late)


def block_entry(dk, rep, group, *came):
    none = jnp.zeros((dk, dk), F32)
    entry = [(jnp.ones((1, 1), F32), none, none) for _ in range(rep)]
    for step, ref in enumerate(came):
        block = load_maps(ref, dk, rep)
        if step > 0:
            block = [join(l, e) for l, e in zip(entry, block)]
        entry = pick((group >> step) & 1, block, entry)
    return entry


def prefix_body(dk, rep, entry_of, where, delta_ref, feed_ref, keep_ref, *refs):
    *came, a_ref, b_ref = refs
    maps = block_maps(delta_ref, feed_ref, keep_ref, rep)
    unit = (iota2((dk, dk), 0) == iota2((dk, dk), 1)).astype(F32)
    none = jnp.zeros((dk, dk), F32)
    entry = entry_of(dk, rep, where[2], *came)
    states = [jnp.concatenate([k * unit - d, f], axis=1) for k, d, f in entry]
    for c in range(a_ref.shape[0]):
        for h in range(rep):
            a_ref[c, h] = states[h][:, 0:dk].astype(BF16)
            b_ref[c, h] = states[h][:, dk:]
            keep, delta, feed = maps[h][c]
            if c + 1 < a_ref.shape[0]:
                feed = jnp.concatenate([none, feed], axis=1)
                states[h] = advance(keep, delta, feed, states[h])


def enter_body(dk, rep, feed_of, where, a_ref, b_ref, *refs):
    *feeds, out_ref = refs
    feed = feed_of(where[2], *feeds).astype(BF16)
    for c in range(out_ref.shape[0]):
        for h in range(rep):
            rows = slice(h * dk, (h + 1) * dk)
            out_ref[c, rows, :] = (dot(a_ref[c, h], feed[rows]) + b_ref[c, h]).astype(BF16)


def block_feed(step, group, feed_ref):
    return jnp.where((group >> step) & 1 == 1, feed_ref[...].astype(F32), 0.0)


def project_body(dk, dv, rep, slots, span, where, x_ref, y_ref, gate_ref, gain_ref, w_ref, *refs):
    states, *before, out_ref, normed_ref = refs
    outs = []
    for n in span:
        for h in range(rep):
            at = n * rep + h
            state = states[where[0] ^ slots[n], h * dk : (h + 1) * dk, :]
            outs.append(dot(x_ref[at], state) + y_ref[at])
    for at, o in enumerate(outs):
        own = (where[0] ^ slots[span[at // rep]]) * rep + at % rep
        gate = gate_ref[:, pl.ds(pl.multiple_of(own * dv, dv), dv)].astype(F32)
        inverse = lax.rsqrt(jnp.mean(o * o, axis=-1, keepdims=True) + EPS)
        done = o * inverse * gain_ref[...] * (gate / (1.0 + jnp.exp(-gate)))
        normed_ref[:, at * dv : (at + 1) * dv] = done.astype(BF16)
    columns = out_ref.shape[1]
    start = (1 - where[1]) * columns
    width = rep * dv
    step = 256
    for n in range(columns // step):
        at = pl.multiple_of(start + n * step, step)
        cut = slice(n * step, (n + 1) * step)
        total = before[0][:, cut] if before else 0.0
        for k, slot in enumerate(span):
            rows = pl.ds(pl.multiple_of((where[0] ^ slots[slot]) * width, width), width)
            piece = normed_ref[:, k * width : (k + 1) * width]
            total = total + dot(piece, w_ref[rows, pl.ds(at, step)])
        out_ref[:, cut] = total.astype(out_ref.dtype)


def own_body(rep, dv, slots, where, w_ref, *refs):
    *pieces, out_ref = refs
    columns = out_ref.shape[1]
    start = where[1] * columns
    width = rep * dv
    parts_of = [p[:, n : n + width] for p in pieces for n in range(0, p.shape[1], width)]
    step = 256
    for n in range(columns // step):
        at = pl.multiple_of(start + n * step, step)
        total = 0.0
        for s, piece in zip(slots, parts_of):
            rows = pl.ds(pl.multiple_of((where[0] ^ s) * width, width), width)
            total = total + dot(piece, w_ref[rows, pl.ds(at, step)])
        out_ref[:, n * step : (n + 1) * step] = total


def per_device(queries, key_rows, values, out_gate, write_rate, log_decay, norm_gain, out_weight):
    tokens = queries.shape[0]
    heads = write_rate.shape[0]
    dv = norm_gain.shape[0]
    dk = dv
    group = queries.shape[1] // dk
    rep = heads // group
    ranks = lax.axis_size("seq")
    halves = lax.axis_size("head")
    groups = ranks // group
    assert ranks % group == 0 and halves == 2
    assert group & (group - 1) == 0 and groups & (groups - 1) == 0
    steps = groups.bit_length() - 1
    columns = out_weight.shape[1] // halves
    shape = jax.ShapeDtypeStruct
    vmem, hbm = pltpu.VMEM, pltpu.HBM
    cube = 2 * tokens * tokens * (dk + dv)
    map_shape = shape((rep * dk + PAD, dk + dv), BF16)
    feed_shape = shape((rep * dk, dv), BF16)
    slots = sorted(range(group), key=lambda s: (s > 0, -s.bit_count(), s))

    def swap(x, flip):
        return lax.ppermute(x, "seq", [(i, i ^ flip) for i in range(ranks)])

    def cycle(x, tour):
        after = dict(zip(tour, tour[1:] + tour[:1]))
        pairs = [(i, after[i // group] * group + i % group) for i in range(ranks)]
        return lax.ppermute(x, "seq", pairs)

    def swap_slots(made):
        return [swap(x, s) if s else x for s, x in zip(slots, made)]

    q_in, k_in, v_in, rate_in, decay_in = [
        pltpu.with_memory_space_constraint(x, hbm)
        for x in (queries, key_rows, values, write_rate, log_decay)
    ]
    small = [pltpu.VMEM(write_rate.shape, F32), pltpu.VMEM(log_decay.shape, F32)]
    pack_shape = shape(((rep + 1) * tokens + PAD, dk), BF16)
    packs = call(
        placed(functools.partial(pack_body, dk, dv, rep, slots), group),
        [pack_shape] * group,
        [hbm] * 4,
        small + [pltpu.SemaphoreType.DMA((2 + (rep + 1) * group,))],
    )(k_in, v_in, rate_in, decay_in)
    packs = swap_slots(packs)
    x, y = call(
        placed(functools.partial(terms_body, dk, dv, rep, slots), group),
        [shape((heads, tokens, dk), BF16), shape((heads, tokens, dv), F32)],
        [hbm] * 5,
        [pltpu.VMEM(z.shape, BF16) for z in (queries, key_rows, values)]
        + small
        + [pltpu.SemaphoreType.DMA((5,))],
        heads * 16 * cube,
    )(q_in, k_in, v_in, rate_in, decay_in)
    jobs = group * rep
    feed, *blocks = call(
        placed(functools.partial(owner_body, dk, dv, rep, slots), group),
        [
            feed_shape,
            shape((jobs, dk, dk), BF16),
            shape((jobs, dk, dv), F32),
            shape((jobs, dk), F32),
        ],
        [vmem] * group + [pl.ANY],
        [pltpu.VMEM((group,) + pack_shape.shape, BF16)],
        jobs * 16 * cube,
    )(*packs, y)

    came, feeds = [], [feed]
    entry_of, feed_of = block_entry, lambda group, feed: jnp.zeros(feed_shape.shape, F32)
    if steps == 1:
        feeds = [swap(feed, group)]
        feed_of = functools.partial(block_feed, 0)
    if steps > 1:
        if steps == 2:
            before = swap(feed, group)
        wide = map_shape if steps > 2 else shape((map_shape.shape[0], dk), BF16)
        own = call(
            functools.partial(total_body, rep, steps > 2), wide, [vmem] * 3, (), jobs * 2 * cube
        )(*blocks)
    if steps == 2:
        came = [before, swap(own, group)]
        joined = call(
            functools.partial(four_join_body, dk, rep),
            feed_shape,
            [vmem] * 3,
            (),
            jobs * 64 * cube,
        )(own, feed, before)
        feeds = [cycle(joined, [0, 1, 3, 2]), cycle(joined, [0, 1, 2, 3])]
        entry_of, feed_of = four_entry, four_feed
    if steps > 2:
        send = own
        for step in range(steps):
            got = swap(send, group << step)
            if step == steps - 1:
                feeds = [got]
                continue
            whole = step + 2 < steps
            send = call(
                placed(functools.partial(block_body, dk, rep, step, whole), group),
                map_shape if whole else feed_shape,
                [vmem] * 2,
            )(send, got)
            came.append(got)
        feed_of = functools.partial(block_feed, steps - 1)
    a, b = call(
        placed(functools.partial(prefix_body, dk, rep, entry_of), group),
        [shape((group, rep, dk, dk), BF16), shape((group, rep, dk, dv), F32)],
        [vmem] * (3 + len(came)),
        (),
        jobs * 4 * cube,
    )(*blocks, *came)
    states = call(
        placed(functools.partial(enter_body, dk, rep, feed_of), group),
        shape((group,) + feed_shape.shape, BF16),
        [vmem] * (2 + len(feeds)),
        (),
        cube * jobs,
    )(a, b, *feeds)
    members = [[g * group + n for n in range(group)] for g in range(groups)]
    came = lax.all_to_all(states, "seq", 0, 0, axis_index_groups=members)

    work = 2 * tokens * columns * heads * dv
    away, normed = [], []
    for span, source in (([0], states), (list(range(1, group)), came)):
        total, piece = call(
            placed(functools.partial(project_body, dk, dv, rep, slots, span), group),
            [
                shape((tokens, columns), BF16 if away else F32),
                shape((tokens, len(span) * rep * dv), BF16),
            ],
            [vmem] * (6 + len(away)),
            (),
            work // group * len(span),
        )(x, y, out_gate, norm_gain.reshape(1, dv), out_weight, source, *away)
        away = [total]
        normed.append(piece)
    came = lax.ppermute(away[0], "head", [(0, 1), (1, 0)])
    own = call(placed(functools.partial(own_body, rep, dv, slots), group), shape((tokens, columns), F32), [vmem] * 3, (), work)(
        out_weight, *normed
    )
    return (own + came.astype(F32)).astype(BF16)


def solution(mesh):
    return jax.shard_map(
        per_device,
        mesh=mesh,
        in_specs=(
            P("seq", "head"),
            P("seq", "head"),
            P("seq", "head"),
            P("seq", "head"),
            P("head", "seq"),
            P("head", "seq"),
            P(),
            P("head", None),
        ),
        out_specs=P("seq", "head"),
        check_vma=False,
    )
```

```python
import functools

import jax
import jax.numpy as jnp
from jax import lax
from jax.experimental import pallas as pl
from jax.experimental.pallas import tpu as pltpu
from jax.sharding import PartitionSpec as P

F32 = jnp.float32
BF16 = jnp.bfloat16
EPS = 1e-06
LEAF = 16
PAD = 16
SMALL = pltpu.CompilerParams(vmem_limit_bytes=24 * 1024 * 1024)


def dot(a, b):
    return jnp.dot(a.astype(BF16), b.astype(BF16), preferred_element_type=F32)


def dot_nt(a, b):
    return lax.dot_general(
        a.astype(BF16), b.astype(BF16), (((1,), (1,)), ((), ())), preferred_element_type=F32
    )


def dot_tn(a, b):
    return lax.dot_general(
        a.astype(BF16), b.astype(BF16), (((0,), (0,)), ((), ())), preferred_element_type=F32
    )


def exact_dot(a, b, dims):
    return lax.dot_general(
        a, b, (dims, ((), ())), precision=lax.Precision.HIGHEST, preferred_element_type=F32
    )


def parts(x):
    first = x.astype(BF16)
    rest = x - first.astype(F32)
    second = rest.astype(BF16)
    third = (rest - second.astype(F32)).astype(BF16)
    return [first, second, third]


def iota2(shape, dim):
    return lax.broadcasted_iota(jnp.int32, shape, dim)


def call(body, outs, specs, scratch=(), flops=0):
    return pl.pallas_call(
        body,
        out_shape=outs,
        in_specs=[pl.BlockSpec(memory_space=space) for space in specs],
        out_specs=jax.tree.map(lambda _: pl.BlockSpec(memory_space=pltpu.VMEM), outs),
        scratch_shapes=list(scratch),
        compiler_params=SMALL,
        cost_estimate=pl.CostEstimate(flops=flops, bytes_accessed=1 << 20, transcendentals=0),
    )


def unit_rows(x):
    return x * lax.rsqrt(jnp.sum(x * x, axis=-1, keepdims=True) + EPS)


def advance(keep, delta, feed, state):
    return keep * state - dot(delta, state) + feed


def join(late, early, whole=True):
    keep, delta, feed = late
    keep_e, delta_e, feed_e = early
    if not whole:
        return None, None, advance(keep, delta, feed, feed_e)
    dk = delta.shape[1]
    both = dot(delta, jnp.concatenate([delta_e, feed_e], axis=1))
    delta_new = keep * delta_e + keep_e * delta - both[:, 0:dk]
    return keep * keep_e, delta_new, keep * feed_e + feed - both[:, dk:]


def key_block(ref, col, dk):
    return unit_rows(ref[:, pl.ds(pl.multiple_of(col * dk, dk), dk)].astype(F32))


def slot_rows(ref, rank, slots, rep):
    return jnp.concatenate(
        [ref[pl.ds((rank ^ s) * rep + h, 1), :] for s in slots for h in range(rep)], axis=0
    )


def solve(lows, sides, i, j):
    tokens = i.shape[0]
    leaf = (i // LEAF) == (j // LEAF)
    unit = (i == j).astype(F32)
    power = [jnp.where(leaf, low, 0.0) for low in lows]
    inverse = [unit - p for p in power]
    power = [p.astype(BF16) for p in power]
    power = [dot(p, p).astype(BF16) for p in power]
    inverse = neumann(power, inverse, LEAF // 2, 1.0)
    full = [
        jnp.concatenate([jnp.where(leaf, 0.0, low), side], axis=1) for low, side in zip(lows, sides)
    ]
    full = [f + dot(t - unit, f) for t, f in zip(inverse, full)]
    power = [f[:, 0:tokens].astype(BF16) for f in full]
    return neumann(power, [f[:, tokens:] for f in full], tokens // LEAF, -1.0)


def neumann(power, sides, order, sign):
    width = power[0].shape[1]
    reach = 1
    while 2 * reach < order:
        both = [
            dot(p, jnp.concatenate([p, s.astype(BF16)], axis=1)) for p, s in zip(power, sides)
        ]
        power = [b[:, 0:width].astype(BF16) for b in both]
        sides = [s + sign * b[:, width:] for s, b in zip(sides, both)]
        sign, reach = 1.0, 2 * reach
    return [s + sign * dot(p, s) for p, s in zip(power, sides)]


def placed(body, group):
    def run(*refs):
        index = lax.axis_index("seq")
        spot = (index & (group - 1), lax.axis_index("head"), index >> (group.bit_length() - 1))
        body(spot, *refs)

    return run


def pack_body(dk, dv, rep, slots, where, k_in, v_in, rate_in, decay_in, *refs):
    *outs, rate_ref, decay_ref, sems = refs
    tokens = k_in.shape[0]
    rank = where[0]
    pairs = [(rate_in, rate_ref), (decay_in, decay_ref)]
    for s, out in zip(slots, outs):
        at = pl.multiple_of((rank ^ s) * dk, dk)
        pairs.append((k_in.at[:, pl.ds(at, dk)], out.at[0:tokens, :]))
        for h in range(rep):
            at = pl.multiple_of(((rank ^ s) * rep + h) * dv, dv)
            rows = out.at[(h + 1) * tokens : (h + 2) * tokens, :]
            pairs.append((v_in.at[:, pl.ds(at, dv)], rows))
    copies = [pltpu.make_async_copy(*p, sems.at[n]) for n, p in enumerate(pairs)]
    for copy in copies:
        copy.start()
    copies[0].wait()
    copies[1].wait()
    for s, out in zip(slots, outs):
        rows = [slot_rows(ref, rank, [s], rep) for ref in (rate_ref, decay_ref)]
        terms = [t.astype(F32) for t in parts(jnp.concatenate(rows, axis=0))]
        terms.append(jnp.zeros((PAD - 6 * rep, tokens), F32))
        out[(rep + 1) * tokens :, :] = jnp.concatenate(terms, axis=0).astype(BF16)
    for copy in copies[2:]:
        copy.wait()


def block_sides(decays, rates, tokens):
    i = iota2((tokens, tokens), 0)
    j = iota2((tokens, tokens), 1)
    lower = (i >= j).astype(F32)
    unit = (i == j).astype(F32)
    cum_rows = exact_dot(decays, lower, ((1,), (1,)))
    cum_cols = exact_dot(lower, decays, ((1,), (1,)))
    rate_cols = exact_dot(unit, rates, ((1,), (1,)))
    return i, j, cum_rows, cum_cols, rate_cols


def solve_blocks(keys, values, sides, rep):
    i, j, cum_rows, cum_cols, rate_cols = sides
    dots = [dot_nt(key, key) for key in keys]
    lows, rhs = [], []
    for n, value in enumerate(values):
        rate = rate_cols[:, n : n + 1]
        cum_col = cum_cols[:, n : n + 1]
        gap = jnp.where(i > j, cum_col - cum_rows[n : n + 1, :], 0.0)
        lows.append(jnp.where(i > j, rate * dots[n // rep] * jnp.exp(gap), 0.0))
        rhs.append(
            jnp.concatenate([(rate * jnp.exp(cum_col)) * keys[n // rep], rate * value], axis=1)
        )
    return solve(lows, rhs, i, j)


def owner_body(dk, dv, rep, slots, whole, where, *refs):
    *packs, _, send_ref, delta_ref, feed_ref, keep_ref, scr = refs
    blocks = len(packs)
    tokens = (packs[0].shape[0] - PAD) // (rep + 1)
    for s, pack in zip(slots, packs):
        scr[where[0] ^ s] = pack[...]
    tails = [scr[c, (rep + 1) * tokens :, :].astype(F32) for c in range(blocks)]
    size = 2 * rep
    tails = [t[0:size] + t[size : 2 * size] + t[2 * size : 3 * size] for t in tails]
    rates = jnp.concatenate([t[0:rep] for t in tails], axis=0)
    decays = jnp.concatenate([t[rep:] for t in tails], axis=0)
    sides = block_sides(decays, rates, tokens)
    cum_rows, cum_cols = sides[2], sides[3]
    keys = [unit_rows(scr[c, 0:tokens, :].astype(F32)) for c in range(blocks)]
    jobs = [(c, h) for c in range(blocks) for h in range(rep)]
    values = [scr[c, (h + 1) * tokens : (h + 2) * tokens, :].astype(F32) for c, h in jobs]
    solved = solve_blocks(keys, values, sides, rep)
    entries = []
    for n, (c, h) in enumerate(jobs):
        last = cum_rows[n : n + 1, tokens - 1 : tokens]
        moved = dot_tn(keys[c] * jnp.exp(last - cum_cols[:, n : n + 1]), solved[n])
        entries.append((jnp.exp(last), moved[:, 0:dk], moved[:, dk:]))
        delta_ref[n] = moved[:, 0:dk].astype(BF16)
        feed_ref[n] = moved[:, dk:]
        keep_ref[n : n + 1, :] = jnp.broadcast_to(jnp.exp(last), (1, keep_ref.shape[1]))
    store_send(send_ref, [fold(entries[h::rep], whole) for h in range(rep)], whole)


def fold(maps, whole):
    while len(maps) > 1:
        maps = [join(maps[n + 1], maps[n], whole or n > 0) for n in range(0, len(maps), 2)]
    return maps[0]


def block_maps(delta_ref, feed_ref, keep_ref, rep):
    maps = [
        (keep_ref[n : n + 1, 0:1], delta_ref[n].astype(F32), feed_ref[n])
        for n in range(delta_ref.shape[0])
    ]
    return [maps[h::rep] for h in range(rep)]


def terms_body(dk, dv, rep, slots, where, q_in, k_in, v_in, rate_in, decay_in, *refs):
    x_ref, y_ref, q_ref, k_ref, v_ref, rate_ref, decay_ref, sems = refs
    tokens = k_in.shape[0]
    rank = where[0]
    pairs = [(rate_in, rate_ref), (decay_in, decay_ref), (k_in, k_ref), (v_in, v_ref), (q_in, q_ref)]
    copies = [pltpu.make_async_copy(*p, sems.at[n]) for n, p in enumerate(pairs)]
    for copy in copies:
        copy.start()
    copies[0].wait()
    copies[1].wait()
    sides = block_sides(
        slot_rows(decay_ref, rank, slots, rep), slot_rows(rate_ref, rank, slots, rep), tokens
    )
    i, j, cum_rows, cum_cols, _ = sides
    copies[2].wait()
    keys = [key_block(k_ref, rank ^ s, dk) for s in slots]
    copies[3].wait()
    values = []
    for n in range(len(slots) * rep):
        at = pl.multiple_of(((rank ^ slots[n // rep]) * rep + n % rep) * dv, dv)
        values.append(v_ref[:, pl.ds(at, dv)].astype(F32))
    solved = solve_blocks(keys, values, sides, rep)
    copies[4].wait()
    queries = [key_block(q_ref, rank ^ s, dk) * dk**-0.5 for s in slots]
    dots = [dot_nt(query, key) for query, key in zip(queries, keys)]
    for n in range(len(slots) * rep):
        cum_col = cum_cols[:, n : n + 1]
        gap = jnp.where(i >= j, cum_col - cum_rows[n : n + 1, :], 0.0)
        scores = jnp.where(i >= j, dots[n // rep] * jnp.exp(gap), 0.0)
        inner = dot(scores, solved[n])
        x_ref[n] = (queries[n // rep] * jnp.exp(cum_col) - inner[:, 0:dk]).astype(BF16)
        y_ref[n] = inner[:, dk:]


def store_maps(ref, entries):
    dk = entries[0][1].shape[0]
    for h, (_, delta, feed) in enumerate(entries):
        rows = slice(h * dk, (h + 1) * dk)
        ref[rows, 0:dk] = delta.astype(BF16)
        ref[rows, dk:] = feed.astype(BF16)
    width = ref.shape[1]
    rows = [jnp.broadcast_to(t.astype(F32), (1, width)) for e in entries for t in parts(e[0])]
    rows.append(jnp.zeros((PAD - len(rows), width), F32))
    ref[len(entries) * dk :, :] = jnp.concatenate(rows, axis=0).astype(BF16)


def load_maps(ref, dk, rep):
    tail = ref[rep * dk :, 0:dk].astype(F32)
    out = []
    for h in range(rep):
        keep = (tail[3 * h : 3 * h + 1] + tail[3 * h + 1 : 3 * h + 2]) + tail[3 * h + 2 : 3 * h + 3]
        rows = slice(h * dk, (h + 1) * dk)
        out.append((keep[:, 0:1], ref[rows, 0:dk].astype(F32), ref[rows, dk:].astype(F32)))
    return out


def pick(flag, yes, no):
    return [tuple(jnp.where(flag == 1, a, b) for a, b in zip(y, n)) for y, n in zip(yes, no)]


def store_send(ref, entries, whole):
    if whole:
        store_maps(ref, entries)
        return
    for h, (_, _, feed) in enumerate(entries):
        ref[h * feed.shape[0] : (h + 1) * feed.shape[0], :] = feed.astype(BF16)


def block_body(dk, rep, step, whole, where, own_ref, came_ref, out_ref):
    own, came = load_maps(own_ref, dk, rep), load_maps(came_ref, dk, rep)
    flag = (where[2] >> step) & 1
    late, early = pick(flag, own, came), pick(flag, came, own)
    store_send(out_ref, [join(l, e, whole) for l, e in zip(late, early)], whole)


def block_entry(dk, rep, group, *came):
    none = jnp.zeros((dk, dk), F32)
    entry = [(jnp.ones((1, 1), F32), none, none) for _ in range(rep)]
    for step, ref in enumerate(came):
        block = load_maps(ref, dk, rep)
        if step > 0:
            block = [join(l, e) for l, e in zip(entry, block)]
        entry = pick((group >> step) & 1, block, entry)
    return entry


def prefix_body(dk, rep, where, delta_ref, feed_ref, keep_ref, *refs):
    *came, a_ref, b_ref = refs
    maps = block_maps(delta_ref, feed_ref, keep_ref, rep)
    unit = (iota2((dk, dk), 0) == iota2((dk, dk), 1)).astype(F32)
    none = jnp.zeros((dk, dk), F32)
    entry = block_entry(dk, rep, where[2], *came)
    states = [jnp.concatenate([k * unit - d, f], axis=1) for k, d, f in entry]
    for c in range(a_ref.shape[0]):
        for h in range(rep):
            a_ref[c, h] = states[h][:, 0:dk].astype(BF16)
            b_ref[c, h] = states[h][:, dk:]
            keep, delta, feed = maps[h][c]
            if c + 1 < a_ref.shape[0]:
                feed = jnp.concatenate([none, feed], axis=1)
                states[h] = advance(keep, delta, feed, states[h])


def enter_body(dk, rep, slots, steps, where, a_ref, b_ref, feed_ref, *outs):
    late = (where[2] >> (steps - 1)) & 1 if steps else 0
    feed = jnp.where(late == 1, feed_ref[...].astype(F32), 0.0).astype(BF16)
    for s, out in zip(slots, outs):
        for h in range(rep):
            rows = slice(h * dk, (h + 1) * dk)
            at = where[0] ^ s
            out[rows, :] = (dot(a_ref[at, h], feed[rows]) + b_ref[at, h]).astype(BF16)


def project_body(dk, dv, rep, slots, at, where, x_ref, y_ref, gate_ref, gain_ref, w_ref, state, *refs):
    *before, out_ref, normed_ref = refs
    own = (where[0] ^ slots[at]) * rep
    outs = []
    for h in range(rep):
        n = at * rep + h
        outs.append(dot(x_ref[n], state[h * dk : (h + 1) * dk, :]) + y_ref[n])
    for h, o in enumerate(outs):
        gate = gate_ref[:, pl.ds(pl.multiple_of((own + h) * dv, dv), dv)].astype(F32)
        inverse = lax.rsqrt(jnp.mean(o * o, axis=-1, keepdims=True) + EPS)
        done = o * inverse * gain_ref[...] * (gate / (1.0 + jnp.exp(-gate)))
        normed_ref[:, h * dv : (h + 1) * dv] = done.astype(BF16)
    columns = out_ref.shape[1]
    start = (1 - where[1]) * columns
    normed = normed_ref[...]
    rows = pl.ds(pl.multiple_of(own * dv, rep * dv), rep * dv)
    step = 256
    for n in range(columns // step):
        at = pl.multiple_of(start + n * step, step)
        cut = slice(n * step, (n + 1) * step)
        total = dot(normed, w_ref[rows, pl.ds(at, step)])
        if before:
            total = total + before[0][:, cut]
        out_ref[:, cut] = total.astype(out_ref.dtype)


def own_body(slots, where, w_ref, *refs):
    *pieces, out_ref = refs
    columns = out_ref.shape[1]
    start = where[1] * columns
    width = pieces[0].shape[1]
    step = 256
    for n in range(columns // step):
        at = pl.multiple_of(start + n * step, step)
        total = 0.0
        for s, piece in zip(slots, pieces):
            rows = pl.ds(pl.multiple_of((where[0] ^ s) * width, width), width)
            total = total + dot(piece[...], w_ref[rows, pl.ds(at, step)])
        out_ref[:, n * step : (n + 1) * step] = total


def per_device(queries, key_rows, values, out_gate, write_rate, log_decay, norm_gain, out_weight):
    tokens = queries.shape[0]
    heads = write_rate.shape[0]
    dv = norm_gain.shape[0]
    dk = dv
    group = queries.shape[1] // dk
    rep = heads // group
    ranks = lax.axis_size("seq")
    halves = lax.axis_size("head")
    groups = ranks // group
    assert ranks % group == 0 and halves == 2
    assert group & (group - 1) == 0 and groups & (groups - 1) == 0
    steps = groups.bit_length() - 1
    columns = out_weight.shape[1] // halves
    shape = jax.ShapeDtypeStruct
    vmem, hbm = pltpu.VMEM, pltpu.HBM
    cube = 2 * tokens * tokens * (dk + dv)
    map_shape = shape((rep * dk + PAD, dk + dv), BF16)
    feed_shape = shape((rep * dk, dv), BF16)
    slots = sorted(range(group), key=lambda s: (s > 0, -s.bit_count(), s))

    def swap(x, flip):
        return lax.ppermute(x, "seq", [(i, i ^ flip) for i in range(ranks)])

    def swap_slots(made):
        return [swap(x, s) if s else x for s, x in zip(slots, made)]

    q_in, k_in, v_in, rate_in, decay_in = [
        pltpu.with_memory_space_constraint(x, hbm)
        for x in (queries, key_rows, values, write_rate, log_decay)
    ]
    small = [pltpu.VMEM(write_rate.shape, F32), pltpu.VMEM(log_decay.shape, F32)]
    pack_shape = shape(((rep + 1) * tokens + PAD, dk), BF16)
    packs = call(
        placed(functools.partial(pack_body, dk, dv, rep, slots), group),
        [pack_shape] * group,
        [hbm] * 4,
        small + [pltpu.SemaphoreType.DMA((2 + (rep + 1) * group,))],
    )(k_in, v_in, rate_in, decay_in)
    packs = swap_slots(packs)
    x, y = call(
        placed(functools.partial(terms_body, dk, dv, rep, slots), group),
        [shape((heads, tokens, dk), BF16), shape((heads, tokens, dv), F32)],
        [hbm] * 5,
        [pltpu.VMEM(z.shape, BF16) for z in (queries, key_rows, values)]
        + small
        + [pltpu.SemaphoreType.DMA((5,))],
        heads * 16 * cube,
    )(q_in, k_in, v_in, rate_in, decay_in)
    jobs = group * rep
    send, *blocks = call(
        placed(functools.partial(owner_body, dk, dv, rep, slots, steps > 1), group),
        [
            map_shape if steps > 1 else feed_shape,
            shape((jobs, dk, dk), BF16),
            shape((jobs, dk, dv), F32),
            shape((jobs, dk), F32),
        ],
        [vmem] * group + [pl.ANY],
        [pltpu.VMEM((group,) + pack_shape.shape, BF16)],
        jobs * 16 * cube,
    )(*packs, y)

    came, feed = [], send
    for step in range(steps):
        got = swap(send, group << step)
        if step == steps - 1:
            feed = got
            continue
        whole = step + 2 < steps
        send = call(
            placed(functools.partial(block_body, dk, rep, step, whole), group),
            map_shape if whole else feed_shape,
            [vmem] * 2,
        )(send, got)
        came.append(got)
    a, b = call(
        placed(functools.partial(prefix_body, dk, rep), group),
        [shape((group, rep, dk, dk), BF16), shape((group, rep, dk, dv), F32)],
        [vmem] * (3 + len(came)),
        (),
        jobs * 4 * cube,
    )(*blocks, *came)
    states = call(
        placed(functools.partial(enter_body, dk, rep, slots, steps), group),
        [feed_shape] * group,
        [vmem] * 3,
        (),
        cube * jobs,
    )(a, b, feed)
    states = swap_slots(states)

    work = 2 * tokens * columns * heads * dv
    away, normed = [], []
    for n, state in enumerate(states):
        kind = F32 if n < group - 1 else BF16
        total, piece = call(
            placed(functools.partial(project_body, dk, dv, rep, slots, n), group),
            [shape((tokens, columns), kind), shape((tokens, rep * dv), BF16)],
            [vmem] * (6 + len(away)),
            (),
            work // group,
        )(x, y, out_gate, norm_gain.reshape(1, dv), out_weight, state, *away)
        away = [total]
        normed.append(piece)
    came = lax.ppermute(away[0], "head", [(0, 1), (1, 0)])
    own = call(placed(functools.partial(own_body, slots), group), shape((tokens, columns), F32), [vmem] * (1 + group), (), work)(
        out_weight, *normed
    )
    return (own + came.astype(F32)).astype(BF16)


def solution(mesh):
    return jax.shard_map(
        per_device,
        mesh=mesh,
        in_specs=(
            P("seq", "head"),
            P("seq", "head"),
            P("seq", "head"),
            P("seq", "head"),
            P("head", "seq"),
            P("head", "seq"),
            P(),
            P("head", None),
        ),
        out_specs=P("seq", "head"),
        check_vma=False,
    )
```

```python
import functools

import jax
import jax.numpy as jnp
from jax import lax
from jax.experimental import pallas as pl
from jax.experimental.pallas import tpu as pltpu
from jax.sharding import PartitionSpec as P

F32 = jnp.float32
BF16 = jnp.bfloat16
EPS = 1e-06
LEAF = 16
PAD = 16
SMALL = pltpu.CompilerParams(vmem_limit_bytes=24 * 1024 * 1024)


def dot(a, b):
    return jnp.dot(a.astype(BF16), b.astype(BF16), preferred_element_type=F32)


def dot_nt(a, b):
    return lax.dot_general(
        a.astype(BF16), b.astype(BF16), (((1,), (1,)), ((), ())), preferred_element_type=F32
    )


def dot_tn(a, b):
    return lax.dot_general(
        a.astype(BF16), b.astype(BF16), (((0,), (0,)), ((), ())), preferred_element_type=F32
    )


def exact_dot(a, b, dims):
    return lax.dot_general(
        a, b, (dims, ((), ())), precision=lax.Precision.HIGHEST, preferred_element_type=F32
    )


def parts(x):
    first = x.astype(BF16)
    rest = x - first.astype(F32)
    second = rest.astype(BF16)
    third = (rest - second.astype(F32)).astype(BF16)
    return [first, second, third]


def iota2(shape, dim):
    return lax.broadcasted_iota(jnp.int32, shape, dim)


def call(body, outs, specs, scratch=(), flops=0):
    return pl.pallas_call(
        body,
        out_shape=outs,
        in_specs=[pl.BlockSpec(memory_space=space) for space in specs],
        out_specs=jax.tree.map(lambda _: pl.BlockSpec(memory_space=pltpu.VMEM), outs),
        scratch_shapes=list(scratch),
        compiler_params=SMALL,
        cost_estimate=pl.CostEstimate(flops=flops, bytes_accessed=1 << 20, transcendentals=0),
    )


def unit_rows(x):
    return x * lax.rsqrt(jnp.sum(x * x, axis=-1, keepdims=True) + EPS)


def advance(keep, delta, feed, state):
    return keep * state - dot(delta, state) + feed


def join(late, early, whole=True):
    keep, delta, feed = late
    keep_e, delta_e, feed_e = early
    if not whole:
        return None, None, advance(keep, delta, feed, feed_e)
    dk = delta.shape[1]
    both = dot(delta, jnp.concatenate([delta_e, feed_e], axis=1))
    delta_new = keep * delta_e + keep_e * delta - both[:, 0:dk]
    return keep * keep_e, delta_new, keep * feed_e + feed - both[:, dk:]


def key_block(ref, col, dk):
    return unit_rows(ref[:, pl.ds(pl.multiple_of(col * dk, dk), dk)].astype(F32))


def slot_rows(ref, rank, slots, rep):
    return jnp.concatenate(
        [ref[pl.ds((rank ^ s) * rep + h, 1), :] for s in slots for h in range(rep)], axis=0
    )


def solve(lows, sides, i, j):
    tokens = i.shape[0]
    leaf = (i // LEAF) == (j // LEAF)
    unit = (i == j).astype(F32)
    power = [jnp.where(leaf, low, 0.0) for low in lows]
    inverse = [unit - p for p in power]
    power = [p.astype(BF16) for p in power]
    power = [dot(p, p).astype(BF16) for p in power]
    inverse = neumann(power, inverse, LEAF // 2, 1.0)
    full = [
        jnp.concatenate([jnp.where(leaf, 0.0, low), side], axis=1) for low, side in zip(lows, sides)
    ]
    full = [f + dot(t - unit, f) for t, f in zip(inverse, full)]
    power = [f[:, 0:tokens].astype(BF16) for f in full]
    return neumann(power, [f[:, tokens:] for f in full], tokens // LEAF, -1.0)


def neumann(power, sides, order, sign):
    width = power[0].shape[1]
    reach = 1
    while 2 * reach < order:
        both = [
            dot(p, jnp.concatenate([p, s.astype(BF16)], axis=1)) for p, s in zip(power, sides)
        ]
        power = [b[:, 0:width].astype(BF16) for b in both]
        sides = [s + sign * b[:, width:] for s, b in zip(sides, both)]
        sign, reach = 1.0, 2 * reach
    return [s + sign * dot(p, s) for p, s in zip(power, sides)]


def tours(group):
    near = [s for s in range(1, group) if s.bit_count() == 1]
    far = sorted((s for s in range(1, group) if s.bit_count() > 1), key=lambda s: -s.bit_count())
    return [0] + far + near, [0] + far + near[::-1]


def flips(group, core):
    even, odd = tours(group)
    return [a if a == b else a + (b - a) * core for a, b in zip(even, odd)]


def placed(body, group):
    def run(*refs):
        index = lax.axis_index("seq")
        spot = (index & (group - 1), lax.axis_index("head"), index >> (group.bit_length() - 1))
        body(spot, *refs)

    return run


def pack_body(dk, dv, rep, group, where, k_in, v_in, rate_in, decay_in, *refs):
    slots = flips(group, where[1])
    *outs, rate_ref, decay_ref, sems = refs
    tokens = k_in.shape[0]
    rank = where[0]
    pairs = [(rate_in, rate_ref), (decay_in, decay_ref)]
    for s, out in zip(slots, outs):
        at = pl.multiple_of((rank ^ s) * dk, dk)
        pairs.append((k_in.at[:, pl.ds(at, dk)], out.at[0:tokens, :]))
        for h in range(rep):
            at = pl.multiple_of(((rank ^ s) * rep + h) * dv, dv)
            rows = out.at[(h + 1) * tokens : (h + 2) * tokens, :]
            pairs.append((v_in.at[:, pl.ds(at, dv)], rows))
    copies = [pltpu.make_async_copy(*p, sems.at[n]) for n, p in enumerate(pairs)]
    for copy in copies:
        copy.start()
    copies[0].wait()
    copies[1].wait()
    for s, out in zip(slots, outs):
        rows = [slot_rows(ref, rank, [s], rep) for ref in (rate_ref, decay_ref)]
        terms = [t.astype(F32) for t in parts(jnp.concatenate(rows, axis=0))]
        terms.append(jnp.zeros((PAD - 6 * rep, tokens), F32))
        out[(rep + 1) * tokens :, :] = jnp.concatenate(terms, axis=0).astype(BF16)
    for copy in copies[2:]:
        copy.wait()


def block_sides(decays, rates, tokens):
    i = iota2((tokens, tokens), 0)
    j = iota2((tokens, tokens), 1)
    lower = (i >= j).astype(F32)
    unit = (i == j).astype(F32)
    cum_rows = exact_dot(decays, lower, ((1,), (1,)))
    cum_cols = exact_dot(lower, decays, ((1,), (1,)))
    rate_cols = exact_dot(unit, rates, ((1,), (1,)))
    return i, j, cum_rows, cum_cols, rate_cols


def solve_blocks(keys, values, sides, rep):
    i, j, cum_rows, cum_cols, rate_cols = sides
    dots = [dot_nt(key, key) for key in keys]
    lows, rhs = [], []
    for n, value in enumerate(values):
        rate = rate_cols[:, n : n + 1]
        cum_col = cum_cols[:, n : n + 1]
        gap = jnp.where(i > j, cum_col - cum_rows[n : n + 1, :], 0.0)
        lows.append(jnp.where(i > j, rate * dots[n // rep] * jnp.exp(gap), 0.0))
        rhs.append(
            jnp.concatenate([(rate * jnp.exp(cum_col)) * keys[n // rep], rate * value], axis=1)
        )
    return solve(lows, rhs, i, j)


def owner_body(dk, dv, rep, group, whole, where, *refs):
    slots = flips(group, where[1])
    *packs, _, send_ref, delta_ref, feed_ref, keep_ref, scr = refs
    blocks = len(packs)
    tokens = (packs[0].shape[0] - PAD) // (rep + 1)
    for s, pack in zip(slots, packs):
        scr[where[0] ^ s] = pack[...]
    tails = [scr[c, (rep + 1) * tokens :, :].astype(F32) for c in range(blocks)]
    size = 2 * rep
    tails = [t[0:size] + t[size : 2 * size] + t[2 * size : 3 * size] for t in tails]
    rates = jnp.concatenate([t[0:rep] for t in tails], axis=0)
    decays = jnp.concatenate([t[rep:] for t in tails], axis=0)
    sides = block_sides(decays, rates, tokens)
    cum_rows, cum_cols = sides[2], sides[3]
    keys = [unit_rows(scr[c, 0:tokens, :].astype(F32)) for c in range(blocks)]
    jobs = [(c, h) for c in range(blocks) for h in range(rep)]
    values = [scr[c, (h + 1) * tokens : (h + 2) * tokens, :].astype(F32) for c, h in jobs]
    solved = solve_blocks(keys, values, sides, rep)
    entries = []
    for n, (c, h) in enumerate(jobs):
        last = cum_rows[n : n + 1, tokens - 1 : tokens]
        moved = dot_tn(keys[c] * jnp.exp(last - cum_cols[:, n : n + 1]), solved[n])
        entries.append((jnp.exp(last), moved[:, 0:dk], moved[:, dk:]))
        delta_ref[n] = moved[:, 0:dk].astype(BF16)
        feed_ref[n] = moved[:, dk:]
        keep_ref[n : n + 1, :] = jnp.broadcast_to(jnp.exp(last), (1, keep_ref.shape[1]))
    store_send(send_ref, [fold(entries[h::rep], whole) for h in range(rep)], whole)


def fold(maps, whole):
    while len(maps) > 1:
        maps = [join(maps[n + 1], maps[n], whole or n > 0) for n in range(0, len(maps), 2)]
    return maps[0]


def block_maps(delta_ref, feed_ref, keep_ref, rep):
    maps = [
        (keep_ref[n : n + 1, 0:1], delta_ref[n].astype(F32), feed_ref[n])
        for n in range(delta_ref.shape[0])
    ]
    return [maps[h::rep] for h in range(rep)]


def terms_body(dk, dv, rep, group, where, q_in, k_in, v_in, rate_in, decay_in, *refs):
    slots = flips(group, where[1])
    x_ref, y_ref, q_ref, k_ref, v_ref, rate_ref, decay_ref, sems = refs
    tokens = k_in.shape[0]
    rank = where[0]
    pairs = [(rate_in, rate_ref), (decay_in, decay_ref), (k_in, k_ref), (v_in, v_ref), (q_in, q_ref)]
    copies = [pltpu.make_async_copy(*p, sems.at[n]) for n, p in enumerate(pairs)]
    for copy in copies:
        copy.start()
    copies[0].wait()
    copies[1].wait()
    sides = block_sides(
        slot_rows(decay_ref, rank, slots, rep), slot_rows(rate_ref, rank, slots, rep), tokens
    )
    i, j, cum_rows, cum_cols, _ = sides
    copies[2].wait()
    keys = [key_block(k_ref, rank ^ s, dk) for s in slots]
    copies[3].wait()
    values = []
    for n in range(len(slots) * rep):
        at = pl.multiple_of(((rank ^ slots[n // rep]) * rep + n % rep) * dv, dv)
        values.append(v_ref[:, pl.ds(at, dv)].astype(F32))
    solved = solve_blocks(keys, values, sides, rep)
    copies[4].wait()
    queries = [key_block(q_ref, rank ^ s, dk) * dk**-0.5 for s in slots]
    dots = [dot_nt(query, key) for query, key in zip(queries, keys)]
    for n in range(len(slots) * rep):
        cum_col = cum_cols[:, n : n + 1]
        gap = jnp.where(i >= j, cum_col - cum_rows[n : n + 1, :], 0.0)
        scores = jnp.where(i >= j, dots[n // rep] * jnp.exp(gap), 0.0)
        inner = dot(scores, solved[n])
        x_ref[n] = (queries[n // rep] * jnp.exp(cum_col) - inner[:, 0:dk]).astype(BF16)
        y_ref[n] = inner[:, dk:]


def store_maps(ref, entries):
    dk = entries[0][1].shape[0]
    for h, (_, delta, feed) in enumerate(entries):
        rows = slice(h * dk, (h + 1) * dk)
        ref[rows, 0:dk] = delta.astype(BF16)
        ref[rows, dk:] = feed.astype(BF16)
    width = ref.shape[1]
    rows = [jnp.broadcast_to(t.astype(F32), (1, width)) for e in entries for t in parts(e[0])]
    rows.append(jnp.zeros((PAD - len(rows), width), F32))
    ref[len(entries) * dk :, :] = jnp.concatenate(rows, axis=0).astype(BF16)


def load_maps(ref, dk, rep):
    tail = ref[rep * dk :, 0:dk].astype(F32)
    out = []
    for h in range(rep):
        keep = (tail[3 * h : 3 * h + 1] + tail[3 * h + 1 : 3 * h + 2]) + tail[3 * h + 2 : 3 * h + 3]
        rows = slice(h * dk, (h + 1) * dk)
        out.append((keep[:, 0:1], ref[rows, 0:dk].astype(F32), ref[rows, dk:].astype(F32)))
    return out


def pick(flag, yes, no):
    return [tuple(jnp.where(flag == 1, a, b) for a, b in zip(y, n)) for y, n in zip(yes, no)]


def store_send(ref, entries, whole):
    if whole:
        store_maps(ref, entries)
        return
    for h, (_, _, feed) in enumerate(entries):
        ref[h * feed.shape[0] : (h + 1) * feed.shape[0], :] = feed.astype(BF16)


def block_body(dk, rep, step, whole, where, own_ref, came_ref, out_ref):
    own, came = load_maps(own_ref, dk, rep), load_maps(came_ref, dk, rep)
    flag = (where[2] >> step) & 1
    late, early = pick(flag, own, came), pick(flag, came, own)
    store_send(out_ref, [join(l, e, whole) for l, e in zip(late, early)], whole)


def block_entry(dk, rep, group, *came):
    none = jnp.zeros((dk, dk), F32)
    entry = [(jnp.ones((1, 1), F32), none, none) for _ in range(rep)]
    for step, ref in enumerate(came):
        block = load_maps(ref, dk, rep)
        if step > 0:
            block = [join(l, e) for l, e in zip(entry, block)]
        entry = pick((group >> step) & 1, block, entry)
    return entry


def prefix_body(dk, rep, where, delta_ref, feed_ref, keep_ref, *refs):
    *came, a_ref, b_ref = refs
    maps = block_maps(delta_ref, feed_ref, keep_ref, rep)
    unit = (iota2((dk, dk), 0) == iota2((dk, dk), 1)).astype(F32)
    none = jnp.zeros((dk, dk), F32)
    entry = block_entry(dk, rep, where[2], *came)
    states = [jnp.concatenate([k * unit - d, f], axis=1) for k, d, f in entry]
    for c in range(a_ref.shape[0]):
        for h in range(rep):
            a_ref[c, h] = states[h][:, 0:dk].astype(BF16)
            b_ref[c, h] = states[h][:, dk:]
            keep, delta, feed = maps[h][c]
            if c + 1 < a_ref.shape[0]:
                feed = jnp.concatenate([none, feed], axis=1)
                states[h] = advance(keep, delta, feed, states[h])


def enter_body(dk, rep, group, steps, where, a_ref, b_ref, feed_ref, *outs):
    slots = flips(group, where[1])
    late = (where[2] >> (steps - 1)) & 1 if steps else 0
    feed = jnp.where(late == 1, feed_ref[...].astype(F32), 0.0).astype(BF16)
    for s, out in zip(slots, outs):
        for h in range(rep):
            rows = slice(h * dk, (h + 1) * dk)
            at = where[0] ^ s
            out[rows, :] = (dot(a_ref[at, h], feed[rows]) + b_ref[at, h]).astype(BF16)


def project_body(dk, dv, rep, group, at, where, x_ref, y_ref, gate_ref, gain_ref, w_ref, state, *refs):
    slots = flips(group, where[1])
    *before, out_ref, normed_ref = refs
    own = (where[0] ^ slots[at]) * rep
    outs = []
    for h in range(rep):
        n = at * rep + h
        outs.append(dot(x_ref[n], state[h * dk : (h + 1) * dk, :]) + y_ref[n])
    for h, o in enumerate(outs):
        gate = gate_ref[:, pl.ds(pl.multiple_of((own + h) * dv, dv), dv)].astype(F32)
        inverse = lax.rsqrt(jnp.mean(o * o, axis=-1, keepdims=True) + EPS)
        done = o * inverse * gain_ref[...] * (gate / (1.0 + jnp.exp(-gate)))
        normed_ref[:, h * dv : (h + 1) * dv] = done.astype(BF16)
    columns = out_ref.shape[1]
    start = (1 - where[1]) * columns
    normed = normed_ref[...]
    rows = pl.ds(pl.multiple_of(own * dv, rep * dv), rep * dv)
    step = 256
    for n in range(columns // step):
        at = pl.multiple_of(start + n * step, step)
        cut = slice(n * step, (n + 1) * step)
        total = dot(normed, w_ref[rows, pl.ds(at, step)])
        if before:
            total = total + before[0][:, cut]
        out_ref[:, cut] = total.astype(out_ref.dtype)


def own_body(group, where, w_ref, *refs):
    slots = flips(group, where[1])
    *pieces, out_ref = refs
    columns = out_ref.shape[1]
    start = where[1] * columns
    width = pieces[0].shape[1]
    step = 256
    for n in range(columns // step):
        at = pl.multiple_of(start + n * step, step)
        total = 0.0
        for s, piece in zip(slots, pieces):
            rows = pl.ds(pl.multiple_of((where[0] ^ s) * width, width), width)
            total = total + dot(piece[...], w_ref[rows, pl.ds(at, step)])
        out_ref[:, n * step : (n + 1) * step] = total


def per_device(queries, key_rows, values, out_gate, write_rate, log_decay, norm_gain, out_weight):
    tokens = queries.shape[0]
    heads = write_rate.shape[0]
    dv = norm_gain.shape[0]
    dk = dv
    group = queries.shape[1] // dk
    rep = heads // group
    ranks = lax.axis_size("seq")
    halves = lax.axis_size("head")
    groups = ranks // group
    assert ranks % group == 0 and halves == 2
    assert group & (group - 1) == 0 and groups & (groups - 1) == 0
    steps = groups.bit_length() - 1
    columns = out_weight.shape[1] // halves
    shape = jax.ShapeDtypeStruct
    vmem, hbm = pltpu.VMEM, pltpu.HBM
    cube = 2 * tokens * tokens * (dk + dv)
    map_shape = shape((rep * dk + PAD, dk + dv), BF16)
    feed_shape = shape((rep * dk, dv), BF16)

    def swap(x, flip):
        return lax.ppermute(x, "seq", [(i, i ^ flip) for i in range(ranks)])

    def swap_slots(made):
        came = [made[0]]
        for x, *flip in list(zip(made, *tours(group)))[1:]:
            pairs = [(i * halves + c, (i ^ flip[c]) * halves + c) for i in range(ranks) for c in (0, 1)]
            came.append(lax.ppermute(x, ("seq", "head"), pairs))
        return came

    q_in, k_in, v_in, rate_in, decay_in = [
        pltpu.with_memory_space_constraint(x, hbm)
        for x in (queries, key_rows, values, write_rate, log_decay)
    ]
    small = [pltpu.VMEM(write_rate.shape, F32), pltpu.VMEM(log_decay.shape, F32)]
    pack_shape = shape(((rep + 1) * tokens + PAD, dk), BF16)
    packs = call(
        placed(functools.partial(pack_body, dk, dv, rep, group), group),
        [pack_shape] * group,
        [hbm] * 4,
        small + [pltpu.SemaphoreType.DMA((2 + (rep + 1) * group,))],
    )(k_in, v_in, rate_in, decay_in)
    packs = swap_slots(packs)
    x, y = call(
        placed(functools.partial(terms_body, dk, dv, rep, group), group),
        [shape((heads, tokens, dk), BF16), shape((heads, tokens, dv), F32)],
        [hbm] * 5,
        [pltpu.VMEM(z.shape, BF16) for z in (queries, key_rows, values)]
        + small
        + [pltpu.SemaphoreType.DMA((5,))],
        heads * 16 * cube,
    )(q_in, k_in, v_in, rate_in, decay_in)
    jobs = group * rep
    send, *blocks = call(
        placed(functools.partial(owner_body, dk, dv, rep, group, steps > 1), group),
        [
            map_shape if steps > 1 else feed_shape,
            shape((jobs, dk, dk), BF16),
            shape((jobs, dk, dv), F32),
            shape((jobs, dk), F32),
        ],
        [vmem] * group + [pl.ANY],
        [pltpu.VMEM((group,) + pack_shape.shape, BF16)],
        jobs * 16 * cube,
    )(*packs, y)

    came, feed = [], send
    for step in range(steps):
        got = swap(send, group << step)
        if step == steps - 1:
            feed = got
            continue
        whole = step + 2 < steps
        send = call(
            placed(functools.partial(block_body, dk, rep, step, whole), group),
            map_shape if whole else feed_shape,
            [vmem] * 2,
        )(send, got)
        came.append(got)
    a, b = call(
        placed(functools.partial(prefix_body, dk, rep), group),
        [shape((group, rep, dk, dk), BF16), shape((group, rep, dk, dv), F32)],
        [vmem] * (3 + len(came)),
        (),
        jobs * 4 * cube,
    )(*blocks, *came)
    states = call(
        placed(functools.partial(enter_body, dk, rep, group, steps), group),
        [feed_shape] * group,
        [vmem] * 3,
        (),
        cube * jobs,
    )(a, b, feed)
    states = swap_slots(states)

    work = 2 * tokens * columns * heads * dv
    away, normed = [], []
    for n, state in enumerate(states):
        kind = F32 if n < group - 1 else BF16
        total, piece = call(
            placed(functools.partial(project_body, dk, dv, rep, group, n), group),
            [shape((tokens, columns), kind), shape((tokens, rep * dv), BF16)],
            [vmem] * (6 + len(away)),
            (),
            work // group,
        )(x, y, out_gate, norm_gain.reshape(1, dv), out_weight, state, *away)
        away = [total]
        normed.append(piece)
    came = lax.ppermute(away[0], "head", [(0, 1), (1, 0)])
    own = call(placed(functools.partial(own_body, group), group), shape((tokens, columns), F32), [vmem] * (1 + group), (), work)(
        out_weight, *normed
    )
    return (own + came.astype(F32)).astype(BF16)


def solution(mesh):
    return jax.shard_map(
        per_device,
        mesh=mesh,
        in_specs=(
            P("seq", "head"),
            P("seq", "head"),
            P("seq", "head"),
            P("seq", "head"),
            P("head", "seq"),
            P("head", "seq"),
            P(),
            P("head", None),
        ),
        out_specs=P("seq", "head"),
        check_vma=False,
    )
```

```python
import functools

import jax
import jax.numpy as jnp
from jax import lax
from jax.experimental import pallas as pl
from jax.experimental.pallas import tpu as pltpu
from jax.sharding import PartitionSpec as P

F32 = jnp.float32
BF16 = jnp.bfloat16
EPS = 1e-06
LEAF = 16
PAD = 16
SMALL = pltpu.CompilerParams(vmem_limit_bytes=24 * 1024 * 1024)


def dot(a, b):
    return jnp.dot(a.astype(BF16), b.astype(BF16), preferred_element_type=F32)


def dot_nt(a, b):
    return lax.dot_general(
        a.astype(BF16), b.astype(BF16), (((1,), (1,)), ((), ())), preferred_element_type=F32
    )


def dot_tn(a, b):
    return lax.dot_general(
        a.astype(BF16), b.astype(BF16), (((0,), (0,)), ((), ())), preferred_element_type=F32
    )


def exact_dot(a, b, dims):
    return lax.dot_general(
        a, b, (dims, ((), ())), precision=lax.Precision.HIGHEST, preferred_element_type=F32
    )


def parts(x):
    first = x.astype(BF16)
    rest = x - first.astype(F32)
    second = rest.astype(BF16)
    third = (rest - second.astype(F32)).astype(BF16)
    return [first, second, third]


def iota2(shape, dim):
    return lax.broadcasted_iota(jnp.int32, shape, dim)


def call(body, outs, specs, scratch=(), flops=0):
    return pl.pallas_call(
        body,
        out_shape=outs,
        in_specs=[pl.BlockSpec(memory_space=space) for space in specs],
        out_specs=jax.tree.map(lambda _: pl.BlockSpec(memory_space=pltpu.VMEM), outs),
        scratch_shapes=list(scratch),
        compiler_params=SMALL,
        cost_estimate=pl.CostEstimate(flops=flops, bytes_accessed=1 << 20, transcendentals=0),
    )


def unit_rows(x):
    return x * lax.rsqrt(jnp.sum(x * x, axis=-1, keepdims=True) + EPS)


def advance(keep, delta, feed, state):
    return keep * state - dot(delta, state) + feed


def join(late, early, whole=True):
    keep, delta, feed = late
    keep_e, delta_e, feed_e = early
    if not whole:
        return None, None, advance(keep, delta, feed, feed_e)
    dk = delta.shape[1]
    both = dot(delta, jnp.concatenate([delta_e, feed_e], axis=1))
    delta_new = keep * delta_e + keep_e * delta - both[:, 0:dk]
    return keep * keep_e, delta_new, keep * feed_e + feed - both[:, dk:]


def key_block(ref, col, dk):
    return unit_rows(ref[:, pl.ds(pl.multiple_of(col * dk, dk), dk)].astype(F32))


def slot_rows(ref, rank, slots, rep):
    return jnp.concatenate(
        [ref[pl.ds((rank ^ s) * rep + h, 1), :] for s in slots for h in range(rep)], axis=0
    )


def solve(lows, sides, i, j):
    tokens = i.shape[0]
    leaf = (i // LEAF) == (j // LEAF)
    unit = (i == j).astype(F32)
    power = [jnp.where(leaf, low, 0.0) for low in lows]
    inverse = [unit - p for p in power]
    power = [p.astype(BF16) for p in power]
    power = [dot(p, p).astype(BF16) for p in power]
    inverse = neumann(power, inverse, LEAF // 2, 1.0)
    full = [
        jnp.concatenate([jnp.where(leaf, 0.0, low), side], axis=1) for low, side in zip(lows, sides)
    ]
    full = [f + dot(t - unit, f) for t, f in zip(inverse, full)]
    power = [f[:, 0:tokens].astype(BF16) for f in full]
    return neumann(power, [f[:, tokens:] for f in full], tokens // LEAF, -1.0)


def neumann(power, sides, order, sign):
    width = power[0].shape[1]
    reach = 1
    while 2 * reach < order:
        both = [
            dot(p, jnp.concatenate([p, s.astype(BF16)], axis=1)) for p, s in zip(power, sides)
        ]
        power = [b[:, 0:width].astype(BF16) for b in both]
        sides = [s + sign * b[:, width:] for s, b in zip(sides, both)]
        sign, reach = 1.0, 2 * reach
    return [s + sign * dot(p, s) for p, s in zip(power, sides)]


def tours(group):
    near = [s for s in range(1, group) if s.bit_count() == 1]
    far = sorted((s for s in range(1, group) if s.bit_count() > 1), key=lambda s: -s.bit_count())
    return [0] + far + near, [0] + far + near[::-1]


def flips(group, core):
    even, odd = tours(group)
    return [a if a == b else a + (b - a) * core for a, b in zip(even, odd)]


def placed(body, group):
    def run(*refs):
        index = lax.axis_index("seq")
        spot = (index & (group - 1), lax.axis_index("head"), index >> (group.bit_length() - 1))
        body(spot, *refs)

    return run


def pack_body(dk, dv, rep, group, where, k_in, v_in, rate_in, decay_in, *refs):
    slots = flips(group, where[1])
    *outs, rate_ref, decay_ref, sems = refs
    tokens = k_in.shape[0]
    rank = where[0]
    pairs = [(rate_in, rate_ref), (decay_in, decay_ref)]
    for s, out in zip(slots, outs):
        at = pl.multiple_of((rank ^ s) * dk, dk)
        pairs.append((k_in.at[:, pl.ds(at, dk)], out.at[0:tokens, :]))
        for h in range(rep):
            at = pl.multiple_of(((rank ^ s) * rep + h) * dv, dv)
            rows = out.at[(h + 1) * tokens : (h + 2) * tokens, :]
            pairs.append((v_in.at[:, pl.ds(at, dv)], rows))
    copies = [pltpu.make_async_copy(*p, sems.at[n]) for n, p in enumerate(pairs)]
    for copy in copies:
        copy.start()
    copies[0].wait()
    copies[1].wait()
    for s, out in zip(slots, outs):
        rows = [slot_rows(ref, rank, [s], rep) for ref in (rate_ref, decay_ref)]
        terms = [t.astype(F32) for t in parts(jnp.concatenate(rows, axis=0))]
        terms.append(jnp.zeros((PAD - 6 * rep, tokens), F32))
        out[(rep + 1) * tokens :, :] = jnp.concatenate(terms, axis=0).astype(BF16)
    for copy in copies[2:]:
        copy.wait()


def block_sides(decays, rates, tokens):
    i = iota2((tokens, tokens), 0)
    j = iota2((tokens, tokens), 1)
    lower = (i >= j).astype(F32)
    unit = (i == j).astype(F32)
    cum_rows = exact_dot(decays, lower, ((1,), (1,)))
    cum_cols = exact_dot(lower, decays, ((1,), (1,)))
    rate_cols = exact_dot(unit, rates, ((1,), (1,)))
    return i, j, cum_rows, cum_cols, rate_cols


def solve_blocks(keys, values, sides, rep):
    i, j, cum_rows, cum_cols, rate_cols = sides
    dots = [dot_nt(key, key) for key in keys]
    lows, rhs = [], []
    for n, value in enumerate(values):
        rate = rate_cols[:, n : n + 1]
        cum_col = cum_cols[:, n : n + 1]
        gap = jnp.where(i > j, cum_col - cum_rows[n : n + 1, :], 0.0)
        lows.append(jnp.where(i > j, rate * dots[n // rep] * jnp.exp(gap), 0.0))
        rhs.append(
            jnp.concatenate([(rate * jnp.exp(cum_col)) * keys[n // rep], rate * value], axis=1)
        )
    return solve(lows, rhs, i, j)


def owner_body(dk, dv, rep, group, whole, where, *refs):
    slots = flips(group, where[1])
    *packs, _, send_ref, delta_ref, feed_ref, keep_ref, scr = refs
    blocks = len(packs)
    tokens = (packs[0].shape[0] - PAD) // (rep + 1)
    for s, pack in zip(slots, packs):
        scr[where[0] ^ s] = pack[...]
    tails = [scr[c, (rep + 1) * tokens :, :].astype(F32) for c in range(blocks)]
    size = 2 * rep
    tails = [t[0:size] + t[size : 2 * size] + t[2 * size : 3 * size] for t in tails]
    rates = jnp.concatenate([t[0:rep] for t in tails], axis=0)
    decays = jnp.concatenate([t[rep:] for t in tails], axis=0)
    sides = block_sides(decays, rates, tokens)
    cum_rows, cum_cols = sides[2], sides[3]
    keys = [unit_rows(scr[c, 0:tokens, :].astype(F32)) for c in range(blocks)]
    jobs = [(c, h) for c in range(blocks) for h in range(rep)]
    values = [scr[c, (h + 1) * tokens : (h + 2) * tokens, :].astype(F32) for c, h in jobs]
    solved = solve_blocks(keys, values, sides, rep)
    entries = []
    for n, (c, h) in enumerate(jobs):
        last = cum_rows[n : n + 1, tokens - 1 : tokens]
        moved = dot_tn(keys[c] * jnp.exp(last - cum_cols[:, n : n + 1]), solved[n])
        entries.append((jnp.exp(last), moved[:, 0:dk], moved[:, dk:]))
        delta_ref[n] = moved[:, 0:dk].astype(BF16)
        feed_ref[n] = moved[:, dk:]
        keep_ref[n : n + 1, :] = jnp.broadcast_to(jnp.exp(last), (1, keep_ref.shape[1]))
    store_send(send_ref, [fold(entries[h::rep], whole) for h in range(rep)], whole)


def fold(maps, whole):
    while len(maps) > 1:
        maps = [join(maps[n + 1], maps[n], whole or n > 0) for n in range(0, len(maps), 2)]
    return maps[0]


def block_maps(delta_ref, feed_ref, keep_ref, rep):
    maps = [
        (keep_ref[n : n + 1, 0:1], delta_ref[n].astype(F32), feed_ref[n])
        for n in range(delta_ref.shape[0])
    ]
    return [maps[h::rep] for h in range(rep)]


def terms_body(dk, dv, rep, group, where, q_in, k_in, v_in, rate_in, decay_in, *refs):
    slots = flips(group, where[1])
    x_ref, y_ref, q_ref, k_ref, v_ref, rate_ref, decay_ref, sems = refs
    tokens = k_in.shape[0]
    rank = where[0]
    pairs = [(rate_in, rate_ref), (decay_in, decay_ref), (k_in, k_ref), (v_in, v_ref), (q_in, q_ref)]
    copies = [pltpu.make_async_copy(*p, sems.at[n]) for n, p in enumerate(pairs)]
    for copy in copies:
        copy.start()
    copies[0].wait()
    copies[1].wait()
    sides = block_sides(
        slot_rows(decay_ref, rank, slots, rep), slot_rows(rate_ref, rank, slots, rep), tokens
    )
    i, j, cum_rows, cum_cols, _ = sides
    copies[2].wait()
    keys = [key_block(k_ref, rank ^ s, dk) for s in slots]
    copies[3].wait()
    values = []
    for n in range(len(slots) * rep):
        at = pl.multiple_of(((rank ^ slots[n // rep]) * rep + n % rep) * dv, dv)
        values.append(v_ref[:, pl.ds(at, dv)].astype(F32))
    solved = solve_blocks(keys, values, sides, rep)
    copies[4].wait()
    queries = [key_block(q_ref, rank ^ s, dk) * dk**-0.5 for s in slots]
    dots = [dot_nt(query, key) for query, key in zip(queries, keys)]
    for n in range(len(slots) * rep):
        cum_col = cum_cols[:, n : n + 1]
        gap = jnp.where(i >= j, cum_col - cum_rows[n : n + 1, :], 0.0)
        scores = jnp.where(i >= j, dots[n // rep] * jnp.exp(gap), 0.0)
        inner = dot(scores, solved[n])
        x_ref[n] = (queries[n // rep] * jnp.exp(cum_col) - inner[:, 0:dk]).astype(BF16)
        y_ref[n] = inner[:, dk:]


def store_maps(ref, entries):
    dk = entries[0][1].shape[0]
    for h, (_, delta, feed) in enumerate(entries):
        rows = slice(h * dk, (h + 1) * dk)
        ref[rows, 0:dk] = delta.astype(BF16)
        ref[rows, dk:] = feed.astype(BF16)
    width = ref.shape[1]
    rows = [jnp.broadcast_to(t.astype(F32), (1, width)) for e in entries for t in parts(e[0])]
    rows.append(jnp.zeros((PAD - len(rows), width), F32))
    ref[len(entries) * dk :, :] = jnp.concatenate(rows, axis=0).astype(BF16)


def load_maps(ref, dk, rep):
    tail = ref[rep * dk :, 0:dk].astype(F32)
    out = []
    for h in range(rep):
        keep = (tail[3 * h : 3 * h + 1] + tail[3 * h + 1 : 3 * h + 2]) + tail[3 * h + 2 : 3 * h + 3]
        rows = slice(h * dk, (h + 1) * dk)
        out.append((keep[:, 0:1], ref[rows, 0:dk].astype(F32), ref[rows, dk:].astype(F32)))
    return out


def pick(flag, yes, no):
    return [tuple(jnp.where(flag == 1, a, b) for a, b in zip(y, n)) for y, n in zip(yes, no)]


def store_send(ref, entries, whole):
    if whole:
        store_maps(ref, entries)
        return
    for h, (_, _, feed) in enumerate(entries):
        ref[h * feed.shape[0] : (h + 1) * feed.shape[0], :] = feed.astype(BF16)


def block_body(dk, rep, step, whole, where, own_ref, came_ref, out_ref):
    own, came = load_maps(own_ref, dk, rep), load_maps(came_ref, dk, rep)
    flag = (where[2] >> step) & 1
    late, early = pick(flag, own, came), pick(flag, came, own)
    store_send(out_ref, [join(l, e, whole) for l, e in zip(late, early)], whole)


def block_entry(dk, rep, group, *came):
    none = jnp.zeros((dk, dk), F32)
    entry = [(jnp.ones((1, 1), F32), none, none) for _ in range(rep)]
    for step, ref in enumerate(came):
        block = load_maps(ref, dk, rep)
        if step > 0:
            block = [join(l, e) for l, e in zip(entry, block)]
        entry = pick((group >> step) & 1, block, entry)
    return entry


def prefix_body(dk, rep, where, delta_ref, feed_ref, keep_ref, *refs):
    *came, a_ref, b_ref = refs
    maps = block_maps(delta_ref, feed_ref, keep_ref, rep)
    unit = (iota2((dk, dk), 0) == iota2((dk, dk), 1)).astype(F32)
    none = jnp.zeros((dk, dk), F32)
    entry = block_entry(dk, rep, where[2], *came)
    states = [jnp.concatenate([k * unit - d, f], axis=1) for k, d, f in entry]
    for c in range(a_ref.shape[0]):
        for h in range(rep):
            a_ref[c, h] = states[h][:, 0:dk].astype(BF16)
            b_ref[c, h] = states[h][:, dk:]
            keep, delta, feed = maps[h][c]
            if c + 1 < a_ref.shape[0]:
                feed = jnp.concatenate([none, feed], axis=1)
                states[h] = advance(keep, delta, feed, states[h])


def enter_body(dk, rep, group, steps, where, a_ref, b_ref, *refs):
    feeds, outs = refs[: len(refs) - a_ref.shape[0]], refs[len(refs) - a_ref.shape[0] :]
    slots = flips(group, where[1])
    late = (where[2] >> (steps - 1)) & 1 if steps else 0
    feed = feeds[0][...].astype(F32)
    if len(feeds) > 1:
        feed = jnp.where(where[2] & 1 == 1, feeds[1][...].astype(F32), feed)
    feed = jnp.where(late == 1, feed, 0.0).astype(BF16)
    for s, out in zip(slots, outs):
        for h in range(rep):
            rows = slice(h * dk, (h + 1) * dk)
            at = where[0] ^ s
            out[rows, :] = (dot(a_ref[at, h], feed[rows]) + b_ref[at, h]).astype(BF16)


def project_body(dk, dv, rep, group, at, where, x_ref, y_ref, gate_ref, gain_ref, w_ref, state, *refs):
    slots = flips(group, where[1])
    *before, out_ref, normed_ref = refs
    own = (where[0] ^ slots[at]) * rep
    outs = []
    for h in range(rep):
        n = at * rep + h
        outs.append(dot(x_ref[n], state[h * dk : (h + 1) * dk, :]) + y_ref[n])
    for h, o in enumerate(outs):
        gate = gate_ref[:, pl.ds(pl.multiple_of((own + h) * dv, dv), dv)].astype(F32)
        inverse = lax.rsqrt(jnp.mean(o * o, axis=-1, keepdims=True) + EPS)
        done = o * inverse * gain_ref[...] * (gate / (1.0 + jnp.exp(-gate)))
        normed_ref[:, h * dv : (h + 1) * dv] = done.astype(BF16)
    columns = out_ref.shape[1]
    start = (1 - where[1]) * columns
    normed = normed_ref[...]
    rows = pl.ds(pl.multiple_of(own * dv, rep * dv), rep * dv)
    step = 256
    for n in range(columns // step):
        at = pl.multiple_of(start + n * step, step)
        cut = slice(n * step, (n + 1) * step)
        total = dot(normed, w_ref[rows, pl.ds(at, step)])
        if before:
            total = total + before[0][:, cut]
        out_ref[:, cut] = total.astype(out_ref.dtype)


def own_body(group, where, w_ref, *refs):
    slots = flips(group, where[1])
    *pieces, out_ref = refs
    columns = out_ref.shape[1]
    start = where[1] * columns
    width = pieces[0].shape[1]
    step = 256
    for n in range(columns // step):
        at = pl.multiple_of(start + n * step, step)
        total = 0.0
        for s, piece in zip(slots, pieces):
            rows = pl.ds(pl.multiple_of((where[0] ^ s) * width, width), width)
            total = total + dot(piece[...], w_ref[rows, pl.ds(at, step)])
        out_ref[:, n * step : (n + 1) * step] = total


def per_device(queries, key_rows, values, out_gate, write_rate, log_decay, norm_gain, out_weight):
    tokens = queries.shape[0]
    heads = write_rate.shape[0]
    dv = norm_gain.shape[0]
    dk = dv
    group = queries.shape[1] // dk
    rep = heads // group
    ranks = lax.axis_size("seq")
    halves = lax.axis_size("head")
    groups = ranks // group
    assert ranks % group == 0 and halves == 2
    assert group & (group - 1) == 0 and groups & (groups - 1) == 0
    steps = groups.bit_length() - 1
    columns = out_weight.shape[1] // halves
    shape = jax.ShapeDtypeStruct
    vmem, hbm = pltpu.VMEM, pltpu.HBM
    cube = 2 * tokens * tokens * (dk + dv)
    map_shape = shape((rep * dk + PAD, dk + dv), BF16)
    feed_shape = shape((rep * dk, dv), BF16)

    def swap(x, flip):
        return lax.ppermute(x, "seq", [(i, i ^ flip) for i in range(ranks)])

    def cycle(x, tour):
        after = dict(zip(tour, tour[1:] + tour[:1]))
        pairs = [(i, after[i // group] * group + i % group) for i in range(ranks)]
        return lax.ppermute(x, "seq", pairs)

    def swap_slots(made):
        came = [made[0]]
        for x, *flip in list(zip(made, *tours(group)))[1:]:
            pairs = [(i * halves + c, (i ^ flip[c]) * halves + c) for i in range(ranks) for c in (0, 1)]
            came.append(lax.ppermute(x, ("seq", "head"), pairs))
        return came

    q_in, k_in, v_in, rate_in, decay_in = [
        pltpu.with_memory_space_constraint(x, hbm)
        for x in (queries, key_rows, values, write_rate, log_decay)
    ]
    small = [pltpu.VMEM(write_rate.shape, F32), pltpu.VMEM(log_decay.shape, F32)]
    pack_shape = shape(((rep + 1) * tokens + PAD, dk), BF16)
    packs = call(
        placed(functools.partial(pack_body, dk, dv, rep, group), group),
        [pack_shape] * group,
        [hbm] * 4,
        small + [pltpu.SemaphoreType.DMA((2 + (rep + 1) * group,))],
    )(k_in, v_in, rate_in, decay_in)
    packs = swap_slots(packs)
    x, y = call(
        placed(functools.partial(terms_body, dk, dv, rep, group), group),
        [shape((heads, tokens, dk), BF16), shape((heads, tokens, dv), F32)],
        [hbm] * 5,
        [pltpu.VMEM(z.shape, BF16) for z in (queries, key_rows, values)]
        + small
        + [pltpu.SemaphoreType.DMA((5,))],
        heads * 16 * cube,
    )(q_in, k_in, v_in, rate_in, decay_in)
    jobs = group * rep
    send, *blocks = call(
        placed(functools.partial(owner_body, dk, dv, rep, group, steps > 1), group),
        [
            map_shape if steps > 1 else feed_shape,
            shape((jobs, dk, dk), BF16),
            shape((jobs, dk, dv), F32),
            shape((jobs, dk), F32),
        ],
        [vmem] * group + [pl.ANY],
        [pltpu.VMEM((group,) + pack_shape.shape, BF16)],
        jobs * 16 * cube,
    )(*packs, y)

    came, feeds = [], [send]
    for step in range(steps):
        if step == 1 and steps == 2:
            feeds = [cycle(send, [0, 2, 3, 1]), cycle(send, [0, 3, 2, 1])]
            break
        got = swap(send, group << step)
        if step == steps - 1:
            feeds = [got]
            continue
        whole = step + 2 < steps
        send = call(
            placed(functools.partial(block_body, dk, rep, step, whole), group),
            map_shape if whole else feed_shape,
            [vmem] * 2,
        )(send, got)
        came.append(got)
    a, b = call(
        placed(functools.partial(prefix_body, dk, rep), group),
        [shape((group, rep, dk, dk), BF16), shape((group, rep, dk, dv), F32)],
        [vmem] * (3 + len(came)),
        (),
        jobs * 4 * cube,
    )(*blocks, *came)
    states = call(
        placed(functools.partial(enter_body, dk, rep, group, steps), group),
        [feed_shape] * group,
        [vmem] * (2 + len(feeds)),
        (),
        cube * jobs,
    )(a, b, *feeds)
    states = swap_slots(states)

    work = 2 * tokens * columns * heads * dv
    away, normed = [], []
    for n, state in enumerate(states):
        kind = F32 if n < group - 1 else BF16
        total, piece = call(
            placed(functools.partial(project_body, dk, dv, rep, group, n), group),
            [shape((tokens, columns), kind), shape((tokens, rep * dv), BF16)],
            [vmem] * (6 + len(away)),
            (),
            work // group,
        )(x, y, out_gate, norm_gain.reshape(1, dv), out_weight, state, *away)
        away = [total]
        normed.append(piece)
    came = lax.ppermute(away[0], "head", [(0, 1), (1, 0)])
    own = call(placed(functools.partial(own_body, group), group), shape((tokens, columns), F32), [vmem] * (1 + group), (), work)(
        out_weight, *normed
    )
    return (own + came.astype(F32)).astype(BF16)


def solution(mesh):
    return jax.shard_map(
        per_device,
        mesh=mesh,
        in_specs=(
            P("seq", "head"),
            P("seq", "head"),
            P("seq", "head"),
            P("seq", "head"),
            P("head", "seq"),
            P("head", "seq"),
            P(),
            P("head", None),
        ),
        out_specs=P("seq", "head"),
        check_vma=False,
    )
```

```python
import functools

import jax
import jax.numpy as jnp
from jax import lax
from jax.experimental import pallas as pl
from jax.experimental.pallas import tpu as pltpu
from jax.sharding import PartitionSpec as P

F32 = jnp.float32
BF16 = jnp.bfloat16
EPS = 1e-06
LEAF = 16
PAD = 16
SMALL = pltpu.CompilerParams(vmem_limit_bytes=24 * 1024 * 1024)


def dot(a, b):
    return jnp.dot(a.astype(BF16), b.astype(BF16), preferred_element_type=F32)


def dot_nt(a, b):
    return lax.dot_general(
        a.astype(BF16), b.astype(BF16), (((1,), (1,)), ((), ())), preferred_element_type=F32
    )


def dot_tn(a, b):
    return lax.dot_general(
        a.astype(BF16), b.astype(BF16), (((0,), (0,)), ((), ())), preferred_element_type=F32
    )


def exact_dot(a, b, dims):
    return lax.dot_general(
        a, b, (dims, ((), ())), precision=lax.Precision.HIGHEST, preferred_element_type=F32
    )


def parts(x):
    first = x.astype(BF16)
    rest = x - first.astype(F32)
    second = rest.astype(BF16)
    third = (rest - second.astype(F32)).astype(BF16)
    return [first, second, third]


def iota2(shape, dim):
    return lax.broadcasted_iota(jnp.int32, shape, dim)


def call(body, outs, specs, scratch=(), flops=0):
    return pl.pallas_call(
        body,
        out_shape=outs,
        in_specs=[pl.BlockSpec(memory_space=space) for space in specs],
        out_specs=jax.tree.map(lambda _: pl.BlockSpec(memory_space=pltpu.VMEM), outs),
        scratch_shapes=list(scratch),
        compiler_params=SMALL,
        cost_estimate=pl.CostEstimate(flops=flops, bytes_accessed=1 << 20, transcendentals=0),
    )


def unit_rows(x):
    return x * lax.rsqrt(jnp.sum(x * x, axis=-1, keepdims=True) + EPS)


def advance(keep, delta, feed, state):
    return keep * state - dot(delta, state) + feed


def join(late, early, whole=True):
    keep, delta, feed = late
    keep_e, delta_e, feed_e = early
    if not whole:
        return None, None, advance(keep, delta, feed, feed_e)
    dk = delta.shape[1]
    both = dot(delta, jnp.concatenate([delta_e, feed_e], axis=1))
    delta_new = keep * delta_e + keep_e * delta - both[:, 0:dk]
    return keep * keep_e, delta_new, keep * feed_e + feed - both[:, dk:]


def key_block(ref, col, dk):
    return ref[:, pl.ds(pl.multiple_of(col * dk, dk), dk)]


def slot_rows(ref, rank, slots, rep):
    return jnp.concatenate(
        [ref[pl.ds((rank ^ s) * rep + h, 1), :] for s in slots for h in range(rep)], axis=0
    )


def solve(lows, sides, i, j):
    tokens = i.shape[0]
    leaf = (i // LEAF) == (j // LEAF)
    unit = (i == j).astype(F32)
    power = [jnp.where(leaf, low, 0.0) for low in lows]
    inverse = [unit - p for p in power]
    power = [p.astype(BF16) for p in power]
    power = [dot(p, p).astype(BF16) for p in power]
    inverse = neumann(power, inverse, LEAF // 2, 1.0)
    full = [
        jnp.concatenate([jnp.where(leaf, 0.0, low), side], axis=1) for low, side in zip(lows, sides)
    ]
    full = [f + dot(t - unit, f) for t, f in zip(inverse, full)]
    power = [f[:, 0:tokens].astype(BF16) for f in full]
    return neumann(power, [f[:, tokens:] for f in full], tokens // LEAF, -1.0)


def neumann(power, sides, order, sign):
    width = power[0].shape[1]
    reach = 1
    while 2 * reach < order:
        both = [
            dot(p, jnp.concatenate([p, s.astype(BF16)], axis=1)) for p, s in zip(power, sides)
        ]
        power = [b[:, 0:width].astype(BF16) for b in both]
        sides = [s + sign * b[:, width:] for s, b in zip(sides, both)]
        sign, reach = 1.0, 2 * reach
    return [s + sign * dot(p, s) for p, s in zip(power, sides)]


def tours(group):
    near = [s for s in range(1, group) if s.bit_count() == 1]
    far = sorted((s for s in range(1, group) if s.bit_count() > 1), key=lambda s: -s.bit_count())
    return [0] + far + near, [0] + far + near[::-1]


def flips(group, core):
    even, odd = tours(group)
    return [a if a == b else a + (b - a) * core for a, b in zip(even, odd)]


def placed(body, group):
    def run(*refs):
        index = lax.axis_index("seq")
        spot = (index & (group - 1), lax.axis_index("head"), index >> (group.bit_length() - 1))
        body(spot, *refs)

    return run


def pack_body(dk, dv, rep, group, where, k_in, v_in, rate_in, decay_in, *refs):
    slots = flips(group, where[1])
    *outs, rate_ref, decay_ref, sems = refs
    tokens = k_in.shape[0]
    rank = where[0]
    pairs = [(rate_in, rate_ref), (decay_in, decay_ref)]
    for s, out in zip(slots, outs):
        at = pl.multiple_of((rank ^ s) * dk, dk)
        pairs.append((k_in.at[:, pl.ds(at, dk)], out.at[0:tokens, :]))
        for h in range(rep):
            at = pl.multiple_of(((rank ^ s) * rep + h) * dv, dv)
            rows = out.at[(h + 1) * tokens : (h + 2) * tokens, :]
            pairs.append((v_in.at[:, pl.ds(at, dv)], rows))
    copies = [pltpu.make_async_copy(*p, sems.at[n]) for n, p in enumerate(pairs)]
    for copy in copies:
        copy.start()
    copies[0].wait()
    copies[1].wait()
    for s, out in zip(slots, outs):
        rows = [slot_rows(ref, rank, [s], rep) for ref in (rate_ref, decay_ref)]
        terms = [t.astype(F32) for t in parts(jnp.concatenate(rows, axis=0))]
        terms.append(jnp.zeros((PAD - 6 * rep, tokens), F32))
        out[(rep + 1) * tokens :, :] = jnp.concatenate(terms, axis=0).astype(BF16)
    for copy in copies[2:]:
        copy.wait()


def block_sides(decays, rates, tokens):
    i = iota2((tokens, tokens), 0)
    j = iota2((tokens, tokens), 1)
    lower = (i >= j).astype(F32)
    unit = (i == j).astype(F32)
    cum_rows = exact_dot(decays, lower, ((1,), (1,)))
    cum_cols = exact_dot(lower, decays, ((1,), (1,)))
    rate_cols = exact_dot(unit, rates, ((1,), (1,)))
    return i, j, cum_rows, cum_cols, rate_cols


def solve_blocks(raw, values, sides, rep):
    i, j, cum_rows, cum_cols, rate_cols = sides
    dots = [dot_nt(key, key) for key in raw]
    across = [
        lax.rsqrt(jnp.sum(jnp.where(i == j, d, 0.0), axis=0, keepdims=True) + EPS) for d in dots
    ]
    raw = [key.astype(F32) for key in raw]
    down = [lax.rsqrt(jnp.sum(key * key, axis=-1, keepdims=True) + EPS) for key in raw]
    keys = [key * scale for key, scale in zip(raw, down)]
    lows, rhs = [], []
    for n, value in enumerate(values):
        m = n // rep
        rate = rate_cols[:, n : n + 1]
        cum_col = cum_cols[:, n : n + 1]
        gap = jnp.where(i > j, cum_col - cum_rows[n : n + 1, :], 0.0)
        low = ((rate * down[m]) * dots[m]) * (across[m] * jnp.exp(gap))
        lows.append(jnp.where(i > j, low, 0.0))
        rhs.append(jnp.concatenate([(rate * jnp.exp(cum_col)) * keys[m], rate * value], axis=1))
    return solve(lows, rhs, i, j), keys


def owner_body(dk, dv, rep, group, whole, where, *refs):
    slots = flips(group, where[1])
    *packs, _, send_ref, delta_ref, feed_ref, keep_ref, scr = refs
    blocks = len(packs)
    tokens = (packs[0].shape[0] - PAD) // (rep + 1)
    for s, pack in zip(slots, packs):
        scr[where[0] ^ s] = pack[...]
    tails = [scr[c, (rep + 1) * tokens :, :].astype(F32) for c in range(blocks)]
    size = 2 * rep
    tails = [t[0:size] + t[size : 2 * size] + t[2 * size : 3 * size] for t in tails]
    rates = jnp.concatenate([t[0:rep] for t in tails], axis=0)
    decays = jnp.concatenate([t[rep:] for t in tails], axis=0)
    sides = block_sides(decays, rates, tokens)
    cum_rows, cum_cols = sides[2], sides[3]
    keys = [scr[c, 0:tokens, :] for c in range(blocks)]
    jobs = [(c, h) for c in range(blocks) for h in range(rep)]
    values = [scr[c, (h + 1) * tokens : (h + 2) * tokens, :].astype(F32) for c, h in jobs]
    solved, keys = solve_blocks(keys, values, sides, rep)
    entries = []
    for n, (c, h) in enumerate(jobs):
        last = cum_rows[n : n + 1, tokens - 1 : tokens]
        moved = dot_tn(keys[c] * jnp.exp(last - cum_cols[:, n : n + 1]), solved[n])
        entries.append((jnp.exp(last), moved[:, 0:dk], moved[:, dk:]))
        delta_ref[n] = moved[:, 0:dk].astype(BF16)
        feed_ref[n] = moved[:, dk:]
        keep_ref[n : n + 1, :] = jnp.broadcast_to(jnp.exp(last), (1, keep_ref.shape[1]))
    store_send(send_ref, [fold(entries[h::rep], whole) for h in range(rep)], whole)


def fold(maps, whole):
    while len(maps) > 1:
        maps = [join(maps[n + 1], maps[n], whole or n > 0) for n in range(0, len(maps), 2)]
    return maps[0]


def block_maps(delta_ref, feed_ref, keep_ref, rep):
    maps = [
        (keep_ref[n : n + 1, 0:1], delta_ref[n].astype(F32), feed_ref[n])
        for n in range(delta_ref.shape[0])
    ]
    return [maps[h::rep] for h in range(rep)]


def terms_body(dk, dv, rep, group, where, q_in, k_in, v_in, rate_in, decay_in, *refs):
    slots = flips(group, where[1])
    x_ref, y_ref, q_ref, k_ref, v_ref, rate_ref, decay_ref, sems = refs
    tokens = k_in.shape[0]
    rank = where[0]
    pairs = [(rate_in, rate_ref), (decay_in, decay_ref), (k_in, k_ref), (v_in, v_ref), (q_in, q_ref)]
    copies = [pltpu.make_async_copy(*p, sems.at[n]) for n, p in enumerate(pairs)]
    for copy in copies:
        copy.start()
    copies[0].wait()
    copies[1].wait()
    sides = block_sides(
        slot_rows(decay_ref, rank, slots, rep), slot_rows(rate_ref, rank, slots, rep), tokens
    )
    i, j, cum_rows, cum_cols, _ = sides
    copies[2].wait()
    keys = [key_block(k_ref, rank ^ s, dk) for s in slots]
    copies[3].wait()
    values = []
    for n in range(len(slots) * rep):
        at = pl.multiple_of(((rank ^ slots[n // rep]) * rep + n % rep) * dv, dv)
        values.append(v_ref[:, pl.ds(at, dv)].astype(F32))
    solved, keys = solve_blocks(keys, values, sides, rep)
    copies[4].wait()
    queries = [
        unit_rows(key_block(q_ref, rank ^ s, dk).astype(F32)) * dk**-0.5 for s in slots
    ]
    dots = [dot_nt(query, key) for query, key in zip(queries, keys)]
    for n in range(len(slots) * rep):
        cum_col = cum_cols[:, n : n + 1]
        gap = jnp.where(i >= j, cum_col - cum_rows[n : n + 1, :], 0.0)
        scores = jnp.where(i >= j, dots[n // rep] * jnp.exp(gap), 0.0)
        inner = dot(scores, solved[n])
        x_ref[n] = (queries[n // rep] * jnp.exp(cum_col) - inner[:, 0:dk]).astype(BF16)
        y_ref[n] = inner[:, dk:]


def store_maps(ref, entries):
    dk = entries[0][1].shape[0]
    for h, (_, delta, feed) in enumerate(entries):
        rows = slice(h * dk, (h + 1) * dk)
        ref[rows, 0:dk] = delta.astype(BF16)
        ref[rows, dk:] = feed.astype(BF16)
    width = ref.shape[1]
    rows = [jnp.broadcast_to(t.astype(F32), (1, width)) for e in entries for t in parts(e[0])]
    rows.append(jnp.zeros((PAD - len(rows), width), F32))
    ref[len(entries) * dk :, :] = jnp.concatenate(rows, axis=0).astype(BF16)


def load_maps(ref, dk, rep):
    tail = ref[rep * dk :, 0:dk].astype(F32)
    out = []
    for h in range(rep):
        keep = (tail[3 * h : 3 * h + 1] + tail[3 * h + 1 : 3 * h + 2]) + tail[3 * h + 2 : 3 * h + 3]
        rows = slice(h * dk, (h + 1) * dk)
        out.append((keep[:, 0:1], ref[rows, 0:dk].astype(F32), ref[rows, dk:].astype(F32)))
    return out


def pick(flag, yes, no):
    return [tuple(jnp.where(flag == 1, a, b) for a, b in zip(y, n)) for y, n in zip(yes, no)]


def store_send(ref, entries, whole):
    if whole:
        store_maps(ref, entries)
        return
    for h, (_, _, feed) in enumerate(entries):
        ref[h * feed.shape[0] : (h + 1) * feed.shape[0], :] = feed.astype(BF16)


def block_body(dk, rep, step, whole, where, own_ref, came_ref, out_ref):
    own, came = load_maps(own_ref, dk, rep), load_maps(came_ref, dk, rep)
    flag = (where[2] >> step) & 1
    late, early = pick(flag, own, came), pick(flag, came, own)
    store_send(out_ref, [join(l, e, whole) for l, e in zip(late, early)], whole)


def block_entry(dk, rep, group, *came):
    none = jnp.zeros((dk, dk), F32)
    entry = [(jnp.ones((1, 1), F32), none, none) for _ in range(rep)]
    for step, ref in enumerate(came):
        block = load_maps(ref, dk, rep)
        if step > 0:
            block = [join(l, e) for l, e in zip(entry, block)]
        entry = pick((group >> step) & 1, block, entry)
    return entry


def prefix_body(dk, rep, where, delta_ref, feed_ref, keep_ref, *refs):
    *came, a_ref, b_ref = refs
    maps = block_maps(delta_ref, feed_ref, keep_ref, rep)
    unit = (iota2((dk, dk), 0) == iota2((dk, dk), 1)).astype(F32)
    none = jnp.zeros((dk, dk), F32)
    entry = block_entry(dk, rep, where[2], *came)
    states = [jnp.concatenate([k * unit - d, f], axis=1) for k, d, f in entry]
    for c in range(a_ref.shape[0]):
        for h in range(rep):
            a_ref[c, h] = states[h][:, 0:dk].astype(BF16)
            b_ref[c, h] = states[h][:, dk:]
            keep, delta, feed = maps[h][c]
            if c + 1 < a_ref.shape[0]:
                feed = jnp.concatenate([none, feed], axis=1)
                states[h] = advance(keep, delta, feed, states[h])


def enter_body(dk, rep, group, steps, where, a_ref, b_ref, feed_ref, *outs):
    slots = flips(group, where[1])
    late = (where[2] >> (steps - 1)) & 1 if steps else 0
    feed = jnp.where(late == 1, feed_ref[...].astype(F32), 0.0).astype(BF16)
    for s, out in zip(slots, outs):
        for h in range(rep):
            rows = slice(h * dk, (h + 1) * dk)
            at = where[0] ^ s
            out[rows, :] = (dot(a_ref[at, h], feed[rows]) + b_ref[at, h]).astype(BF16)


def project_body(dk, dv, rep, group, at, where, x_ref, y_ref, gate_ref, gain_ref, w_ref, state, *refs):
    slots = flips(group, where[1])
    *before, out_ref, normed_ref = refs
    own = (where[0] ^ slots[at]) * rep
    outs = []
    for h in range(rep):
        n = at * rep + h
        outs.append(dot(x_ref[n], state[h * dk : (h + 1) * dk, :]) + y_ref[n])
    scaled, scales = [], []
    for h, o in enumerate(outs):
        gate = gate_ref[:, pl.ds(pl.multiple_of((own + h) * dv, dv), dv)].astype(F32)
        scales.append(lax.rsqrt(jnp.mean(o * o, axis=-1, keepdims=True) + EPS))
        scaled.append(o * (gain_ref[...] * (gate / (1.0 + jnp.exp(-gate)))))
        normed_ref[:, h * dv : (h + 1) * dv] = (scaled[h] * scales[h]).astype(BF16)
    columns = out_ref.shape[1]
    start = (1 - where[1]) * columns
    step = 256
    for n in range(columns // step):
        at = pl.multiple_of(start + n * step, step)
        cut = slice(n * step, (n + 1) * step)
        total = before[0][:, cut] if before else 0.0
        for h, (piece, scale) in enumerate(zip(scaled, scales)):
            rows = pl.ds(pl.multiple_of((own + h) * dv, dv), dv)
            total = total + scale * dot(piece, w_ref[rows, pl.ds(at, step)])
        out_ref[:, cut] = total.astype(out_ref.dtype)


def own_body(group, where, w_ref, *refs):
    slots = flips(group, where[1])
    *pieces, out_ref = refs
    columns = out_ref.shape[1]
    start = where[1] * columns
    width = pieces[0].shape[1]
    step = 256
    for n in range(columns // step):
        at = pl.multiple_of(start + n * step, step)
        total = 0.0
        for s, piece in zip(slots, pieces):
            rows = pl.ds(pl.multiple_of((where[0] ^ s) * width, width), width)
            total = total + dot(piece[...], w_ref[rows, pl.ds(at, step)])
        out_ref[:, n * step : (n + 1) * step] = total


def per_device(queries, key_rows, values, out_gate, write_rate, log_decay, norm_gain, out_weight):
    tokens = queries.shape[0]
    heads = write_rate.shape[0]
    dv = norm_gain.shape[0]
    dk = dv
    group = queries.shape[1] // dk
    rep = heads // group
    ranks = lax.axis_size("seq")
    halves = lax.axis_size("head")
    groups = ranks // group
    assert ranks % group == 0 and halves == 2
    assert group & (group - 1) == 0 and groups & (groups - 1) == 0
    steps = groups.bit_length() - 1
    columns = out_weight.shape[1] // halves
    shape = jax.ShapeDtypeStruct
    vmem, hbm = pltpu.VMEM, pltpu.HBM
    cube = 2 * tokens * tokens * (dk + dv)
    map_shape = shape((rep * dk + PAD, dk + dv), BF16)
    feed_shape = shape((rep * dk, dv), BF16)

    def swap(x, flip):
        return lax.ppermute(x, "seq", [(i, i ^ flip) for i in range(ranks)])

    def swap_slots(made):
        came = [made[0]]
        for x, *flip in list(zip(made, *tours(group)))[1:]:
            pairs = [(i * halves + c, (i ^ flip[c]) * halves + c) for i in range(ranks) for c in (0, 1)]
            came.append(lax.ppermute(x, ("seq", "head"), pairs))
        return came

    q_in, k_in, v_in, rate_in, decay_in = [
        pltpu.with_memory_space_constraint(x, hbm)
        for x in (queries, key_rows, values, write_rate, log_decay)
    ]
    small = [pltpu.VMEM(write_rate.shape, F32), pltpu.VMEM(log_decay.shape, F32)]
    pack_shape = shape(((rep + 1) * tokens + PAD, dk), BF16)
    packs = call(
        placed(functools.partial(pack_body, dk, dv, rep, group), group),
        [pack_shape] * group,
        [hbm] * 4,
        small + [pltpu.SemaphoreType.DMA((2 + (rep + 1) * group,))],
    )(k_in, v_in, rate_in, decay_in)
    packs = swap_slots(packs)
    x, y = call(
        placed(functools.partial(terms_body, dk, dv, rep, group), group),
        [shape((heads, tokens, dk), BF16), shape((heads, tokens, dv), F32)],
        [hbm] * 5,
        [pltpu.VMEM(z.shape, BF16) for z in (queries, key_rows, values)]
        + small
        + [pltpu.SemaphoreType.DMA((5,))],
        heads * 16 * cube,
    )(q_in, k_in, v_in, rate_in, decay_in)
    jobs = group * rep
    send, *blocks = call(
        placed(functools.partial(owner_body, dk, dv, rep, group, steps > 1), group),
        [
            map_shape if steps > 1 else feed_shape,
            shape((jobs, dk, dk), BF16),
            shape((jobs, dk, dv), F32),
            shape((jobs, dk), F32),
        ],
        [vmem] * group + [pl.ANY],
        [pltpu.VMEM((group,) + pack_shape.shape, BF16)],
        jobs * 16 * cube,
    )(*packs, y)

    came, feed = [], send
    for step in range(steps):
        got = swap(send, group << step)
        if step == steps - 1:
            feed = got
            continue
        whole = step + 2 < steps
        send = call(
            placed(functools.partial(block_body, dk, rep, step, whole), group),
            map_shape if whole else feed_shape,
            [vmem] * 2,
        )(send, got)
        came.append(got)
    a, b = call(
        placed(functools.partial(prefix_body, dk, rep), group),
        [shape((group, rep, dk, dk), BF16), shape((group, rep, dk, dv), F32)],
        [vmem] * (3 + len(came)),
        (),
        jobs * 4 * cube,
    )(*blocks, *came)
    states = call(
        placed(functools.partial(enter_body, dk, rep, group, steps), group),
        [feed_shape] * group,
        [vmem] * 3,
        (),
        cube * jobs,
    )(a, b, feed)
    states = swap_slots(states)

    work = 2 * tokens * columns * heads * dv
    away, normed = [], []
    for n, state in enumerate(states):
        kind = F32 if n < group - 1 else BF16
        total, piece = call(
            placed(functools.partial(project_body, dk, dv, rep, group, n), group),
            [shape((tokens, columns), kind), shape((tokens, rep * dv), BF16)],
            [vmem] * (6 + len(away)),
            (),
            work // group,
        )(x, y, out_gate, norm_gain.reshape(1, dv), out_weight, state, *away)
        away = [total]
        normed.append(piece)
    came = lax.ppermute(away[0], "head", [(0, 1), (1, 0)])
    own = call(placed(functools.partial(own_body, group), group), shape((tokens, columns), F32), [vmem] * (1 + group), (), work)(
        out_weight, *normed
    )
    return (own + came.astype(F32)).astype(BF16)


def solution(mesh):
    return jax.shard_map(
        per_device,
        mesh=mesh,
        in_specs=(
            P("seq", "head"),
            P("seq", "head"),
            P("seq", "head"),
            P("seq", "head"),
            P("head", "seq"),
            P("head", "seq"),
            P(),
            P("head", None),
        ),
        out_specs=P("seq", "head"),
        check_vma=False,
    )
```

```python
import functools

import jax
import jax.numpy as jnp
from jax import lax
from jax.experimental import pallas as pl
from jax.experimental.pallas import tpu as pltpu
from jax.sharding import PartitionSpec as P

F32 = jnp.float32
BF16 = jnp.bfloat16
EPS = 1e-06
LEAF = 32
PAD = 16
SMALL = pltpu.CompilerParams(vmem_limit_bytes=24 * 1024 * 1024)


def dot(a, b):
    return jnp.dot(a.astype(BF16), b.astype(BF16), preferred_element_type=F32)


def dot_nt(a, b):
    return lax.dot_general(
        a.astype(BF16), b.astype(BF16), (((1,), (1,)), ((), ())), preferred_element_type=F32
    )


def dot_tn(a, b):
    return lax.dot_general(
        a.astype(BF16), b.astype(BF16), (((0,), (0,)), ((), ())), preferred_element_type=F32
    )


def exact_dot(a, b, dims):
    return lax.dot_general(
        a, b, (dims, ((), ())), precision=lax.Precision.HIGHEST, preferred_element_type=F32
    )


def parts(x):
    first = x.astype(BF16)
    rest = x - first.astype(F32)
    second = rest.astype(BF16)
    third = (rest - second.astype(F32)).astype(BF16)
    return [first, second, third]


def iota2(shape, dim):
    return lax.broadcasted_iota(jnp.int32, shape, dim)


def call(body, outs, specs, scratch=(), flops=0):
    return pl.pallas_call(
        body,
        out_shape=outs,
        in_specs=[pl.BlockSpec(memory_space=space) for space in specs],
        out_specs=jax.tree.map(lambda _: pl.BlockSpec(memory_space=pltpu.VMEM), outs),
        scratch_shapes=list(scratch),
        compiler_params=SMALL,
        cost_estimate=pl.CostEstimate(flops=flops, bytes_accessed=1 << 20, transcendentals=0),
    )


def unit_rows(x):
    return x * lax.rsqrt(jnp.sum(x * x, axis=-1, keepdims=True) + EPS)


def advance(keep, delta, feed, state):
    return keep * state - dot(delta, state) + feed


def join(late, early, whole=True):
    keep, delta, feed = late
    keep_e, delta_e, feed_e = early
    if not whole:
        return None, None, advance(keep, delta, feed, feed_e)
    dk = delta.shape[1]
    both = dot(delta, jnp.concatenate([delta_e, feed_e], axis=1))
    delta_new = keep * delta_e + keep_e * delta - both[:, 0:dk]
    return keep * keep_e, delta_new, keep * feed_e + feed - both[:, dk:]


def key_block(ref, col, dk):
    return unit_rows(ref[:, pl.ds(pl.multiple_of(col * dk, dk), dk)].astype(F32))


def slot_rows(ref, rank, slots, rep):
    return jnp.concatenate(
        [ref[pl.ds((rank ^ s) * rep + h, 1), :] for s in slots for h in range(rep)], axis=0
    )


def solve(lows, sides, i, j):
    tokens = i.shape[0]
    leaf = (i // LEAF) == (j // LEAF)
    unit = (i == j).astype(F32)
    power = [jnp.where(leaf, low, 0.0) for low in lows]
    inverse = [unit - p for p in power]
    power = [p.astype(BF16) for p in power]
    power = [dot(p, p).astype(BF16) for p in power]
    inverse = neumann(power, inverse, LEAF // 2, 1.0)
    both = [
        dot(t - unit, jnp.concatenate([jnp.where(leaf, 0.0, low), side], axis=1))
        for t, low, side in zip(inverse, lows, sides)
    ]
    power = [
        (jnp.where(leaf, 0.0, low) + b[:, 0:tokens]).astype(BF16) for low, b in zip(lows, both)
    ]
    sides = [side + b[:, tokens:] for side, b in zip(sides, both)]
    return neumann(power, sides, tokens // LEAF, -1.0)


def neumann(power, sides, order, sign):
    width = power[0].shape[1]
    reach = 1
    while 2 * reach < order:
        both = [
            dot(p, jnp.concatenate([p, s.astype(BF16)], axis=1)) for p, s in zip(power, sides)
        ]
        power = [b[:, 0:width].astype(BF16) for b in both]
        sides = [s + sign * b[:, width:] for s, b in zip(sides, both)]
        sign, reach = 1.0, 2 * reach
    return [s + sign * dot(p, s) for p, s in zip(power, sides)]


def tours(group):
    near = [s for s in range(1, group) if s.bit_count() == 1]
    far = sorted((s for s in range(1, group) if s.bit_count() > 1), key=lambda s: -s.bit_count())
    return [0] + far + near, [0] + far + near[::-1]


def flips(group, core):
    even, odd = tours(group)
    return [a if a == b else a + (b - a) * core for a, b in zip(even, odd)]


def placed(body, group):
    def run(*refs):
        index = lax.axis_index("seq")
        spot = (index & (group - 1), lax.axis_index("head"), index >> (group.bit_length() - 1))
        body(spot, *refs)

    return run


def pack_body(dk, dv, rep, group, where, k_in, v_in, rate_in, decay_in, *refs):
    slots = flips(group, where[1])
    *outs, rate_ref, decay_ref, sems = refs
    tokens = k_in.shape[0]
    rank = where[0]
    pairs = [(rate_in, rate_ref), (decay_in, decay_ref)]
    for s, out in zip(slots, outs):
        at = pl.multiple_of((rank ^ s) * dk, dk)
        pairs.append((k_in.at[:, pl.ds(at, dk)], out.at[0:tokens, :]))
        for h in range(rep):
            at = pl.multiple_of(((rank ^ s) * rep + h) * dv, dv)
            rows = out.at[(h + 1) * tokens : (h + 2) * tokens, :]
            pairs.append((v_in.at[:, pl.ds(at, dv)], rows))
    copies = [pltpu.make_async_copy(*p, sems.at[n]) for n, p in enumerate(pairs)]
    for copy in copies:
        copy.start()
    copies[0].wait()
    copies[1].wait()
    for s, out in zip(slots, outs):
        rows = [slot_rows(ref, rank, [s], rep) for ref in (rate_ref, decay_ref)]
        terms = [t.astype(F32) for t in parts(jnp.concatenate(rows, axis=0))]
        terms.append(jnp.zeros((PAD - 6 * rep, tokens), F32))
        out[(rep + 1) * tokens :, :] = jnp.concatenate(terms, axis=0).astype(BF16)
    for copy in copies[2:]:
        copy.wait()


def block_sides(decays, rates, tokens):
    i = iota2((tokens, tokens), 0)
    j = iota2((tokens, tokens), 1)
    lower = (i >= j).astype(F32)
    unit = (i == j).astype(F32)
    cum_rows = exact_dot(decays, lower, ((1,), (1,)))
    cum_cols = exact_dot(lower, decays, ((1,), (1,)))
    rate_cols = exact_dot(unit, rates, ((1,), (1,)))
    return i, j, cum_rows, cum_cols, rate_cols


def solve_blocks(keys, values, sides, rep):
    i, j, cum_rows, cum_cols, rate_cols = sides
    dots = [dot_nt(key, key) for key in keys]
    lows, rhs = [], []
    for n, value in enumerate(values):
        rate = rate_cols[:, n : n + 1]
        cum_col = cum_cols[:, n : n + 1]
        gap = cum_col - cum_rows[n : n + 1, :]
        lows.append(jnp.where(i > j, (rate * dots[n // rep]) * jnp.exp(gap), 0.0))
        rhs.append(
            jnp.concatenate([(rate * jnp.exp(cum_col)) * keys[n // rep], rate * value], axis=1)
        )
    return solve(lows, rhs, i, j)


def owner_body(dk, dv, rep, group, whole, where, *refs):
    slots = flips(group, where[1])
    *packs, _, send_ref, delta_ref, feed_ref, keep_ref, scr = refs
    blocks = len(packs)
    tokens = (packs[0].shape[0] - PAD) // (rep + 1)
    for s, pack in zip(slots, packs):
        scr[where[0] ^ s] = pack[...]
    tails = [scr[c, (rep + 1) * tokens :, :].astype(F32) for c in range(blocks)]
    size = 2 * rep
    tails = [t[0:size] + t[size : 2 * size] + t[2 * size : 3 * size] for t in tails]
    rates = jnp.concatenate([t[0:rep] for t in tails], axis=0)
    decays = jnp.concatenate([t[rep:] for t in tails], axis=0)
    sides = block_sides(decays, rates, tokens)
    cum_rows, cum_cols = sides[2], sides[3]
    keys = [unit_rows(scr[c, 0:tokens, :].astype(F32)) for c in range(blocks)]
    jobs = [(c, h) for c in range(blocks) for h in range(rep)]
    values = [scr[c, (h + 1) * tokens : (h + 2) * tokens, :].astype(F32) for c, h in jobs]
    solved = solve_blocks(keys, values, sides, rep)
    entries = []
    for n, (c, h) in enumerate(jobs):
        last = cum_rows[n : n + 1, tokens - 1 : tokens]
        moved = dot_tn(keys[c] * jnp.exp(last - cum_cols[:, n : n + 1]), solved[n])
        entries.append((jnp.exp(last), moved[:, 0:dk], moved[:, dk:]))
        delta_ref[n] = moved[:, 0:dk].astype(BF16)
        feed_ref[n] = moved[:, dk:]
        keep_ref[n : n + 1, :] = jnp.broadcast_to(jnp.exp(last), (1, keep_ref.shape[1]))
    store_send(send_ref, [fold(entries[h::rep], whole) for h in range(rep)], whole)


def fold(maps, whole):
    while len(maps) > 1:
        maps = [join(maps[n + 1], maps[n], whole or n > 0) for n in range(0, len(maps), 2)]
    return maps[0]


def block_maps(delta_ref, feed_ref, keep_ref, rep):
    maps = [
        (keep_ref[n : n + 1, 0:1], delta_ref[n].astype(F32), feed_ref[n])
        for n in range(delta_ref.shape[0])
    ]
    return [maps[h::rep] for h in range(rep)]


def terms_body(dk, dv, rep, group, where, q_in, k_in, v_in, rate_in, decay_in, *refs):
    slots = flips(group, where[1])
    x_ref, y_ref, q_ref, k_ref, v_ref, rate_ref, decay_ref, sems = refs
    tokens = k_in.shape[0]
    rank = where[0]
    pairs = [(rate_in, rate_ref), (decay_in, decay_ref), (k_in, k_ref), (v_in, v_ref), (q_in, q_ref)]
    copies = [pltpu.make_async_copy(*p, sems.at[n]) for n, p in enumerate(pairs)]
    for copy in copies:
        copy.start()
    copies[0].wait()
    copies[1].wait()
    sides = block_sides(
        slot_rows(decay_ref, rank, slots, rep), slot_rows(rate_ref, rank, slots, rep), tokens
    )
    i, j, cum_rows, cum_cols, _ = sides
    copies[2].wait()
    keys = [key_block(k_ref, rank ^ s, dk) for s in slots]
    copies[3].wait()
    values = []
    for n in range(len(slots) * rep):
        at = pl.multiple_of(((rank ^ slots[n // rep]) * rep + n % rep) * dv, dv)
        values.append(v_ref[:, pl.ds(at, dv)].astype(F32))
    solved = solve_blocks(keys, values, sides, rep)
    copies[4].wait()
    queries = [key_block(q_ref, rank ^ s, dk) * dk**-0.5 for s in slots]
    dots = [dot_nt(query, key) for query, key in zip(queries, keys)]
    for n in range(len(slots) * rep):
        cum_col = cum_cols[:, n : n + 1]
        gap = cum_col - cum_rows[n : n + 1, :]
        scores = jnp.where(i >= j, dots[n // rep] * jnp.exp(gap), 0.0)
        inner = dot(scores, solved[n])
        x_ref[n] = (queries[n // rep] * jnp.exp(cum_col) - inner[:, 0:dk]).astype(BF16)
        y_ref[n] = inner[:, dk:]


def store_maps(ref, entries):
    dk = entries[0][1].shape[0]
    for h, (_, delta, feed) in enumerate(entries):
        rows = slice(h * dk, (h + 1) * dk)
        ref[rows, 0:dk] = delta.astype(BF16)
        ref[rows, dk:] = feed.astype(BF16)
    width = ref.shape[1]
    rows = [jnp.broadcast_to(t.astype(F32), (1, width)) for e in entries for t in parts(e[0])]
    rows.append(jnp.zeros((PAD - len(rows), width), F32))
    ref[len(entries) * dk :, :] = jnp.concatenate(rows, axis=0).astype(BF16)


def load_maps(ref, dk, rep):
    tail = ref[rep * dk :, 0:dk].astype(F32)
    out = []
    for h in range(rep):
        keep = (tail[3 * h : 3 * h + 1] + tail[3 * h + 1 : 3 * h + 2]) + tail[3 * h + 2 : 3 * h + 3]
        rows = slice(h * dk, (h + 1) * dk)
        out.append((keep[:, 0:1], ref[rows, 0:dk].astype(F32), ref[rows, dk:].astype(F32)))
    return out


def pick(flag, yes, no):
    return [tuple(jnp.where(flag == 1, a, b) for a, b in zip(y, n)) for y, n in zip(yes, no)]


def store_send(ref, entries, whole):
    if whole:
        store_maps(ref, entries)
        return
    for h, (_, _, feed) in enumerate(entries):
        ref[h * feed.shape[0] : (h + 1) * feed.shape[0], :] = feed.astype(BF16)


def block_body(dk, rep, step, whole, where, own_ref, came_ref, out_ref):
    own, came = load_maps(own_ref, dk, rep), load_maps(came_ref, dk, rep)
    flag = (where[2] >> step) & 1
    late, early = pick(flag, own, came), pick(flag, came, own)
    store_send(out_ref, [join(l, e, whole) for l, e in zip(late, early)], whole)


def block_entry(dk, rep, group, *came):
    none = jnp.zeros((dk, dk), F32)
    entry = [(jnp.ones((1, 1), F32), none, none) for _ in range(rep)]
    for step, ref in enumerate(came):
        block = load_maps(ref, dk, rep)
        if step > 0:
            block = [join(l, e) for l, e in zip(entry, block)]
        entry = pick((group >> step) & 1, block, entry)
    return entry


def prefix_body(dk, rep, where, delta_ref, feed_ref, keep_ref, *refs):
    *came, a_ref, b_ref = refs
    maps = block_maps(delta_ref, feed_ref, keep_ref, rep)
    unit = (iota2((dk, dk), 0) == iota2((dk, dk), 1)).astype(F32)
    none = jnp.zeros((dk, dk), F32)
    entry = block_entry(dk, rep, where[2], *came)
    states = [jnp.concatenate([k * unit - d, f], axis=1) for k, d, f in entry]
    for c in range(a_ref.shape[0]):
        for h in range(rep):
            a_ref[c, h] = states[h][:, 0:dk].astype(BF16)
            b_ref[c, h] = states[h][:, dk:]
            keep, delta, feed = maps[h][c]
            if c + 1 < a_ref.shape[0]:
                feed = jnp.concatenate([none, feed], axis=1)
                states[h] = advance(keep, delta, feed, states[h])


def enter_body(dk, rep, group, steps, where, a_ref, b_ref, feed_ref, *outs):
    slots = flips(group, where[1])
    late = (where[2] >> (steps - 1)) & 1 if steps else 0
    feed = jnp.where(late == 1, feed_ref[...].astype(F32), 0.0).astype(BF16)
    for s, out in zip(slots, outs):
        for h in range(rep):
            rows = slice(h * dk, (h + 1) * dk)
            at = where[0] ^ s
            out[rows, :] = (dot(a_ref[at, h], feed[rows]) + b_ref[at, h]).astype(BF16)


def project_body(dk, dv, rep, group, at, where, x_ref, y_ref, gate_ref, gain_ref, w_ref, state, *refs):
    slots = flips(group, where[1])
    *before, out_ref, normed_ref = refs
    own = (where[0] ^ slots[at]) * rep
    outs = []
    for h in range(rep):
        n = at * rep + h
        outs.append(dot(x_ref[n], state[h * dk : (h + 1) * dk, :]) + y_ref[n])
    scaled, scales = [], []
    for h, o in enumerate(outs):
        gate = gate_ref[:, pl.ds(pl.multiple_of((own + h) * dv, dv), dv)].astype(F32)
        scales.append(lax.rsqrt(jnp.mean(o * o, axis=-1, keepdims=True) + EPS))
        scaled.append(o * (gain_ref[...] * (gate / (1.0 + jnp.exp(-gate)))))
        normed_ref[:, h * dv : (h + 1) * dv] = (scaled[h] * scales[h]).astype(BF16)
    columns = out_ref.shape[1]
    start = (1 - where[1]) * columns
    step = 256
    for n in range(columns // step):
        at = pl.multiple_of(start + n * step, step)
        cut = slice(n * step, (n + 1) * step)
        total = before[0][:, cut] if before else 0.0
        for h, (piece, scale) in enumerate(zip(scaled, scales)):
            rows = pl.ds(pl.multiple_of((own + h) * dv, dv), dv)
            total = total + scale * dot(piece, w_ref[rows, pl.ds(at, step)])
        out_ref[:, cut] = total.astype(out_ref.dtype)


def own_body(group, where, w_ref, *refs):
    slots = flips(group, where[1])
    *pieces, out_ref = refs
    columns = out_ref.shape[1]
    start = where[1] * columns
    width = pieces[0].shape[1]
    step = 256
    for n in range(columns // step):
        at = pl.multiple_of(start + n * step, step)
        total = 0.0
        for s, piece in zip(slots, pieces):
            rows = pl.ds(pl.multiple_of((where[0] ^ s) * width, width), width)
            total = total + dot(piece[...], w_ref[rows, pl.ds(at, step)])
        out_ref[:, n * step : (n + 1) * step] = total


def per_device(queries, key_rows, values, out_gate, write_rate, log_decay, norm_gain, out_weight):
    tokens = queries.shape[0]
    heads = write_rate.shape[0]
    dv = norm_gain.shape[0]
    dk = dv
    group = queries.shape[1] // dk
    rep = heads // group
    ranks = lax.axis_size("seq")
    halves = lax.axis_size("head")
    groups = ranks // group
    assert ranks % group == 0 and halves == 2
    assert group & (group - 1) == 0 and groups & (groups - 1) == 0
    steps = groups.bit_length() - 1
    columns = out_weight.shape[1] // halves
    shape = jax.ShapeDtypeStruct
    vmem, hbm = pltpu.VMEM, pltpu.HBM
    cube = 2 * tokens * tokens * (dk + dv)
    map_shape = shape((rep * dk + PAD, dk + dv), BF16)
    feed_shape = shape((rep * dk, dv), BF16)

    def swap(x, flip):
        return lax.ppermute(x, "seq", [(i, i ^ flip) for i in range(ranks)])

    def swap_slots(made):
        came = [made[0]]
        for x, *flip in list(zip(made, *tours(group)))[1:]:
            pairs = [(i * halves + c, (i ^ flip[c]) * halves + c) for i in range(ranks) for c in (0, 1)]
            came.append(lax.ppermute(x, ("seq", "head"), pairs))
        return came

    q_in, k_in, v_in, rate_in, decay_in = [
        pltpu.with_memory_space_constraint(x, hbm)
        for x in (queries, key_rows, values, write_rate, log_decay)
    ]
    small = [pltpu.VMEM(write_rate.shape, F32), pltpu.VMEM(log_decay.shape, F32)]
    pack_shape = shape(((rep + 1) * tokens + PAD, dk), BF16)
    packs = call(
        placed(functools.partial(pack_body, dk, dv, rep, group), group),
        [pack_shape] * group,
        [hbm] * 4,
        small + [pltpu.SemaphoreType.DMA((2 + (rep + 1) * group,))],
    )(k_in, v_in, rate_in, decay_in)
    packs = swap_slots(packs)
    x, y = call(
        placed(functools.partial(terms_body, dk, dv, rep, group), group),
        [shape((heads, tokens, dk), BF16), shape((heads, tokens, dv), F32)],
        [hbm] * 5,
        [pltpu.VMEM(z.shape, BF16) for z in (queries, key_rows, values)]
        + small
        + [pltpu.SemaphoreType.DMA((5,))],
        heads * 16 * cube,
    )(q_in, k_in, v_in, rate_in, decay_in)
    jobs = group * rep
    send, *blocks = call(
        placed(functools.partial(owner_body, dk, dv, rep, group, steps > 1), group),
        [
            map_shape if steps > 1 else feed_shape,
            shape((jobs, dk, dk), BF16),
            shape((jobs, dk, dv), F32),
            shape((jobs, dk), F32),
        ],
        [vmem] * group + [pl.ANY],
        [pltpu.VMEM((group,) + pack_shape.shape, BF16)],
        jobs * 16 * cube,
    )(*packs, y)

    came, feed = [], send
    for step in range(steps):
        got = swap(send, group << step)
        if step == steps - 1:
            feed = got
            continue
        whole = step + 2 < steps
        send = call(
            placed(functools.partial(block_body, dk, rep, step, whole), group),
            map_shape if whole else feed_shape,
            [vmem] * 2,
        )(send, got)
        came.append(got)
    a, b = call(
        placed(functools.partial(prefix_body, dk, rep), group),
        [shape((group, rep, dk, dk), BF16), shape((group, rep, dk, dv), F32)],
        [vmem] * (3 + len(came)),
        (),
        jobs * 4 * cube,
    )(*blocks, *came)
    states = call(
        placed(functools.partial(enter_body, dk, rep, group, steps), group),
        [feed_shape] * group,
        [vmem] * 3,
        (),
        cube * jobs,
    )(a, b, feed)
    states = swap_slots(states)

    work = 2 * tokens * columns * heads * dv
    away, normed = [], []
    for n, state in enumerate(states):
        kind = F32 if n < group - 1 else BF16
        total, piece = call(
            placed(functools.partial(project_body, dk, dv, rep, group, n), group),
            [shape((tokens, columns), kind), shape((tokens, rep * dv), BF16)],
            [vmem] * (6 + len(away)),
            (),
            work // group,
        )(x, y, out_gate, norm_gain.reshape(1, dv), out_weight, state, *away)
        away = [total]
        normed.append(piece)
    came = lax.ppermute(away[0], "head", [(0, 1), (1, 0)])
    own = call(placed(functools.partial(own_body, group), group), shape((tokens, columns), F32), [vmem] * (1 + group), (), work)(
        out_weight, *normed
    )
    return (own + came.astype(F32)).astype(BF16)


def solution(mesh):
    return jax.shard_map(
        per_device,
        mesh=mesh,
        in_specs=(
            P("seq", "head"),
            P("seq", "head"),
            P("seq", "head"),
            P("seq", "head"),
            P("head", "seq"),
            P("head", "seq"),
            P(),
            P("head", None),
        ),
        out_specs=P("seq", "head"),
        check_vma=False,
    )
```

```python
import functools

import jax
import jax.numpy as jnp
from jax import lax
from jax.experimental import pallas as pl
from jax.experimental.pallas import tpu as pltpu
from jax.sharding import PartitionSpec as P

F32 = jnp.float32
BF16 = jnp.bfloat16
EPS = 1e-06
LEAF = 16
PAD = 16
SMALL = pltpu.CompilerParams(vmem_limit_bytes=24 * 1024 * 1024)


def dot(a, b):
    return jnp.dot(a.astype(BF16), b.astype(BF16), preferred_element_type=F32)


def dot_nt(a, b):
    return lax.dot_general(
        a.astype(BF16), b.astype(BF16), (((1,), (1,)), ((), ())), preferred_element_type=F32
    )


def dot_tn(a, b):
    return lax.dot_general(
        a.astype(BF16), b.astype(BF16), (((0,), (0,)), ((), ())), preferred_element_type=F32
    )


def exact_dot(a, b, dims):
    return lax.dot_general(
        a, b, (dims, ((), ())), precision=lax.Precision.HIGHEST, preferred_element_type=F32
    )


def parts(x):
    first = x.astype(BF16)
    rest = x - first.astype(F32)
    second = rest.astype(BF16)
    third = (rest - second.astype(F32)).astype(BF16)
    return [first, second, third]


def iota2(shape, dim):
    return lax.broadcasted_iota(jnp.int32, shape, dim)


def call(body, outs, specs, scratch=(), flops=0):
    return pl.pallas_call(
        body,
        out_shape=outs,
        in_specs=[pl.BlockSpec(memory_space=space) for space in specs],
        out_specs=jax.tree.map(lambda _: pl.BlockSpec(memory_space=pltpu.VMEM), outs),
        scratch_shapes=list(scratch),
        compiler_params=SMALL,
        cost_estimate=pl.CostEstimate(flops=flops, bytes_accessed=1 << 20, transcendentals=0),
    )


def unit_rows(x):
    return x * lax.rsqrt(jnp.sum(x * x, axis=-1, keepdims=True) + EPS)


def advance(keep, delta, feed, state):
    return keep * state - dot(delta, state) + feed


def join(late, early, whole=True):
    keep, delta, feed = late
    keep_e, delta_e, feed_e = early
    if not whole:
        return None, None, advance(keep, delta, feed, feed_e)
    dk = delta.shape[1]
    both = dot(delta, jnp.concatenate([delta_e, feed_e], axis=1))
    delta_new = keep * delta_e + keep_e * delta - both[:, 0:dk]
    return keep * keep_e, delta_new, keep * feed_e + feed - both[:, dk:]


def key_block(ref, col, dk):
    return unit_rows(ref[:, pl.ds(pl.multiple_of(col * dk, dk), dk)].astype(F32))


def slot_rows(ref, rank, slots, rep):
    return jnp.concatenate(
        [ref[pl.ds((rank ^ s) * rep + h, 1), :] for s in slots for h in range(rep)], axis=0
    )


def solve(lows, sides, i, j):
    tokens = i.shape[0]
    leaf = (i // LEAF) == (j // LEAF)
    unit = (i == j).astype(F32)
    power = [jnp.where(leaf, low, 0.0) for low in lows]
    inverse = [unit - p for p in power]
    power = [p.astype(BF16) for p in power]
    power = [dot(p, p).astype(BF16) for p in power]
    inverse = neumann(power, inverse, LEAF // 2, 1.0)
    both = [
        dot(t - unit, jnp.concatenate([jnp.where(leaf, 0.0, low), side], axis=1))
        for t, low, side in zip(inverse, lows, sides)
    ]
    power = [
        (jnp.where(leaf, 0.0, low) + b[:, 0:tokens]).astype(BF16) for low, b in zip(lows, both)
    ]
    sides = [side + b[:, tokens:] for side, b in zip(sides, both)]
    return neumann(power, sides, tokens // LEAF, -1.0)


def neumann(power, sides, order, sign):
    width = power[0].shape[1]
    reach = 1
    while 2 * reach < order:
        both = [
            dot(p, jnp.concatenate([p, s.astype(BF16)], axis=1)) for p, s in zip(power, sides)
        ]
        power = [b[:, 0:width].astype(BF16) for b in both]
        sides = [s + sign * b[:, width:] for s, b in zip(sides, both)]
        sign, reach = 1.0, 2 * reach
    return [s + sign * dot(p, s) for p, s in zip(power, sides)]


def tours(group):
    near = [s for s in range(1, group) if s.bit_count() == 1]
    far = sorted((s for s in range(1, group) if s.bit_count() > 1), key=lambda s: -s.bit_count())
    return [0] + far + near, [0] + far + near[::-1]


def flips(group, core):
    even, odd = tours(group)
    return [a if a == b else a + (b - a) * core for a, b in zip(even, odd)]


def placed(body, group):
    def run(*refs):
        index = lax.axis_index("seq")
        spot = (index & (group - 1), lax.axis_index("head"), index >> (group.bit_length() - 1))
        body(spot, *refs)

    return run


def pack_body(dk, dv, rep, group, where, k_in, v_in, rate_in, decay_in, *refs):
    slots = flips(group, where[1])
    *outs, rate_ref, decay_ref, sems = refs
    tokens = k_in.shape[0]
    rank = where[0]
    pairs = [(rate_in, rate_ref), (decay_in, decay_ref)]
    for s, out in zip(slots, outs):
        at = pl.multiple_of((rank ^ s) * dk, dk)
        pairs.append((k_in.at[:, pl.ds(at, dk)], out.at[0:tokens, :]))
        for h in range(rep):
            at = pl.multiple_of(((rank ^ s) * rep + h) * dv, dv)
            rows = out.at[(h + 1) * tokens : (h + 2) * tokens, :]
            pairs.append((v_in.at[:, pl.ds(at, dv)], rows))
    copies = [pltpu.make_async_copy(*p, sems.at[n]) for n, p in enumerate(pairs)]
    for copy in copies:
        copy.start()
    copies[0].wait()
    copies[1].wait()
    for s, out in zip(slots, outs):
        rows = [slot_rows(ref, rank, [s], rep) for ref in (rate_ref, decay_ref)]
        terms = [t.astype(F32) for t in parts(jnp.concatenate(rows, axis=0))]
        terms.append(jnp.zeros((PAD - 6 * rep, tokens), F32))
        out[(rep + 1) * tokens :, :] = jnp.concatenate(terms, axis=0).astype(BF16)
    for copy in copies[2:]:
        copy.wait()


def block_sides(decays, rates, tokens):
    i = iota2((tokens, tokens), 0)
    j = iota2((tokens, tokens), 1)
    lower = (i >= j).astype(F32)
    unit = (i == j).astype(F32)
    cum_rows = exact_dot(decays, lower, ((1,), (1,)))
    cum_cols = exact_dot(lower, decays, ((1,), (1,)))
    rate_cols = exact_dot(unit, rates, ((1,), (1,)))
    return i, j, cum_rows, cum_cols, rate_cols


def solve_blocks(keys, values, sides, rep):
    i, j, cum_rows, cum_cols, rate_cols = sides
    dots = [dot_nt(key, key) for key in keys]
    lows, rhs = [], []
    for n, value in enumerate(values):
        rate = rate_cols[:, n : n + 1]
        cum_col = cum_cols[:, n : n + 1]
        gap = cum_col - cum_rows[n : n + 1, :]
        lows.append(jnp.where(i > j, (rate * dots[n // rep]) * jnp.exp(gap), 0.0))
        rhs.append(
            jnp.concatenate([(rate * jnp.exp(cum_col)) * keys[n // rep], rate * value], axis=1)
        )
    return solve(lows, rhs, i, j)


def owner_body(dk, dv, rep, group, whole, where, *refs):
    slots = flips(group, where[1])
    *packs, _, send_ref, delta_ref, feed_ref, keep_ref, scr = refs
    blocks = len(packs)
    tokens = (packs[0].shape[0] - PAD) // (rep + 1)
    for s, pack in zip(slots, packs):
        scr[where[0] ^ s] = pack[...]
    tails = [scr[c, (rep + 1) * tokens :, :].astype(F32) for c in range(blocks)]
    size = 2 * rep
    tails = [t[0:size] + t[size : 2 * size] + t[2 * size : 3 * size] for t in tails]
    rates = jnp.concatenate([t[0:rep] for t in tails], axis=0)
    decays = jnp.concatenate([t[rep:] for t in tails], axis=0)
    sides = block_sides(decays, rates, tokens)
    cum_rows, cum_cols = sides[2], sides[3]
    keys = [unit_rows(scr[c, 0:tokens, :].astype(F32)) for c in range(blocks)]
    jobs = [(c, h) for c in range(blocks) for h in range(rep)]
    values = [scr[c, (h + 1) * tokens : (h + 2) * tokens, :].astype(F32) for c, h in jobs]
    solved = solve_blocks(keys, values, sides, rep)
    entries = []
    for n, (c, h) in enumerate(jobs):
        last = cum_rows[n : n + 1, tokens - 1 : tokens]
        moved = dot_tn(keys[c] * jnp.exp(last - cum_cols[:, n : n + 1]), solved[n])
        entries.append((jnp.exp(last), moved[:, 0:dk], moved[:, dk:]))
        delta_ref[n] = moved[:, 0:dk].astype(BF16)
        feed_ref[n] = moved[:, dk:]
        keep_ref[n : n + 1, :] = jnp.broadcast_to(jnp.exp(last), (1, keep_ref.shape[1]))
    store_send(send_ref, [fold(entries[h::rep], whole) for h in range(rep)], whole)


def fold(maps, whole):
    while len(maps) > 1:
        maps = [join(maps[n + 1], maps[n], whole or n > 0) for n in range(0, len(maps), 2)]
    return maps[0]


def block_maps(delta_ref, feed_ref, keep_ref, rep):
    maps = [
        (keep_ref[n : n + 1, 0:1], delta_ref[n].astype(F32), feed_ref[n])
        for n in range(delta_ref.shape[0])
    ]
    return [maps[h::rep] for h in range(rep)]


def terms_body(dk, dv, rep, group, where, q_in, k_in, v_in, rate_in, decay_in, *refs):
    slots = flips(group, where[1])
    x_ref, y_ref, q_ref, k_ref, v_ref, rate_ref, decay_ref, sems = refs
    tokens = k_in.shape[0]
    rank = where[0]
    pairs = [(rate_in, rate_ref), (decay_in, decay_ref), (k_in, k_ref), (v_in, v_ref), (q_in, q_ref)]
    copies = [pltpu.make_async_copy(*p, sems.at[n]) for n, p in enumerate(pairs)]
    for copy in copies:
        copy.start()
    copies[0].wait()
    copies[1].wait()
    sides = block_sides(
        slot_rows(decay_ref, rank, slots, rep), slot_rows(rate_ref, rank, slots, rep), tokens
    )
    i, j, cum_rows, cum_cols, _ = sides
    copies[2].wait()
    keys = [key_block(k_ref, rank ^ s, dk) for s in slots]
    copies[3].wait()
    values = []
    for n in range(len(slots) * rep):
        at = pl.multiple_of(((rank ^ slots[n // rep]) * rep + n % rep) * dv, dv)
        values.append(v_ref[:, pl.ds(at, dv)].astype(F32))
    solved = solve_blocks(keys, values, sides, rep)
    copies[4].wait()
    queries = [key_block(q_ref, rank ^ s, dk) * dk**-0.5 for s in slots]
    dots = [dot_nt(query, key) for query, key in zip(queries, keys)]
    for n in range(len(slots) * rep):
        cum_col = cum_cols[:, n : n + 1]
        gap = cum_col - cum_rows[n : n + 1, :]
        scores = jnp.where(i >= j, dots[n // rep] * jnp.exp(gap), 0.0)
        inner = dot(scores, solved[n])
        x_ref[n] = (queries[n // rep] * jnp.exp(cum_col) - inner[:, 0:dk]).astype(BF16)
        y_ref[n] = inner[:, dk:]


def store_maps(ref, entries):
    dk = entries[0][1].shape[0]
    for h, (_, delta, feed) in enumerate(entries):
        rows = slice(h * dk, (h + 1) * dk)
        ref[rows, 0:dk] = delta.astype(BF16)
        ref[rows, dk:] = feed.astype(BF16)
    width = ref.shape[1]
    rows = [jnp.broadcast_to(t.astype(F32), (1, width)) for e in entries for t in parts(e[0])]
    rows.append(jnp.zeros((PAD - len(rows), width), F32))
    ref[len(entries) * dk :, :] = jnp.concatenate(rows, axis=0).astype(BF16)


def load_maps(ref, dk, rep):
    tail = ref[rep * dk :, 0:dk].astype(F32)
    out = []
    for h in range(rep):
        keep = (tail[3 * h : 3 * h + 1] + tail[3 * h + 1 : 3 * h + 2]) + tail[3 * h + 2 : 3 * h + 3]
        rows = slice(h * dk, (h + 1) * dk)
        out.append((keep[:, 0:1], ref[rows, 0:dk].astype(F32), ref[rows, dk:].astype(F32)))
    return out


def pick(flag, yes, no):
    return [tuple(jnp.where(flag == 1, a, b) for a, b in zip(y, n)) for y, n in zip(yes, no)]


def store_send(ref, entries, whole):
    if whole:
        store_maps(ref, entries)
        return
    for h, (_, _, feed) in enumerate(entries):
        ref[h * feed.shape[0] : (h + 1) * feed.shape[0], :] = feed.astype(BF16)


def block_body(dk, rep, step, whole, where, own_ref, came_ref, out_ref):
    own, came = load_maps(own_ref, dk, rep), load_maps(came_ref, dk, rep)
    flag = (where[2] >> step) & 1
    late, early = pick(flag, own, came), pick(flag, came, own)
    store_send(out_ref, [join(l, e, whole) for l, e in zip(late, early)], whole)


def block_entry(dk, rep, group, *came):
    none = jnp.zeros((dk, dk), F32)
    entry = [(jnp.ones((1, 1), F32), none, none) for _ in range(rep)]
    for step, ref in enumerate(came):
        block = load_maps(ref, dk, rep)
        if step > 0:
            block = [join(l, e) for l, e in zip(entry, block)]
        entry = pick((group >> step) & 1, block, entry)
    return entry


def prefix_body(dk, rep, where, delta_ref, feed_ref, keep_ref, *refs):
    *came, a_ref, b_ref = refs
    maps = block_maps(delta_ref, feed_ref, keep_ref, rep)
    unit = (iota2((dk, dk), 0) == iota2((dk, dk), 1)).astype(F32)
    none = jnp.zeros((dk, dk), F32)
    entry = block_entry(dk, rep, where[2], *came)
    states = [jnp.concatenate([k * unit - d, f], axis=1) for k, d, f in entry]
    for c in range(a_ref.shape[0]):
        for h in range(rep):
            a_ref[c, h] = states[h][:, 0:dk].astype(BF16)
            b_ref[c, h] = states[h][:, dk:]
            keep, delta, feed = maps[h][c]
            if c + 1 < a_ref.shape[0]:
                feed = jnp.concatenate([none, feed], axis=1)
                states[h] = advance(keep, delta, feed, states[h])


def enter_body(dk, rep, group, steps, where, a_ref, b_ref, feed_ref, *outs):
    slots = flips(group, where[1])
    late = (where[2] >> (steps - 1)) & 1 if steps else 0
    feed = jnp.where(late == 1, feed_ref[...].astype(F32), 0.0).astype(BF16)
    for s, out in zip(slots, outs):
        for h in range(rep):
            rows = slice(h * dk, (h + 1) * dk)
            at = where[0] ^ s
            out[rows, :] = (dot(a_ref[at, h], feed[rows]) + b_ref[at, h]).astype(BF16)


def project_body(dk, dv, rep, group, at, where, x_ref, y_ref, gate_ref, gain_ref, w_ref, state, *refs):
    slots = flips(group, where[1])
    *before, out_ref, normed_ref = refs
    own = (where[0] ^ slots[at]) * rep
    outs = []
    for h in range(rep):
        n = at * rep + h
        outs.append(dot(x_ref[n], state[h * dk : (h + 1) * dk, :]) + y_ref[n])
    scaled, scales = [], []
    for h, o in enumerate(outs):
        gate = gate_ref[:, pl.ds(pl.multiple_of((own + h) * dv, dv), dv)].astype(F32)
        scales.append(lax.rsqrt(jnp.mean(o * o, axis=-1, keepdims=True) + EPS))
        scaled.append(o * (gain_ref[...] * (gate / (1.0 + jnp.exp(-gate)))))
        normed_ref[:, h * dv : (h + 1) * dv] = (scaled[h] * scales[h]).astype(BF16)
    columns = out_ref.shape[1]
    start = (1 - where[1]) * columns
    step = 256
    for n in range(columns // step):
        at = pl.multiple_of(start + n * step, step)
        cut = slice(n * step, (n + 1) * step)
        total = before[0][:, cut] if before else 0.0
        for h, (piece, scale) in enumerate(zip(scaled, scales)):
            rows = pl.ds(pl.multiple_of((own + h) * dv, dv), dv)
            total = total + scale * dot(piece, w_ref[rows, pl.ds(at, step)])
        out_ref[:, cut] = total.astype(out_ref.dtype)


def own_body(group, where, w_ref, *refs):
    slots = flips(group, where[1])
    *pieces, out_ref = refs
    columns = out_ref.shape[1]
    start = where[1] * columns
    width = pieces[0].shape[1]
    step = 256
    for n in range(columns // step):
        at = pl.multiple_of(start + n * step, step)
        total = 0.0
        for s, piece in zip(slots, pieces):
            rows = pl.ds(pl.multiple_of((where[0] ^ s) * width, width), width)
            total = total + dot(piece[...], w_ref[rows, pl.ds(at, step)])
        out_ref[:, n * step : (n + 1) * step] = total


def per_device(queries, key_rows, values, out_gate, write_rate, log_decay, norm_gain, out_weight):
    tokens = queries.shape[0]
    heads = write_rate.shape[0]
    dv = norm_gain.shape[0]
    dk = dv
    group = queries.shape[1] // dk
    rep = heads // group
    ranks = lax.axis_size("seq")
    halves = lax.axis_size("head")
    groups = ranks // group
    assert ranks % group == 0 and halves == 2
    assert group & (group - 1) == 0 and groups & (groups - 1) == 0
    steps = groups.bit_length() - 1
    columns = out_weight.shape[1] // halves
    shape = jax.ShapeDtypeStruct
    vmem, hbm = pltpu.VMEM, pltpu.HBM
    cube = 2 * tokens * tokens * (dk + dv)
    map_shape = shape((rep * dk + PAD, dk + dv), BF16)
    feed_shape = shape((rep * dk, dv), BF16)

    def swap(x, flip):
        return lax.ppermute(x, "seq", [(i, i ^ flip) for i in range(ranks)])

    def swap_slots(made, order):
        came = [made[0]] + [None] * (group - 1)
        for n in order:
            x, flip = made[n], [tour[n] for tour in tours(group)]
            pairs = [(i * halves + c, (i ^ flip[c]) * halves + c) for i in range(ranks) for c in (0, 1)]
            came[n] = lax.ppermute(x, ("seq", "head"), pairs)
        return came

    q_in, k_in, v_in, rate_in, decay_in = [
        pltpu.with_memory_space_constraint(x, hbm)
        for x in (queries, key_rows, values, write_rate, log_decay)
    ]
    small = [pltpu.VMEM(write_rate.shape, F32), pltpu.VMEM(log_decay.shape, F32)]
    pack_shape = shape(((rep + 1) * tokens + PAD, dk), BF16)
    packs = call(
        placed(functools.partial(pack_body, dk, dv, rep, group), group),
        [pack_shape] * group,
        [hbm] * 4,
        small + [pltpu.SemaphoreType.DMA((2 + (rep + 1) * group,))],
    )(k_in, v_in, rate_in, decay_in)
    packs = swap_slots(packs, range(1, group))
    x, y = call(
        placed(functools.partial(terms_body, dk, dv, rep, group), group),
        [shape((heads, tokens, dk), BF16), shape((heads, tokens, dv), F32)],
        [hbm] * 5,
        [pltpu.VMEM(z.shape, BF16) for z in (queries, key_rows, values)]
        + small
        + [pltpu.SemaphoreType.DMA((5,))],
        heads * 16 * cube,
    )(q_in, k_in, v_in, rate_in, decay_in)
    jobs = group * rep
    send, *blocks = call(
        placed(functools.partial(owner_body, dk, dv, rep, group, steps > 1), group),
        [
            map_shape if steps > 1 else feed_shape,
            shape((jobs, dk, dk), BF16),
            shape((jobs, dk, dv), F32),
            shape((jobs, dk), F32),
        ],
        [vmem] * group + [pl.ANY],
        [pltpu.VMEM((group,) + pack_shape.shape, BF16)],
        jobs * 16 * cube,
    )(*packs, y)

    came, feed = [], send
    for step in range(steps):
        got = swap(send, group << step)
        if step == steps - 1:
            feed = got
            continue
        whole = step + 2 < steps
        send = call(
            placed(functools.partial(block_body, dk, rep, step, whole), group),
            map_shape if whole else feed_shape,
            [vmem] * 2,
        )(send, got)
        came.append(got)
    a, b = call(
        placed(functools.partial(prefix_body, dk, rep), group),
        [shape((group, rep, dk, dk), BF16), shape((group, rep, dk, dv), F32)],
        [vmem] * (3 + len(came)),
        (),
        jobs * 4 * cube,
    )(*blocks, *came)
    states = call(
        placed(functools.partial(enter_body, dk, rep, group, steps), group),
        [feed_shape] * group,
        [vmem] * 3,
        (),
        cube * jobs,
    )(a, b, feed)
    last = list(range(1, group))[::-1]
    states = swap_slots(states, last)

    work = 2 * tokens * columns * heads * dv
    away, normed = [], [None] * group
    for n in [0] + last:
        state, kind = states[n], F32 if n != last[-1] else BF16
        total, piece = call(
            placed(functools.partial(project_body, dk, dv, rep, group, n), group),
            [shape((tokens, columns), kind), shape((tokens, rep * dv), BF16)],
            [vmem] * (6 + len(away)),
            (),
            work // group,
        )(x, y, out_gate, norm_gain.reshape(1, dv), out_weight, state, *away)
        away = [total]
        normed[n] = piece
    came = lax.ppermute(away[0], "head", [(0, 1), (1, 0)])
    own = call(placed(functools.partial(own_body, group), group), shape((tokens, columns), F32), [vmem] * (1 + group), (), work)(
        out_weight, *normed
    )
    return (own + came.astype(F32)).astype(BF16)


def solution(mesh):
    return jax.shard_map(
        per_device,
        mesh=mesh,
        in_specs=(
            P("seq", "head"),
            P("seq", "head"),
            P("seq", "head"),
            P("seq", "head"),
            P("head", "seq"),
            P("head", "seq"),
            P(),
            P("head", None),
        ),
        out_specs=P("seq", "head"),
        check_vma=False,
    )
```

```python
import functools

import jax
import jax.numpy as jnp
from jax import lax
from jax.experimental import pallas as pl
from jax.experimental.pallas import tpu as pltpu
from jax.sharding import PartitionSpec as P

F32 = jnp.float32
BF16 = jnp.bfloat16
EPS = 1e-06
LEAF = 16
PAD = 16
SMALL = pltpu.CompilerParams(vmem_limit_bytes=24 * 1024 * 1024)


def dot(a, b):
    return jnp.dot(a.astype(BF16), b.astype(BF16), preferred_element_type=F32)


def dot_nt(a, b):
    return lax.dot_general(
        a.astype(BF16), b.astype(BF16), (((1,), (1,)), ((), ())), preferred_element_type=F32
    )


def dot_tn(a, b):
    return lax.dot_general(
        a.astype(BF16), b.astype(BF16), (((0,), (0,)), ((), ())), preferred_element_type=F32
    )


def exact_dot(a, b, dims):
    return lax.dot_general(
        a, b, (dims, ((), ())), precision=lax.Precision.HIGHEST, preferred_element_type=F32
    )


def parts(x):
    first = x.astype(BF16)
    rest = x - first.astype(F32)
    second = rest.astype(BF16)
    third = (rest - second.astype(F32)).astype(BF16)
    return [first, second, third]


def iota2(shape, dim):
    return lax.broadcasted_iota(jnp.int32, shape, dim)


def call(body, outs, specs, scratch=(), flops=0):
    return pl.pallas_call(
        body,
        out_shape=outs,
        in_specs=[pl.BlockSpec(memory_space=space) for space in specs],
        out_specs=jax.tree.map(lambda _: pl.BlockSpec(memory_space=pltpu.VMEM), outs),
        scratch_shapes=list(scratch),
        compiler_params=SMALL,
        cost_estimate=pl.CostEstimate(flops=flops, bytes_accessed=1 << 20, transcendentals=0),
    )


def unit_rows(x):
    return x * lax.rsqrt(jnp.sum(x * x, axis=-1, keepdims=True) + EPS)


def advance(keep, delta, feed, state):
    return keep * state - dot(delta, state) + feed


def join(late, early, whole=True):
    keep, delta, feed = late
    keep_e, delta_e, feed_e = early
    if not whole:
        return None, None, advance(keep, delta, feed, feed_e)
    dk = delta.shape[1]
    both = dot(delta, jnp.concatenate([delta_e, feed_e], axis=1))
    delta_new = keep * delta_e + keep_e * delta - both[:, 0:dk]
    return keep * keep_e, delta_new, keep * feed_e + feed - both[:, dk:]


def key_block(ref, col, dk):
    return unit_rows(ref[:, pl.ds(pl.multiple_of(col * dk, dk), dk)].astype(F32))


def slot_rows(ref, rank, slots, rep):
    return jnp.concatenate(
        [ref[pl.ds((rank ^ s) * rep + h, 1), :] for s in slots for h in range(rep)], axis=0
    )


def solve(lows, sides, i, j):
    tokens = i.shape[0]
    leaf = (i // LEAF) == (j // LEAF)
    unit = (i == j).astype(F32)
    power = [jnp.where(leaf, low, 0.0) for low in lows]
    inverse = [unit - p for p in power]
    power = [p.astype(BF16) for p in power]
    power = [dot(p, p).astype(BF16) for p in power]
    inverse = neumann(power, inverse, LEAF // 2, 1.0)
    both = [
        dot(t - unit, jnp.concatenate([jnp.where(leaf, 0.0, low), side], axis=1))
        for t, low, side in zip(inverse, lows, sides)
    ]
    power = [
        (jnp.where(leaf, 0.0, low) + b[:, 0:tokens]).astype(BF16) for low, b in zip(lows, both)
    ]
    sides = [side + b[:, tokens:] for side, b in zip(sides, both)]
    return neumann(power, sides, tokens // LEAF, -1.0)


def neumann(power, sides, order, sign):
    width = power[0].shape[1]
    reach = 1
    while 2 * reach < order:
        both = [
            dot(p, jnp.concatenate([p, s.astype(BF16)], axis=1)) for p, s in zip(power, sides)
        ]
        power = [b[:, 0:width].astype(BF16) for b in both]
        sides = [s + sign * b[:, width:] for s, b in zip(sides, both)]
        sign, reach = 1.0, 2 * reach
    return [s + sign * dot(p, s) for p, s in zip(power, sides)]


def tours(group):
    near = [s for s in range(1, group) if s.bit_count() == 1]
    far = sorted((s for s in range(1, group) if s.bit_count() > 1), key=lambda s: -s.bit_count())
    return [0] + far + near, [0] + far + near[::-1]


def flips(group, core):
    even, odd = tours(group)
    return [a if a == b else a + (b - a) * core for a, b in zip(even, odd)]


def placed(body, group):
    def run(*refs):
        index = lax.axis_index("seq")
        spot = (index & (group - 1), lax.axis_index("head"), index >> (group.bit_length() - 1))
        body(spot, *refs)

    return run


def pack_body(dk, dv, rep, group, where, k_in, v_in, rate_in, decay_in, *refs):
    slots = flips(group, where[1])
    *outs, rate_ref, decay_ref, sems = refs
    tokens = k_in.shape[0]
    rank = where[0]
    pairs = [(rate_in, rate_ref), (decay_in, decay_ref)]
    for s, out in zip(slots, outs):
        at = pl.multiple_of((rank ^ s) * dk, dk)
        pairs.append((k_in.at[:, pl.ds(at, dk)], out.at[0:tokens, :]))
        for h in range(rep):
            at = pl.multiple_of(((rank ^ s) * rep + h) * dv, dv)
            rows = out.at[(h + 1) * tokens : (h + 2) * tokens, :]
            pairs.append((v_in.at[:, pl.ds(at, dv)], rows))
    copies = [pltpu.make_async_copy(*p, sems.at[n]) for n, p in enumerate(pairs)]
    for copy in copies:
        copy.start()
    copies[0].wait()
    copies[1].wait()
    for s, out in zip(slots, outs):
        rows = [slot_rows(ref, rank, [s], rep) for ref in (rate_ref, decay_ref)]
        terms = [t.astype(F32) for t in parts(jnp.concatenate(rows, axis=0))]
        terms.append(jnp.zeros((PAD - 6 * rep, tokens), F32))
        out[(rep + 1) * tokens :, :] = jnp.concatenate(terms, axis=0).astype(BF16)
    for copy in copies[2:]:
        copy.wait()


def block_sides(decays, rates, tokens):
    i = iota2((tokens, tokens), 0)
    j = iota2((tokens, tokens), 1)
    lower = (i >= j).astype(F32)
    unit = (i == j).astype(F32)
    cum_rows = exact_dot(decays, lower, ((1,), (1,)))
    cum_cols = exact_dot(lower, decays, ((1,), (1,)))
    rate_cols = exact_dot(unit, rates, ((1,), (1,)))
    return i, j, cum_rows, cum_cols, rate_cols


def solve_blocks(keys, values, sides, rep):
    i, j, cum_rows, cum_cols, rate_cols = sides
    dots = [dot_nt(key, key) for key in keys]
    lows, rhs = [], []
    for n, value in enumerate(values):
        rate = rate_cols[:, n : n + 1]
        cum_col = cum_cols[:, n : n + 1]
        gap = cum_col - cum_rows[n : n + 1, :]
        lows.append(jnp.where(i > j, (rate * dots[n // rep]) * jnp.exp(gap), 0.0))
        rhs.append(
            jnp.concatenate([(rate * jnp.exp(cum_col)) * keys[n // rep], rate * value], axis=1)
        )
    return solve(lows, rhs, i, j)


def owner_body(dk, dv, rep, group, whole, where, *refs):
    slots = flips(group, where[1])
    *packs, _, send_ref, delta_ref, feed_ref, keep_ref, scr = refs
    blocks = len(packs)
    tokens = (packs[0].shape[0] - PAD) // (rep + 1)
    for s, pack in zip(slots, packs):
        scr[where[0] ^ s] = pack[...]
    tails = [scr[c, (rep + 1) * tokens :, :].astype(F32) for c in range(blocks)]
    size = 2 * rep
    tails = [t[0:size] + t[size : 2 * size] + t[2 * size : 3 * size] for t in tails]
    rates = jnp.concatenate([t[0:rep] for t in tails], axis=0)
    decays = jnp.concatenate([t[rep:] for t in tails], axis=0)
    sides = block_sides(decays, rates, tokens)
    cum_rows, cum_cols = sides[2], sides[3]
    keys = [unit_rows(scr[c, 0:tokens, :].astype(F32)) for c in range(blocks)]
    jobs = [(c, h) for c in range(blocks) for h in range(rep)]
    values = [scr[c, (h + 1) * tokens : (h + 2) * tokens, :].astype(F32) for c, h in jobs]
    solved = solve_blocks(keys, values, sides, rep)
    entries = []
    for n, (c, h) in enumerate(jobs):
        last = cum_rows[n : n + 1, tokens - 1 : tokens]
        moved = dot_tn(keys[c] * jnp.exp(last - cum_cols[:, n : n + 1]), solved[n])
        entries.append((jnp.exp(last), moved[:, 0:dk], moved[:, dk:]))
        delta_ref[n] = moved[:, 0:dk].astype(BF16)
        feed_ref[n] = moved[:, dk:]
        keep_ref[n : n + 1, :] = jnp.broadcast_to(jnp.exp(last), (1, keep_ref.shape[1]))
    store_send(send_ref, [fold(entries[h::rep], whole) for h in range(rep)], whole)


def fold(maps, whole):
    while len(maps) > 1:
        maps = [join(maps[n + 1], maps[n], whole or n > 0) for n in range(0, len(maps), 2)]
    return maps[0]


def block_maps(delta_ref, feed_ref, keep_ref, rep):
    maps = [
        (keep_ref[n : n + 1, 0:1], delta_ref[n].astype(F32), feed_ref[n])
        for n in range(delta_ref.shape[0])
    ]
    return [maps[h::rep] for h in range(rep)]


def terms_body(dk, dv, rep, group, span, where, q_in, k_in, v_in, rate_in, decay_in, *refs):
    slots = [flips(group, where[1])[n] for n in span]
    x_ref, y_ref, q_ref, k_ref, v_ref, rate_ref, decay_ref, sems = refs[-8:]
    tokens = k_in.shape[0]
    rank = where[0]
    pairs = [(rate_in, rate_ref), (decay_in, decay_ref), (k_in, k_ref), (v_in, v_ref), (q_in, q_ref)]
    copies = [pltpu.make_async_copy(*p, sems.at[n]) for n, p in enumerate(pairs)]
    for copy in copies:
        copy.start()
    copies[0].wait()
    copies[1].wait()
    sides = block_sides(
        slot_rows(decay_ref, rank, slots, rep), slot_rows(rate_ref, rank, slots, rep), tokens
    )
    i, j, cum_rows, cum_cols, _ = sides
    copies[2].wait()
    keys = [key_block(k_ref, rank ^ s, dk) for s in slots]
    copies[3].wait()
    values = []
    for n in range(len(slots) * rep):
        at = pl.multiple_of(((rank ^ slots[n // rep]) * rep + n % rep) * dv, dv)
        values.append(v_ref[:, pl.ds(at, dv)].astype(F32))
    solved = solve_blocks(keys, values, sides, rep)
    copies[4].wait()
    queries = [key_block(q_ref, rank ^ s, dk) * dk**-0.5 for s in slots]
    dots = [dot_nt(query, key) for query, key in zip(queries, keys)]
    for n in range(len(slots) * rep):
        cum_col = cum_cols[:, n : n + 1]
        gap = cum_col - cum_rows[n : n + 1, :]
        scores = jnp.where(i >= j, dots[n // rep] * jnp.exp(gap), 0.0)
        inner = dot(scores, solved[n])
        x_ref[n] = (queries[n // rep] * jnp.exp(cum_col) - inner[:, 0:dk]).astype(BF16)
        y_ref[n] = inner[:, dk:]


def store_maps(ref, entries):
    dk = entries[0][1].shape[0]
    for h, (_, delta, feed) in enumerate(entries):
        rows = slice(h * dk, (h + 1) * dk)
        ref[rows, 0:dk] = delta.astype(BF16)
        ref[rows, dk:] = feed.astype(BF16)
    width = ref.shape[1]
    rows = [jnp.broadcast_to(t.astype(F32), (1, width)) for e in entries for t in parts(e[0])]
    rows.append(jnp.zeros((PAD - len(rows), width), F32))
    ref[len(entries) * dk :, :] = jnp.concatenate(rows, axis=0).astype(BF16)


def load_maps(ref, dk, rep):
    tail = ref[rep * dk :, 0:dk].astype(F32)
    out = []
    for h in range(rep):
        keep = (tail[3 * h : 3 * h + 1] + tail[3 * h + 1 : 3 * h + 2]) + tail[3 * h + 2 : 3 * h + 3]
        rows = slice(h * dk, (h + 1) * dk)
        out.append((keep[:, 0:1], ref[rows, 0:dk].astype(F32), ref[rows, dk:].astype(F32)))
    return out


def pick(flag, yes, no):
    return [tuple(jnp.where(flag == 1, a, b) for a, b in zip(y, n)) for y, n in zip(yes, no)]


def store_send(ref, entries, whole):
    if whole:
        store_maps(ref, entries)
        return
    for h, (_, _, feed) in enumerate(entries):
        ref[h * feed.shape[0] : (h + 1) * feed.shape[0], :] = feed.astype(BF16)


def block_body(dk, rep, step, whole, where, own_ref, came_ref, *rest):
    out_ref = rest[-1]
    own, came = load_maps(own_ref, dk, rep), load_maps(came_ref, dk, rep)
    flag = (where[2] >> step) & 1
    late, early = pick(flag, own, came), pick(flag, came, own)
    store_send(out_ref, [join(l, e, whole) for l, e in zip(late, early)], whole)


def block_entry(dk, rep, group, *came):
    none = jnp.zeros((dk, dk), F32)
    entry = [(jnp.ones((1, 1), F32), none, none) for _ in range(rep)]
    for step, ref in enumerate(came):
        block = load_maps(ref, dk, rep)
        if step > 0:
            block = [join(l, e) for l, e in zip(entry, block)]
        entry = pick((group >> step) & 1, block, entry)
    return entry


def prefix_body(dk, rep, where, delta_ref, feed_ref, keep_ref, *refs):
    *came, a_ref, b_ref = refs
    maps = block_maps(delta_ref, feed_ref, keep_ref, rep)
    unit = (iota2((dk, dk), 0) == iota2((dk, dk), 1)).astype(F32)
    none = jnp.zeros((dk, dk), F32)
    entry = block_entry(dk, rep, where[2], *came)
    states = [jnp.concatenate([k * unit - d, f], axis=1) for k, d, f in entry]
    for c in range(a_ref.shape[0]):
        for h in range(rep):
            a_ref[c, h] = states[h][:, 0:dk].astype(BF16)
            b_ref[c, h] = states[h][:, dk:]
            keep, delta, feed = maps[h][c]
            if c + 1 < a_ref.shape[0]:
                feed = jnp.concatenate([none, feed], axis=1)
                states[h] = advance(keep, delta, feed, states[h])


def enter_body(dk, rep, group, steps, where, a_ref, b_ref, feed_ref, *outs):
    slots = flips(group, where[1])
    late = (where[2] >> (steps - 1)) & 1 if steps else 0
    feed = jnp.where(late == 1, feed_ref[...].astype(F32), 0.0).astype(BF16)
    for s, out in zip(slots, outs):
        for h in range(rep):
            rows = slice(h * dk, (h + 1) * dk)
            at = where[0] ^ s
            out[rows, :] = (dot(a_ref[at, h], feed[rows]) + b_ref[at, h]).astype(BF16)


def project_body(dk, dv, rep, group, at, first, where, x_ref, y_ref, gate_ref, gain_ref, w_ref, state, *refs):
    slots = flips(group, where[1])
    *before, out_ref, normed_ref = refs
    own = (where[0] ^ slots[at]) * rep
    outs = []
    for h in range(rep):
        n = (at - first) * rep + h
        outs.append(dot(x_ref[n], state[h * dk : (h + 1) * dk, :]) + y_ref[n])
    scaled, scales = [], []
    for h, o in enumerate(outs):
        gate = gate_ref[:, pl.ds(pl.multiple_of((own + h) * dv, dv), dv)].astype(F32)
        scales.append(lax.rsqrt(jnp.mean(o * o, axis=-1, keepdims=True) + EPS))
        scaled.append(o * (gain_ref[...] * (gate / (1.0 + jnp.exp(-gate)))))
        normed_ref[:, h * dv : (h + 1) * dv] = (scaled[h] * scales[h]).astype(BF16)
    columns = out_ref.shape[1]
    start = (1 - where[1]) * columns
    step = 256
    for n in range(columns // step):
        at = pl.multiple_of(start + n * step, step)
        cut = slice(n * step, (n + 1) * step)
        total = before[0][:, cut] if before else 0.0
        for h, (piece, scale) in enumerate(zip(scaled, scales)):
            rows = pl.ds(pl.multiple_of((own + h) * dv, dv), dv)
            total = total + scale * dot(piece, w_ref[rows, pl.ds(at, step)])
        out_ref[:, cut] = total.astype(out_ref.dtype)


def own_body(group, where, w_ref, *refs):
    slots = flips(group, where[1])
    *pieces, out_ref = refs
    columns = out_ref.shape[1]
    start = where[1] * columns
    width = pieces[0].shape[1]
    step = 256
    for n in range(columns // step):
        at = pl.multiple_of(start + n * step, step)
        total = 0.0
        for s, piece in zip(slots, pieces):
            rows = pl.ds(pl.multiple_of((where[0] ^ s) * width, width), width)
            total = total + dot(piece[...], w_ref[rows, pl.ds(at, step)])
        out_ref[:, n * step : (n + 1) * step] = total


def per_device(queries, key_rows, values, out_gate, write_rate, log_decay, norm_gain, out_weight):
    tokens = queries.shape[0]
    heads = write_rate.shape[0]
    dv = norm_gain.shape[0]
    dk = dv
    group = queries.shape[1] // dk
    rep = heads // group
    ranks = lax.axis_size("seq")
    halves = lax.axis_size("head")
    groups = ranks // group
    assert ranks % group == 0 and halves == 2
    assert group & (group - 1) == 0 and groups & (groups - 1) == 0
    steps = groups.bit_length() - 1
    columns = out_weight.shape[1] // halves
    shape = jax.ShapeDtypeStruct
    vmem, hbm = pltpu.VMEM, pltpu.HBM
    cube = 2 * tokens * tokens * (dk + dv)
    map_shape = shape((rep * dk + PAD, dk + dv), BF16)
    feed_shape = shape((rep * dk, dv), BF16)

    def swap(x, flip):
        return lax.ppermute(x, "seq", [(i, i ^ flip) for i in range(ranks)])

    def swap_slots(made, order):
        came = [made[0]] + [None] * (group - 1)
        for n in order:
            x, flip = made[n], [tour[n] for tour in tours(group)]
            pairs = [(i * halves + c, (i ^ flip[c]) * halves + c) for i in range(ranks) for c in (0, 1)]
            came[n] = lax.ppermute(x, ("seq", "head"), pairs)
        return came

    q_in, k_in, v_in, rate_in, decay_in = [
        pltpu.with_memory_space_constraint(x, hbm)
        for x in (queries, key_rows, values, write_rate, log_decay)
    ]
    small = [pltpu.VMEM(write_rate.shape, F32), pltpu.VMEM(log_decay.shape, F32)]
    pack_shape = shape(((rep + 1) * tokens + PAD, dk), BF16)
    packs = call(
        placed(functools.partial(pack_body, dk, dv, rep, group), group),
        [pack_shape] * group,
        [hbm] * 4,
        small + [pltpu.SemaphoreType.DMA((2 + (rep + 1) * group,))],
    )(k_in, v_in, rate_in, decay_in)
    packs = swap_slots(packs, range(1, group))
    inputs = q_in, k_in, v_in, rate_in, decay_in

    def terms(span, *after):
        count = len(span) * rep
        return call(
            placed(functools.partial(terms_body, dk, dv, rep, group, span), group),
            [shape((count, tokens, dk), BF16), shape((count, tokens, dv), F32)],
            [hbm] * 5 + [pl.ANY] * len(after),
            [pltpu.VMEM(z.shape, BF16) for z in (queries, key_rows, values)]
            + small
            + [pltpu.SemaphoreType.DMA((5,))],
            count * 16 * cube,
        )(*inputs, *after)

    cut = group // 2
    xy = [terms(list(range(cut)))]
    jobs = group * rep
    send, *blocks = call(
        placed(functools.partial(owner_body, dk, dv, rep, group, steps > 1), group),
        [
            map_shape if steps > 1 else feed_shape,
            shape((jobs, dk, dk), BF16),
            shape((jobs, dk, dv), F32),
            shape((jobs, dk), F32),
        ],
        [vmem] * group + [pl.ANY],
        [pltpu.VMEM((group,) + pack_shape.shape, BF16)],
        jobs * 16 * cube,
    )(*packs, xy[0][1])
    xy.append(terms(list(range(cut, group)), send))

    came, feed = [], send
    for step in range(steps):
        got = swap(send, group << step)
        if step == steps - 1:
            feed = got
            continue
        whole = step + 2 < steps
        send = call(
            placed(functools.partial(block_body, dk, rep, step, whole), group),
            map_shape if whole else feed_shape,
            [vmem] * 2 + [pl.ANY],
        )(send, got, xy[1][1])
        came.append(got)
    a, b = call(
        placed(functools.partial(prefix_body, dk, rep), group),
        [shape((group, rep, dk, dk), BF16), shape((group, rep, dk, dv), F32)],
        [vmem] * (3 + len(came)),
        (),
        jobs * 4 * cube,
    )(*blocks, *came)
    states = call(
        placed(functools.partial(enter_body, dk, rep, group, steps), group),
        [feed_shape] * group,
        [vmem] * 3,
        (),
        cube * jobs,
    )(a, b, feed)
    last = list(range(1, group))[::-1]
    states = swap_slots(states, last)

    work = 2 * tokens * columns * heads * dv
    away, normed = [], [None] * group
    for n in [0] + last:
        state, kind = states[n], F32 if n != last[-1] else BF16
        total, piece = call(
            placed(functools.partial(project_body, dk, dv, rep, group, n, n // cut * cut), group),
            [shape((tokens, columns), kind), shape((tokens, rep * dv), BF16)],
            [vmem] * (6 + len(away)),
            (),
            work // group,
        )(*xy[n // cut], out_gate, norm_gain.reshape(1, dv), out_weight, state, *away)
        away = [total]
        normed[n] = piece
    came = lax.ppermute(away[0], "head", [(0, 1), (1, 0)])
    own = call(placed(functools.partial(own_body, group), group), shape((tokens, columns), F32), [vmem] * (1 + group), (), work)(
        out_weight, *normed
    )
    return (own + came.astype(F32)).astype(BF16)


def solution(mesh):
    return jax.shard_map(
        per_device,
        mesh=mesh,
        in_specs=(
            P("seq", "head"),
            P("seq", "head"),
            P("seq", "head"),
            P("seq", "head"),
            P("head", "seq"),
            P("head", "seq"),
            P(),
            P("head", None),
        ),
        out_specs=P("seq", "head"),
        check_vma=False,
    )
```

```python
import functools

import jax
import jax.numpy as jnp
from jax import lax
from jax.experimental import pallas as pl
from jax.experimental.pallas import tpu as pltpu
from jax.sharding import PartitionSpec as P

F32 = jnp.float32
BF16 = jnp.bfloat16
EPS = 1e-06
LEAF = 16
PAD = 16
SMALL = pltpu.CompilerParams(vmem_limit_bytes=24 * 1024 * 1024)


def dot(a, b):
    return jnp.dot(a.astype(BF16), b.astype(BF16), preferred_element_type=F32)


def dot_nt(a, b):
    return lax.dot_general(
        a.astype(BF16), b.astype(BF16), (((1,), (1,)), ((), ())), preferred_element_type=F32
    )


def dot_tn(a, b):
    return lax.dot_general(
        a.astype(BF16), b.astype(BF16), (((0,), (0,)), ((), ())), preferred_element_type=F32
    )


def exact_dot(a, b, dims):
    return lax.dot_general(
        a, b, (dims, ((), ())), precision=lax.Precision.HIGHEST, preferred_element_type=F32
    )


def parts(x):
    first = x.astype(BF16)
    rest = x - first.astype(F32)
    second = rest.astype(BF16)
    third = (rest - second.astype(F32)).astype(BF16)
    return [first, second, third]


def iota2(shape, dim):
    return lax.broadcasted_iota(jnp.int32, shape, dim)


def call(body, outs, specs, scratch=(), flops=0):
    return pl.pallas_call(
        body,
        out_shape=outs,
        in_specs=[pl.BlockSpec(memory_space=space) for space in specs],
        out_specs=jax.tree.map(lambda _: pl.BlockSpec(memory_space=pltpu.VMEM), outs),
        scratch_shapes=list(scratch),
        compiler_params=SMALL,
        cost_estimate=pl.CostEstimate(flops=flops, bytes_accessed=1 << 20, transcendentals=0),
    )


def unit_rows(x):
    return x * lax.rsqrt(jnp.sum(x * x, axis=-1, keepdims=True) + EPS)


def advance(keep, delta, feed, state):
    return keep * state - dot(delta, state) + feed


def join(late, early, whole=True):
    keep, delta, feed = late
    keep_e, delta_e, feed_e = early
    if not whole:
        return None, None, advance(keep, delta, feed, feed_e)
    dk = delta.shape[1]
    both = dot(delta, jnp.concatenate([delta_e, feed_e], axis=1))
    delta_new = keep * delta_e + keep_e * delta - both[:, 0:dk]
    return keep * keep_e, delta_new, keep * feed_e + feed - both[:, dk:]


def key_block(ref, col, dk):
    return unit_rows(ref[:, pl.ds(pl.multiple_of(col * dk, dk), dk)].astype(F32))


def slot_rows(ref, rank, slots, rep):
    return jnp.concatenate(
        [ref[pl.ds((rank ^ s) * rep + h, 1), :] for s in slots for h in range(rep)], axis=0
    )


def solve(lows, sides, i, j):
    tokens = i.shape[0]
    leaf = (i // LEAF) == (j // LEAF)
    unit = (i == j).astype(F32)
    power = [jnp.where(leaf, low, 0.0) for low in lows]
    inverse = [unit - p for p in power]
    power = [p.astype(BF16) for p in power]
    power = [dot(p, p).astype(BF16) for p in power]
    inverse = neumann(power, inverse, LEAF // 2, 1.0)
    both = [
        dot(t - unit, jnp.concatenate([jnp.where(leaf, 0.0, low), side], axis=1))
        for t, low, side in zip(inverse, lows, sides)
    ]
    power = [
        (jnp.where(leaf, 0.0, low) + b[:, 0:tokens]).astype(BF16) for low, b in zip(lows, both)
    ]
    sides = [side + b[:, tokens:] for side, b in zip(sides, both)]
    return neumann(power, sides, tokens // LEAF, -1.0)


def neumann(power, sides, order, sign):
    width = power[0].shape[1]
    reach = 1
    while 2 * reach < order:
        both = [
            dot(p, jnp.concatenate([p, s.astype(BF16)], axis=1)) for p, s in zip(power, sides)
        ]
        power = [b[:, 0:width].astype(BF16) for b in both]
        sides = [s + sign * b[:, width:] for s, b in zip(sides, both)]
        sign, reach = 1.0, 2 * reach
    return [s + sign * dot(p, s) for p, s in zip(power, sides)]


def tours(group):
    near = [s for s in range(1, group) if s.bit_count() == 1]
    far = sorted((s for s in range(1, group) if s.bit_count() > 1), key=lambda s: -s.bit_count())
    return [0] + near + far, [0] + near[::-1] + far


def flips(group, core):
    even, odd = tours(group)
    return [a if a == b else a + (b - a) * core for a, b in zip(even, odd)]


def placed(body, group):
    def run(*refs):
        index = lax.axis_index("seq")
        spot = (index & (group - 1), lax.axis_index("head"), index >> (group.bit_length() - 1))
        body(spot, *refs)

    return run


def pack_body(dk, dv, rep, group, where, k_in, v_in, rate_in, decay_in, *refs):
    slots = flips(group, where[1])
    *outs, rate_ref, decay_ref, sems = refs
    tokens = k_in.shape[0]
    rank = where[0]
    pairs = [(rate_in, rate_ref), (decay_in, decay_ref)]
    for s, out in zip(slots, outs):
        at = pl.multiple_of((rank ^ s) * dk, dk)
        pairs.append((k_in.at[:, pl.ds(at, dk)], out.at[0:tokens, :]))
        for h in range(rep):
            at = pl.multiple_of(((rank ^ s) * rep + h) * dv, dv)
            rows = out.at[(h + 1) * tokens : (h + 2) * tokens, :]
            pairs.append((v_in.at[:, pl.ds(at, dv)], rows))
    copies = [pltpu.make_async_copy(*p, sems.at[n]) for n, p in enumerate(pairs)]
    for copy in copies:
        copy.start()
    copies[0].wait()
    copies[1].wait()
    for s, out in zip(slots, outs):
        rows = [slot_rows(ref, rank, [s], rep) for ref in (rate_ref, decay_ref)]
        terms = [t.astype(F32) for t in parts(jnp.concatenate(rows, axis=0))]
        terms.append(jnp.zeros((PAD - 6 * rep, tokens), F32))
        out[(rep + 1) * tokens :, :] = jnp.concatenate(terms, axis=0).astype(BF16)
    for copy in copies[2:]:
        copy.wait()


def block_sides(decays, rates, tokens):
    i = iota2((tokens, tokens), 0)
    j = iota2((tokens, tokens), 1)
    lower = (i >= j).astype(F32)
    unit = (i == j).astype(F32)
    cum_rows = exact_dot(decays, lower, ((1,), (1,)))
    cum_cols = exact_dot(lower, decays, ((1,), (1,)))
    rate_cols = exact_dot(unit, rates, ((1,), (1,)))
    return i, j, cum_rows, cum_cols, rate_cols


def solve_blocks(keys, values, sides, rep):
    i, j, cum_rows, cum_cols, rate_cols = sides
    dots = [dot_nt(key, key) for key in keys]
    lows, rhs = [], []
    for n, value in enumerate(values):
        rate = rate_cols[:, n : n + 1]
        cum_col = cum_cols[:, n : n + 1]
        gap = cum_col - cum_rows[n : n + 1, :]
        lows.append(jnp.where(i > j, (rate * dots[n // rep]) * jnp.exp(gap), 0.0))
        rhs.append(
            jnp.concatenate([(rate * jnp.exp(cum_col)) * keys[n // rep], rate * value], axis=1)
        )
    return solve(lows, rhs, i, j)


def owner_body(dk, dv, rep, group, whole, where, *refs):
    slots = flips(group, where[1])
    *packs, _, send_ref, delta_ref, feed_ref, keep_ref, scr = refs
    blocks = len(packs)
    tokens = (packs[0].shape[0] - PAD) // (rep + 1)
    for s, pack in zip(slots, packs):
        scr[where[0] ^ s] = pack[...]
    tails = [scr[c, (rep + 1) * tokens :, :].astype(F32) for c in range(blocks)]
    size = 2 * rep
    tails = [t[0:size] + t[size : 2 * size] + t[2 * size : 3 * size] for t in tails]
    rates = jnp.concatenate([t[0:rep] for t in tails], axis=0)
    decays = jnp.concatenate([t[rep:] for t in tails], axis=0)
    sides = block_sides(decays, rates, tokens)
    cum_rows, cum_cols = sides[2], sides[3]
    keys = [unit_rows(scr[c, 0:tokens, :].astype(F32)) for c in range(blocks)]
    jobs = [(c, h) for c in range(blocks) for h in range(rep)]
    values = [scr[c, (h + 1) * tokens : (h + 2) * tokens, :].astype(F32) for c, h in jobs]
    solved = solve_blocks(keys, values, sides, rep)
    entries = []
    for n, (c, h) in enumerate(jobs):
        last = cum_rows[n : n + 1, tokens - 1 : tokens]
        moved = dot_tn(keys[c] * jnp.exp(last - cum_cols[:, n : n + 1]), solved[n])
        entries.append((jnp.exp(last), moved[:, 0:dk], moved[:, dk:]))
        delta_ref[n] = moved[:, 0:dk].astype(BF16)
        feed_ref[n] = moved[:, dk:]
        keep_ref[n : n + 1, :] = jnp.broadcast_to(jnp.exp(last), (1, keep_ref.shape[1]))
    store_send(send_ref, [fold(entries[h::rep], whole) for h in range(rep)], whole)


def fold(maps, whole):
    while len(maps) > 1:
        maps = [join(maps[n + 1], maps[n], whole or n > 0) for n in range(0, len(maps), 2)]
    return maps[0]


def block_maps(delta_ref, feed_ref, keep_ref, rep):
    maps = [
        (keep_ref[n : n + 1, 0:1], delta_ref[n].astype(F32), feed_ref[n])
        for n in range(delta_ref.shape[0])
    ]
    return [maps[h::rep] for h in range(rep)]


def terms_body(dk, dv, rep, group, where, q_in, k_in, v_in, rate_in, decay_in, *refs):
    slots = flips(group, where[1])
    x_ref, y_ref, q_ref, k_ref, v_ref, rate_ref, decay_ref, sems = refs
    tokens = k_in.shape[0]
    rank = where[0]
    pairs = [(rate_in, rate_ref), (decay_in, decay_ref), (k_in, k_ref), (v_in, v_ref), (q_in, q_ref)]
    copies = [pltpu.make_async_copy(*p, sems.at[n]) for n, p in enumerate(pairs)]
    for copy in copies:
        copy.start()
    copies[0].wait()
    copies[1].wait()
    sides = block_sides(
        slot_rows(decay_ref, rank, slots, rep), slot_rows(rate_ref, rank, slots, rep), tokens
    )
    i, j, cum_rows, cum_cols, _ = sides
    copies[2].wait()
    keys = [key_block(k_ref, rank ^ s, dk) for s in slots]
    copies[3].wait()
    values = []
    for n in range(len(slots) * rep):
        at = pl.multiple_of(((rank ^ slots[n // rep]) * rep + n % rep) * dv, dv)
        values.append(v_ref[:, pl.ds(at, dv)].astype(F32))
    solved = solve_blocks(keys, values, sides, rep)
    copies[4].wait()
    queries = [key_block(q_ref, rank ^ s, dk) * dk**-0.5 for s in slots]
    dots = [dot_nt(query, key) for query, key in zip(queries, keys)]
    for n in range(len(slots) * rep):
        cum_col = cum_cols[:, n : n + 1]
        gap = cum_col - cum_rows[n : n + 1, :]
        scores = jnp.where(i >= j, dots[n // rep] * jnp.exp(gap), 0.0)
        inner = dot(scores, solved[n])
        x_ref[n] = (queries[n // rep] * jnp.exp(cum_col) - inner[:, 0:dk]).astype(BF16)
        y_ref[n] = inner[:, dk:]


def store_maps(ref, entries):
    dk = entries[0][1].shape[0]
    for h, (_, delta, feed) in enumerate(entries):
        rows = slice(h * dk, (h + 1) * dk)
        ref[rows, 0:dk] = delta.astype(BF16)
        ref[rows, dk:] = feed.astype(BF16)
    width = ref.shape[1]
    rows = [jnp.broadcast_to(t.astype(F32), (1, width)) for e in entries for t in parts(e[0])]
    rows.append(jnp.zeros((PAD - len(rows), width), F32))
    ref[len(entries) * dk :, :] = jnp.concatenate(rows, axis=0).astype(BF16)


def load_maps(ref, dk, rep):
    tail = ref[rep * dk :, 0:dk].astype(F32)
    out = []
    for h in range(rep):
        keep = (tail[3 * h : 3 * h + 1] + tail[3 * h + 1 : 3 * h + 2]) + tail[3 * h + 2 : 3 * h + 3]
        rows = slice(h * dk, (h + 1) * dk)
        out.append((keep[:, 0:1], ref[rows, 0:dk].astype(F32), ref[rows, dk:].astype(F32)))
    return out


def pick(flag, yes, no):
    return [tuple(jnp.where(flag == 1, a, b) for a, b in zip(y, n)) for y, n in zip(yes, no)]


def store_send(ref, entries, whole):
    if whole:
        store_maps(ref, entries)
        return
    for h, (_, _, feed) in enumerate(entries):
        ref[h * feed.shape[0] : (h + 1) * feed.shape[0], :] = feed.astype(BF16)


def block_body(dk, rep, step, whole, where, own_ref, came_ref, out_ref):
    own, came = load_maps(own_ref, dk, rep), load_maps(came_ref, dk, rep)
    flag = (where[2] >> step) & 1
    late, early = pick(flag, own, came), pick(flag, came, own)
    store_send(out_ref, [join(l, e, whole) for l, e in zip(late, early)], whole)


def block_entry(dk, rep, group, *came):
    none = jnp.zeros((dk, dk), F32)
    entry = [(jnp.ones((1, 1), F32), none, none) for _ in range(rep)]
    for step, ref in enumerate(came):
        block = load_maps(ref, dk, rep)
        if step > 0:
            block = [join(l, e) for l, e in zip(entry, block)]
        entry = pick((group >> step) & 1, block, entry)
    return entry


def prefix_body(dk, rep, where, delta_ref, feed_ref, keep_ref, *refs):
    *came, a_ref, b_ref = refs
    maps = block_maps(delta_ref, feed_ref, keep_ref, rep)
    unit = (iota2((dk, dk), 0) == iota2((dk, dk), 1)).astype(F32)
    none = jnp.zeros((dk, dk), F32)
    entry = block_entry(dk, rep, where[2], *came)
    states = [jnp.concatenate([k * unit - d, f], axis=1) for k, d, f in entry]
    for c in range(a_ref.shape[0]):
        for h in range(rep):
            a_ref[c, h] = states[h][:, 0:dk].astype(BF16)
            b_ref[c, h] = states[h][:, dk:]
            keep, delta, feed = maps[h][c]
            if c + 1 < a_ref.shape[0]:
                feed = jnp.concatenate([none, feed], axis=1)
                states[h] = advance(keep, delta, feed, states[h])


def enter_body(dk, rep, group, steps, where, a_ref, b_ref, feed_ref, *outs):
    slots = flips(group, where[1])
    late = (where[2] >> (steps - 1)) & 1 if steps else 0
    feed = jnp.where(late == 1, feed_ref[...].astype(F32), 0.0).astype(BF16)
    for s, out in zip(slots, outs):
        for h in range(rep):
            rows = slice(h * dk, (h + 1) * dk)
            at = where[0] ^ s
            out[rows, :] = (dot(a_ref[at, h], feed[rows]) + b_ref[at, h]).astype(BF16)


def project_body(dk, dv, rep, group, at, where, x_ref, y_ref, gate_ref, gain_ref, w_ref, state, *refs):
    slots = flips(group, where[1])
    *before, out_ref, normed_ref = refs
    own = (where[0] ^ slots[at]) * rep
    outs = []
    for h in range(rep):
        n = at * rep + h
        outs.append(dot(x_ref[n], state[h * dk : (h + 1) * dk, :]) + y_ref[n])
    scaled, scales = [], []
    for h, o in enumerate(outs):
        gate = gate_ref[:, pl.ds(pl.multiple_of((own + h) * dv, dv), dv)].astype(F32)
        scales.append(lax.rsqrt(jnp.mean(o * o, axis=-1, keepdims=True) + EPS))
        scaled.append(o * (gain_ref[...] * (gate / (1.0 + jnp.exp(-gate)))))
        normed_ref[:, h * dv : (h + 1) * dv] = (scaled[h] * scales[h]).astype(BF16)
    columns = out_ref.shape[1]
    start = (1 - where[1]) * columns
    step = 256
    for n in range(columns // step):
        at = pl.multiple_of(start + n * step, step)
        cut = slice(n * step, (n + 1) * step)
        total = before[0][:, cut] if before else 0.0
        for h, (piece, scale) in enumerate(zip(scaled, scales)):
            rows = pl.ds(pl.multiple_of((own + h) * dv, dv), dv)
            total = total + scale * dot(piece, w_ref[rows, pl.ds(at, step)])
        out_ref[:, cut] = total.astype(out_ref.dtype)


def own_body(group, where, w_ref, *refs):
    slots = flips(group, where[1])
    *pieces, out_ref = refs
    columns = out_ref.shape[1]
    start = where[1] * columns
    width = pieces[0].shape[1]
    step = 256
    for n in range(columns // step):
        at = pl.multiple_of(start + n * step, step)
        total = 0.0
        for s, piece in zip(slots, pieces):
            rows = pl.ds(pl.multiple_of((where[0] ^ s) * width, width), width)
            total = total + dot(piece[...], w_ref[rows, pl.ds(at, step)])
        out_ref[:, n * step : (n + 1) * step] = total


def per_device(queries, key_rows, values, out_gate, write_rate, log_decay, norm_gain, out_weight):
    tokens = queries.shape[0]
    heads = write_rate.shape[0]
    dv = norm_gain.shape[0]
    dk = dv
    group = queries.shape[1] // dk
    rep = heads // group
    ranks = lax.axis_size("seq")
    halves = lax.axis_size("head")
    groups = ranks // group
    assert ranks % group == 0 and halves == 2
    assert group & (group - 1) == 0 and groups & (groups - 1) == 0
    steps = groups.bit_length() - 1
    columns = out_weight.shape[1] // halves
    shape = jax.ShapeDtypeStruct
    vmem, hbm = pltpu.VMEM, pltpu.HBM
    cube = 2 * tokens * tokens * (dk + dv)
    map_shape = shape((rep * dk + PAD, dk + dv), BF16)
    feed_shape = shape((rep * dk, dv), BF16)

    def swap(x, flip):
        return lax.ppermute(x, "seq", [(i, i ^ flip) for i in range(ranks)])

    def swap_slots(made, order):
        came = [made[0]] + [None] * (group - 1)
        for n in order:
            x, flip = made[n], [tour[n] for tour in tours(group)]
            pairs = [(i * halves + c, (i ^ flip[c]) * halves + c) for i in range(ranks) for c in (0, 1)]
            came[n] = lax.ppermute(x, ("seq", "head"), pairs)
        return came

    q_in, k_in, v_in, rate_in, decay_in = [
        pltpu.with_memory_space_constraint(x, hbm)
        for x in (queries, key_rows, values, write_rate, log_decay)
    ]
    small = [pltpu.VMEM(write_rate.shape, F32), pltpu.VMEM(log_decay.shape, F32)]
    pack_shape = shape(((rep + 1) * tokens + PAD, dk), BF16)
    packs = call(
        placed(functools.partial(pack_body, dk, dv, rep, group), group),
        [pack_shape] * group,
        [hbm] * 4,
        small + [pltpu.SemaphoreType.DMA((2 + (rep + 1) * group,))],
    )(k_in, v_in, rate_in, decay_in)
    packs = swap_slots(packs, range(1, group))
    x, y = call(
        placed(functools.partial(terms_body, dk, dv, rep, group), group),
        [shape((heads, tokens, dk), BF16), shape((heads, tokens, dv), F32)],
        [hbm] * 5,
        [pltpu.VMEM(z.shape, BF16) for z in (queries, key_rows, values)]
        + small
        + [pltpu.SemaphoreType.DMA((5,))],
        heads * 16 * cube,
    )(q_in, k_in, v_in, rate_in, decay_in)
    jobs = group * rep
    send, *blocks = call(
        placed(functools.partial(owner_body, dk, dv, rep, group, steps > 1), group),
        [
            map_shape if steps > 1 else feed_shape,
            shape((jobs, dk, dk), BF16),
            shape((jobs, dk, dv), F32),
            shape((jobs, dk), F32),
        ],
        [vmem] * group + [pl.ANY],
        [pltpu.VMEM((group,) + pack_shape.shape, BF16)],
        jobs * 16 * cube,
    )(*packs, y)

    came, feed = [], send
    for step in range(steps):
        got = swap(send, group << step)
        if step == steps - 1:
            feed = got
            continue
        whole = step + 2 < steps
        send = call(
            placed(functools.partial(block_body, dk, rep, step, whole), group),
            map_shape if whole else feed_shape,
            [vmem] * 2,
        )(send, got)
        came.append(got)
    a, b = call(
        placed(functools.partial(prefix_body, dk, rep), group),
        [shape((group, rep, dk, dk), BF16), shape((group, rep, dk, dv), F32)],
        [vmem] * (3 + len(came)),
        (),
        jobs * 4 * cube,
    )(*blocks, *came)
    states = call(
        placed(functools.partial(enter_body, dk, rep, group, steps), group),
        [feed_shape] * group,
        [vmem] * 3,
        (),
        cube * jobs,
    )(a, b, feed)
    last = list(range(1, group))
    states = swap_slots(states, last)

    work = 2 * tokens * columns * heads * dv
    away, normed = [], [None] * group
    for n in [0] + last:
        state, kind = states[n], F32 if n != last[-1] else BF16
        total, piece = call(
            placed(functools.partial(project_body, dk, dv, rep, group, n), group),
            [shape((tokens, columns), kind), shape((tokens, rep * dv), BF16)],
            [vmem] * (6 + len(away)),
            (),
            work // group,
        )(x, y, out_gate, norm_gain.reshape(1, dv), out_weight, state, *away)
        away = [total]
        normed[n] = piece
    came = lax.ppermute(away[0], "head", [(0, 1), (1, 0)])
    own = call(placed(functools.partial(own_body, group), group), shape((tokens, columns), F32), [vmem] * (1 + group), (), work)(
        out_weight, *normed
    )
    return (own + came.astype(F32)).astype(BF16)


def solution(mesh):
    return jax.shard_map(
        per_device,
        mesh=mesh,
        in_specs=(
            P("seq", "head"),
            P("seq", "head"),
            P("seq", "head"),
            P("seq", "head"),
            P("head", "seq"),
            P("head", "seq"),
            P(),
            P("head", None),
        ),
        out_specs=P("seq", "head"),
        check_vma=False,
    )
```

```python
import functools

import jax
import jax.numpy as jnp
from jax import lax
from jax.experimental import pallas as pl
from jax.experimental.pallas import tpu as pltpu
from jax.sharding import PartitionSpec as P

F32 = jnp.float32
BF16 = jnp.bfloat16
EPS = 1e-06
LEAF = 16
PAD = 16
SMALL = pltpu.CompilerParams(vmem_limit_bytes=24 * 1024 * 1024)


def dot(a, b):
    return jnp.dot(a.astype(BF16), b.astype(BF16), preferred_element_type=F32)


def dot_nt(a, b):
    return lax.dot_general(
        a.astype(BF16), b.astype(BF16), (((1,), (1,)), ((), ())), preferred_element_type=F32
    )


def dot_tn(a, b):
    return lax.dot_general(
        a.astype(BF16), b.astype(BF16), (((0,), (0,)), ((), ())), preferred_element_type=F32
    )


def exact_dot(a, b, dims):
    return lax.dot_general(
        a, b, (dims, ((), ())), precision=lax.Precision.HIGHEST, preferred_element_type=F32
    )


def parts(x):
    first = x.astype(BF16)
    rest = x - first.astype(F32)
    second = rest.astype(BF16)
    third = (rest - second.astype(F32)).astype(BF16)
    return [first, second, third]


def iota2(shape, dim):
    return lax.broadcasted_iota(jnp.int32, shape, dim)


def call(body, outs, specs, scratch=(), flops=0):
    return pl.pallas_call(
        body,
        out_shape=outs,
        in_specs=[pl.BlockSpec(memory_space=space) for space in specs],
        out_specs=jax.tree.map(lambda _: pl.BlockSpec(memory_space=pltpu.VMEM), outs),
        scratch_shapes=list(scratch),
        compiler_params=SMALL,
        cost_estimate=pl.CostEstimate(flops=flops, bytes_accessed=1 << 20, transcendentals=0),
    )


def unit_rows(x):
    return x * lax.rsqrt(jnp.sum(x * x, axis=-1, keepdims=True) + EPS)


def advance(keep, delta, feed, state):
    return keep * state - dot(delta, state) + feed


def join(late, early, whole=True):
    keep, delta, feed = late
    keep_e, delta_e, feed_e = early
    if not whole:
        return None, None, advance(keep, delta, feed, feed_e)
    dk = delta.shape[1]
    both = dot(delta, jnp.concatenate([delta_e, feed_e], axis=1))
    delta_new = keep * delta_e + keep_e * delta - both[:, 0:dk]
    return keep * keep_e, delta_new, keep * feed_e + feed - both[:, dk:]


def key_block(ref, col, dk):
    return unit_rows(ref[:, pl.ds(pl.multiple_of(col * dk, dk), dk)].astype(F32))


def slot_rows(ref, rank, slots, rep):
    return jnp.concatenate(
        [ref[pl.ds((rank ^ s) * rep + h, 1), :] for s in slots for h in range(rep)], axis=0
    )


def solve(lows, sides, i, j):
    tokens = i.shape[0]
    leaf = (i // LEAF) == (j // LEAF)
    unit = (i == j).astype(F32)
    power = [jnp.where(leaf, low, 0.0) for low in lows]
    inverse = [unit - p for p in power]
    power = [p.astype(BF16) for p in power]
    power = [dot(p, p).astype(BF16) for p in power]
    inverse = neumann(power, inverse, LEAF // 2, 1.0)
    both = [
        dot(t - unit, jnp.concatenate([jnp.where(leaf, 0.0, low), side], axis=1))
        for t, low, side in zip(inverse, lows, sides)
    ]
    power = [
        (jnp.where(leaf, 0.0, low) + b[:, 0:tokens]).astype(BF16) for low, b in zip(lows, both)
    ]
    sides = [side + b[:, tokens:] for side, b in zip(sides, both)]
    return neumann(power, sides, tokens // LEAF, -1.0)


def neumann(power, sides, order, sign):
    width = power[0].shape[1]
    reach = 1
    while 2 * reach < order:
        both = [
            dot(p, jnp.concatenate([p, s.astype(BF16)], axis=1)) for p, s in zip(power, sides)
        ]
        power = [b[:, 0:width].astype(BF16) for b in both]
        sides = [s + sign * b[:, width:] for s, b in zip(sides, both)]
        sign, reach = 1.0, 2 * reach
    return [s + sign * dot(p, s) for p, s in zip(power, sides)]


def tours(group):
    near = [s for s in range(1, group) if s.bit_count() == 1]
    far = sorted((s for s in range(1, group) if s.bit_count() > 1), key=lambda s: -s.bit_count())
    return [0] + far + near, [0] + far + near[::-1]


def flips(group, core):
    even, odd = tours(group)
    return [a if a == b else a + (b - a) * core for a, b in zip(even, odd)]


def placed(body, group):
    def run(*refs):
        index = lax.axis_index("seq")
        spot = (index & (group - 1), lax.axis_index("head"), index >> (group.bit_length() - 1))
        body(spot, *refs)

    return run


def store_rates(out, rate_ref, decay_ref, rank, s, rep):
    tokens = rate_ref.shape[1]
    rows = [slot_rows(ref, rank, [s], rep) for ref in (rate_ref, decay_ref)]
    terms = [t.astype(F32) for t in parts(jnp.concatenate(rows, axis=0))]
    terms.append(jnp.zeros((PAD - 6 * rep, tokens), F32))
    out[(rep + 1) * tokens :, :] = jnp.concatenate(terms, axis=0).astype(BF16)


def pack_body(dk, dv, rep, group, where, k_in, v_in, rate_in, decay_in, *refs):
    slots = flips(group, where[1])
    *outs, rate_ref, decay_ref, sems = refs
    tokens = k_in.shape[0]
    rank = where[0]
    pairs = [(rate_in, rate_ref), (decay_in, decay_ref)]
    for s, out in zip(slots[1:], outs):
        at = pl.multiple_of((rank ^ s) * dk, dk)
        pairs.append((k_in.at[:, pl.ds(at, dk)], out.at[0:tokens, :]))
        for h in range(rep):
            at = pl.multiple_of(((rank ^ s) * rep + h) * dv, dv)
            rows = out.at[(h + 1) * tokens : (h + 2) * tokens, :]
            pairs.append((v_in.at[:, pl.ds(at, dv)], rows))
    copies = [pltpu.make_async_copy(*p, sems.at[n]) for n, p in enumerate(pairs)]
    for copy in copies:
        copy.start()
    copies[0].wait()
    copies[1].wait()
    for s, out in zip(slots[1:], outs):
        store_rates(out, rate_ref, decay_ref, rank, s, rep)
    for copy in copies[2:]:
        copy.wait()


def block_sides(decays, rates, tokens):
    i = iota2((tokens, tokens), 0)
    j = iota2((tokens, tokens), 1)
    lower = (i >= j).astype(F32)
    unit = (i == j).astype(F32)
    cum_rows = exact_dot(decays, lower, ((1,), (1,)))
    cum_cols = exact_dot(lower, decays, ((1,), (1,)))
    rate_cols = exact_dot(unit, rates, ((1,), (1,)))
    return i, j, cum_rows, cum_cols, rate_cols


def solve_blocks(keys, values, sides, rep):
    i, j, cum_rows, cum_cols, rate_cols = sides
    dots = [dot_nt(key, key) for key in keys]
    lows, rhs = [], []
    for n, value in enumerate(values):
        rate = rate_cols[:, n : n + 1]
        cum_col = cum_cols[:, n : n + 1]
        gap = cum_col - cum_rows[n : n + 1, :]
        lows.append(jnp.where(i > j, (rate * dots[n // rep]) * jnp.exp(gap), 0.0))
        rhs.append(
            jnp.concatenate([(rate * jnp.exp(cum_col)) * keys[n // rep], rate * value], axis=1)
        )
    return solve(lows, rhs, i, j)


def owner_body(dk, dv, rep, group, whole, where, *refs):
    slots = flips(group, where[1])
    *packs, _, send_ref, delta_ref, feed_ref, keep_ref, scr = refs
    blocks = len(packs)
    tokens = (packs[0].shape[0] - PAD) // (rep + 1)
    for s, pack in zip(slots, packs):
        scr[where[0] ^ s] = pack[...]
    tails = [scr[c, (rep + 1) * tokens :, :].astype(F32) for c in range(blocks)]
    size = 2 * rep
    tails = [t[0:size] + t[size : 2 * size] + t[2 * size : 3 * size] for t in tails]
    rates = jnp.concatenate([t[0:rep] for t in tails], axis=0)
    decays = jnp.concatenate([t[rep:] for t in tails], axis=0)
    sides = block_sides(decays, rates, tokens)
    cum_rows, cum_cols = sides[2], sides[3]
    keys = [unit_rows(scr[c, 0:tokens, :].astype(F32)) for c in range(blocks)]
    jobs = [(c, h) for c in range(blocks) for h in range(rep)]
    values = [scr[c, (h + 1) * tokens : (h + 2) * tokens, :].astype(F32) for c, h in jobs]
    solved = solve_blocks(keys, values, sides, rep)
    entries = []
    for n, (c, h) in enumerate(jobs):
        last = cum_rows[n : n + 1, tokens - 1 : tokens]
        moved = dot_tn(keys[c] * jnp.exp(last - cum_cols[:, n : n + 1]), solved[n])
        entries.append((jnp.exp(last), moved[:, 0:dk], moved[:, dk:]))
        delta_ref[n] = moved[:, 0:dk].astype(BF16)
        feed_ref[n] = moved[:, dk:]
        keep_ref[n : n + 1, :] = jnp.broadcast_to(jnp.exp(last), (1, keep_ref.shape[1]))
    store_send(send_ref, [fold(entries[h::rep], whole) for h in range(rep)], whole)


def fold(maps, whole):
    while len(maps) > 1:
        maps = [join(maps[n + 1], maps[n], whole or n > 0) for n in range(0, len(maps), 2)]
    return maps[0]


def block_maps(delta_ref, feed_ref, keep_ref, rep):
    maps = [
        (keep_ref[n : n + 1, 0:1], delta_ref[n].astype(F32), feed_ref[n])
        for n in range(delta_ref.shape[0])
    ]
    return [maps[h::rep] for h in range(rep)]


def terms_body(dk, dv, rep, group, where, q_in, k_in, v_in, rate_in, decay_in, *refs):
    slots = flips(group, where[1])
    x_ref, y_ref, own_ref, q_ref, k_ref, v_ref, rate_ref, decay_ref, sems = refs
    tokens = k_in.shape[0]
    rank = where[0]
    pairs = [(rate_in, rate_ref), (decay_in, decay_ref), (k_in, k_ref), (v_in, v_ref), (q_in, q_ref)]
    copies = [pltpu.make_async_copy(*p, sems.at[n]) for n, p in enumerate(pairs)]
    for copy in copies:
        copy.start()
    copies[0].wait()
    copies[1].wait()
    sides = block_sides(
        slot_rows(decay_ref, rank, slots, rep), slot_rows(rate_ref, rank, slots, rep), tokens
    )
    i, j, cum_rows, cum_cols, _ = sides
    copies[2].wait()
    keys = [key_block(k_ref, rank ^ s, dk) for s in slots]
    copies[3].wait()
    values = []
    for n in range(len(slots) * rep):
        at = pl.multiple_of(((rank ^ slots[n // rep]) * rep + n % rep) * dv, dv)
        values.append(v_ref[:, pl.ds(at, dv)].astype(F32))
    solved = solve_blocks(keys, values, sides, rep)
    own_ref[0:tokens, :] = k_ref[:, pl.ds(pl.multiple_of(rank * dk, dk), dk)]
    for h in range(rep):
        at = pl.multiple_of((rank * rep + h) * dv, dv)
        own_ref[(h + 1) * tokens : (h + 2) * tokens, :] = v_ref[:, pl.ds(at, dv)]
    store_rates(own_ref, rate_ref, decay_ref, rank, 0, rep)
    copies[4].wait()
    queries = [key_block(q_ref, rank ^ s, dk) * dk**-0.5 for s in slots]
    dots = [dot_nt(query, key) for query, key in zip(queries, keys)]
    for n in range(len(slots) * rep):
        cum_col = cum_cols[:, n : n + 1]
        gap = cum_col - cum_rows[n : n + 1, :]
        scores = jnp.where(i >= j, dots[n // rep] * jnp.exp(gap), 0.0)
        inner = dot(scores, solved[n])
        x_ref[n] = (queries[n // rep] * jnp.exp(cum_col) - inner[:, 0:dk]).astype(BF16)
        y_ref[n] = inner[:, dk:]


def store_maps(ref, entries):
    dk = entries[0][1].shape[0]
    for h, (_, delta, feed) in enumerate(entries):
        rows = slice(h * dk, (h + 1) * dk)
        ref[rows, 0:dk] = delta.astype(BF16)
        ref[rows, dk:] = feed.astype(BF16)
    width = ref.shape[1]
    rows = [jnp.broadcast_to(t.astype(F32), (1, width)) for e in entries for t in parts(e[0])]
    rows.append(jnp.zeros((PAD - len(rows), width), F32))
    ref[len(entries) * dk :, :] = jnp.concatenate(rows, axis=0).astype(BF16)


def load_maps(ref, dk, rep):
    tail = ref[rep * dk :, 0:dk].astype(F32)
    out = []
    for h in range(rep):
        keep = (tail[3 * h : 3 * h + 1] + tail[3 * h + 1 : 3 * h + 2]) + tail[3 * h + 2 : 3 * h + 3]
        rows = slice(h * dk, (h + 1) * dk)
        out.append((keep[:, 0:1], ref[rows, 0:dk].astype(F32), ref[rows, dk:].astype(F32)))
    return out


def pick(flag, yes, no):
    return [tuple(jnp.where(flag == 1, a, b) for a, b in zip(y, n)) for y, n in zip(yes, no)]


def store_send(ref, entries, whole):
    if whole:
        store_maps(ref, entries)
        return
    for h, (_, _, feed) in enumerate(entries):
        ref[h * feed.shape[0] : (h + 1) * feed.shape[0], :] = feed.astype(BF16)


def block_body(dk, rep, step, whole, where, own_ref, came_ref, out_ref):
    own, came = load_maps(own_ref, dk, rep), load_maps(came_ref, dk, rep)
    flag = (where[2] >> step) & 1
    late, early = pick(flag, own, came), pick(flag, came, own)
    store_send(out_ref, [join(l, e, whole) for l, e in zip(late, early)], whole)


def block_entry(dk, rep, group, *came):
    none = jnp.zeros((dk, dk), F32)
    entry = [(jnp.ones((1, 1), F32), none, none) for _ in range(rep)]
    for step, ref in enumerate(came):
        block = load_maps(ref, dk, rep)
        if step > 0:
            block = [join(l, e) for l, e in zip(entry, block)]
        entry = pick((group >> step) & 1, block, entry)
    return entry


def prefix_body(dk, rep, where, delta_ref, feed_ref, keep_ref, *refs):
    *came, a_ref, b_ref = refs
    maps = block_maps(delta_ref, feed_ref, keep_ref, rep)
    unit = (iota2((dk, dk), 0) == iota2((dk, dk), 1)).astype(F32)
    none = jnp.zeros((dk, dk), F32)
    entry = block_entry(dk, rep, where[2], *came)
    states = [jnp.concatenate([k * unit - d, f], axis=1) for k, d, f in entry]
    for c in range(a_ref.shape[0]):
        for h in range(rep):
            a_ref[c, h] = states[h][:, 0:dk].astype(BF16)
            b_ref[c, h] = states[h][:, dk:]
            keep, delta, feed = maps[h][c]
            if c + 1 < a_ref.shape[0]:
                feed = jnp.concatenate([none, feed], axis=1)
                states[h] = advance(keep, delta, feed, states[h])


def enter_body(dk, rep, group, steps, where, a_ref, b_ref, feed_ref, *outs):
    slots = flips(group, where[1])
    late = (where[2] >> (steps - 1)) & 1 if steps else 0
    feed = jnp.where(late == 1, feed_ref[...].astype(F32), 0.0).astype(BF16)
    for s, out in zip(slots, outs):
        for h in range(rep):
            rows = slice(h * dk, (h + 1) * dk)
            at = where[0] ^ s
            out[rows, :] = (dot(a_ref[at, h], feed[rows]) + b_ref[at, h]).astype(BF16)


def project_body(dk, dv, rep, group, at, where, x_ref, y_ref, gate_ref, gain_ref, w_ref, state, *refs):
    slots = flips(group, where[1])
    *before, out_ref, normed_ref = refs
    own = (where[0] ^ slots[at]) * rep
    outs = []
    for h in range(rep):
        n = at * rep + h
        outs.append(dot(x_ref[n], state[h * dk : (h + 1) * dk, :]) + y_ref[n])
    scaled, scales = [], []
    for h, o in enumerate(outs):
        gate = gate_ref[:, pl.ds(pl.multiple_of((own + h) * dv, dv), dv)].astype(F32)
        scales.append(lax.rsqrt(jnp.mean(o * o, axis=-1, keepdims=True) + EPS))
        scaled.append(o * (gain_ref[...] * (gate / (1.0 + jnp.exp(-gate)))))
        normed_ref[:, h * dv : (h + 1) * dv] = (scaled[h] * scales[h]).astype(BF16)
    columns = out_ref.shape[1]
    start = (1 - where[1]) * columns
    step = 256
    for n in range(columns // step):
        at = pl.multiple_of(start + n * step, step)
        cut = slice(n * step, (n + 1) * step)
        total = before[0][:, cut] if before else 0.0
        for h, (piece, scale) in enumerate(zip(scaled, scales)):
            rows = pl.ds(pl.multiple_of((own + h) * dv, dv), dv)
            total = total + scale * dot(piece, w_ref[rows, pl.ds(at, step)])
        out_ref[:, cut] = total.astype(out_ref.dtype)


def own_body(group, where, w_ref, *refs):
    slots = flips(group, where[1])
    *pieces, out_ref = refs
    columns = out_ref.shape[1]
    start = where[1] * columns
    width = pieces[0].shape[1]
    step = 256
    for n in range(columns // step):
        at = pl.multiple_of(start + n * step, step)
        total = 0.0
        for s, piece in zip(slots, pieces):
            rows = pl.ds(pl.multiple_of((where[0] ^ s) * width, width), width)
            total = total + dot(piece[...], w_ref[rows, pl.ds(at, step)])
        out_ref[:, n * step : (n + 1) * step] = total


def per_device(queries, key_rows, values, out_gate, write_rate, log_decay, norm_gain, out_weight):
    tokens = queries.shape[0]
    heads = write_rate.shape[0]
    dv = norm_gain.shape[0]
    dk = dv
    group = queries.shape[1] // dk
    rep = heads // group
    ranks = lax.axis_size("seq")
    halves = lax.axis_size("head")
    groups = ranks // group
    assert ranks % group == 0 and halves == 2
    assert group & (group - 1) == 0 and groups & (groups - 1) == 0
    steps = groups.bit_length() - 1
    columns = out_weight.shape[1] // halves
    shape = jax.ShapeDtypeStruct
    vmem, hbm = pltpu.VMEM, pltpu.HBM
    cube = 2 * tokens * tokens * (dk + dv)
    map_shape = shape((rep * dk + PAD, dk + dv), BF16)
    feed_shape = shape((rep * dk, dv), BF16)

    def swap(x, flip):
        return lax.ppermute(x, "seq", [(i, i ^ flip) for i in range(ranks)])

    def swap_slots(made, order):
        came = [made[0]] + [None] * (group - 1)
        for n in order:
            x, flip = made[n], [tour[n] for tour in tours(group)]
            pairs = [(i * halves + c, (i ^ flip[c]) * halves + c) for i in range(ranks) for c in (0, 1)]
            came[n] = lax.ppermute(x, ("seq", "head"), pairs)
        return came

    q_in, k_in, v_in, rate_in, decay_in = [
        pltpu.with_memory_space_constraint(x, hbm)
        for x in (queries, key_rows, values, write_rate, log_decay)
    ]
    small = [pltpu.VMEM(write_rate.shape, F32), pltpu.VMEM(log_decay.shape, F32)]
    pack_shape = shape(((rep + 1) * tokens + PAD, dk), BF16)
    packs = call(
        placed(functools.partial(pack_body, dk, dv, rep, group), group),
        [pack_shape] * (group - 1),
        [hbm] * 4,
        small + [pltpu.SemaphoreType.DMA((2 + (rep + 1) * (group - 1),))],
    )(k_in, v_in, rate_in, decay_in)
    packs = swap_slots([None, *packs], range(1, group))
    x, y, packs[0] = call(
        placed(functools.partial(terms_body, dk, dv, rep, group), group),
        [shape((heads, tokens, dk), BF16), shape((heads, tokens, dv), F32), pack_shape],
        [hbm] * 5,
        [pltpu.VMEM(z.shape, BF16) for z in (queries, key_rows, values)]
        + small
        + [pltpu.SemaphoreType.DMA((5,))],
        heads * 16 * cube,
    )(q_in, k_in, v_in, rate_in, decay_in)
    jobs = group * rep
    send, *blocks = call(
        placed(functools.partial(owner_body, dk, dv, rep, group, steps > 1), group),
        [
            map_shape if steps > 1 else feed_shape,
            shape((jobs, dk, dk), BF16),
            shape((jobs, dk, dv), F32),
            shape((jobs, dk), F32),
        ],
        [vmem] * group + [pl.ANY],
        [pltpu.VMEM((group,) + pack_shape.shape, BF16)],
        jobs * 16 * cube,
    )(*packs, y)

    came, feed = [], send
    for step in range(steps):
        got = swap(send, group << step)
        if step == steps - 1:
            feed = got
            continue
        whole = step + 2 < steps
        send = call(
            placed(functools.partial(block_body, dk, rep, step, whole), group),
            map_shape if whole else feed_shape,
            [vmem] * 2,
        )(send, got)
        came.append(got)
    a, b = call(
        placed(functools.partial(prefix_body, dk, rep), group),
        [shape((group, rep, dk, dk), BF16), shape((group, rep, dk, dv), F32)],
        [vmem] * (3 + len(came)),
        (),
        jobs * 4 * cube,
    )(*blocks, *came)
    states = call(
        placed(functools.partial(enter_body, dk, rep, group, steps), group),
        [feed_shape] * group,
        [vmem] * 3,
        (),
        cube * jobs,
    )(a, b, feed)
    last = list(range(1, group))[::-1]
    states = swap_slots(states, last)

    work = 2 * tokens * columns * heads * dv
    away, normed = [], [None] * group
    for n in [0] + last:
        state, kind = states[n], F32 if n != last[-1] else BF16
        total, piece = call(
            placed(functools.partial(project_body, dk, dv, rep, group, n), group),
            [shape((tokens, columns), kind), shape((tokens, rep * dv), BF16)],
            [vmem] * (6 + len(away)),
            (),
            work // group,
        )(x, y, out_gate, norm_gain.reshape(1, dv), out_weight, state, *away)
        away = [total]
        normed[n] = piece
    came = lax.ppermute(away[0], "head", [(0, 1), (1, 0)])
    own = call(placed(functools.partial(own_body, group), group), shape((tokens, columns), F32), [vmem] * (1 + group), (), work)(
        out_weight, *normed
    )
    return (own + came.astype(F32)).astype(BF16)


def solution(mesh):
    return jax.shard_map(
        per_device,
        mesh=mesh,
        in_specs=(
            P("seq", "head"),
            P("seq", "head"),
            P("seq", "head"),
            P("seq", "head"),
            P("head", "seq"),
            P("head", "seq"),
            P(),
            P("head", None),
        ),
        out_specs=P("seq", "head"),
        check_vma=False,
    )
```

```python
import functools

import jax
import jax.numpy as jnp
from jax import lax
from jax.experimental import pallas as pl
from jax.experimental.pallas import tpu as pltpu
from jax.sharding import PartitionSpec as P

F32 = jnp.float32
BF16 = jnp.bfloat16
EPS = 1e-06
LEAF = 16
PAD = 16
SMALL = pltpu.CompilerParams(vmem_limit_bytes=24 * 1024 * 1024)


def dot(a, b):
    return jnp.dot(a.astype(BF16), b.astype(BF16), preferred_element_type=F32)


def dot_nt(a, b):
    return lax.dot_general(
        a.astype(BF16), b.astype(BF16), (((1,), (1,)), ((), ())), preferred_element_type=F32
    )


def dot_tn(a, b):
    return lax.dot_general(
        a.astype(BF16), b.astype(BF16), (((0,), (0,)), ((), ())), preferred_element_type=F32
    )


def exact_dot(a, b, dims):
    return lax.dot_general(
        a, b, (dims, ((), ())), precision=lax.Precision.HIGHEST, preferred_element_type=F32
    )


def parts(x):
    first = x.astype(BF16)
    rest = x - first.astype(F32)
    second = rest.astype(BF16)
    third = (rest - second.astype(F32)).astype(BF16)
    return [first, second, third]


def iota2(shape, dim):
    return lax.broadcasted_iota(jnp.int32, shape, dim)


def call(body, outs, specs, scratch=(), flops=0):
    return pl.pallas_call(
        body,
        out_shape=outs,
        in_specs=[pl.BlockSpec(memory_space=space) for space in specs],
        out_specs=jax.tree.map(lambda _: pl.BlockSpec(memory_space=pltpu.VMEM), outs),
        scratch_shapes=list(scratch),
        compiler_params=SMALL,
        cost_estimate=pl.CostEstimate(flops=flops, bytes_accessed=1 << 20, transcendentals=0),
    )


def unit_rows(x):
    return x * lax.rsqrt(jnp.sum(x * x, axis=-1, keepdims=True) + EPS)


def advance(keep, delta, feed, state):
    return keep * state - dot(delta, state) + feed


def join(late, early, whole=True):
    keep, delta, feed = late
    keep_e, delta_e, feed_e = early
    if not whole:
        return None, None, advance(keep, delta, feed, feed_e)
    dk = delta.shape[1]
    both = dot(delta, jnp.concatenate([delta_e, feed_e], axis=1))
    delta_new = keep * delta_e + keep_e * delta - both[:, 0:dk]
    return keep * keep_e, delta_new, keep * feed_e + feed - both[:, dk:]


def key_block(ref, col, dk):
    return unit_rows(ref[:, pl.ds(pl.multiple_of(col * dk, dk), dk)].astype(F32))


def slot_rows(ref, rank, slots, rep):
    return jnp.concatenate(
        [ref[pl.ds((rank ^ s) * rep + h, 1), :] for s in slots for h in range(rep)], axis=0
    )


def solve(lows, sides, i, j):
    tokens = i.shape[0]
    leaf = (i // LEAF) == (j // LEAF)
    unit = (i == j).astype(F32)
    power = [jnp.where(leaf, low, 0.0) for low in lows]
    inverse = [unit - p for p in power]
    power = [p.astype(BF16) for p in power]
    power = [dot(p, p).astype(BF16) for p in power]
    inverse = neumann(power, inverse, LEAF // 2, 1.0)
    both = [
        dot(t - unit, jnp.concatenate([jnp.where(leaf, 0.0, low), side], axis=1))
        for t, low, side in zip(inverse, lows, sides)
    ]
    power = [
        (jnp.where(leaf, 0.0, low) + b[:, 0:tokens]).astype(BF16) for low, b in zip(lows, both)
    ]
    sides = [side + b[:, tokens:] for side, b in zip(sides, both)]
    return neumann(power, sides, tokens // LEAF, -1.0)


def neumann(power, sides, order, sign):
    width = power[0].shape[1]
    reach = 1
    while 2 * reach < order:
        both = [
            dot(p, jnp.concatenate([p, s.astype(BF16)], axis=1)) for p, s in zip(power, sides)
        ]
        power = [b[:, 0:width].astype(BF16) for b in both]
        sides = [s + sign * b[:, width:] for s, b in zip(sides, both)]
        sign, reach = 1.0, 2 * reach
    return [s + sign * dot(p, s) for p, s in zip(power, sides)]


def tours(group):
    near = [s for s in range(1, group) if s.bit_count() == 1]
    far = sorted((s for s in range(1, group) if s.bit_count() > 1), key=lambda s: -s.bit_count())
    return [0] + far + near, [0] + far + near[::-1]


def flips(group, core):
    even, odd = tours(group)
    return [a if a == b else a + (b - a) * core for a, b in zip(even, odd)]


def placed(body, group):
    def run(*refs):
        index = lax.axis_index("seq")
        spot = (index & (group - 1), lax.axis_index("head"), index >> (group.bit_length() - 1))
        body(spot, *refs)

    return run


def store_rates(out, rate_ref, decay_ref, rank, s, rep):
    tokens = rate_ref.shape[1]
    rows = [slot_rows(ref, rank, [s], rep) for ref in (rate_ref, decay_ref)]
    terms = [t.astype(F32) for t in parts(jnp.concatenate(rows, axis=0))]
    terms.append(jnp.zeros((PAD - 6 * rep, tokens), F32))
    out[(rep + 1) * tokens :, :] = jnp.concatenate(terms, axis=0).astype(BF16)


def pack_body(dk, dv, rep, group, where, k_in, v_in, rate_in, decay_in, *refs):
    slots = flips(group, where[1])
    *outs, rate_ref, decay_ref, sems = refs
    tokens = k_in.shape[0]
    rank = where[0]
    pairs = [(rate_in, rate_ref), (decay_in, decay_ref)]
    for s, out in zip(slots[1:], outs):
        at = pl.multiple_of((rank ^ s) * dk, dk)
        pairs.append((k_in.at[:, pl.ds(at, dk)], out.at[0:tokens, :]))
        for h in range(rep):
            at = pl.multiple_of(((rank ^ s) * rep + h) * dv, dv)
            rows = out.at[(h + 1) * tokens : (h + 2) * tokens, :]
            pairs.append((v_in.at[:, pl.ds(at, dv)], rows))
    copies = [pltpu.make_async_copy(*p, sems.at[n]) for n, p in enumerate(pairs)]
    for copy in copies:
        copy.start()
    copies[0].wait()
    copies[1].wait()
    for s, out in zip(slots[1:], outs):
        store_rates(out, rate_ref, decay_ref, rank, s, rep)
    for copy in copies[2:]:
        copy.wait()


def block_sides(decays, rates, tokens):
    i = iota2((tokens, tokens), 0)
    j = iota2((tokens, tokens), 1)
    lower = (i >= j).astype(F32)
    unit = (i == j).astype(F32)
    cum_rows = exact_dot(decays, lower, ((1,), (1,)))
    cum_cols = exact_dot(lower, decays, ((1,), (1,)))
    rate_cols = exact_dot(unit, rates, ((1,), (1,)))
    return i, j, cum_rows, cum_cols, rate_cols


def solve_blocks(keys, values, sides, rep):
    i, j, cum_rows, cum_cols, rate_cols = sides
    dots = [dot_nt(key, key) for key in keys]
    lows, rhs = [], []
    for n, value in enumerate(values):
        rate = rate_cols[:, n : n + 1]
        cum_col = cum_cols[:, n : n + 1]
        gap = cum_col - cum_rows[n : n + 1, :]
        lows.append(jnp.where(i > j, (rate * dots[n // rep]) * jnp.exp(gap), 0.0))
        rhs.append(
            jnp.concatenate([(rate * jnp.exp(cum_col)) * keys[n // rep], rate * value], axis=1)
        )
    return solve(lows, rhs, i, j)


def owner_body(dk, dv, rep, group, whole, where, *refs):
    slots = flips(group, where[1])
    *packs, _, send_ref, delta_ref, feed_ref, keep_ref, scr = refs
    blocks = len(packs)
    tokens = (packs[0].shape[0] - PAD) // (rep + 1)
    for s, pack in zip(slots, packs):
        scr[where[0] ^ s] = pack[...]
    tails = [scr[c, (rep + 1) * tokens :, :].astype(F32) for c in range(blocks)]
    size = 2 * rep
    tails = [t[0:size] + t[size : 2 * size] + t[2 * size : 3 * size] for t in tails]
    rates = jnp.concatenate([t[0:rep] for t in tails], axis=0)
    decays = jnp.concatenate([t[rep:] for t in tails], axis=0)
    sides = block_sides(decays, rates, tokens)
    cum_rows, cum_cols = sides[2], sides[3]
    keys = [unit_rows(scr[c, 0:tokens, :].astype(F32)) for c in range(blocks)]
    jobs = [(c, h) for c in range(blocks) for h in range(rep)]
    values = [scr[c, (h + 1) * tokens : (h + 2) * tokens, :].astype(F32) for c, h in jobs]
    solved = solve_blocks(keys, values, sides, rep)
    entries = []
    for n, (c, h) in enumerate(jobs):
        last = cum_rows[n : n + 1, tokens - 1 : tokens]
        moved = dot_tn(keys[c] * jnp.exp(last - cum_cols[:, n : n + 1]), solved[n])
        entries.append((jnp.exp(last), moved[:, 0:dk], moved[:, dk:]))
        delta_ref[n] = moved[:, 0:dk].astype(BF16)
        feed_ref[n] = moved[:, dk:]
        keep_ref[n : n + 1, :] = jnp.broadcast_to(jnp.exp(last), (1, keep_ref.shape[1]))
    store_send(send_ref, [fold(entries[h::rep], whole) for h in range(rep)], whole)


def fold(maps, whole):
    while len(maps) > 1:
        maps = [join(maps[n + 1], maps[n], whole or n > 0) for n in range(0, len(maps), 2)]
    return maps[0]


def block_maps(delta_ref, feed_ref, keep_ref, rep):
    maps = [
        (keep_ref[n : n + 1, 0:1], delta_ref[n].astype(F32), feed_ref[n])
        for n in range(delta_ref.shape[0])
    ]
    return [maps[h::rep] for h in range(rep)]


def terms_body(dk, dv, rep, group, where, q_in, k_in, v_in, rate_in, decay_in, *refs):
    slots = flips(group, where[1])
    x_ref, y_ref, own_ref, q_ref, k_ref, v_ref, rate_ref, decay_ref, sems = refs
    tokens = k_in.shape[0]
    rank = where[0]
    pairs = [(rate_in, rate_ref), (decay_in, decay_ref), (k_in, k_ref), (v_in, v_ref), (q_in, q_ref)]
    copies = [pltpu.make_async_copy(*p, sems.at[n]) for n, p in enumerate(pairs)]
    for copy in copies:
        copy.start()
    copies[0].wait()
    copies[1].wait()
    sides = block_sides(
        slot_rows(decay_ref, rank, slots, rep), slot_rows(rate_ref, rank, slots, rep), tokens
    )
    i, j, cum_rows, cum_cols, _ = sides
    copies[2].wait()
    keys = [key_block(k_ref, rank ^ s, dk) for s in slots]
    copies[3].wait()
    values = []
    for n in range(len(slots) * rep):
        at = pl.multiple_of(((rank ^ slots[n // rep]) * rep + n % rep) * dv, dv)
        values.append(v_ref[:, pl.ds(at, dv)].astype(F32))
    solved = solve_blocks(keys, values, sides, rep)
    own_ref[0:tokens, :] = k_ref[:, pl.ds(pl.multiple_of(rank * dk, dk), dk)]
    for h in range(rep):
        at = pl.multiple_of((rank * rep + h) * dv, dv)
        own_ref[(h + 1) * tokens : (h + 2) * tokens, :] = v_ref[:, pl.ds(at, dv)]
    store_rates(own_ref, rate_ref, decay_ref, rank, 0, rep)
    copies[4].wait()
    queries = [key_block(q_ref, rank ^ s, dk) * dk**-0.5 for s in slots]
    dots = [dot_nt(query, key) for query, key in zip(queries, keys)]
    for n in range(len(slots) * rep):
        cum_col = cum_cols[:, n : n + 1]
        gap = cum_col - cum_rows[n : n + 1, :]
        scores = jnp.where(i >= j, dots[n // rep] * jnp.exp(gap), 0.0)
        inner = dot(scores, solved[n])
        x_ref[n] = (queries[n // rep] * jnp.exp(cum_col) - inner[:, 0:dk]).astype(BF16)
        y_ref[n] = inner[:, dk:]


def store_maps(ref, entries):
    dk = entries[0][1].shape[0]
    for h, (_, delta, feed) in enumerate(entries):
        rows = slice(h * dk, (h + 1) * dk)
        ref[rows, 0:dk] = delta.astype(BF16)
        ref[rows, dk:] = feed.astype(BF16)
    width = ref.shape[1]
    rows = [jnp.broadcast_to(t.astype(F32), (1, width)) for e in entries for t in parts(e[0])]
    rows.append(jnp.zeros((PAD - len(rows), width), F32))
    ref[len(entries) * dk :, :] = jnp.concatenate(rows, axis=0).astype(BF16)


def load_maps(ref, dk, rep):
    tail = ref[rep * dk :, 0:dk].astype(F32)
    out = []
    for h in range(rep):
        keep = (tail[3 * h : 3 * h + 1] + tail[3 * h + 1 : 3 * h + 2]) + tail[3 * h + 2 : 3 * h + 3]
        rows = slice(h * dk, (h + 1) * dk)
        out.append((keep[:, 0:1], ref[rows, 0:dk].astype(F32), ref[rows, dk:].astype(F32)))
    return out


def pick(flag, yes, no):
    return [tuple(jnp.where(flag == 1, a, b) for a, b in zip(y, n)) for y, n in zip(yes, no)]


def store_send(ref, entries, whole):
    if whole:
        store_maps(ref, entries)
        return
    for h, (_, _, feed) in enumerate(entries):
        ref[h * feed.shape[0] : (h + 1) * feed.shape[0], :] = feed.astype(BF16)


def block_body(dk, rep, step, whole, where, own_ref, came_ref, out_ref):
    own, came = load_maps(own_ref, dk, rep), load_maps(came_ref, dk, rep)
    flag = (where[2] >> step) & 1
    late, early = pick(flag, own, came), pick(flag, came, own)
    store_send(out_ref, [join(l, e, whole) for l, e in zip(late, early)], whole)


def block_entry(dk, rep, group, *came):
    none = jnp.zeros((dk, dk), F32)
    entry = [(jnp.ones((1, 1), F32), none, none) for _ in range(rep)]
    for step, ref in enumerate(came):
        block = load_maps(ref, dk, rep)
        if step > 0:
            block = [join(l, e) for l, e in zip(entry, block)]
        entry = pick((group >> step) & 1, block, entry)
    return entry


def prefix_body(dk, rep, where, delta_ref, feed_ref, keep_ref, *refs):
    *came, a_ref, b_ref = refs
    maps = block_maps(delta_ref, feed_ref, keep_ref, rep)
    unit = (iota2((dk, dk), 0) == iota2((dk, dk), 1)).astype(F32)
    none = jnp.zeros((dk, dk), F32)
    entry = block_entry(dk, rep, where[2], *came)
    states = [jnp.concatenate([k * unit - d, f], axis=1) for k, d, f in entry]
    for c in range(a_ref.shape[0]):
        for h in range(rep):
            a_ref[c, h] = states[h][:, 0:dk].astype(BF16)
            b_ref[c, h] = states[h][:, dk:]
            keep, delta, feed = maps[h][c]
            if c + 1 < a_ref.shape[0]:
                feed = jnp.concatenate([none, feed], axis=1)
                states[h] = advance(keep, delta, feed, states[h])


def enter_body(dk, rep, group, steps, where, a_ref, b_ref, feed_ref, *outs):
    slots = flips(group, where[1])
    late = (where[2] >> (steps - 1)) & 1 if steps else 0
    feed = jnp.where(late == 1, feed_ref[...].astype(F32), 0.0).astype(BF16)
    for s, out in zip(slots, outs):
        for h in range(rep):
            rows = slice(h * dk, (h + 1) * dk)
            at = where[0] ^ s
            out[rows, :] = (dot(a_ref[at, h], feed[rows]) + b_ref[at, h]).astype(BF16)


def project_body(dk, dv, rep, group, at, where, x_ref, y_ref, gate_ref, gain_ref, w_ref, state, *refs):
    slots = flips(group, where[1])
    *before, out_ref, normed_ref = refs
    own = (where[0] ^ slots[at]) * rep
    outs = []
    for h in range(rep):
        n = at * rep + h
        outs.append(dot(x_ref[n], state[h * dk : (h + 1) * dk, :]) + y_ref[n])
    scaled, scales = [], []
    for h, o in enumerate(outs):
        gate = gate_ref[:, pl.ds(pl.multiple_of((own + h) * dv, dv), dv)].astype(F32)
        scales.append(lax.rsqrt(jnp.mean(o * o, axis=-1, keepdims=True) + EPS))
        scaled.append(o * (gain_ref[...] * (gate / (1.0 + jnp.exp(-gate)))))
        normed_ref[:, h * dv : (h + 1) * dv] = (scaled[h] * scales[h]).astype(BF16)
    columns = out_ref.shape[1]
    start = (1 - where[1]) * columns
    step = 512
    for n in range(columns // step):
        at = pl.multiple_of(start + n * step, step)
        cut = slice(n * step, (n + 1) * step)
        total = before[0][:, cut] if before else 0.0
        for h, (piece, scale) in enumerate(zip(scaled, scales)):
            rows = pl.ds(pl.multiple_of((own + h) * dv, dv), dv)
            total = total + scale * dot(piece, w_ref[rows, pl.ds(at, step)])
        out_ref[:, cut] = total.astype(out_ref.dtype)


def own_body(group, where, w_ref, *refs):
    slots = flips(group, where[1])
    *pieces, out_ref = refs
    columns = out_ref.shape[1]
    start = where[1] * columns
    width = pieces[0].shape[1]
    step = 512
    for n in range(columns // step):
        at = pl.multiple_of(start + n * step, step)
        total = 0.0
        for s, piece in zip(slots, pieces):
            rows = pl.ds(pl.multiple_of((where[0] ^ s) * width, width), width)
            total = total + dot(piece[...], w_ref[rows, pl.ds(at, step)])
        out_ref[:, n * step : (n + 1) * step] = total


def per_device(queries, key_rows, values, out_gate, write_rate, log_decay, norm_gain, out_weight):
    tokens = queries.shape[0]
    heads = write_rate.shape[0]
    dv = norm_gain.shape[0]
    dk = dv
    group = queries.shape[1] // dk
    rep = heads // group
    ranks = lax.axis_size("seq")
    halves = lax.axis_size("head")
    groups = ranks // group
    assert ranks % group == 0 and halves == 2
    assert group & (group - 1) == 0 and groups & (groups - 1) == 0
    steps = groups.bit_length() - 1
    columns = out_weight.shape[1] // halves
    shape = jax.ShapeDtypeStruct
    vmem, hbm = pltpu.VMEM, pltpu.HBM
    cube = 2 * tokens * tokens * (dk + dv)
    map_shape = shape((rep * dk + PAD, dk + dv), BF16)
    feed_shape = shape((rep * dk, dv), BF16)

    def swap(x, flip):
        return lax.ppermute(x, "seq", [(i, i ^ flip) for i in range(ranks)])

    def swap_slots(made, order):
        came = [made[0]] + [None] * (group - 1)
        for n in order:
            x, flip = made[n], [tour[n] for tour in tours(group)]
            pairs = [(i * halves + c, (i ^ flip[c]) * halves + c) for i in range(ranks) for c in (0, 1)]
            came[n] = lax.ppermute(x, ("seq", "head"), pairs)
        return came

    q_in, k_in, v_in, rate_in, decay_in = [
        pltpu.with_memory_space_constraint(x, hbm)
        for x in (queries, key_rows, values, write_rate, log_decay)
    ]
    small = [pltpu.VMEM(write_rate.shape, F32), pltpu.VMEM(log_decay.shape, F32)]
    pack_shape = shape(((rep + 1) * tokens + PAD, dk), BF16)
    packs = call(
        placed(functools.partial(pack_body, dk, dv, rep, group), group),
        [pack_shape] * (group - 1),
        [hbm] * 4,
        small + [pltpu.SemaphoreType.DMA((2 + (rep + 1) * (group - 1),))],
    )(k_in, v_in, rate_in, decay_in)
    packs = swap_slots([None, *packs], range(1, group))
    x, y, packs[0] = call(
        placed(functools.partial(terms_body, dk, dv, rep, group), group),
        [shape((heads, tokens, dk), BF16), shape((heads, tokens, dv), F32), pack_shape],
        [hbm] * 5,
        [pltpu.VMEM(z.shape, BF16) for z in (queries, key_rows, values)]
        + small
        + [pltpu.SemaphoreType.DMA((5,))],
        heads * 16 * cube,
    )(q_in, k_in, v_in, rate_in, decay_in)
    jobs = group * rep
    send, *blocks = call(
        placed(functools.partial(owner_body, dk, dv, rep, group, steps > 1), group),
        [
            map_shape if steps > 1 else feed_shape,
            shape((jobs, dk, dk), BF16),
            shape((jobs, dk, dv), F32),
            shape((jobs, dk), F32),
        ],
        [vmem] * group + [pl.ANY],
        [pltpu.VMEM((group,) + pack_shape.shape, BF16)],
        jobs * 16 * cube,
    )(*packs, y)

    came, feed = [], send
    for step in range(steps):
        got = swap(send, group << step)
        if step == steps - 1:
            feed = got
            continue
        whole = step + 2 < steps
        send = call(
            placed(functools.partial(block_body, dk, rep, step, whole), group),
            map_shape if whole else feed_shape,
            [vmem] * 2,
        )(send, got)
        came.append(got)
    a, b = call(
        placed(functools.partial(prefix_body, dk, rep), group),
        [shape((group, rep, dk, dk), BF16), shape((group, rep, dk, dv), F32)],
        [vmem] * (3 + len(came)),
        (),
        jobs * 4 * cube,
    )(*blocks, *came)
    states = call(
        placed(functools.partial(enter_body, dk, rep, group, steps), group),
        [feed_shape] * group,
        [vmem] * 3,
        (),
        cube * jobs,
    )(a, b, feed)
    last = list(range(1, group))[::-1]
    states = swap_slots(states, last)

    work = 2 * tokens * columns * heads * dv
    away, normed = [], [None] * group
    for n in [0] + last:
        state, kind = states[n], F32 if n != last[-1] else BF16
        total, piece = call(
            placed(functools.partial(project_body, dk, dv, rep, group, n), group),
            [shape((tokens, columns), kind), shape((tokens, rep * dv), BF16)],
            [vmem] * (6 + len(away)),
            (),
            work // group,
        )(x, y, out_gate, norm_gain.reshape(1, dv), out_weight, state, *away)
        away = [total]
        normed[n] = piece
    came = lax.ppermute(away[0], "head", [(0, 1), (1, 0)])
    own = call(placed(functools.partial(own_body, group), group), shape((tokens, columns), F32), [vmem] * (1 + group), (), work)(
        out_weight, *normed
    )
    return (own + came.astype(F32)).astype(BF16)


def solution(mesh):
    return jax.shard_map(
        per_device,
        mesh=mesh,
        in_specs=(
            P("seq", "head"),
            P("seq", "head"),
            P("seq", "head"),
            P("seq", "head"),
            P("head", "seq"),
            P("head", "seq"),
            P(),
            P("head", None),
        ),
        out_specs=P("seq", "head"),
        check_vma=False,
    )
```
